32 devices in a mesh: row: 8 (over z, x), panel: 4 (over y, core).
Axes of the slice: x: 2, y: 2, z: 4, core: 2. Of those that a mesh axis runs over, the one named last changes fastest.
Arguments:
- pixel_ids: int32 [8192], P('row'), may hold values from 0 to 8191, each once
- quad_offsets: int32 [2, 16, 8192], P(None, None, 'row'), may hold values from 0 to 7
- prior_factor: float32 [8192, 2048], P('row', 'panel'), may hold values from -0.036 to 0.036, as said below
Outputs:
- panel_factor: float32 [8192, 1024], P(('row', 'panel'))
The draws below stay inside these ranges and needn't reach their ends.
Inputs may be any that keep to these rules, and one draw needn't show every extreme that they name: `pixel_ids`: each pixel of the grid appears in exactly one row. `prior_factor`: schur[panel_index] is positive definite.
All inputs are finite; a program needn't handle non-finite values.
Results may differ from the reference program's by a relative error of at most 0.0003.
Values sent between devices are 32-bit elements; how exact they have to be, the bound alone decides.
No kernel may reach another device: no remote copies, remote signals or barrier semaphores. Data moves between devices by JAX's collectives and lax.ppermute only.
A program may use at most 128 MiB of HBM per device.

```python
import jax
import jax.numpy as jnp
from jax import lax

Q = 16
B = 1024
ROWS = 8192
QUARTER = 256
PANEL_DEV = 32
K0 = 2048


def draw_prior_factor(key, part):
    values = jnp.clip(jax.random.normal(key, (ROWS, K0), jnp.float32), -4.0, 4.0)
    return values * 0.009


def set_ends(values, stream_key, least, high):
    extent = values.shape
    spot = [jax.random.randint(jax.random.fold_in(stream_key, axis), (), 0, extent[axis]) for axis in range(len(extent))]
    values = values.at[tuple(spot)].set(least)
    longest = extent.index(max(extent))
    spot[longest] = (spot[longest] + 1) % extent[longest]
    return values.at[tuple(spot)].set(high)


def setup_inputs(seed: int = 0) -> dict:
    streams_of = jax.random.split(jax.random.key(seed), 4)
    return {
        "pixel_ids": jax.random.permutation(streams_of[0], ROWS).astype(jnp.int32),
        "quad_offsets": set_ends(jax.random.randint(streams_of[1], (2, Q, ROWS), 0, 8), jax.random.fold_in(streams_of[1], 1), 0, 7).astype(jnp.int32),
        "prior_factor": draw_prior_factor(jax.random.fold_in(streams_of[3], 71), 0),
    }


range_inverse = 1.0

def locate(pixel_ids, quad_offsets):
    column = (pixel_ids % 256).astype(jnp.float32)
    lines = (pixel_ids // 256).astype(jnp.float32)
    east = column[None, :] + (quad_offsets[0].astype(jnp.float32) + 0.5) / 8.0
    north = lines[None, :] + (quad_offsets[1].astype(jnp.float32) + 0.5) / 8.0
    return (east, north)

def cover_tile(east_rows, north_rows, east_cols, north_cols):
    count = east_rows.shape[0]

    def accumulate(index, running):
        east_one = lax.dynamic_index_in_dim(east_rows, index, 0, keepdims=False)
        north_one = lax.dynamic_index_in_dim(north_rows, index, 0, keepdims=False)
        apart_east = east_cols[:, :, None] - east_one[None, None, :]
        apart_north = north_cols[:, :, None] - north_one[None, None, :]
        return running + jnp.sum(jnp.exp(-(apart_east * apart_east + apart_north * apart_north) * range_inverse), axis=0)
    start = jnp.zeros((east_cols.shape[1], east_rows.shape[1]), jnp.float32)
    total = lax.fori_loop(0, count, accumulate, start)
    return total.T / float(count * count)

def reference(pixel_ids, quad_offsets, prior_factor):
    east, north = locate(pixel_ids, quad_offsets)
    column_ids = jnp.arange(B, dtype=jnp.int32)
    panel_index = (column_ids // PANEL_DEV * QUARTER + column_ids % PANEL_DEV).astype(jnp.int32)
    east_panel = east[:, panel_index]
    north_panel = north[:, panel_index]
    prior_panel = prior_factor[panel_index]
    blocks = ROWS // QUARTER

    def one_block(block_id):
        first = (block_id * QUARTER).astype(jnp.int32)
        east_rows = lax.dynamic_slice_in_dim(east, first, QUARTER, 1)
        north_rows = lax.dynamic_slice_in_dim(north, first, QUARTER, 1)
        tile = cover_tile(east_rows, north_rows, east_panel, north_panel)
        row_ids = first + jnp.arange(QUARTER, dtype=jnp.int32)
        tile = tile + jnp.where(row_ids[:, None] == panel_index[None, :], 1.0, 0.0).astype(jnp.float32)
        prior_rows = lax.dynamic_slice_in_dim(prior_factor, first, QUARTER, 0)
        update = jnp.dot(prior_rows.astype(jnp.float32), prior_panel.T.astype(jnp.float32), precision=lax.Precision.HIGHEST, preferred_element_type=jnp.float32)
        return tile - update
    schur = lax.map(one_block, jnp.arange(blocks, dtype=jnp.int32)).reshape(ROWS, B)
    diag_factor = jnp.linalg.cholesky(schur[panel_index])
    return lax.linalg.triangular_solve(diag_factor, schur, left_side=False, lower=True, transpose_a=True)
```

```python
import functools

import jax
import jax.numpy as jnp
from jax import lax
from jax.experimental import pallas as pl
from jax.experimental.pallas import tpu as pltpu
from jax.sharding import PartitionSpec as P

B = 1024
NB = 128
GROUP = 8
F32 = jnp.float32
BF = jnp.bfloat16
NT = (((1,), (1,)), ((), ()))
SCALE = -1.4426950408889634 / 64.0
CENTRE = 1024.0


def locate(pixel_ids, quad_offsets):
    column = (pixel_ids % 256) * 8
    lines = (pixel_ids // 256) * 8
    east = (column[None, :] + quad_offsets[0]).astype(F32) - CENTRE
    north = (lines[None, :] + quad_offsets[1]).astype(F32) - CENTRE
    return east, north


def pieces(value):
    high = jnp.floor(value * (1.0 / 65536.0)) * 65536.0
    rest = value - high
    mid = jnp.floor(rest * (1.0 / 256.0)) * 256.0
    return [high, mid, rest - mid]


def halves(value):
    high = jnp.floor(value * (1.0 / 128.0)) * 128.0
    return high, value - high


def row_features(x, y):
    xh, xl = halves(x)
    yh, yl = halves(y)
    one = jnp.ones_like(x)
    zero = jnp.zeros_like(x)
    cross = [-2 * xh, -2 * xh, -2 * xl, -2 * xl, -2 * yh, -2 * yh, -2 * yl, -2 * yl]
    return jnp.concatenate(cross + pieces(x * x + y * y) + [one] * 3 + [zero] * 2, 0)


def col_features(x, y):
    xh, xl = halves(x)
    yh, yl = halves(y)
    one = jnp.ones_like(x)
    zero = jnp.zeros_like(x)
    cross = [xh, xl, xh, xl, yh, yl, yh, yl]
    return jnp.concatenate(cross + [one] * 3 + pieces(x * x + y * y) + [zero] * 2, 0)


def cover_kernel(row_ref, col_ref, o_ref, f_ref, g_ref, *, block):
    count, rows = row_ref.shape[1:]

    for a in range(count):
        one = row_features(row_ref[0, a : a + 1, :], row_ref[1, a : a + 1, :])
        f_ref[a] = one.T.astype(BF)
        g_ref[a] = col_features(col_ref[0, a : a + 1, :], col_ref[1, a : a + 1, :]).astype(BF)

    def tile(index, _):
        first = pl.multiple_of(index * block, block)
        rows_here = jnp.concatenate([f_ref[a, pl.ds(first, block)] for a in range(count)], 0)

        def column_point(b, total):
            apart = jnp.dot(rows_here, g_ref[b], preferred_element_type=F32)
            near = jnp.exp2(apart * SCALE)
            for a in range(count):
                total = total + near[a * block : (a + 1) * block]
            return total

        total = lax.fori_loop(0, count, column_point, jnp.zeros((block, o_ref.shape[1]), F32))
        o_ref[pl.ds(first, block)] = total * (1.0 / (count * count))
        return 0

    lax.fori_loop(0, rows // block, tile, 0)


def cover_rows(row_points, col_points):
    count, rows = row_points.shape[1:]
    cols = col_points.shape[2]
    return pl.pallas_call(
        functools.partial(cover_kernel, block=32),
        out_shape=jax.ShapeDtypeStruct((rows, cols), F32),
        in_specs=[pl.BlockSpec(memory_space=pltpu.VMEM)] * 2,
        out_specs=pl.BlockSpec(memory_space=pltpu.VMEM),
        scratch_shapes=[pltpu.VMEM((count, rows, 16), BF), pltpu.VMEM((count, 16, cols), BF)],
        compiler_params=pltpu.CompilerParams(vmem_limit_bytes=32 << 20),
        name="cover",
    )(row_points, col_points)


def inverse_factor(tiles):
    width = 8 * len(tiles)
    lane = lax.broadcasted_iota(jnp.int32, (8, width), 1)
    sub = lax.broadcasted_iota(jnp.int32, (8, width), 0)
    tiles = list(tiles)
    n = len(tiles)
    out = []
    for v in range(n):
        pivots = jnp.ones((8, width), F32)
        for g in range(0, 8, GROUP):
            cols = [
                [
                    jnp.broadcast_to(tiles[r][:, 8 * v + g + q : 8 * v + g + q + 1], (8, width))
                    for q in range(GROUP)
                ]
                for r in range(v, n)
            ]
            for q in range(GROUP):
                s = g + q
                p = 8 * v + s
                pivot = jnp.broadcast_to(cols[0][q][s : s + 1], (8, width))
                inverse = 1.0 / pivot
                pivots = jnp.where(sub == s, pivot, pivots)
                row = jnp.where(lane == p, 1.0, jnp.broadcast_to(tiles[v][s : s + 1], (8, width)))
                heads = [
                    jnp.broadcast_to(cols[0][k][s : s + 1], (8, width)) for k in range(q + 1, GROUP)
                ]
                for r in range(v, n):
                    part = cols[r - v][q] * inverse
                    if r == v:
                        part = jnp.where(sub > s, part, 0.0)
                    tiles[r] = jnp.where(lane == p, 0.0, tiles[r]) - part * row
                    for k in range(q + 1, GROUP):
                        cols[r - v][k] = cols[r - v][k] - part * heads[k - q - 1]
        row_id = sub + 8 * v
        unit = jnp.where(lane == row_id, 1.0, 0.0)
        out.append(jnp.where(lane < row_id, tiles[v], unit) * lax.rsqrt(pivots))
    return jnp.concatenate(out, 0)


def split(x):
    high = x.astype(BF)
    return high, (x - high.astype(F32)).astype(BF)


def dot3(ah, al, bh, bl):
    dot = functools.partial(lax.dot_general, dimension_numbers=NT, preferred_element_type=F32)
    return dot(ah, bh) + (dot(ah, bl) + dot(al, bh))


def factor_solve_kernel(diag_ref, rest_ref, o_ref, a_ref, high_ref, low_ref):
    n = diag_ref.shape[0]
    m = rest_ref.shape[0]
    a_ref[0:n] = diag_ref[...]
    a_ref[n : n + m] = rest_ref[...]
    blocks = (n + m) // NB

    def step(j, _):
        c = pl.multiple_of(j * NB, NB)
        tiles = [a_ref[pl.ds(c + 8 * v, 8), pl.ds(c, NB)] for v in range(NB // 8)]
        wh, wl = split(inverse_factor(tiles))

        def panel(i, _):
            r = pl.multiple_of(i * NB, NB)
            bh, bl = split(a_ref[pl.ds(r, NB), pl.ds(c, NB)])
            part = dot3(bh, bl, wh, wl)
            a_ref[pl.ds(r, NB), pl.ds(c, NB)] = part
            high, low = split(part)
            high_ref[pl.ds(r, NB)] = high
            low_ref[pl.ds(r, NB)] = low
            return 0

        lax.fori_loop(j + 1, blocks, panel, 0)
        o_ref[:, pl.ds(c, NB)] = a_ref[n : n + m, pl.ds(c, NB)]

        def trail(i, _):
            r = pl.multiple_of(i * NB, NB)
            a_ref[pl.ds(r, NB)] = a_ref[pl.ds(r, NB)] - dot3(
                high_ref[pl.ds(r, NB)], low_ref[pl.ds(r, NB)], high_ref[0:n], low_ref[0:n]
            )
            return 0

        lax.fori_loop(j + 1, blocks, trail, 0)
        return 0

    lax.fori_loop(0, n // NB, step, 0)


def factor_solve(diag_rows, schur):
    n = diag_rows.shape[0]
    m = schur.shape[0]
    return pl.pallas_call(
        factor_solve_kernel,
        out_shape=jax.ShapeDtypeStruct((m, n), F32),
        in_specs=[pl.BlockSpec(memory_space=pltpu.VMEM)] * 2,
        out_specs=pl.BlockSpec(memory_space=pltpu.VMEM),
        scratch_shapes=[
            pltpu.VMEM((n + m, n), F32),
            pltpu.VMEM((n + m, NB), BF),
            pltpu.VMEM((n + m, NB), BF),
        ],
        compiler_params=pltpu.CompilerParams(vmem_limit_bytes=40 << 20),
        name="factor_solve",
    )(diag_rows, schur)


def local(pixel_ids, quad_offsets, prior_factor):
    panel_count = lax.axis_size("panel")
    row_count = lax.axis_size("row")
    block_rows = pixel_ids.shape[0]
    quarter_rows = block_rows // panel_count
    per_device = B // (row_count * panel_count)
    span_cols = panel_count * per_device
    row_pos = lax.axis_index("row")
    panel_pos = lax.axis_index("panel")
    points = jnp.stack(locate(pixel_ids, quad_offsets))
    count = points.shape[1]
    own_points = lax.dynamic_slice_in_dim(points, panel_pos * quarter_rows, quarter_rows, 2)
    local_points = points.reshape(2, count, panel_count, quarter_rows)[:, :, :, :per_device]
    local_points = local_points.reshape(1, 2 * count, span_cols)
    copies = jnp.broadcast_to(local_points, (row_count, 2 * count, span_cols))
    spread = lax.all_to_all(copies, "row", split_axis=0, concat_axis=0, tiled=True)
    panel_points = spread.transpose(1, 0, 2).reshape(2, count, B)
    columns = cover_rows(own_points, panel_points)
    device_pos = row_pos * panel_count + panel_pos
    row_ids = jnp.arange(quarter_rows, dtype=jnp.int32)[:, None]
    col_ids = jnp.arange(B, dtype=jnp.int32)[None, :]
    on_diagonal = (row_ids < per_device) & (col_ids == device_pos * per_device + row_ids)
    cover = columns + jnp.where(on_diagonal, 1.0, 0.0).astype(F32)
    whole_rows = lax.all_to_all(prior_factor, "panel", split_axis=0, concat_axis=1, tiled=True)
    panel_prior = lax.all_gather(whole_rows[:per_device], ("row", "panel"), axis=0, tiled=True)
    update = jnp.dot(
        whole_rows, panel_prior.T, precision=lax.Precision.HIGH, preferred_element_type=F32
    )
    schur = cover - update
    diag_rows = lax.all_gather(schur[:per_device], ("row", "panel"), axis=0, tiled=True)
    return factor_solve(diag_rows, schur)


def solution(mesh):
    return jax.shard_map(
        local,
        mesh=mesh,
        in_specs=(P("row"), P(None, None, "row"), P("row", "panel")),
        out_specs=P(("row", "panel"), None),
        check_vma=False,
    )
```

```python
import functools

import jax
import jax.numpy as jnp
from jax import lax
from jax.experimental import pallas as pl
from jax.experimental.pallas import tpu as pltpu
from jax.sharding import PartitionSpec as P

B = 1024
NB = 128
GROUP = 8
F32 = jnp.float32
BF = jnp.bfloat16
NT = (((1,), (1,)), ((), ()))
SCALE = -1.4426950408889634 / 64.0
CENTRE = 1024.0


def locate(pixel_ids, quad_offsets):
    column = (pixel_ids % 256) * 8
    lines = (pixel_ids // 256) * 8
    east = (column[None, :] + quad_offsets[0]).astype(F32) - CENTRE
    north = (lines[None, :] + quad_offsets[1]).astype(F32) - CENTRE
    return east, north


def pieces(value):
    high = jnp.floor(value * (1.0 / 65536.0)) * 65536.0
    rest = value - high
    mid = jnp.floor(rest * (1.0 / 256.0)) * 256.0
    return [high, mid, rest - mid]


def halves(value):
    high = jnp.floor(value * (1.0 / 128.0)) * 128.0
    return high, value - high


def row_features(x, y):
    xh, xl = halves(x)
    yh, yl = halves(y)
    one = jnp.ones_like(x)
    zero = jnp.zeros_like(x)
    cross = [-2 * xh, -2 * xh, -2 * xl, -2 * xl, -2 * yh, -2 * yh, -2 * yl, -2 * yl]
    return jnp.concatenate(cross + pieces(x * x + y * y) + [one] * 3 + [zero] * 2, 0)


def col_features(x, y):
    xh, xl = halves(x)
    yh, yl = halves(y)
    one = jnp.ones_like(x)
    zero = jnp.zeros_like(x)
    cross = [xh, xl, xh, xl, yh, yl, yh, yl]
    return jnp.concatenate(cross + [one] * 3 + pieces(x * x + y * y) + [zero] * 2, 0)


def feature_kernel(row_ref, col_ref, f_ref, g_ref):
    for a in range(row_ref.shape[1]):
        one = row_features(row_ref[0, a : a + 1, :], row_ref[1, a : a + 1, :])
        f_ref[a] = one.T.astype(BF)
        g_ref[a] = col_features(col_ref[0, a : a + 1, :], col_ref[1, a : a + 1, :]).astype(BF)


def features(row_points, col_points):
    count, rows = row_points.shape[1:]
    cols = col_points.shape[2]
    return pl.pallas_call(
        feature_kernel,
        out_shape=[
            jax.ShapeDtypeStruct((count, rows, 16), BF),
            jax.ShapeDtypeStruct((count, 16, cols), BF),
        ],
        in_specs=[pl.BlockSpec(memory_space=pltpu.VMEM)] * 2,
        out_specs=[pl.BlockSpec(memory_space=pltpu.VMEM)] * 2,
        compiler_params=pltpu.CompilerParams(vmem_limit_bytes=8 << 20),
        name="features",
    )(row_points, col_points)


def cover_kernel(f_ref, g_ref, o_ref):
    count, block = f_ref.shape[:2]
    rows_here = f_ref[...].reshape(count * block, 16)

    def column_point(b, total):
        apart = jnp.dot(rows_here, g_ref[b], preferred_element_type=F32)
        near = jnp.exp2(apart * SCALE)
        for a in range(count):
            total = total + near[a * block : (a + 1) * block]
        return total

    total = lax.fori_loop(0, count, column_point, jnp.zeros(o_ref.shape, F32))
    o_ref[...] = total * (1.0 / (count * count))


def cover_rows(row_part, col_part, first, block):
    count, rows, depth = row_part.shape
    cols = col_part.shape[2]
    index = first // block
    return pl.pallas_call(
        cover_kernel,
        grid=(1,),
        out_shape=jax.ShapeDtypeStruct((block, cols), F32),
        in_specs=[
            pl.BlockSpec((count, block, depth), lambda i: (0, index, 0)),
            pl.BlockSpec((count, depth, cols), lambda i: (0, 0, 0)),
        ],
        out_specs=pl.BlockSpec((block, cols), lambda i: (0, 0)),
        compiler_params=pltpu.CompilerParams(vmem_limit_bytes=16 << 20),
        cost_estimate=pl.CostEstimate(
            flops=7 * 10**9, bytes_accessed=1 << 20, transcendentals=count * count * block * cols
        ),
        name="cover",
    )(row_part, col_part)


def inverse_factor(tiles):
    width = 8 * len(tiles)
    lane = lax.broadcasted_iota(jnp.int32, (8, width), 1)
    sub = lax.broadcasted_iota(jnp.int32, (8, width), 0)
    tiles = list(tiles)
    n = len(tiles)
    out = []
    for v in range(n):
        pivots = jnp.ones((8, width), F32)
        for g in range(0, 8, GROUP):
            cols = [
                [
                    jnp.broadcast_to(tiles[r][:, 8 * v + g + q : 8 * v + g + q + 1], (8, width))
                    for q in range(GROUP)
                ]
                for r in range(v, n)
            ]
            for q in range(GROUP):
                s = g + q
                p = 8 * v + s
                pivot = jnp.broadcast_to(cols[0][q][s : s + 1], (8, width))
                inverse = 1.0 / pivot
                pivots = jnp.where(sub == s, pivot, pivots)
                row = jnp.where(lane == p, 1.0, jnp.broadcast_to(tiles[v][s : s + 1], (8, width)))
                heads = [
                    jnp.broadcast_to(cols[0][k][s : s + 1], (8, width)) for k in range(q + 1, GROUP)
                ]
                for r in range(v, n):
                    part = cols[r - v][q] * inverse
                    if r == v:
                        part = jnp.where(sub > s, part, 0.0)
                    tiles[r] = jnp.where(lane == p, 0.0, tiles[r]) - part * row
                    for k in range(q + 1, GROUP):
                        cols[r - v][k] = cols[r - v][k] - part * heads[k - q - 1]
        row_id = sub + 8 * v
        unit = jnp.where(lane == row_id, 1.0, 0.0)
        out.append(jnp.where(lane < row_id, tiles[v], unit) * lax.rsqrt(pivots))
    return jnp.concatenate(out, 0)


def split(x):
    high = x.astype(BF)
    return high, (x - high.astype(F32)).astype(BF)


def dot3(ah, al, bh, bl):
    dot = functools.partial(lax.dot_general, dimension_numbers=NT, preferred_element_type=F32)
    return dot(ah, bh) + (dot(ah, bl) + dot(al, bh))


def factor_blocks(a_ref, lh_ref, ll_ref, wh_ref, wl_ref):
    n = a_ref.shape[0]
    blocks = n // NB

    def step(j, _):
        c = pl.multiple_of(j * NB, NB)
        tiles = [a_ref[pl.ds(c + 8 * v, 8), pl.ds(c, NB)] for v in range(NB // 8)]
        wh, wl = split(inverse_factor(tiles))
        wh_ref[pl.ds(c, NB)] = wh
        wl_ref[pl.ds(c, NB)] = wl

        def panel(i, _):
            r = pl.multiple_of(i * NB, NB)
            bh, bl = split(a_ref[pl.ds(r, NB), pl.ds(c, NB)])
            high, low = split(dot3(bh, bl, wh, wl))
            lh_ref[pl.ds(r, NB), pl.ds(c, NB)] = high
            ll_ref[pl.ds(r, NB), pl.ds(c, NB)] = low
            return 0

        lax.fori_loop(j + 1, blocks, panel, 0)

        def trail(i, _):
            r = pl.multiple_of(i * NB, NB)
            a_ref[pl.ds(r, NB)] = a_ref[pl.ds(r, NB)] - dot3(
                lh_ref[pl.ds(r, NB), pl.ds(c, NB)],
                ll_ref[pl.ds(r, NB), pl.ds(c, NB)],
                lh_ref[:, pl.ds(c, NB)],
                ll_ref[:, pl.ds(c, NB)],
            )
            return 0

        lax.fori_loop(j + 1, blocks, trail, 0)
        return 0

    lax.fori_loop(0, blocks, step, 0)


def factor_kernel(diag_ref, lh_ref, ll_ref, wh_ref, wl_ref, a_ref):
    a_ref[...] = diag_ref[...]
    lh_ref[...] = jnp.zeros_like(lh_ref)
    ll_ref[...] = jnp.zeros_like(ll_ref)
    factor_blocks(a_ref, lh_ref, ll_ref, wh_ref, wl_ref)


def fold_block(r, k):
    if k < 2:
        return r ^ (4 * k)
    m = k - 1
    low = r & 3
    second = (low >> (m.bit_length() - 1)) & 1
    return (r ^ m) ^ (4 * second)


def unfold_kernel(place_ref, here_ref, there_ref, lh_ref, ll_ref, wh_ref, wl_ref, a_ref):
    row_pos = place_ref[0]
    panel_pos = place_ref[1]
    per_device = here_ref.shape[1]
    lh_ref[...] = jnp.zeros_like(lh_ref)
    ll_ref[...] = jnp.zeros_like(ll_ref)

    def rows_of(r, _):
        away = r ^ row_pos
        slot = ((away >> 1) & 1) | (((away >> 2) & 1) << 1) | ((away & 1) << 2)
        low = r & 3
        for k in range(5):
            parts = []
            for p in range(4):
                gone = p ^ panel_pos
                at = slot | ((gone >> 1) << 3)
                parts.append((at, gone & 1))
            picked = [
                jnp.where(core == 0, here_ref[at, :, NB * k : NB * k + NB], there_ref[at, :, NB * k : NB * k + NB])
                for at, core in parts
            ]
            block = jnp.concatenate(picked, 0)
            if k < 2:
                s = r ^ (4 * k)
            else:
                m = k - 1
                second = (low >> (m.bit_length() - 1)) & 1
                s = (r ^ m) ^ (4 * second)
            rr = pl.multiple_of(r * NB, NB)
            ss = pl.multiple_of(s * NB, NB)

            @pl.when(r >= s)
            def _():
                a_ref[pl.ds(rr, NB), pl.ds(ss, NB)] = block

            if k >= 2:

                @pl.when(r < s)
                def _():
                    a_ref[pl.ds(ss, NB), pl.ds(rr, NB)] = block.T

        return 0

    lax.fori_loop(0, 8, rows_of, 0)
    factor_blocks(a_ref, lh_ref, ll_ref, wh_ref, wl_ref)


def factor(kernel, operands, n):
    in_specs = [pl.BlockSpec(memory_space=pltpu.VMEM)] * len(operands)
    if kernel is unfold_kernel:
        in_specs[0] = pl.BlockSpec(memory_space=pltpu.SMEM)
    return pl.pallas_call(
        kernel,
        out_shape=[jax.ShapeDtypeStruct((n, n), BF)] * 2 + [jax.ShapeDtypeStruct((n, NB), BF)] * 2,
        in_specs=in_specs,
        out_specs=[pl.BlockSpec(memory_space=pltpu.VMEM)] * 4,
        scratch_shapes=[pltpu.VMEM((n, n), F32)],
        compiler_params=pltpu.CompilerParams(vmem_limit_bytes=32 << 20),
        cost_estimate=pl.CostEstimate(flops=5 * 10**10, bytes_accessed=8 << 20, transcendentals=0),
        name="factor",
    )(*operands)


def solve_kernel(*refs):
    covers, (parts_ref, lh_ref, ll_ref, wh_ref, wl_ref, o_ref, xh_ref, xl_ref) = refs[:-8], refs[-8:]
    n = o_ref.shape[1]
    first = 0
    for ref in covers:
        rows = pl.ds(first, ref.shape[0])
        taken = parts_ref[0, rows]
        for p in range(1, parts_ref.shape[0]):
            taken = taken + parts_ref[p, rows]
        o_ref[rows] = ref[...] - taken
        first += ref.shape[0]
    for c in range(0, n, NB):
        here = o_ref[:, c : c + NB]
        if c:
            here = here - dot3(
                xh_ref[:, :c], xl_ref[:, :c], lh_ref[c : c + NB, :c], ll_ref[c : c + NB, :c]
            )
        bh, bl = split(here)
        x = dot3(bh, bl, wh_ref[c : c + NB], wl_ref[c : c + NB])
        o_ref[:, c : c + NB] = x
        xh, xl = split(x)
        xh_ref[:, c : c + NB] = xh
        xl_ref[:, c : c + NB] = xl


def solve(covers, parts, factors):
    rows = sum(c.shape[0] for c in covers)
    n = covers[0].shape[1]
    operands = (*covers, parts, *factors)
    return pl.pallas_call(
        solve_kernel,
        out_shape=jax.ShapeDtypeStruct((rows, n), F32),
        in_specs=[pl.BlockSpec(memory_space=pltpu.VMEM)] * len(operands),
        out_specs=pl.BlockSpec(memory_space=pltpu.VMEM),
        scratch_shapes=[pltpu.VMEM((rows, n), BF)] * 2,
        compiler_params=pltpu.CompilerParams(vmem_limit_bytes=32 << 20),
        name="solve",
    )(*operands)


def swap(block, axis, bit):
    return lax.ppermute(block, axis, [(i, i ^ bit) for i in range(lax.axis_size(axis))])


def dot_rows(left, right):
    return lax.dot_general(
        left, right, NT, precision=lax.Precision.HIGH, preferred_element_type=F32
    )


def local(pixel_ids, quad_offsets, prior_factor):
    panel_count = lax.axis_size("panel")
    row_count = lax.axis_size("row")
    block_rows = pixel_ids.shape[0]
    quarter_rows = block_rows // panel_count
    per_device = B // (row_count * panel_count)
    span_cols = panel_count * per_device
    row_pos = lax.axis_index("row")
    panel_pos = lax.axis_index("panel")
    device_pos = row_pos * panel_count + panel_pos
    lead = 32

    points = jnp.stack(locate(pixel_ids, quad_offsets))
    count = points.shape[1]
    own_points = lax.dynamic_slice_in_dim(points, panel_pos * quarter_rows, quarter_rows, 2)
    local_points = points.reshape(2, count, panel_count, quarter_rows)[:, :, :, :per_device]
    local_points = local_points.reshape(1, 2 * count, span_cols)

    row_ids = jnp.arange(lead, dtype=jnp.int32)[:, None]
    col_ids = jnp.arange(B, dtype=jnp.int32)[None, :]
    on_diagonal = (row_ids < per_device) & (col_ids == device_pos * per_device + row_ids)
    unit = jnp.where(on_diagonal, 1.0, 0.0).astype(F32)

    def covers_of(panel_points):
        row_part, col_part = features(own_points, panel_points)
        tiles = [cover_rows(row_part, col_part, i, lead) for i in range(0, quarter_rows, lead)]
        return [tiles[0] + unit] + tiles[1:]

    own_prior = prior_factor.reshape(panel_count, quarter_rows, -1)[:, :per_device]
    own_prior = own_prior.reshape(span_cols, -1)

    if not (span_cols == NB and row_count == 8 and panel_count == 4):
        copies = jnp.broadcast_to(local_points, (row_count, 2 * count, span_cols))
        spread = lax.all_to_all(copies, "row", split_axis=0, concat_axis=0, tiled=True)
        covers = covers_of(spread.transpose(1, 0, 2).reshape(2, count, B))
        panel_prior = lax.all_gather(own_prior, "row", axis=0, tiled=True)
        partial = dot_rows(prior_factor, panel_prior)
        parts = lax.all_to_all(
            partial.reshape(panel_count, quarter_rows, B), "panel", split_axis=0, concat_axis=0, tiled=True
        )
        mine = covers[0][:per_device] - jnp.sum(parts[:, :per_device], axis=0)
        diag_rows = lax.all_gather(mine, ("row", "panel"), axis=0, tiled=True)
        return solve(covers, parts, factor(factor_kernel, (diag_rows,), B))

    held = local_points
    for bit in (1, 2, 4):
        held = jnp.concatenate([held, swap(held, "row", bit)], 0)
    order = row_pos ^ jnp.arange(8, dtype=jnp.int32)
    panel_points = held[order].transpose(1, 0, 2).reshape(2, count, B)
    covers = covers_of(panel_points)

    far = swap(own_prior, "row", 4)
    firsts, seconds = [], []
    for m in (1, 2, 3):
        second = ((row_pos >> (m.bit_length() - 1)) & 1) == 1
        firsts.append(swap(jnp.where(second, own_prior, far), "row", m))
        seconds.append((m, jnp.where(second, far, own_prior)))
    folded = jnp.concatenate([own_prior, far] + firsts, 0)
    partial = dot_rows(own_prior, folded)
    sums = lax.all_to_all(
        partial.reshape(4, per_device, 5 * NB), "panel", split_axis=0, concat_axis=0, tiled=True
    )
    places = [fold_block(row_pos, k) for k in range(5)]
    lead_cover = jnp.concatenate(
        [lax.dynamic_slice(covers[0], (jnp.int32(0), s * NB), (per_device, NB)) for s in places], 1
    )
    shard = lead_cover - jnp.sum(sums, axis=0)

    held = shard[None]
    for axis, bit in (("row", 2), ("row", 4), ("row", 1), ("panel", 2)):
        held = jnp.concatenate([held, swap(held, axis, bit)], 0)
    there = swap(held, "panel", 1)

    rest = [swap(block, "row", m) for m, block in seconds]
    panel_prior = jnp.zeros((8, NB, own_prior.shape[1]), F32)
    for k, block in enumerate([own_prior, far] + firsts):
        panel_prior = lax.dynamic_update_slice(panel_prior, block[None], (places[k], 0, 0))
    for m, block in zip((1, 2, 3), rest):
        panel_prior = lax.dynamic_update_slice(panel_prior, block[None], (places[m + 1] ^ 4, 0, 0))
    partial = dot_rows(prior_factor, panel_prior.reshape(B, -1))
    partial, there = lax.optimization_barrier((partial, there))
    parts = lax.all_to_all(
        partial.reshape(4, quarter_rows, B), "panel", split_axis=0, concat_axis=0, tiled=True
    )
    place = jnp.stack([row_pos, panel_pos]).astype(jnp.int32)
    factors = factor(unfold_kernel, (place, held, there), B)
    return solve(covers, parts, factors)


def solution(mesh):
    return jax.shard_map(
        local,
        mesh=mesh,
        in_specs=(P("row"), P(None, None, "row"), P("row", "panel")),
        out_specs=P(("row", "panel"), None),
        check_vma=False,
    )
```

```python
import functools

import jax
import jax.numpy as jnp
from jax import lax
from jax.experimental import pallas as pl
from jax.experimental.pallas import tpu as pltpu
from jax.sharding import PartitionSpec as P

B = 1024
NB = 128
GROUP = 8
F32 = jnp.float32
BF = jnp.bfloat16
NT = (((1,), (1,)), ((), ()))
SCALE = -1.4426950408889634 / 64.0
CENTRE = 1024.0


def locate(pixel_ids, quad_offsets):
    column = (pixel_ids % 256) * 8
    lines = (pixel_ids // 256) * 8
    east = (column[None, :] + quad_offsets[0]).astype(F32) - CENTRE
    north = (lines[None, :] + quad_offsets[1]).astype(F32) - CENTRE
    return east, north


def pieces(value):
    high = jnp.floor(value * (1.0 / 65536.0)) * 65536.0
    rest = value - high
    mid = jnp.floor(rest * (1.0 / 256.0)) * 256.0
    return [high, mid, rest - mid]


def halves(value):
    high = jnp.floor(value * (1.0 / 128.0)) * 128.0
    return high, value - high


def row_features(x, y):
    xh, xl = halves(x)
    yh, yl = halves(y)
    one = jnp.ones_like(x)
    zero = jnp.zeros_like(x)
    cross = [-2 * xh, -2 * xh, -2 * xl, -2 * xl, -2 * yh, -2 * yh, -2 * yl, -2 * yl]
    return jnp.concatenate(cross + pieces(x * x + y * y) + [one] * 3 + [zero] * 2, 0)


def col_features(x, y):
    xh, xl = halves(x)
    yh, yl = halves(y)
    one = jnp.ones_like(x)
    zero = jnp.zeros_like(x)
    cross = [xh, xl, xh, xl, yh, yl, yh, yl]
    return jnp.concatenate(cross + [one] * 3 + pieces(x * x + y * y) + [zero] * 2, 0)


def feature_kernel(row_ref, col_ref, f_ref, g_ref):
    for a in range(row_ref.shape[1]):
        one = row_features(row_ref[0, a : a + 1, :], row_ref[1, a : a + 1, :])
        f_ref[a] = one.T.astype(BF)
        g_ref[a] = col_features(col_ref[0, a : a + 1, :], col_ref[1, a : a + 1, :]).astype(BF)


def features(row_points, col_points):
    count, rows = row_points.shape[1:]
    cols = col_points.shape[2]
    return pl.pallas_call(
        feature_kernel,
        out_shape=[
            jax.ShapeDtypeStruct((count, rows, 16), BF),
            jax.ShapeDtypeStruct((count, 16, cols), BF),
        ],
        in_specs=[pl.BlockSpec(memory_space=pltpu.VMEM)] * 2,
        out_specs=[pl.BlockSpec(memory_space=pltpu.VMEM)] * 2,
        compiler_params=pltpu.CompilerParams(vmem_limit_bytes=8 << 20),
        name="features",
    )(row_points, col_points)


def cover_kernel(f_ref, g_ref, o_ref):
    count, block = f_ref.shape[:2]
    rows_here = f_ref[...].reshape(count * block, 16)

    def column_point(b, total):
        apart = jnp.dot(rows_here, g_ref[b], preferred_element_type=F32)
        near = jnp.exp2(apart * SCALE)
        for a in range(count):
            total = total + near[a * block : (a + 1) * block]
        return total

    total = lax.fori_loop(0, count, column_point, jnp.zeros(o_ref.shape, F32))
    o_ref[...] = total * (1.0 / (count * count))


def cover_rows(row_part, col_part, first, block):
    count, rows, depth = row_part.shape
    cols = col_part.shape[2]
    index = first // block
    return pl.pallas_call(
        cover_kernel,
        grid=(1,),
        out_shape=jax.ShapeDtypeStruct((block, cols), F32),
        in_specs=[
            pl.BlockSpec((count, block, depth), lambda i: (0, index, 0)),
            pl.BlockSpec((count, depth, cols), lambda i: (0, 0, 0)),
        ],
        out_specs=pl.BlockSpec((block, cols), lambda i: (0, 0)),
        compiler_params=pltpu.CompilerParams(vmem_limit_bytes=16 << 20),
        cost_estimate=pl.CostEstimate(flops=10**8, bytes_accessed=1 << 18, transcendentals=0),
        name="cover",
    )(row_part, col_part)


def inverse_factor(tiles):
    width = 8 * len(tiles)
    lane = lax.broadcasted_iota(jnp.int32, (8, width), 1)
    sub = lax.broadcasted_iota(jnp.int32, (8, width), 0)
    tiles = list(tiles)
    n = len(tiles)
    out = []
    for v in range(n):
        pivots = jnp.ones((8, width), F32)
        for g in range(0, 8, GROUP):
            cols = [
                [
                    jnp.broadcast_to(tiles[r][:, 8 * v + g + q : 8 * v + g + q + 1], (8, width))
                    for q in range(GROUP)
                ]
                for r in range(v, n)
            ]
            for q in range(GROUP):
                s = g + q
                p = 8 * v + s
                pivot = jnp.broadcast_to(cols[0][q][s : s + 1], (8, width))
                inverse = 1.0 / pivot
                pivots = jnp.where(sub == s, pivot, pivots)
                row = jnp.where(lane == p, 1.0, jnp.broadcast_to(tiles[v][s : s + 1], (8, width)))
                heads = [
                    jnp.broadcast_to(cols[0][k][s : s + 1], (8, width)) for k in range(q + 1, GROUP)
                ]
                for r in range(v, n):
                    part = cols[r - v][q] * inverse
                    if r == v:
                        part = jnp.where(sub > s, part, 0.0)
                    tiles[r] = jnp.where(lane == p, 0.0, tiles[r]) - part * row
                    for k in range(q + 1, GROUP):
                        cols[r - v][k] = cols[r - v][k] - part * heads[k - q - 1]
        row_id = sub + 8 * v
        unit = jnp.where(lane == row_id, 1.0, 0.0)
        out.append(jnp.where(lane < row_id, tiles[v], unit) * lax.rsqrt(pivots))
    return jnp.concatenate(out, 0)


def split(x):
    high = x.astype(BF)
    return high, (x - high.astype(F32)).astype(BF)


def dot3(ah, al, bh, bl):
    dot = functools.partial(lax.dot_general, dimension_numbers=NT, preferred_element_type=F32)
    return dot(ah, bh) + (dot(ah, bl) + dot(al, bh))


def factor_blocks(a_ref, lh_ref, ll_ref, wh_ref, wl_ref):
    n = a_ref.shape[0]
    blocks = n // NB

    def step(j, _):
        c = pl.multiple_of(j * NB, NB)
        tiles = [a_ref[pl.ds(c + 8 * v, 8), pl.ds(c, NB)] for v in range(NB // 8)]
        wh, wl = split(inverse_factor(tiles))
        wh_ref[pl.ds(c, NB)] = wh
        wl_ref[pl.ds(c, NB)] = wl

        def panel(i, _):
            r = pl.multiple_of(i * NB, NB)
            bh, bl = split(a_ref[pl.ds(r, NB), pl.ds(c, NB)])
            high, low = split(dot3(bh, bl, wh, wl))
            lh_ref[pl.ds(r, NB), pl.ds(c, NB)] = high
            ll_ref[pl.ds(r, NB), pl.ds(c, NB)] = low
            return 0

        lax.fori_loop(j + 1, blocks, panel, 0)

        def trail(i, _):
            r = pl.multiple_of(i * NB, NB)
            a_ref[pl.ds(r, NB)] = a_ref[pl.ds(r, NB)] - dot3(
                lh_ref[pl.ds(r, NB), pl.ds(c, NB)],
                ll_ref[pl.ds(r, NB), pl.ds(c, NB)],
                lh_ref[:, pl.ds(c, NB)],
                ll_ref[:, pl.ds(c, NB)],
            )
            return 0

        lax.fori_loop(j + 1, blocks, trail, 0)
        return 0

    lax.fori_loop(0, blocks, step, 0)


def factor_kernel(diag_ref, lh_ref, ll_ref, wh_ref, wl_ref, a_ref):
    a_ref[...] = diag_ref[...]
    lh_ref[...] = jnp.zeros_like(lh_ref)
    ll_ref[...] = jnp.zeros_like(ll_ref)
    factor_blocks(a_ref, lh_ref, ll_ref, wh_ref, wl_ref)


def fold_block(r, k):
    if k < 2:
        return r ^ (4 * k)
    m = k - 1
    low = r & 3
    second = (low >> (m.bit_length() - 1)) & 1
    return (r ^ m) ^ (4 * second)


def unfold_kernel(place_ref, *refs):
    pieces_refs, (lh_ref, ll_ref, wh_ref, wl_ref, a_ref, g_ref) = refs[:8], refs[8:]
    row_pos = place_ref[0]
    panel_pos = place_ref[1]
    lh_ref[...] = jnp.zeros_like(lh_ref)
    ll_ref[...] = jnp.zeros_like(ll_ref)
    for i, ref in enumerate(pieces_refs):
        g_ref[4 * i : 4 * i + 4] = ref[...]

    def rows_of(r, _):
        away = r ^ row_pos
        slot = (away >> 1) | ((away & 1) << 2)
        low = r & 3
        ats = []
        for p in range(4):
            gone = p ^ panel_pos
            ats.append(slot | ((gone >> 1) << 3) | ((gone & 1) << 4))
        for k in range(5):
            block = jnp.concatenate([g_ref[at, :, NB * k : NB * k + NB] for at in ats], 0)
            if k < 2:
                s = r ^ (4 * k)
            else:
                m = k - 1
                second = (low >> (m.bit_length() - 1)) & 1
                s = (r ^ m) ^ (4 * second)
            rr = pl.multiple_of(r * NB, NB)
            ss = pl.multiple_of(s * NB, NB)

            @pl.when(r >= s)
            def _():
                a_ref[pl.ds(rr, NB), pl.ds(ss, NB)] = block

            if k >= 2:

                @pl.when(r < s)
                def _():
                    a_ref[pl.ds(ss, NB), pl.ds(rr, NB)] = block.T

        return 0

    lax.fori_loop(0, 8, rows_of, 0)
    factor_blocks(a_ref, lh_ref, ll_ref, wh_ref, wl_ref)


def factor(kernel, operands, n):
    in_specs = [pl.BlockSpec(memory_space=pltpu.VMEM)] * len(operands)
    scratch = [pltpu.VMEM((n, n), F32)]
    if kernel is unfold_kernel:
        in_specs[0] = pl.BlockSpec(memory_space=pltpu.SMEM)
        scratch.append(pltpu.VMEM((32, *operands[1].shape[1:]), F32))
    return pl.pallas_call(
        kernel,
        out_shape=[jax.ShapeDtypeStruct((n, n), BF)] * 2 + [jax.ShapeDtypeStruct((n, NB), BF)] * 2,
        in_specs=in_specs,
        out_specs=[pl.BlockSpec(memory_space=pltpu.VMEM)] * 4,
        scratch_shapes=scratch,
        compiler_params=pltpu.CompilerParams(vmem_limit_bytes=32 << 20),
        cost_estimate=pl.CostEstimate(flops=5 * 10**10, bytes_accessed=8 << 20, transcendentals=0),
        name="factor",
    )(*operands)


def solve_kernel(*refs, covers):
    cover_refs, parts_refs = refs[:covers], refs[covers:-7]
    lh_ref, ll_ref, wh_ref, wl_ref, o_ref, xh_ref, xl_ref = refs[-7:]
    n = o_ref.shape[1]
    first = 0
    for ref in cover_refs:
        rows = pl.ds(first, ref.shape[0])
        taken = parts_refs[0][rows]
        for part in parts_refs[1:]:
            taken = taken + part[rows]
        o_ref[rows] = ref[...] - taken
        first += ref.shape[0]
    for c in range(0, n, NB):
        here = o_ref[:, c : c + NB]
        if c:
            here = here - dot3(
                xh_ref[:, :c], xl_ref[:, :c], lh_ref[c : c + NB, :c], ll_ref[c : c + NB, :c]
            )
        bh, bl = split(here)
        x = dot3(bh, bl, wh_ref[c : c + NB], wl_ref[c : c + NB])
        o_ref[:, c : c + NB] = x
        xh, xl = split(x)
        xh_ref[:, c : c + NB] = xh
        xl_ref[:, c : c + NB] = xl


def solve(covers, parts, factors):
    rows = sum(c.shape[0] for c in covers)
    n = covers[0].shape[1]
    operands = (*covers, *parts, *factors)
    return pl.pallas_call(
        functools.partial(solve_kernel, covers=len(covers)),
        out_shape=jax.ShapeDtypeStruct((rows, n), F32),
        in_specs=[pl.BlockSpec(memory_space=pltpu.VMEM)] * len(operands),
        out_specs=pl.BlockSpec(memory_space=pltpu.VMEM),
        scratch_shapes=[pltpu.VMEM((rows, n), BF)] * 2,
        compiler_params=pltpu.CompilerParams(vmem_limit_bytes=32 << 20),
        name="solve",
    )(*operands)


def swap(block, axis, bit):
    return lax.ppermute(block, axis, [(i, i ^ bit) for i in range(lax.axis_size(axis))])


def dot_rows(left, right):
    return lax.dot_general(
        left, right, NT, precision=lax.Precision.HIGH, preferred_element_type=F32
    )


def local(pixel_ids, quad_offsets, prior_factor):
    panel_count = lax.axis_size("panel")
    row_count = lax.axis_size("row")
    block_rows = pixel_ids.shape[0]
    quarter_rows = block_rows // panel_count
    per_device = B // (row_count * panel_count)
    span_cols = panel_count * per_device
    row_pos = lax.axis_index("row")
    panel_pos = lax.axis_index("panel")
    device_pos = row_pos * panel_count + panel_pos
    lead = 32

    points = jnp.stack(locate(pixel_ids, quad_offsets))
    count = points.shape[1]
    own_points = lax.dynamic_slice_in_dim(points, panel_pos * quarter_rows, quarter_rows, 2)
    local_points = points.reshape(2, count, panel_count, quarter_rows)[:, :, :, :per_device]
    local_points = local_points.reshape(1, 2 * count, span_cols)

    row_ids = jnp.arange(lead, dtype=jnp.int32)[:, None]
    col_ids = jnp.arange(B, dtype=jnp.int32)[None, :]
    on_diagonal = (row_ids < per_device) & (col_ids == device_pos * per_device + row_ids)
    unit = jnp.where(on_diagonal, 1.0, 0.0).astype(F32)

    own_prior = prior_factor.reshape(panel_count, quarter_rows, -1)[:, :per_device]
    own_prior = own_prior.reshape(span_cols, -1)

    if not (span_cols == NB and row_count == 8 and panel_count == 4):
        copies = jnp.broadcast_to(local_points, (row_count, 2 * count, span_cols))
        spread = lax.all_to_all(copies, "row", split_axis=0, concat_axis=0, tiled=True)
        parted = features(own_points, spread.transpose(1, 0, 2).reshape(2, count, B))
        covers = [cover_rows(*parted, i, lead) for i in range(0, quarter_rows, lead)]
        covers[0] = covers[0] + unit
        panel_prior = lax.all_gather(own_prior, "row", axis=0, tiled=True)
        partial = dot_rows(prior_factor, panel_prior)
        parts = lax.all_to_all(
            partial.reshape(panel_count, quarter_rows, B), "panel", split_axis=0, concat_axis=0, tiled=True
        )
        parts = jnp.sum(parts, axis=0)
        mine = covers[0][:per_device] - parts[:per_device]
        diag_rows = lax.all_gather(mine, ("row", "panel"), axis=0, tiled=True)
        return solve(covers, [parts], factor(factor_kernel, (diag_rows,), B))

    far = swap(own_prior, "row", 4)
    held = jnp.concatenate([local_points] + [swap(local_points, "row", bit) for bit in (2, 4, 6)], 0)
    held = jnp.concatenate([held, swap(held, "row", 1)], 0)
    away = row_pos ^ jnp.arange(8, dtype=jnp.int32)
    order = (away >> 1) | ((away & 1) << 2)
    panel_points = held[order].transpose(1, 0, 2).reshape(2, count, B)
    row_part, col_part = features(own_points, panel_points)
    row_part, far = lax.optimization_barrier((row_part, far))
    covers = []

    def beside(operands, transfer, calls):
        tied = lax.optimization_barrier((operands, row_part))
        received = transfer(tied[0])
        done = [
            cover_rows(tied[1], col_part, lead * (len(covers) + i), lead) for i in range(calls)
        ]
        received, done = lax.optimization_barrier((received, done))
        covers.extend(done)
        return received

    seconds = [((row_pos >> (m.bit_length() - 1)) & 1) == 1 for m in (1, 2, 3)]
    firsts = beside(
        [jnp.where(second, own_prior, far) for second in seconds],
        lambda blocks: [swap(block, "row", m) for m, block in zip((1, 2, 3), blocks)],
        2,
    )
    partial = dot_rows(own_prior, jnp.concatenate([own_prior, far] + firsts, 0))
    others = [jnp.where(second, far, own_prior) for second in seconds]

    shares = [
        lax.dynamic_slice_in_dim(partial, (panel_pos ^ m) * per_device, per_device, 0)
        for m in range(4)
    ]

    def reduce_and_swap(operands):
        shares, others = operands
        sums = [swap(share, "panel", m) for m, share in zip((1, 2, 3), shares[1:])]
        return sums, [swap(block, "row", m) for m, block in zip((1, 2, 3), others)]

    sums, rest = beside((shares, others), reduce_and_swap, 1)
    covers[0] = covers[0] + unit
    places = [fold_block(row_pos, k) for k in range(5)]
    lead_cover = jnp.concatenate(
        [lax.dynamic_slice(covers[0], (jnp.int32(0), s * NB), (per_device, NB)) for s in places], 1
    )
    shard = lead_cover - (shares[0] + sums[0] + sums[1] + sums[2])

    along = beside(shard[None], lambda x: [swap(x, "row", bit) for bit in (2, 4, 6)], 2)
    held = jnp.concatenate([shard[None]] + along, 0)

    def across(x):
        corner = [(i, i ^ 6) for i in range(32)]
        return swap(x, "row", 1), swap(x, "panel", 2), lax.ppermute(x, ("row", "panel"), corner)

    here = [held, *beside(held, across, 3)]

    panel_prior = jnp.zeros((8, NB, own_prior.shape[1]), F32)
    for k, block in enumerate([own_prior, far] + firsts):
        panel_prior = lax.dynamic_update_slice(panel_prior, block[None], (places[k], 0, 0))
    for m, block in zip((1, 2, 3), rest):
        panel_prior = lax.dynamic_update_slice(panel_prior, block[None], (places[m + 1] ^ 4, 0, 0))
    here, panel_prior = lax.optimization_barrier((here, panel_prior))
    there = [swap(x, "panel", 1) for x in here]
    parts = []
    for m in (3, 2, 1, 0):
        rows = lax.dynamic_slice_in_dim(
            prior_factor, (panel_pos ^ m) * quarter_rows, quarter_rows, 0
        )
        part = dot_rows(rows, panel_prior.reshape(B, -1))
        parts.append(swap(part, "panel", m) if m else part)
    place = jnp.stack([row_pos, panel_pos]).astype(jnp.int32)
    factors = factor(unfold_kernel, (place, *here, *there), B)
    return solve(covers, parts, factors)


def solution(mesh):
    return jax.shard_map(
        local,
        mesh=mesh,
        in_specs=(P("row"), P(None, None, "row"), P("row", "panel")),
        out_specs=P(("row", "panel"), None),
        check_vma=False,
    )
```

```python
import functools

import jax
import jax.numpy as jnp
from jax import lax
from jax.experimental import pallas as pl
from jax.experimental.pallas import tpu as pltpu
from jax.sharding import PartitionSpec as P

B = 1024
NB = 128
NEAR = 4
F32 = jnp.float32
BF = jnp.bfloat16
NT = (((1,), (1,)), ((), ()))
SCALE = -1.4426950408889634 / 64.0
CENTRE = 1024.0


def locate(pixel_ids, quad_offsets):
    column = (pixel_ids % 256) * 8
    lines = (pixel_ids // 256) * 8
    east = (column[None, :] + quad_offsets[0]).astype(F32) - CENTRE
    north = (lines[None, :] + quad_offsets[1]).astype(F32) - CENTRE
    return east, north


def pieces(value):
    high = jnp.floor(value * (1.0 / 65536.0)) * 65536.0
    rest = value - high
    mid = jnp.floor(rest * (1.0 / 256.0)) * 256.0
    return [high, mid, rest - mid]


def halves(value):
    high = jnp.floor(value * (1.0 / 128.0)) * 128.0
    return high, value - high


def row_features(x, y):
    xh, xl = halves(x)
    yh, yl = halves(y)
    one = jnp.ones_like(x)
    zero = jnp.zeros_like(x)
    cross = [-2 * xh, -2 * xh, -2 * xl, -2 * xl, -2 * yh, -2 * yh, -2 * yl, -2 * yl]
    return jnp.concatenate(cross + pieces(x * x + y * y) + [one] * 3 + [zero] * 2, 0)


def col_features(x, y):
    xh, xl = halves(x)
    yh, yl = halves(y)
    one = jnp.ones_like(x)
    zero = jnp.zeros_like(x)
    cross = [xh, xl, xh, xl, yh, yl, yh, yl]
    return jnp.concatenate(cross + [one] * 3 + pieces(x * x + y * y) + [zero] * 2, 0)


def feature_kernel(row_ref, col_ref, f_ref, g_ref):
    for a in range(row_ref.shape[1]):
        one = row_features(row_ref[0, a : a + 1, :], row_ref[1, a : a + 1, :])
        f_ref[a] = one.T.astype(BF)
        g_ref[a] = col_features(col_ref[0, a : a + 1, :], col_ref[1, a : a + 1, :]).astype(BF)


def features(row_points, col_points):
    count, rows = row_points.shape[1:]
    cols = col_points.shape[2]
    return pl.pallas_call(
        feature_kernel,
        out_shape=[
            jax.ShapeDtypeStruct((count, rows, 16), BF),
            jax.ShapeDtypeStruct((count, 16, cols), BF),
        ],
        in_specs=[pl.BlockSpec(memory_space=pltpu.VMEM)] * 2,
        out_specs=[pl.BlockSpec(memory_space=pltpu.VMEM)] * 2,
        compiler_params=pltpu.CompilerParams(vmem_limit_bytes=8 << 20),
        name="features",
    )(row_points, col_points)


def cover_kernel(f_ref, g_ref, o_ref):
    count, block = f_ref.shape[:2]
    rows_here = f_ref[...].reshape(count * block, 16)

    def column_point(b, total):
        apart = jnp.dot(rows_here, g_ref[b], preferred_element_type=F32)
        near = jnp.exp2(apart * SCALE)
        for a in range(count):
            total = total + near[a * block : (a + 1) * block]
        return total

    total = lax.fori_loop(0, count, column_point, jnp.zeros(o_ref.shape, F32), unroll=8)
    o_ref[...] = total * (1.0 / (count * count))


def cover_rows(row_part, col_part, first, block):
    count, rows, depth = row_part.shape
    cols = col_part.shape[2]
    index = first // block
    return pl.pallas_call(
        cover_kernel,
        grid=(1,),
        out_shape=jax.ShapeDtypeStruct((block, cols), F32),
        in_specs=[
            pl.BlockSpec((count, block, depth), lambda i: (0, index, 0)),
            pl.BlockSpec((count, depth, cols), lambda i: (0, 0, 0)),
        ],
        out_specs=pl.BlockSpec((block, cols), lambda i: (0, 0)),
        compiler_params=pltpu.CompilerParams(vmem_limit_bytes=16 << 20),
        cost_estimate=pl.CostEstimate(flops=10**8, bytes_accessed=1 << 18, transcendentals=0),
        name="cover",
    )(row_part, col_part)


def inverse_factor(tiles):
    n = len(tiles)
    width = 8 * n
    lane = lax.broadcasted_iota(jnp.int32, (8, width), 1)
    sub = lax.broadcasted_iota(jnp.int32, (8, width), 0)
    tiles = list(tiles)
    out = []

    def spread(x):
        return jnp.broadcast_to(x, (8, width))

    def lanes(tile, v):
        return [spread(tile[:, 8 * v + q : 8 * v + q + 1]) for q in range(8)]

    following = lanes(tiles[0], 0)
    for v in range(n):
        near = min(n, v + NEAR)
        cols = {v: following}
        if v + 1 < n:
            cols[v] = cols[v] + lanes(tiles[v], v + 1)
            cols[v + 1] = lanes(tiles[v + 1], v) + lanes(tiles[v + 1], v + 1)
        for r in range(v + 2, near):
            cols[r] = lanes(tiles[r], v)
        here = (lane >= 8 * v) & (lane < 8 * v + 8)
        for r in range(v + 1, n):
            tiles[r] = jnp.where(here, 0.0, tiles[r])
        tiles[v] = jnp.where(here, jnp.where(lane == sub + 8 * v, 1.0, 0.0), tiles[v])
        pivots = jnp.ones((8, width), F32)
        for s in range(8):
            head = cols[v]
            pivot = spread(head[s][s : s + 1])
            inverse = 1.0 / pivot
            pivots = jnp.where(sub == s, pivot, pivots)
            row = spread(tiles[v][s : s + 1])
            heads = [spread(head[k][s : s + 1]) for k in range(s + 1, len(head))]
            for r in range(v, near):
                part = cols[r][s] * inverse
                if r == v:
                    part = jnp.where(sub > s, part, 0.0)
                tiles[r] = tiles[r] - part * row
                for k in range(s + 1, len(cols[r])):
                    cols[r][k] = cols[r][k] - part * heads[k - s - 1]
        if v + 1 < n:
            following = cols[v + 1][8:]
        rows = tiles[v] * lax.rsqrt(pivots)
        if near < n:
            high = rows.astype(BF).astype(F32)
            low = rows - high
            left = jnp.concatenate([high, high, low, low], 0).astype(BF)
            right = jnp.concatenate([high, low, high, low], 0).astype(BF)
            update = lax.dot_general(
                left, right, (((0,), (0,)), ((), ())), preferred_element_type=F32
            )
            for r in range(near, n):
                tiles[r] = tiles[r] - update[8 * r : 8 * r + 8]
        out.append(jnp.where(lane <= sub + 8 * v, rows, 0.0))
    return jnp.concatenate(out, 0)


def split(x):
    high = x.astype(BF)
    return high, (x - high.astype(F32)).astype(BF)


def dot3(ah, al, bh, bl):
    dot = functools.partial(lax.dot_general, dimension_numbers=NT, preferred_element_type=F32)
    return dot(ah, bh) + (dot(ah, bl) + dot(al, bh))


def factor_blocks(a_ref, lh_ref, ll_ref, wh_ref, wl_ref):
    n = a_ref.shape[0]
    blocks = n // NB

    def column(first):
        end = first + NB
        bh, bl = split(a_ref[end:, first:end])
        high, low = split(dot3(bh, bl, wh_ref[first:end], wl_ref[first:end]))
        lh_ref[end:, first:end] = high
        ll_ref[end:, first:end] = low
        a_ref[end:, end : end + NB] = a_ref[end:, end : end + NB] - dot3(
            lh_ref[end:, :end],
            ll_ref[end:, :end],
            lh_ref[end : end + NB, :end],
            ll_ref[end : end + NB, :end],
        )

    def step(j, _):
        c = pl.multiple_of(j * NB, NB)
        tiles = [a_ref[pl.ds(c + 8 * v, 8), pl.ds(c, NB)] for v in range(NB // 8)]
        wh, wl = split(inverse_factor(tiles))
        wh_ref[pl.ds(c, NB)] = wh
        wl_ref[pl.ds(c, NB)] = wl
        for block in range(blocks - 1):
            pl.when(j == block)(functools.partial(column, block * NB))
        return 0

    lax.fori_loop(0, blocks, step, 0)


def factor_kernel(diag_ref, lh_ref, ll_ref, wh_ref, wl_ref, a_ref):
    a_ref[...] = diag_ref[...]
    factor_blocks(a_ref, lh_ref, ll_ref, wh_ref, wl_ref)


def fold_block(r, k):
    if k < 2:
        return r ^ (4 * k)
    m = k - 1
    low = r & 3
    second = (low >> (m.bit_length() - 1)) & 1
    return (r ^ m) ^ (4 * second)


def unfold_kernel(place_ref, *refs):
    pieces_refs, (lh_ref, ll_ref, wh_ref, wl_ref, a_ref, g_ref) = refs[:8], refs[8:]
    row_pos = place_ref[0]
    panel_pos = place_ref[1]
    for i, ref in enumerate(pieces_refs):
        g_ref[4 * i : 4 * i + 4] = ref[...]

    def rows_of(r, _):
        away = r ^ row_pos
        slot = (away >> 1) | ((away & 1) << 2)
        low = r & 3
        ats = []
        for p in range(4):
            gone = p ^ panel_pos
            ats.append(slot | ((gone >> 1) << 3) | ((gone & 1) << 4))
        for k in range(5):
            block = jnp.concatenate([g_ref[at, :, NB * k : NB * k + NB] for at in ats], 0)
            if k < 2:
                s = r ^ (4 * k)
            else:
                m = k - 1
                second = (low >> (m.bit_length() - 1)) & 1
                s = (r ^ m) ^ (4 * second)
            rr = pl.multiple_of(r * NB, NB)
            ss = pl.multiple_of(s * NB, NB)

            @pl.when(r >= s)
            def _():
                a_ref[pl.ds(rr, NB), pl.ds(ss, NB)] = block

            if k >= 2:

                @pl.when(r < s)
                def _():
                    a_ref[pl.ds(ss, NB), pl.ds(rr, NB)] = block.T

        return 0

    lax.fori_loop(0, 8, rows_of, 0)
    factor_blocks(a_ref, lh_ref, ll_ref, wh_ref, wl_ref)


def factor(kernel, operands, n):
    in_specs = [pl.BlockSpec(memory_space=pltpu.VMEM)] * len(operands)
    scratch = [pltpu.VMEM((n, n), F32)]
    if kernel is unfold_kernel:
        in_specs[0] = pl.BlockSpec(memory_space=pltpu.SMEM)
        scratch.append(pltpu.VMEM((32, *operands[1].shape[1:]), F32))
    return pl.pallas_call(
        kernel,
        out_shape=[jax.ShapeDtypeStruct((n, n), BF)] * 2 + [jax.ShapeDtypeStruct((n, NB), BF)] * 2,
        in_specs=in_specs,
        out_specs=[pl.BlockSpec(memory_space=pltpu.VMEM)] * 4,
        scratch_shapes=scratch,
        compiler_params=pltpu.CompilerParams(vmem_limit_bytes=32 << 20),
        cost_estimate=pl.CostEstimate(flops=5 * 10**10, bytes_accessed=8 << 20, transcendentals=0),
        name="factor",
    )(*operands)


def solve_kernel(*refs, covers):
    cover_refs, parts_refs = refs[:covers], refs[covers:-7]
    lh_ref, ll_ref, wh_ref, wl_ref, o_ref, xh_ref, xl_ref = refs[-7:]
    n = o_ref.shape[1]
    first = 0
    for ref in cover_refs:
        rows = pl.ds(first, ref.shape[0])
        taken = parts_refs[0][rows]
        for part in parts_refs[1:]:
            taken = taken + part[rows]
        o_ref[rows] = ref[...] - taken
        first += ref.shape[0]
    for c in range(0, n, NB):
        here = o_ref[:, c : c + NB]
        if c:
            here = here - dot3(
                xh_ref[:, :c], xl_ref[:, :c], lh_ref[c : c + NB, :c], ll_ref[c : c + NB, :c]
            )
        bh, bl = split(here)
        x = dot3(bh, bl, wh_ref[c : c + NB], wl_ref[c : c + NB])
        o_ref[:, c : c + NB] = x
        xh, xl = split(x)
        xh_ref[:, c : c + NB] = xh
        xl_ref[:, c : c + NB] = xl


def solve(covers, parts, factors):
    rows = sum(c.shape[0] for c in covers)
    n = covers[0].shape[1]
    operands = (*covers, *parts, *factors)
    return pl.pallas_call(
        functools.partial(solve_kernel, covers=len(covers)),
        out_shape=jax.ShapeDtypeStruct((rows, n), F32),
        in_specs=[pl.BlockSpec(memory_space=pltpu.VMEM)] * len(operands),
        out_specs=pl.BlockSpec(memory_space=pltpu.VMEM),
        scratch_shapes=[pltpu.VMEM((rows, n), BF)] * 2,
        compiler_params=pltpu.CompilerParams(vmem_limit_bytes=32 << 20),
        name="solve",
    )(*operands)


def vmem_call(kernel, out_shape, place, operands, scratch=(), name=None):
    return pl.pallas_call(
        kernel,
        out_shape=out_shape,
        in_specs=[pl.BlockSpec(memory_space=pltpu.SMEM)]
        + [pl.BlockSpec(memory_space=pltpu.VMEM)] * len(operands),
        out_specs=jax.tree.map(lambda _: pl.BlockSpec(memory_space=pltpu.VMEM), out_shape),
        scratch_shapes=list(scratch),
        compiler_params=pltpu.CompilerParams(vmem_limit_bytes=16 << 20),
        cost_estimate=pl.CostEstimate(flops=10**8, bytes_accessed=1 << 18, transcendentals=0),
        name=name,
    )(place, *operands)


def fold_products_kernel(place_ref, *refs):
    blocks, shares, total_ref = refs[:5], refs[5:-1], refs[-1]
    own_high, own_low = split(blocks[0][...])
    for k, ref in enumerate(blocks):
        high, low = split(ref[...])
        total_ref[:, NB * k : NB * k + NB] = dot3(own_high, own_low, high, low)
    rows = shares[0].shape[0]
    for m, ref in enumerate(shares):
        first = pl.multiple_of((place_ref[1] ^ m) * rows, rows)
        ref[...] = total_ref[pl.ds(first, rows)]


def gather_split_kernel(place_ref, *refs):
    blocks, (high_ref, low_ref) = refs[:-2], refs[-2:]
    row_pos = place_ref[0]
    order = [fold_block(row_pos, k) for k in range(5)]
    order = order + [order[k] ^ 4 for k in (2, 3, 4)]
    for s, ref in zip(order, blocks):
        first = pl.multiple_of(s * NB, NB)
        high, low = split(ref[...])
        high_ref[pl.ds(first, NB)] = high
        low_ref[pl.ds(first, NB)] = low


def rest_products_kernel(place_ref, prior_ref, high_ref, low_ref, o_ref, *, m):
    rows = o_ref.shape[0]
    first = pl.multiple_of((place_ref[1] ^ m) * rows, rows)
    own_high, own_low = split(prior_ref[pl.ds(first, rows)])
    for c in range(0, o_ref.shape[1], 2 * NB):
        o_ref[:, c : c + 2 * NB] = dot3(
            own_high, own_low, high_ref[c : c + 2 * NB], low_ref[c : c + 2 * NB]
        )


def swap(block, axis, bit):
    return lax.ppermute(block, axis, [(i, i ^ bit) for i in range(lax.axis_size(axis))])


def dot_rows(left, right):
    return lax.dot_general(
        left, right, NT, precision=lax.Precision.HIGH, preferred_element_type=F32
    )


def local(pixel_ids, quad_offsets, prior_factor):
    panel_count = lax.axis_size("panel")
    row_count = lax.axis_size("row")
    block_rows = pixel_ids.shape[0]
    quarter_rows = block_rows // panel_count
    per_device = B // (row_count * panel_count)
    span_cols = panel_count * per_device
    row_pos = lax.axis_index("row")
    panel_pos = lax.axis_index("panel")
    device_pos = row_pos * panel_count + panel_pos
    lead = 32

    points = jnp.stack(locate(pixel_ids, quad_offsets))
    count = points.shape[1]
    own_points = lax.dynamic_slice_in_dim(points, panel_pos * quarter_rows, quarter_rows, 2)
    local_points = points.reshape(2, count, panel_count, quarter_rows)[:, :, :, :per_device]
    local_points = local_points.reshape(1, 2 * count, span_cols)

    row_ids = jnp.arange(lead, dtype=jnp.int32)[:, None]
    col_ids = jnp.arange(B, dtype=jnp.int32)[None, :]
    on_diagonal = (row_ids < per_device) & (col_ids == device_pos * per_device + row_ids)
    unit = jnp.where(on_diagonal, 1.0, 0.0).astype(F32)

    own_prior = prior_factor.reshape(panel_count, quarter_rows, -1)[:, :per_device]
    own_prior = own_prior.reshape(span_cols, -1)

    if not (span_cols == NB and row_count == 8 and panel_count == 4):
        copies = jnp.broadcast_to(local_points, (row_count, 2 * count, span_cols))
        spread = lax.all_to_all(copies, "row", split_axis=0, concat_axis=0, tiled=True)
        parted = features(own_points, spread.transpose(1, 0, 2).reshape(2, count, B))
        covers = [cover_rows(*parted, i, lead) for i in range(0, quarter_rows, lead)]
        covers[0] = covers[0] + unit
        panel_prior = lax.all_gather(own_prior, "row", axis=0, tiled=True)
        partial = dot_rows(prior_factor, panel_prior)
        parts = lax.all_to_all(
            partial.reshape(panel_count, quarter_rows, B), "panel", split_axis=0, concat_axis=0, tiled=True
        )
        parts = jnp.sum(parts, axis=0)
        mine = covers[0][:per_device] - parts[:per_device]
        diag_rows = lax.all_gather(mine, ("row", "panel"), axis=0, tiled=True)
        return solve(covers, [parts], factor(factor_kernel, (diag_rows,), B))

    far = swap(own_prior, "row", 4)
    held = jnp.concatenate([local_points] + [swap(local_points, "row", bit) for bit in (2, 4, 6)], 0)
    held = jnp.concatenate([held, swap(held, "row", 1)], 0)
    away = row_pos ^ jnp.arange(8, dtype=jnp.int32)
    order = (away >> 1) | ((away & 1) << 2)
    panel_points = held[order].transpose(1, 0, 2).reshape(2, count, B)
    row_part, col_part = features(own_points, panel_points)
    row_part, far = lax.optimization_barrier((row_part, far))
    covers = []

    def beside(operands, transfer, calls):
        tied = lax.optimization_barrier((operands, row_part))
        received = transfer(tied[0])
        done = [
            cover_rows(tied[1], col_part, lead * (len(covers) + i), lead) for i in range(calls)
        ]
        received, done = lax.optimization_barrier((received, done))
        covers.extend(done)
        return received

    seconds = [((row_pos >> (m.bit_length() - 1)) & 1) == 1 for m in (1, 2, 3)]
    firsts = beside(
        [jnp.where(second, own_prior, far) for second in seconds],
        lambda blocks: [swap(block, "row", m) for m, block in zip((1, 2, 3), blocks)],
        2,
    )
    place = jnp.stack([row_pos, panel_pos]).astype(jnp.int32)
    shares = vmem_call(
        fold_products_kernel,
        [jax.ShapeDtypeStruct((per_device, 5 * NB), F32)] * 4,
        place,
        [own_prior, far, *firsts],
        [pltpu.VMEM((NB, 5 * NB), F32)],
        "fold_products",
    )
    others = [jnp.where(second, far, own_prior) for second in seconds]

    def reduce_and_swap(operands):
        shares, others = operands
        sums = [swap(share, "panel", m) for m, share in zip((1, 2, 3), shares[1:])]
        return sums, [swap(block, "row", m) for m, block in zip((1, 2, 3), others)]

    sums, rest = beside((shares, others), reduce_and_swap, 2)
    covers[0] = covers[0] + unit
    places = [fold_block(row_pos, k) for k in range(5)]
    lead_cover = jnp.concatenate(
        [lax.dynamic_slice(covers[0], (jnp.int32(0), s * NB), (per_device, NB)) for s in places], 1
    )
    shard = lead_cover - (shares[0] + sums[0] + sums[1] + sums[2])

    along = beside(shard[None], lambda x: [swap(x, "row", bit) for bit in (2, 4, 6)], 2)
    held = jnp.concatenate([shard[None]] + along, 0)

    def across(x):
        corner = [(i, i ^ 6) for i in range(32)]
        return swap(x, "row", 1), swap(x, "panel", 2), lax.ppermute(x, ("row", "panel"), corner)

    here = [held, *beside(held, across, 2)]

    panel_prior = vmem_call(
        gather_split_kernel,
        [jax.ShapeDtypeStruct((B, own_prior.shape[1]), BF)] * 2,
        place,
        [own_prior, far, *firsts, *rest],
        name="gather_split",
    )
    here, panel_prior = lax.optimization_barrier((here, panel_prior))
    there = [swap(x, "panel", 1) for x in here]
    parts = []
    for m in (3, 2, 1, 0):
        part = vmem_call(
            functools.partial(rest_products_kernel, m=m),
            jax.ShapeDtypeStruct((quarter_rows, B), F32),
            place,
            [prior_factor, *panel_prior],
            name="rest_products",
        )
        parts.append(swap(part, "panel", m) if m else part)
    factors = factor(unfold_kernel, (place, *here, *there), B)
    return solve(covers, parts, factors)


def solution(mesh):
    return jax.shard_map(
        local,
        mesh=mesh,
        in_specs=(P("row"), P(None, None, "row"), P("row", "panel")),
        out_specs=P(("row", "panel"), None),
        check_vma=False,
    )
```

```python
import functools

import jax
import jax.numpy as jnp
from jax import lax
from jax.experimental import pallas as pl
from jax.experimental.pallas import tpu as pltpu
from jax.sharding import PartitionSpec as P

B = 1024
NB = 128
NEAR = 4
F32 = jnp.float32
BF = jnp.bfloat16
NT = (((1,), (1,)), ((), ()))
SCALE = -1.4426950408889634 / 64.0
CENTRE = 1024.0


def locate(pixel_ids, quad_offsets):
    column = (pixel_ids % 256) * 8
    lines = (pixel_ids // 256) * 8
    east = (column[None, :] + quad_offsets[0]).astype(F32) - CENTRE
    north = (lines[None, :] + quad_offsets[1]).astype(F32) - CENTRE
    return east, north


def pieces(value):
    high = jnp.floor(value * (1.0 / 65536.0)) * 65536.0
    rest = value - high
    mid = jnp.floor(rest * (1.0 / 256.0)) * 256.0
    return [high, mid, rest - mid]


def halves(value):
    high = jnp.floor(value * (1.0 / 128.0)) * 128.0
    return high, value - high


def row_features(x, y):
    xh, xl = halves(x)
    yh, yl = halves(y)
    one = jnp.ones_like(x)
    zero = jnp.zeros_like(x)
    cross = [-2 * xh, -2 * xh, -2 * xl, -2 * xl, -2 * yh, -2 * yh, -2 * yl, -2 * yl]
    return jnp.concatenate(cross + pieces(x * x + y * y) + [one] * 3 + [zero] * 2, 0)


def col_features(x, y):
    xh, xl = halves(x)
    yh, yl = halves(y)
    one = jnp.ones_like(x)
    zero = jnp.zeros_like(x)
    cross = [xh, xl, xh, xl, yh, yl, yh, yl]
    return jnp.concatenate(cross + [one] * 3 + pieces(x * x + y * y) + [zero] * 2, 0)


def feature_kernel(row_ref, col_ref, f_ref, g_ref):
    for a in range(row_ref.shape[1]):
        one = row_features(row_ref[0, a : a + 1, :], row_ref[1, a : a + 1, :])
        f_ref[a] = one.T.astype(BF)
        g_ref[a] = col_features(col_ref[0, a : a + 1, :], col_ref[1, a : a + 1, :]).astype(BF)


def features(row_points, col_points):
    count, rows = row_points.shape[1:]
    cols = col_points.shape[2]
    return pl.pallas_call(
        feature_kernel,
        out_shape=[
            jax.ShapeDtypeStruct((count, rows, 16), BF),
            jax.ShapeDtypeStruct((count, 16, cols), BF),
        ],
        in_specs=[pl.BlockSpec(memory_space=pltpu.VMEM)] * 2,
        out_specs=[pl.BlockSpec(memory_space=pltpu.VMEM)] * 2,
        compiler_params=pltpu.CompilerParams(vmem_limit_bytes=8 << 20),
        name="features",
    )(row_points, col_points)


def cover_kernel(f_ref, g_ref, o_ref):
    count, block = f_ref.shape[:2]
    rows_here = f_ref[...].reshape(count * block, 16)

    def column_point(b, total):
        apart = jnp.dot(rows_here, g_ref[b], preferred_element_type=F32)
        near = jnp.exp2(apart * SCALE)
        for a in range(count):
            total = total + near[a * block : (a + 1) * block]
        return total

    total = lax.fori_loop(0, count, column_point, jnp.zeros(o_ref.shape, F32), unroll=8)
    o_ref[...] = total * (1.0 / (count * count))


def cover_rows(row_part, col_part, first, block):
    count, rows, depth = row_part.shape
    cols = col_part.shape[2]
    index = first // block
    return pl.pallas_call(
        cover_kernel,
        grid=(1,),
        out_shape=jax.ShapeDtypeStruct((block, cols), F32),
        in_specs=[
            pl.BlockSpec((count, block, depth), lambda i: (0, index, 0)),
            pl.BlockSpec((count, depth, cols), lambda i: (0, 0, 0)),
        ],
        out_specs=pl.BlockSpec((block, cols), lambda i: (0, 0)),
        compiler_params=pltpu.CompilerParams(vmem_limit_bytes=16 << 20),
        cost_estimate=pl.CostEstimate(flops=10**8, bytes_accessed=1 << 18, transcendentals=0),
        name="cover",
    )(row_part, col_part)


def inverse_factor(tiles):
    n = len(tiles)
    width = 8 * n
    lane = lax.broadcasted_iota(jnp.int32, (8, width), 1)
    sub = lax.broadcasted_iota(jnp.int32, (8, width), 0)
    tiles = list(tiles)
    out = []

    def spread(x):
        return jnp.broadcast_to(x, (8, width))

    def lanes(tile, v):
        return [spread(tile[:, 8 * v + q : 8 * v + q + 1]) for q in range(8)]

    following = lanes(tiles[0], 0)
    for v in range(n):
        near = min(n, v + NEAR)
        cols = {v: following}
        if v + 1 < n:
            cols[v] = cols[v] + lanes(tiles[v], v + 1)
            cols[v + 1] = lanes(tiles[v + 1], v) + lanes(tiles[v + 1], v + 1)
        for r in range(v + 2, near):
            cols[r] = lanes(tiles[r], v)
        here = (lane >= 8 * v) & (lane < 8 * v + 8)
        for r in range(v + 1, n):
            tiles[r] = jnp.where(here, 0.0, tiles[r])
        tiles[v] = jnp.where(here, jnp.where(lane == sub + 8 * v, 1.0, 0.0), tiles[v])
        pivots = jnp.ones((8, width), F32)
        for s in range(8):
            head = cols[v]
            pivot = spread(head[s][s : s + 1])
            inverse = 1.0 / pivot
            pivots = jnp.where(sub == s, pivot, pivots)
            row = spread(tiles[v][s : s + 1])
            heads = [spread(head[k][s : s + 1]) for k in range(s + 1, len(head))]
            for r in range(v, near):
                part = cols[r][s] * inverse
                if r == v:
                    part = jnp.where(sub > s, part, 0.0)
                tiles[r] = tiles[r] - part * row
                for k in range(s + 1, len(cols[r])):
                    cols[r][k] = cols[r][k] - part * heads[k - s - 1]
        if v + 1 < n:
            following = cols[v + 1][8:]
        rows = tiles[v] * lax.rsqrt(pivots)
        if near < n:
            high = rows.astype(BF).astype(F32)
            low = rows - high
            left = jnp.concatenate([high, high, low, low], 0).astype(BF)
            right = jnp.concatenate([high, low, high, low], 0).astype(BF)
            update = lax.dot_general(
                left, right, (((0,), (0,)), ((), ())), preferred_element_type=F32
            )
            for r in range(near, n):
                tiles[r] = tiles[r] - update[8 * r : 8 * r + 8]
        out.append(jnp.where(lane <= sub + 8 * v, rows, 0.0))
    return jnp.concatenate(out, 0)


def split(x):
    high = x.astype(BF)
    return high, (x - high.astype(F32)).astype(BF)


def dot3(ah, al, bh, bl):
    dot = functools.partial(lax.dot_general, dimension_numbers=NT, preferred_element_type=F32)
    return dot(ah, bh) + (dot(ah, bl) + dot(al, bh))


def factor_blocks(a_ref, lh_ref, ll_ref, wh_ref, wl_ref):
    n = a_ref.shape[0]
    blocks = n // NB

    def column(first):
        end = first + NB
        bh, bl = split(a_ref[end:, first:end])
        high, low = split(dot3(bh, bl, wh_ref[first:end], wl_ref[first:end]))
        lh_ref[end:, first:end] = high
        ll_ref[end:, first:end] = low
        a_ref[end:, end : end + NB] = a_ref[end:, end : end + NB] - dot3(
            lh_ref[end:, :end],
            ll_ref[end:, :end],
            lh_ref[end : end + NB, :end],
            ll_ref[end : end + NB, :end],
        )

    def step(j, _):
        c = pl.multiple_of(j * NB, NB)
        tiles = [a_ref[pl.ds(c + 8 * v, 8), pl.ds(c, NB)] for v in range(NB // 8)]
        wh, wl = split(inverse_factor(tiles))
        wh_ref[pl.ds(c, NB)] = wh
        wl_ref[pl.ds(c, NB)] = wl
        for block in range(blocks - 1):
            pl.when(j == block)(functools.partial(column, block * NB))
        return 0

    lax.fori_loop(0, blocks, step, 0)


def factor_kernel(diag_ref, lh_ref, ll_ref, wh_ref, wl_ref, a_ref):
    a_ref[...] = diag_ref[...]
    factor_blocks(a_ref, lh_ref, ll_ref, wh_ref, wl_ref)


def fold_block(r, k):
    if k < 2:
        return r ^ (4 * k)
    m = k - 1
    low = r & 3
    second = (low >> (m.bit_length() - 1)) & 1
    return (r ^ m) ^ (4 * second)


def unfold_kernel(place_ref, *refs):
    pieces_refs, (lh_ref, ll_ref, wh_ref, wl_ref, a_ref, g_ref) = refs[:8], refs[8:]
    row_pos = place_ref[0]
    panel_pos = place_ref[1]
    for i, ref in enumerate(pieces_refs):
        g_ref[4 * i : 4 * i + 4] = ref[...]

    def rows_of(r, _):
        away = r ^ row_pos
        slot = (away >> 1) | ((away & 1) << 2)
        low = r & 3
        ats = []
        for p in range(4):
            gone = p ^ panel_pos
            ats.append(slot | ((gone >> 1) << 3) | ((gone & 1) << 4))
        for k in range(5):
            block = jnp.concatenate([g_ref[at, :, NB * k : NB * k + NB] for at in ats], 0)
            if k < 2:
                s = r ^ (4 * k)
            else:
                m = k - 1
                second = (low >> (m.bit_length() - 1)) & 1
                s = (r ^ m) ^ (4 * second)
            rr = pl.multiple_of(r * NB, NB)
            ss = pl.multiple_of(s * NB, NB)

            @pl.when(r >= s)
            def _():
                a_ref[pl.ds(rr, NB), pl.ds(ss, NB)] = block

            if k >= 2:

                @pl.when(r < s)
                def _():
                    a_ref[pl.ds(ss, NB), pl.ds(rr, NB)] = block.T

        return 0

    lax.fori_loop(0, 8, rows_of, 0)
    factor_blocks(a_ref, lh_ref, ll_ref, wh_ref, wl_ref)


def factor(kernel, operands, n):
    in_specs = [pl.BlockSpec(memory_space=pltpu.VMEM)] * len(operands)
    scratch = [pltpu.VMEM((n, n), F32)]
    if kernel is unfold_kernel:
        in_specs[0] = pl.BlockSpec(memory_space=pltpu.SMEM)
        scratch.append(pltpu.VMEM((32, *operands[1].shape[1:]), F32))
    return pl.pallas_call(
        kernel,
        out_shape=[jax.ShapeDtypeStruct((n, n), BF)] * 2 + [jax.ShapeDtypeStruct((n, NB), BF)] * 2,
        in_specs=in_specs,
        out_specs=[pl.BlockSpec(memory_space=pltpu.VMEM)] * 4,
        scratch_shapes=scratch,
        compiler_params=pltpu.CompilerParams(vmem_limit_bytes=32 << 20),
        cost_estimate=pl.CostEstimate(flops=5 * 10**10, bytes_accessed=8 << 20, transcendentals=0),
        name="factor",
    )(*operands)


def solve_kernel(*refs, covers):
    cover_refs, parts_refs = refs[:covers], refs[covers:-7]
    lh_ref, ll_ref, wh_ref, wl_ref, o_ref, xh_ref, xl_ref = refs[-7:]
    n = o_ref.shape[1]
    first = 0
    for ref in cover_refs:
        rows = pl.ds(first, ref.shape[0])
        taken = parts_refs[0][rows]
        for part in parts_refs[1:]:
            taken = taken + part[rows]
        o_ref[rows] = ref[...] - taken
        first += ref.shape[0]
    for c in range(0, n, NB):
        here = o_ref[:, c : c + NB]
        if c:
            here = here - dot3(
                xh_ref[:, :c], xl_ref[:, :c], lh_ref[c : c + NB, :c], ll_ref[c : c + NB, :c]
            )
        bh, bl = split(here)
        x = dot3(bh, bl, wh_ref[c : c + NB], wl_ref[c : c + NB])
        o_ref[:, c : c + NB] = x
        xh, xl = split(x)
        xh_ref[:, c : c + NB] = xh
        xl_ref[:, c : c + NB] = xl


def solve(covers, parts, factors):
    rows = sum(c.shape[0] for c in covers)
    n = covers[0].shape[1]
    operands = (*covers, *parts, *factors)
    return pl.pallas_call(
        functools.partial(solve_kernel, covers=len(covers)),
        out_shape=jax.ShapeDtypeStruct((rows, n), F32),
        in_specs=[pl.BlockSpec(memory_space=pltpu.VMEM)] * len(operands),
        out_specs=pl.BlockSpec(memory_space=pltpu.VMEM),
        scratch_shapes=[pltpu.VMEM((rows, n), BF)] * 2,
        compiler_params=pltpu.CompilerParams(vmem_limit_bytes=32 << 20),
        name="solve",
    )(*operands)


def vmem_call(kernel, out_shape, place, operands, scratch=(), name=None):
    return pl.pallas_call(
        kernel,
        out_shape=out_shape,
        in_specs=[pl.BlockSpec(memory_space=pltpu.SMEM)]
        + [pl.BlockSpec(memory_space=pltpu.VMEM)] * len(operands),
        out_specs=jax.tree.map(lambda _: pl.BlockSpec(memory_space=pltpu.VMEM), out_shape),
        scratch_shapes=list(scratch),
        compiler_params=pltpu.CompilerParams(vmem_limit_bytes=16 << 20),
        cost_estimate=pl.CostEstimate(flops=10**8, bytes_accessed=1 << 18, transcendentals=0),
        name=name,
    )(place, *operands)


def fold_products_kernel(place_ref, *refs):
    blocks, shares, total_ref = refs[:5], refs[5:-1], refs[-1]
    own_high, own_low = split(blocks[0][...])
    for k, ref in enumerate(blocks):
        high, low = split(ref[...])
        total_ref[:, NB * k : NB * k + NB] = dot3(own_high, own_low, high, low)
    rows = shares[0].shape[0]
    for m, ref in enumerate(shares):
        first = pl.multiple_of((place_ref[1] ^ m) * rows, rows)
        ref[...] = total_ref[pl.ds(first, rows)]


def gather_split_kernel(place_ref, *refs):
    blocks, (high_ref, low_ref) = refs[:-2], refs[-2:]
    row_pos = place_ref[0]
    order = [fold_block(row_pos, k) for k in range(5)]
    order = order + [order[k] ^ 4 for k in (2, 3, 4)]
    for s, ref in zip(order, blocks):
        first = pl.multiple_of(s * NB, NB)
        high, low = split(ref[...])
        high_ref[pl.ds(first, NB)] = high
        low_ref[pl.ds(first, NB)] = low


def rest_products_kernel(place_ref, prior_ref, high_ref, low_ref, *refs, m):
    o_ref = refs[-1]
    rows = o_ref.shape[0]
    first = pl.multiple_of((place_ref[1] ^ m) * rows, rows)
    own_high, own_low = split(prior_ref[pl.ds(first, rows)])
    for c in range(0, o_ref.shape[1], 2 * NB):
        cols = slice(c, c + 2 * NB)
        total = dot3(own_high, own_low, high_ref[cols], low_ref[cols])
        for plus_ref in refs[:-1]:
            total = total + plus_ref[:, cols]
        o_ref[:, cols] = total


def swap(block, axis, bit):
    return lax.ppermute(block, axis, [(i, i ^ bit) for i in range(lax.axis_size(axis))])


def dot_rows(left, right):
    return lax.dot_general(
        left, right, NT, precision=lax.Precision.HIGH, preferred_element_type=F32
    )


def local(pixel_ids, quad_offsets, prior_factor):
    panel_count = lax.axis_size("panel")
    row_count = lax.axis_size("row")
    block_rows = pixel_ids.shape[0]
    quarter_rows = block_rows // panel_count
    per_device = B // (row_count * panel_count)
    span_cols = panel_count * per_device
    row_pos = lax.axis_index("row")
    panel_pos = lax.axis_index("panel")
    device_pos = row_pos * panel_count + panel_pos
    lead = 32

    points = jnp.stack(locate(pixel_ids, quad_offsets))
    count = points.shape[1]
    own_points = lax.dynamic_slice_in_dim(points, panel_pos * quarter_rows, quarter_rows, 2)
    local_points = points.reshape(2, count, panel_count, quarter_rows)[:, :, :, :per_device]
    local_points = local_points.reshape(1, 2 * count, span_cols)

    row_ids = jnp.arange(lead, dtype=jnp.int32)[:, None]
    col_ids = jnp.arange(B, dtype=jnp.int32)[None, :]
    on_diagonal = (row_ids < per_device) & (col_ids == device_pos * per_device + row_ids)
    unit = jnp.where(on_diagonal, 1.0, 0.0).astype(F32)

    own_prior = prior_factor.reshape(panel_count, quarter_rows, -1)[:, :per_device]
    own_prior = own_prior.reshape(span_cols, -1)

    if not (span_cols == NB and row_count == 8 and panel_count == 4):
        copies = jnp.broadcast_to(local_points, (row_count, 2 * count, span_cols))
        spread = lax.all_to_all(copies, "row", split_axis=0, concat_axis=0, tiled=True)
        parted = features(own_points, spread.transpose(1, 0, 2).reshape(2, count, B))
        covers = [cover_rows(*parted, i, lead) for i in range(0, quarter_rows, lead)]
        covers[0] = covers[0] + unit
        panel_prior = lax.all_gather(own_prior, "row", axis=0, tiled=True)
        partial = dot_rows(prior_factor, panel_prior)
        parts = lax.all_to_all(
            partial.reshape(panel_count, quarter_rows, B), "panel", split_axis=0, concat_axis=0, tiled=True
        )
        parts = jnp.sum(parts, axis=0)
        mine = covers[0][:per_device] - parts[:per_device]
        diag_rows = lax.all_gather(mine, ("row", "panel"), axis=0, tiled=True)
        return solve(covers, [parts], factor(factor_kernel, (diag_rows,), B))

    far = swap(own_prior, "row", 4)
    held = jnp.concatenate([local_points] + [swap(local_points, "row", bit) for bit in (2, 4, 6)], 0)
    held = jnp.concatenate([held, swap(held, "row", 1)], 0)
    away = row_pos ^ jnp.arange(8, dtype=jnp.int32)
    order = (away >> 1) | ((away & 1) << 2)
    panel_points = held[order].transpose(1, 0, 2).reshape(2, count, B)
    row_part, col_part = features(own_points, panel_points)
    covers = [cover_rows(row_part, col_part, 0, lead) + unit]
    row_part, far, covers = lax.optimization_barrier((row_part, far, covers))

    def beside(operands, transfer, calls, extra=lambda *_: ()):
        tied = lax.optimization_barrier((operands, row_part))
        received = transfer(tied[0])
        done = [
            cover_rows(tied[1], col_part, lead * (len(covers) + i), lead) for i in range(calls)
        ]
        received, done, more = lax.optimization_barrier((received, done, extra(tied[0])))
        covers.extend(done)
        return (received, more) if more else received

    seconds = [((row_pos >> (m.bit_length() - 1)) & 1) == 1 for m in (1, 2, 3)]
    firsts = beside(
        [jnp.where(second, own_prior, far) for second in seconds],
        lambda blocks: [swap(block, "row", m) for m, block in zip((1, 2, 3), blocks)],
        2,
    )
    place = jnp.stack([row_pos, panel_pos]).astype(jnp.int32)
    shares = vmem_call(
        fold_products_kernel,
        [jax.ShapeDtypeStruct((per_device, 5 * NB), F32)] * 4,
        place,
        [own_prior, far, *firsts],
        [pltpu.VMEM((NB, 5 * NB), F32)],
        "fold_products",
    )
    others = [jnp.where(second, far, own_prior) for second in seconds]
    shares, others = lax.optimization_barrier((shares, others))
    sums = beside(
        shares,
        lambda shares: [swap(share, "panel", m) for m, share in zip((1, 2, 3), shares[1:])],
        1,
    )
    rest = [swap(block, "row", m) for m, block in zip((1, 2, 3), others)]
    places = [fold_block(row_pos, k) for k in range(5)]
    lead_cover = jnp.concatenate(
        [lax.dynamic_slice(covers[0], (jnp.int32(0), s * NB), (per_device, NB)) for s in places], 1
    )
    shard = lead_cover - (shares[0] + sums[0] + sums[1] + sums[2])

    def rest_part(panel_prior, m, plus=()):
        return vmem_call(
            functools.partial(rest_products_kernel, m=m),
            jax.ShapeDtypeStruct((quarter_rows, B), F32),
            place,
            [prior_factor, *panel_prior, *plus],
            name="rest_products",
        )

    def for_other_core(_):
        panel_prior = vmem_call(
            gather_split_kernel,
            [jax.ShapeDtypeStruct((B, own_prior.shape[1]), BF)] * 2,
            place,
            [own_prior, far, *firsts, *rest],
            name="gather_split",
        )
        return panel_prior, rest_part(panel_prior, 3), rest_part(panel_prior, 1)

    along, (panel_prior, part_3, part_1) = beside(
        shard[None],
        lambda x: [swap(x, "row", bit) for bit in (2, 4, 6)],
        2,
        for_other_core,
    )
    held = jnp.concatenate([shard[None]] + along, 0)

    def across(operands):
        x = operands[0]
        corner = [(i, i ^ 6) for i in range(32)]
        return swap(x, "row", 1), swap(x, "panel", 2), lax.ppermute(x, ("row", "panel"), corner)

    def for_own_core(operands):
        panel_prior, part_3, part_1 = operands[1]
        from_3, from_1 = swap(part_3, "panel", 1), swap(part_1, "panel", 1)
        return rest_part(panel_prior, 0), rest_part(panel_prior, 2, [from_3]), from_1

    received, (part_0, part_2, from_1) = beside(
        (held, (panel_prior, part_3, part_1)), across, 2, for_own_core
    )
    here = [held, *received]
    there = [swap(x, "panel", 1) for x in here]
    parts = [part_0, from_1, swap(part_2, "panel", 2)]
    factors = factor(unfold_kernel, (place, *here, *there), B)
    return solve(covers, parts, factors)


def solution(mesh):
    return jax.shard_map(
        local,
        mesh=mesh,
        in_specs=(P("row"), P(None, None, "row"), P("row", "panel")),
        out_specs=P(("row", "panel"), None),
        check_vma=False,
    )
```

```python
import functools

import jax
import jax.numpy as jnp
from jax import lax
from jax.experimental import pallas as pl
from jax.experimental.pallas import tpu as pltpu
from jax.sharding import PartitionSpec as P

B = 1024
NB = 128
NEAR = 4
F32 = jnp.float32
BF = jnp.bfloat16
NT = (((1,), (1,)), ((), ()))
SCALE = -1.4426950408889634 / 64.0
CENTRE = 1024.0


def locate(pixel_ids, quad_offsets):
    column = (pixel_ids % 256) * 8
    lines = (pixel_ids // 256) * 8
    east = (column[None, :] + quad_offsets[0]).astype(F32) - CENTRE
    north = (lines[None, :] + quad_offsets[1]).astype(F32) - CENTRE
    return east, north


def pieces(value):
    high = jnp.floor(value * (1.0 / 65536.0)) * 65536.0
    rest = value - high
    mid = jnp.floor(rest * (1.0 / 256.0)) * 256.0
    return [high, mid, rest - mid]


def halves(value):
    high = jnp.floor(value * (1.0 / 128.0)) * 128.0
    return high, value - high


def row_features(x, y):
    xh, xl = halves(x)
    yh, yl = halves(y)
    one = jnp.ones_like(x)
    zero = jnp.zeros_like(x)
    cross = [-2 * xh, -2 * xh, -2 * xl, -2 * xl, -2 * yh, -2 * yh, -2 * yl, -2 * yl]
    return jnp.concatenate(cross + pieces(x * x + y * y) + [one] * 3 + [zero] * 2, 0)


def col_features(x, y):
    xh, xl = halves(x)
    yh, yl = halves(y)
    one = jnp.ones_like(x)
    zero = jnp.zeros_like(x)
    cross = [xh, xl, xh, xl, yh, yl, yh, yl]
    return jnp.concatenate(cross + [one] * 3 + pieces(x * x + y * y) + [zero] * 2, 0)


def feature_kernel(row_ref, col_ref, f_ref, g_ref):
    for a in range(row_ref.shape[1]):
        one = row_features(row_ref[0, a : a + 1, :], row_ref[1, a : a + 1, :])
        f_ref[a] = one.T.astype(BF)
        g_ref[a] = col_features(col_ref[0, a : a + 1, :], col_ref[1, a : a + 1, :]).astype(BF)


def features(row_points, col_points):
    count, rows = row_points.shape[1:]
    cols = col_points.shape[2]
    return pl.pallas_call(
        feature_kernel,
        out_shape=[
            jax.ShapeDtypeStruct((count, rows, 16), BF),
            jax.ShapeDtypeStruct((count, 16, cols), BF),
        ],
        in_specs=[pl.BlockSpec(memory_space=pltpu.VMEM)] * 2,
        out_specs=[pl.BlockSpec(memory_space=pltpu.VMEM)] * 2,
        compiler_params=pltpu.CompilerParams(vmem_limit_bytes=8 << 20),
        name="features",
    )(row_points, col_points)


def cover_kernel(f_ref, g_ref, o_ref):
    count, block = f_ref.shape[:2]
    rows_here = f_ref[...].reshape(count * block, 16)

    def column_point(b, total):
        apart = jnp.dot(rows_here, g_ref[b], preferred_element_type=F32)
        near = jnp.exp2(apart * SCALE)
        for a in range(count):
            total = total + near[a * block : (a + 1) * block]
        return total

    total = lax.fori_loop(0, count, column_point, jnp.zeros(o_ref.shape, F32), unroll=8)
    o_ref[...] = total * (1.0 / (count * count))


def cover_rows(row_part, col_part, first, block):
    count, rows, depth = row_part.shape
    cols = col_part.shape[2]
    index = first // block
    return pl.pallas_call(
        cover_kernel,
        grid=(1,),
        out_shape=jax.ShapeDtypeStruct((block, cols), F32),
        in_specs=[
            pl.BlockSpec((count, block, depth), lambda i: (0, index, 0)),
            pl.BlockSpec((count, depth, cols), lambda i: (0, 0, 0)),
        ],
        out_specs=pl.BlockSpec((block, cols), lambda i: (0, 0)),
        compiler_params=pltpu.CompilerParams(vmem_limit_bytes=16 << 20),
        cost_estimate=pl.CostEstimate(flops=10**8, bytes_accessed=1 << 18, transcendentals=0),
        name="cover",
    )(row_part, col_part)


def lattice_kernel(row_ref, col_ref, t_ref, h_ref, row_cell_ref, col_cell_ref, place_ref):
    count, rows = row_ref.shape[1:]
    lines, cols = h_ref.shape[1:]
    row_cell = jnp.floor(row_ref[0] * 0.125) * 8.0
    place_ref[0] = (row_ref[0] - row_cell).T
    place_ref[1] = row_ref[1].T
    row_cell_ref[...] = row_cell[0:1].T
    col_cell_ref[...] = jnp.floor(col_ref[0, 0:1] * 0.125) * 8.0

    def row_tile(index, _):
        here = pl.ds(pl.multiple_of(index * 16, 16), 16)
        offset, north = place_ref[0, here], place_ref[1, here]
        line = lax.broadcasted_iota(jnp.int32, (16, lines), 1).astype(F32) - CENTRE
        total = [jnp.zeros((16, lines), F32) for _ in range(8)]
        for a in range(count):
            apart = jnp.broadcast_to(north[:, a : a + 1], (16, lines)) - line
            near = jnp.exp2(apart * apart * SCALE)
            which = jnp.broadcast_to(offset[:, a : a + 1], (16, lines))
            for p in range(8):
                total[p] = total[p] + jnp.where(which == float(p), near, 0.0)
        for p in range(8):
            high, low = split(total[p])
            t_ref[p, here, :lines] = high
            t_ref[p, here, lines:] = low
        return 0

    lax.fori_loop(0, rows // 16, row_tile, 0)

    def col_tile(index, _):
        here = pl.ds(pl.multiple_of(index * 256, 256), 256)
        east, north = col_ref[0, :, here], col_ref[1, :, here]
        east = east - jnp.floor(east * 0.125) * 8.0
        line = jnp.floor(north[0:1] * 0.125) * 8.0
        north = north - line
        sub = lax.broadcasted_iota(jnp.int32, (8, 256), 0).astype(F32)
        held = [jnp.zeros((8, 256), F32) for _ in range(8)]
        for b in range(count):
            one = jnp.where(sub == jnp.broadcast_to(north[b : b + 1], (8, 256)), 1.0, 0.0)
            which = jnp.broadcast_to(east[b : b + 1], (8, 256))
            for q in range(8):
                held[q] = held[q] + jnp.where(which == float(q), one, 0.0)
        line = jnp.broadcast_to(line, (8, 256))
        for r in range(0, lines, 16):
            low = line == float(r) - CENTRE
            high = line == float(r + 8) - CENTRE
            for q in range(8):
                pair = [jnp.where(low, held[q], 0.0), jnp.where(high, held[q], 0.0)]
                h_ref[q, r : r + 16, here] = jnp.concatenate(pair, 0).astype(BF)
        return 0

    lax.fori_loop(0, cols // 256, col_tile, 0)


def lattice(row_points, col_points, lines):
    count, rows = row_points.shape[1:]
    cols = col_points.shape[2]
    return pl.pallas_call(
        lattice_kernel,
        out_shape=[
            jax.ShapeDtypeStruct((8, rows, 2 * lines), BF),
            jax.ShapeDtypeStruct((8, lines, cols), BF),
            jax.ShapeDtypeStruct((rows, 1), F32),
            jax.ShapeDtypeStruct((1, cols), F32),
        ],
        in_specs=[pl.BlockSpec(memory_space=pltpu.VMEM)] * 2,
        out_specs=[pl.BlockSpec(memory_space=pltpu.VMEM)] * 4,
        scratch_shapes=[pltpu.VMEM((2, rows, count), F32)],
        compiler_params=pltpu.CompilerParams(vmem_limit_bytes=24 << 20),
        cost_estimate=pl.CostEstimate(flops=10**8, bytes_accessed=1 << 18, transcendentals=0),
        name="lattice",
    )(row_points, col_points)


def lattice_cover_kernel(first_ref, t_ref, h_ref, row_cell_ref, col_cell_ref, o_ref, east_ref, *, points):
    block, cols = o_ref.shape
    here = pl.ds(pl.multiple_of(first_ref[0], block), block)
    cell = jnp.broadcast_to(row_cell_ref[here], (block, cols)) - col_cell_ref[...]
    for t in range(15):
        apart = cell + float(t - 7)
        east_ref[t] = jnp.exp2(apart * apart * SCALE)
    rows = t_ref[:, here].reshape(8 * block, t_ref.shape[2])
    total = jnp.zeros((block, cols), F32)
    for q in range(8):
        part = jnp.dot(
            rows, jnp.concatenate([h_ref[q], h_ref[q]], 0), preferred_element_type=F32
        )
        for p in range(8):
            total = total + part[p * block : (p + 1) * block] * east_ref[p - q + 7]
    o_ref[...] = total * (1.0 / (points * points))


def lattice_cover(parts, first, block, points):
    cols = parts[1].shape[2]
    return pl.pallas_call(
        functools.partial(lattice_cover_kernel, points=points),
        out_shape=jax.ShapeDtypeStruct((block, cols), F32),
        in_specs=[pl.BlockSpec(memory_space=pltpu.SMEM)]
        + [pl.BlockSpec(memory_space=pltpu.VMEM)] * 4,
        out_specs=pl.BlockSpec(memory_space=pltpu.VMEM),
        scratch_shapes=[pltpu.VMEM((15, block, cols), F32)],
        compiler_params=pltpu.CompilerParams(vmem_limit_bytes=24 << 20),
        cost_estimate=pl.CostEstimate(flops=10**8, bytes_accessed=1 << 18, transcendentals=0),
        name="cover",
    )(jnp.full((1,), first, jnp.int32), *parts)


def inverse_factor(tiles):
    n = len(tiles)
    width = 8 * n
    lane = lax.broadcasted_iota(jnp.int32, (8, width), 1)
    sub = lax.broadcasted_iota(jnp.int32, (8, width), 0)
    tiles = list(tiles)
    out = []

    def spread(x):
        return jnp.broadcast_to(x, (8, width))

    def lanes(tile, v):
        return [spread(tile[:, 8 * v + q : 8 * v + q + 1]) for q in range(8)]

    following = lanes(tiles[0], 0)
    for v in range(n):
        near = min(n, v + NEAR)
        cols = {v: following}
        if v + 1 < n:
            cols[v] = cols[v] + lanes(tiles[v], v + 1)
            cols[v + 1] = lanes(tiles[v + 1], v) + lanes(tiles[v + 1], v + 1)
        for r in range(v + 2, near):
            cols[r] = lanes(tiles[r], v)
        here = (lane >= 8 * v) & (lane < 8 * v + 8)
        for r in range(v + 1, n):
            tiles[r] = jnp.where(here, 0.0, tiles[r])
        tiles[v] = jnp.where(here, jnp.where(lane == sub + 8 * v, 1.0, 0.0), tiles[v])
        pivots = jnp.ones((8, width), F32)
        for s in range(8):
            head = cols[v]
            pivot = spread(head[s][s : s + 1])
            inverse = 1.0 / pivot
            pivots = jnp.where(sub == s, pivot, pivots)
            row = spread(tiles[v][s : s + 1])
            heads = [spread(head[k][s : s + 1]) for k in range(s + 1, len(head))]
            for r in range(v, near):
                part = cols[r][s] * inverse
                if r == v:
                    part = jnp.where(sub > s, part, 0.0)
                tiles[r] = tiles[r] - part * row
                for k in range(s + 1, len(cols[r])):
                    cols[r][k] = cols[r][k] - part * heads[k - s - 1]
        if v + 1 < n:
            following = cols[v + 1][8:]
        rows = tiles[v] * lax.rsqrt(pivots)
        if near < n:
            high = rows.astype(BF).astype(F32)
            low = rows - high
            left = jnp.concatenate([high, high, low, low], 0).astype(BF)
            right = jnp.concatenate([high, low, high, low], 0).astype(BF)
            update = lax.dot_general(
                left, right, (((0,), (0,)), ((), ())), preferred_element_type=F32
            )
            for r in range(near, n):
                tiles[r] = tiles[r] - update[8 * r : 8 * r + 8]
        out.append(jnp.where(lane <= sub + 8 * v, rows, 0.0))
    return jnp.concatenate(out, 0)


def split(x):
    high = x.astype(BF)
    return high, (x - high.astype(F32)).astype(BF)


def dot3(ah, al, bh, bl):
    dot = functools.partial(lax.dot_general, dimension_numbers=NT, preferred_element_type=F32)
    return dot(ah, bh) + (dot(ah, bl) + dot(al, bh))


def factor_blocks(a_ref, lh_ref, ll_ref, wh_ref, wl_ref):
    n = a_ref.shape[0]
    blocks = n // NB

    def column(first):
        end = first + NB
        bh, bl = split(a_ref[end:, first:end])
        high, low = split(dot3(bh, bl, wh_ref[first:end], wl_ref[first:end]))
        lh_ref[end:, first:end] = high
        ll_ref[end:, first:end] = low
        a_ref[end:, end : end + NB] = a_ref[end:, end : end + NB] - dot3(
            lh_ref[end:, :end],
            ll_ref[end:, :end],
            lh_ref[end : end + NB, :end],
            ll_ref[end : end + NB, :end],
        )

    def step(j, _):
        c = pl.multiple_of(j * NB, NB)
        tiles = [a_ref[pl.ds(c + 8 * v, 8), pl.ds(c, NB)] for v in range(NB // 8)]
        wh, wl = split(inverse_factor(tiles))
        wh_ref[pl.ds(c, NB)] = wh
        wl_ref[pl.ds(c, NB)] = wl
        for block in range(blocks - 1):
            pl.when(j == block)(functools.partial(column, block * NB))
        return 0

    lax.fori_loop(0, blocks, step, 0)


def factor_kernel(diag_ref, lh_ref, ll_ref, wh_ref, wl_ref, a_ref):
    a_ref[...] = diag_ref[...]
    factor_blocks(a_ref, lh_ref, ll_ref, wh_ref, wl_ref)


def fold_block(r, k):
    if k < 2:
        return r ^ (4 * k)
    m = k - 1
    low = r & 3
    second = (low >> (m.bit_length() - 1)) & 1
    return (r ^ m) ^ (4 * second)


def unfold_kernel(place_ref, *refs):
    pieces_refs, (lh_ref, ll_ref, wh_ref, wl_ref, a_ref, g_ref) = refs[:8], refs[8:]
    row_pos = place_ref[0]
    panel_pos = place_ref[1]
    for i, ref in enumerate(pieces_refs):
        g_ref[4 * i : 4 * i + 4] = ref[...]

    def rows_of(r, _):
        away = r ^ row_pos
        slot = (away >> 1) | ((away & 1) << 2)
        low = r & 3
        ats = []
        for p in range(4):
            gone = p ^ panel_pos
            ats.append(slot | ((gone >> 1) << 3) | ((gone & 1) << 4))
        for k in range(5):
            block = jnp.concatenate([g_ref[at, :, NB * k : NB * k + NB] for at in ats], 0)
            if k < 2:
                s = r ^ (4 * k)
            else:
                m = k - 1
                second = (low >> (m.bit_length() - 1)) & 1
                s = (r ^ m) ^ (4 * second)
            rr = pl.multiple_of(r * NB, NB)
            ss = pl.multiple_of(s * NB, NB)

            @pl.when(r >= s)
            def _():
                a_ref[pl.ds(rr, NB), pl.ds(ss, NB)] = block

            if k >= 2:

                @pl.when(r < s)
                def _():
                    a_ref[pl.ds(ss, NB), pl.ds(rr, NB)] = block.T

        return 0

    lax.fori_loop(0, 8, rows_of, 0)
    factor_blocks(a_ref, lh_ref, ll_ref, wh_ref, wl_ref)


def factor(kernel, operands, n):
    in_specs = [pl.BlockSpec(memory_space=pltpu.VMEM)] * len(operands)
    scratch = [pltpu.VMEM((n, n), F32)]
    if kernel is unfold_kernel:
        in_specs[0] = pl.BlockSpec(memory_space=pltpu.SMEM)
        scratch.append(pltpu.VMEM((32, *operands[1].shape[1:]), F32))
    return pl.pallas_call(
        kernel,
        out_shape=[jax.ShapeDtypeStruct((n, n), BF)] * 2 + [jax.ShapeDtypeStruct((n, NB), BF)] * 2,
        in_specs=in_specs,
        out_specs=[pl.BlockSpec(memory_space=pltpu.VMEM)] * 4,
        scratch_shapes=scratch,
        compiler_params=pltpu.CompilerParams(vmem_limit_bytes=32 << 20),
        cost_estimate=pl.CostEstimate(flops=5 * 10**10, bytes_accessed=8 << 20, transcendentals=0),
        name="factor",
    )(*operands)


def solve_kernel(*refs, covers):
    cover_refs, parts_refs = refs[:covers], refs[covers:-7]
    lh_ref, ll_ref, wh_ref, wl_ref, o_ref, xh_ref, xl_ref = refs[-7:]
    n = o_ref.shape[1]
    first = 0
    for ref in cover_refs:
        rows = pl.ds(first, ref.shape[0])
        taken = parts_refs[0][rows]
        for part in parts_refs[1:]:
            taken = taken + part[rows]
        o_ref[rows] = ref[...] - taken
        first += ref.shape[0]
    for c in range(0, n, NB):
        here = o_ref[:, c : c + NB]
        if c:
            here = here - dot3(
                xh_ref[:, :c], xl_ref[:, :c], lh_ref[c : c + NB, :c], ll_ref[c : c + NB, :c]
            )
        bh, bl = split(here)
        x = dot3(bh, bl, wh_ref[c : c + NB], wl_ref[c : c + NB])
        o_ref[:, c : c + NB] = x
        xh, xl = split(x)
        xh_ref[:, c : c + NB] = xh
        xl_ref[:, c : c + NB] = xl


def solve(covers, parts, factors):
    rows = sum(c.shape[0] for c in covers)
    n = covers[0].shape[1]
    operands = (*covers, *parts, *factors)
    return pl.pallas_call(
        functools.partial(solve_kernel, covers=len(covers)),
        out_shape=jax.ShapeDtypeStruct((rows, n), F32),
        in_specs=[pl.BlockSpec(memory_space=pltpu.VMEM)] * len(operands),
        out_specs=pl.BlockSpec(memory_space=pltpu.VMEM),
        scratch_shapes=[pltpu.VMEM((rows, n), BF)] * 2,
        compiler_params=pltpu.CompilerParams(vmem_limit_bytes=32 << 20),
        name="solve",
    )(*operands)


def vmem_call(kernel, out_shape, place, operands, scratch=(), name=None):
    return pl.pallas_call(
        kernel,
        out_shape=out_shape,
        in_specs=[pl.BlockSpec(memory_space=pltpu.SMEM)]
        + [pl.BlockSpec(memory_space=pltpu.VMEM)] * len(operands),
        out_specs=jax.tree.map(lambda _: pl.BlockSpec(memory_space=pltpu.VMEM), out_shape),
        scratch_shapes=list(scratch),
        compiler_params=pltpu.CompilerParams(vmem_limit_bytes=16 << 20),
        cost_estimate=pl.CostEstimate(flops=10**8, bytes_accessed=1 << 18, transcendentals=0),
        name=name,
    )(place, *operands)


def fold_products_kernel(place_ref, *refs):
    blocks, shares, total_ref = refs[:5], refs[5:-1], refs[-1]
    own_high, own_low = split(blocks[0][...])
    for k, ref in enumerate(blocks):
        high, low = split(ref[...])
        total_ref[:, NB * k : NB * k + NB] = dot3(own_high, own_low, high, low)
    rows = shares[0].shape[0]
    for m, ref in enumerate(shares):
        first = pl.multiple_of((place_ref[1] ^ m) * rows, rows)
        ref[...] = total_ref[pl.ds(first, rows)]


def gather_split_kernel(place_ref, *refs):
    blocks, (high_ref, low_ref) = refs[:-2], refs[-2:]
    row_pos = place_ref[0]
    order = [fold_block(row_pos, k) for k in range(5)]
    order = order + [order[k] ^ 4 for k in (2, 3, 4)]
    for s, ref in zip(order, blocks):
        first = pl.multiple_of(s * NB, NB)
        high, low = split(ref[...])
        high_ref[pl.ds(first, NB)] = high
        low_ref[pl.ds(first, NB)] = low


def rest_products_kernel(place_ref, prior_ref, high_ref, low_ref, *refs, m):
    o_ref = refs[-1]
    rows = o_ref.shape[0]
    first = pl.multiple_of((place_ref[1] ^ m) * rows, rows)
    own_high, own_low = split(prior_ref[pl.ds(first, rows)])
    for c in range(0, o_ref.shape[1], 2 * NB):
        cols = slice(c, c + 2 * NB)
        total = dot3(own_high, own_low, high_ref[cols], low_ref[cols])
        for plus_ref in refs[:-1]:
            total = total + plus_ref[:, cols]
        o_ref[:, cols] = total


def swap(block, axis, bit):
    return lax.ppermute(block, axis, [(i, i ^ bit) for i in range(lax.axis_size(axis))])


def dot_rows(left, right):
    return lax.dot_general(
        left, right, NT, precision=lax.Precision.HIGH, preferred_element_type=F32
    )


def local(pixel_ids, quad_offsets, prior_factor):
    panel_count = lax.axis_size("panel")
    row_count = lax.axis_size("row")
    block_rows = pixel_ids.shape[0]
    quarter_rows = block_rows // panel_count
    per_device = B // (row_count * panel_count)
    span_cols = panel_count * per_device
    row_pos = lax.axis_index("row")
    panel_pos = lax.axis_index("panel")
    device_pos = row_pos * panel_count + panel_pos
    lead = 32

    points = jnp.stack(locate(pixel_ids, quad_offsets))
    count = points.shape[1]
    own_points = lax.dynamic_slice_in_dim(points, panel_pos * quarter_rows, quarter_rows, 2)
    local_points = points.reshape(2, count, panel_count, quarter_rows)[:, :, :, :per_device]
    local_points = local_points.reshape(1, 2 * count, span_cols)

    row_ids = jnp.arange(lead, dtype=jnp.int32)[:, None]
    col_ids = jnp.arange(B, dtype=jnp.int32)[None, :]
    on_diagonal = (row_ids < per_device) & (col_ids == device_pos * per_device + row_ids)
    unit = jnp.where(on_diagonal, 1.0, 0.0).astype(F32)

    own_prior = prior_factor.reshape(panel_count, quarter_rows, -1)[:, :per_device]
    own_prior = own_prior.reshape(span_cols, -1)

    lines = block_rows * row_count // 256 * 8
    if not (span_cols == NB and row_count == 8 and panel_count == 4 and lines == 256):
        copies = jnp.broadcast_to(local_points, (row_count, 2 * count, span_cols))
        spread = lax.all_to_all(copies, "row", split_axis=0, concat_axis=0, tiled=True)
        parted = features(own_points, spread.transpose(1, 0, 2).reshape(2, count, B))
        covers = [cover_rows(*parted, i, lead) for i in range(0, quarter_rows, lead)]
        covers[0] = covers[0] + unit
        panel_prior = lax.all_gather(own_prior, "row", axis=0, tiled=True)
        partial = dot_rows(prior_factor, panel_prior)
        parts = lax.all_to_all(
            partial.reshape(panel_count, quarter_rows, B), "panel", split_axis=0, concat_axis=0, tiled=True
        )
        parts = jnp.sum(parts, axis=0)
        mine = covers[0][:per_device] - parts[:per_device]
        diag_rows = lax.all_gather(mine, ("row", "panel"), axis=0, tiled=True)
        return solve(covers, [parts], factor(factor_kernel, (diag_rows,), B))

    own_prior, local_points = lax.optimization_barrier((own_prior, local_points))
    far = swap(own_prior, "row", 4)
    held = jnp.concatenate([local_points] + [swap(local_points, "row", bit) for bit in (2, 4, 6)], 0)
    held = jnp.concatenate([held, swap(held, "row", 1)], 0)
    away = row_pos ^ jnp.arange(8, dtype=jnp.int32)
    order = (away >> 1) | ((away & 1) << 2)
    panel_points = held[order].transpose(1, 0, 2).reshape(2, count, B)
    parted = lattice(own_points, panel_points, lines)
    covers = [lattice_cover(parted, 0, lead, count) + unit]
    parted, far, covers = lax.optimization_barrier((parted, far, covers))

    def beside(operands, transfer, calls, extra=lambda *_: ()):
        tied = lax.optimization_barrier((operands, parted))
        received = transfer(tied[0])
        done = [
            lattice_cover(tied[1], lead * (len(covers) + i), lead, count) for i in range(calls)
        ]
        received, done, more = lax.optimization_barrier((received, done, extra(tied[0])))
        covers.extend(done)
        return (received, more) if more else received

    seconds = [((row_pos >> (m.bit_length() - 1)) & 1) == 1 for m in (1, 2, 3)]
    firsts = beside(
        [jnp.where(second, own_prior, far) for second in seconds],
        lambda blocks: [swap(block, "row", m) for m, block in zip((1, 2, 3), blocks)],
        2,
    )
    place = jnp.stack([row_pos, panel_pos]).astype(jnp.int32)
    shares = vmem_call(
        fold_products_kernel,
        [jax.ShapeDtypeStruct((per_device, 5 * NB), F32)] * 4,
        place,
        [own_prior, far, *firsts],
        [pltpu.VMEM((NB, 5 * NB), F32)],
        "fold_products",
    )
    others = [jnp.where(second, far, own_prior) for second in seconds]
    shares, others = lax.optimization_barrier((shares, others))
    sums = beside(
        shares,
        lambda shares: [swap(share, "panel", m) for m, share in zip((1, 2, 3), shares[1:])],
        1,
    )
    rest = [swap(block, "row", m) for m, block in zip((1, 2, 3), others)]
    places = [fold_block(row_pos, k) for k in range(5)]
    lead_cover = jnp.concatenate(
        [lax.dynamic_slice(covers[0], (jnp.int32(0), s * NB), (per_device, NB)) for s in places], 1
    )
    shard = lead_cover - (shares[0] + sums[0] + sums[1] + sums[2])

    def rest_part(panel_prior, m, plus=()):
        return vmem_call(
            functools.partial(rest_products_kernel, m=m),
            jax.ShapeDtypeStruct((quarter_rows, B), F32),
            place,
            [prior_factor, *panel_prior, *plus],
            name="rest_products",
        )

    def for_other_core(_):
        panel_prior = vmem_call(
            gather_split_kernel,
            [jax.ShapeDtypeStruct((B, own_prior.shape[1]), BF)] * 2,
            place,
            [own_prior, far, *firsts, *rest],
            name="gather_split",
        )
        return panel_prior, rest_part(panel_prior, 3), rest_part(panel_prior, 1)

    along, (panel_prior, part_3, part_1) = beside(
        shard[None],
        lambda x: [swap(x, "row", bit) for bit in (2, 4, 6)],
        2,
        for_other_core,
    )
    held = jnp.concatenate([shard[None]] + along, 0)

    def across(operands):
        x = operands[0]
        corner = [(i, i ^ 6) for i in range(32)]
        return swap(x, "row", 1), swap(x, "panel", 2), lax.ppermute(x, ("row", "panel"), corner)

    def for_own_core(operands):
        panel_prior, part_3, part_1 = operands[1]
        from_3, from_1 = swap(part_3, "panel", 1), swap(part_1, "panel", 1)
        part_0, part_2 = rest_part(panel_prior, 0), rest_part(panel_prior, 2, [from_3])
        return part_0, part_2, from_1, swap(operands[0], "panel", 1)

    received, (part_0, part_2, from_1, held_there) = beside(
        (held, (panel_prior, part_3, part_1)), across, 2, for_own_core
    )
    here = [held, *received]
    there = [held_there] + [swap(x, "panel", 1) for x in received]
    parts = [part_0, from_1, swap(part_2, "panel", 2)]
    factors = factor(unfold_kernel, (place, *here, *there), B)
    return solve(covers, parts, factors)


def solution(mesh):
    return jax.shard_map(
        local,
        mesh=mesh,
        in_specs=(P("row"), P(None, None, "row"), P("row", "panel")),
        out_specs=P(("row", "panel"), None),
        check_vma=False,
    )
```

```python
import functools

import jax
import jax.numpy as jnp
from jax import lax
from jax.experimental import pallas as pl
from jax.experimental.pallas import tpu as pltpu
from jax.sharding import PartitionSpec as P

B = 1024
NB = 128
NEAR = 4
F32 = jnp.float32
BF = jnp.bfloat16
NT = (((1,), (1,)), ((), ()))
SCALE = -1.4426950408889634 / 64.0
CENTRE = 1024.0


def locate(pixel_ids, quad_offsets):
    column = (pixel_ids % 256) * 8
    lines = (pixel_ids // 256) * 8
    east = (column[None, :] + quad_offsets[0]).astype(F32) - CENTRE
    north = (lines[None, :] + quad_offsets[1]).astype(F32) - CENTRE
    return east, north


def pieces(value):
    high = jnp.floor(value * (1.0 / 65536.0)) * 65536.0
    rest = value - high
    mid = jnp.floor(rest * (1.0 / 256.0)) * 256.0
    return [high, mid, rest - mid]


def halves(value):
    high = jnp.floor(value * (1.0 / 128.0)) * 128.0
    return high, value - high


def row_features(x, y):
    xh, xl = halves(x)
    yh, yl = halves(y)
    one = jnp.ones_like(x)
    zero = jnp.zeros_like(x)
    cross = [-2 * xh, -2 * xh, -2 * xl, -2 * xl, -2 * yh, -2 * yh, -2 * yl, -2 * yl]
    return jnp.concatenate(cross + pieces(x * x + y * y) + [one] * 3 + [zero] * 2, 0)


def col_features(x, y):
    xh, xl = halves(x)
    yh, yl = halves(y)
    one = jnp.ones_like(x)
    zero = jnp.zeros_like(x)
    cross = [xh, xl, xh, xl, yh, yl, yh, yl]
    return jnp.concatenate(cross + [one] * 3 + pieces(x * x + y * y) + [zero] * 2, 0)


def feature_kernel(row_ref, col_ref, f_ref, g_ref):
    for a in range(row_ref.shape[1]):
        one = row_features(row_ref[0, a : a + 1, :], row_ref[1, a : a + 1, :])
        f_ref[a] = one.T.astype(BF)
        g_ref[a] = col_features(col_ref[0, a : a + 1, :], col_ref[1, a : a + 1, :]).astype(BF)


def features(row_points, col_points):
    count, rows = row_points.shape[1:]
    cols = col_points.shape[2]
    return pl.pallas_call(
        feature_kernel,
        out_shape=[
            jax.ShapeDtypeStruct((count, rows, 16), BF),
            jax.ShapeDtypeStruct((count, 16, cols), BF),
        ],
        in_specs=[pl.BlockSpec(memory_space=pltpu.VMEM)] * 2,
        out_specs=[pl.BlockSpec(memory_space=pltpu.VMEM)] * 2,
        compiler_params=pltpu.CompilerParams(vmem_limit_bytes=8 << 20),
        name="features",
    )(row_points, col_points)


def cover_kernel(f_ref, g_ref, o_ref):
    count, block = f_ref.shape[:2]
    rows_here = f_ref[...].reshape(count * block, 16)

    def column_point(b, total):
        apart = jnp.dot(rows_here, g_ref[b], preferred_element_type=F32)
        near = jnp.exp2(apart * SCALE)
        for a in range(count):
            total = total + near[a * block : (a + 1) * block]
        return total

    total = lax.fori_loop(0, count, column_point, jnp.zeros(o_ref.shape, F32), unroll=8)
    o_ref[...] = total * (1.0 / (count * count))


def cover_rows(row_part, col_part, first, block):
    count, rows, depth = row_part.shape
    cols = col_part.shape[2]
    index = first // block
    return pl.pallas_call(
        cover_kernel,
        grid=(1,),
        out_shape=jax.ShapeDtypeStruct((block, cols), F32),
        in_specs=[
            pl.BlockSpec((count, block, depth), lambda i: (0, index, 0)),
            pl.BlockSpec((count, depth, cols), lambda i: (0, 0, 0)),
        ],
        out_specs=pl.BlockSpec((block, cols), lambda i: (0, 0)),
        compiler_params=pltpu.CompilerParams(vmem_limit_bytes=16 << 20),
        cost_estimate=pl.CostEstimate(flops=10**8, bytes_accessed=1 << 18, transcendentals=0),
        name="cover",
    )(row_part, col_part)


def row_table_kernel(row_ref, t_ref, row_cell_ref, place_ref):
    count, rows = row_ref.shape[1:]
    lines = t_ref.shape[2] // 2
    row_cell = jnp.floor(row_ref[0] * 0.125) * 8.0
    place_ref[0] = (row_ref[0] - row_cell).T
    place_ref[1] = row_ref[1].T
    row_cell_ref[...] = row_cell[0:1].T

    def row_tile(index, _):
        here = pl.ds(pl.multiple_of(index * 16, 16), 16)
        offset, north = place_ref[0, here], place_ref[1, here]
        line = lax.broadcasted_iota(jnp.int32, (16, lines), 1).astype(F32) - CENTRE
        total = [jnp.zeros((16, lines), F32) for _ in range(8)]
        for a in range(count):
            apart = jnp.broadcast_to(north[:, a : a + 1], (16, lines)) - line
            near = jnp.exp2(apart * apart * SCALE)
            which = jnp.broadcast_to(offset[:, a : a + 1], (16, lines))
            for p in range(8):
                total[p] = total[p] + jnp.where(which == float(p), near, 0.0)
        for p in range(8):
            high, low = split(total[p])
            t_ref[p, here, :lines] = high
            t_ref[p, here, lines:] = low
        return 0

    lax.fori_loop(0, rows // 16, row_tile, 0)


def row_table(row_points, lines):
    count, rows = row_points.shape[1:]
    return pl.pallas_call(
        row_table_kernel,
        out_shape=[
            jax.ShapeDtypeStruct((8, rows, 2 * lines), BF),
            jax.ShapeDtypeStruct((rows, 1), F32),
        ],
        in_specs=[pl.BlockSpec(memory_space=pltpu.VMEM)],
        out_specs=[pl.BlockSpec(memory_space=pltpu.VMEM)] * 2,
        scratch_shapes=[pltpu.VMEM((2, rows, count), F32)],
        compiler_params=pltpu.CompilerParams(vmem_limit_bytes=16 << 20),
        cost_estimate=pl.CostEstimate(flops=10**8, bytes_accessed=1 << 18, transcendentals=0),
        name="row_table",
    )(row_points)


def pack(prior, points):
    flat = points.reshape(-1, NB)
    tiles = prior.shape[1] // NB
    extra = flat.reshape(tiles, flat.shape[0] // tiles, NB).transpose(1, 0, 2)
    return jnp.concatenate([prior, extra.reshape(-1, prior.shape[1])], 0)


def column_counts(block_ref, h_ref, at, stride):
    extra = block_ref.shape[0] - NB
    tiles = block_ref.shape[1] // NB
    flat = jnp.concatenate(
        [block_ref[NB : NB + extra, NB * t : NB * t + NB] for t in range(tiles)], 0
    )
    count = flat.shape[0] // 2
    lines = h_ref.shape[0]
    east, north = flat[:count], flat[count:]
    cell = jnp.floor(east[0:1] * 0.125) * 8.0
    line = jnp.floor(north[0:1] * 0.125) * 8.0
    east, north = east - cell, north - line
    sub = lax.broadcasted_iota(jnp.int32, (8, NB), 0).astype(F32)
    held = [jnp.zeros((8, NB), F32) for _ in range(8)]
    for b in range(count):
        one = jnp.where(sub == jnp.broadcast_to(north[b : b + 1], (8, NB)), 1.0, 0.0)
        which = jnp.broadcast_to(east[b : b + 1], (8, NB))
        for q in range(8):
            held[q] = held[q] + jnp.where(which == float(q), one, 0.0)
    line = jnp.broadcast_to(line, (8, NB))
    for r in range(0, lines, 16):
        low = line == float(r) - CENTRE
        high = line == float(r + 8) - CENTRE
        for q in range(8):
            pair = [jnp.where(low, held[q], 0.0), jnp.where(high, held[q], 0.0)]
            lanes = slice(q * stride + at, q * stride + at + NB)
            h_ref[r : r + 16, lanes] = jnp.concatenate(pair, 0).astype(BF)
    return cell


def group_cover_kernel(place_ref, t_ref, row_cell_ref, *refs, points, unit):
    blocks, (o_ref, h_ref, east_ref) = refs[:-3], refs[-3:]
    rows, cols = o_ref.shape
    chunk = east_ref.shape[1]
    cells = [column_counts(ref, h_ref, NB * i, cols) for i, ref in enumerate(blocks)]
    col_cell = jnp.concatenate(cells, 1)

    def row_chunk(index, _):
        here = pl.ds(pl.multiple_of(index * chunk, chunk), chunk)
        cell = jnp.broadcast_to(row_cell_ref[here], (chunk, cols)) - col_cell
        for t in range(15):
            apart = cell + float(t - 7)
            east_ref[t] = jnp.exp2(apart * apart * SCALE)
        table = t_ref[:, here].reshape(8 * chunk, t_ref.shape[2])
        total = jnp.zeros((chunk, cols), F32)
        for q in range(0, 8, 2):
            counts = h_ref[:, q * cols : (q + 2) * cols]
            part = jnp.dot(
                table, jnp.concatenate([counts, counts], 0), preferred_element_type=F32
            )
            for p in range(8):
                for d in range(2):
                    piece = part[p * chunk : (p + 1) * chunk, d * cols : (d + 1) * cols]
                    total = total + piece * east_ref[p - q - d + 7]
        o_ref[here] = total * (1.0 / (points * points))
        return 0

    lax.fori_loop(0, rows // chunk, row_chunk, 0)
    if unit:
        per_device = NB // 4
        row = lax.broadcasted_iota(jnp.int32, (per_device, NB), 0)
        col = lax.broadcasted_iota(jnp.int32, (per_device, NB), 1)
        one = jnp.where(col == place_ref[1] * per_device + row, 1.0, 0.0)
        o_ref[:per_device, :NB] = o_ref[:per_device, :NB] + one


def inverse_factor(tiles):
    n = len(tiles)
    width = 8 * n
    lane = lax.broadcasted_iota(jnp.int32, (8, width), 1)
    sub = lax.broadcasted_iota(jnp.int32, (8, width), 0)
    tiles = list(tiles)
    out = []

    def spread(x):
        return jnp.broadcast_to(x, (8, width))

    def lanes(tile, v):
        return [spread(tile[:, 8 * v + q : 8 * v + q + 1]) for q in range(8)]

    following = lanes(tiles[0], 0)
    for v in range(n):
        near = min(n, v + NEAR)
        cols = {v: following}
        if v + 1 < n:
            cols[v] = cols[v] + lanes(tiles[v], v + 1)
            cols[v + 1] = lanes(tiles[v + 1], v) + lanes(tiles[v + 1], v + 1)
        for r in range(v + 2, near):
            cols[r] = lanes(tiles[r], v)
        here = (lane >= 8 * v) & (lane < 8 * v + 8)
        for r in range(v + 1, n):
            tiles[r] = jnp.where(here, 0.0, tiles[r])
        tiles[v] = jnp.where(here, jnp.where(lane == sub + 8 * v, 1.0, 0.0), tiles[v])
        pivots = jnp.ones((8, width), F32)
        for s in range(8):
            head = cols[v]
            pivot = spread(head[s][s : s + 1])
            inverse = 1.0 / pivot
            pivots = jnp.where(sub == s, pivot, pivots)
            row = spread(tiles[v][s : s + 1])
            heads = [spread(head[k][s : s + 1]) for k in range(s + 1, len(head))]
            for r in range(v, near):
                part = cols[r][s] * inverse
                if r == v:
                    part = jnp.where(sub > s, part, 0.0)
                tiles[r] = tiles[r] - part * row
                for k in range(s + 1, len(cols[r])):
                    cols[r][k] = cols[r][k] - part * heads[k - s - 1]
        if v + 1 < n:
            following = cols[v + 1][8:]
        rows = tiles[v] * lax.rsqrt(pivots)
        if near < n:
            high = rows.astype(BF).astype(F32)
            low = rows - high
            left = jnp.concatenate([high, high, low, low], 0).astype(BF)
            right = jnp.concatenate([high, low, high, low], 0).astype(BF)
            update = lax.dot_general(
                left, right, (((0,), (0,)), ((), ())), preferred_element_type=F32
            )
            for r in range(near, n):
                tiles[r] = tiles[r] - update[8 * r : 8 * r + 8]
        out.append(jnp.where(lane <= sub + 8 * v, rows, 0.0))
    return jnp.concatenate(out, 0)


def split(x):
    high = x.astype(BF)
    return high, (x - high.astype(F32)).astype(BF)


def dot3(ah, al, bh, bl):
    dot = functools.partial(lax.dot_general, dimension_numbers=NT, preferred_element_type=F32)
    return dot(ah, bh) + (dot(ah, bl) + dot(al, bh))


def factor_blocks(a_ref, lh_ref, ll_ref, wh_ref, wl_ref):
    n = a_ref.shape[0]
    blocks = n // NB

    def column(first):
        end = first + NB
        bh, bl = split(a_ref[end:, first:end])
        high, low = split(dot3(bh, bl, wh_ref[first:end], wl_ref[first:end]))
        lh_ref[end:, first:end] = high
        ll_ref[end:, first:end] = low
        a_ref[end:, end : end + NB] = a_ref[end:, end : end + NB] - dot3(
            lh_ref[end:, :end],
            ll_ref[end:, :end],
            lh_ref[end : end + NB, :end],
            ll_ref[end : end + NB, :end],
        )

    def step(j, _):
        c = pl.multiple_of(j * NB, NB)
        tiles = [a_ref[pl.ds(c + 8 * v, 8), pl.ds(c, NB)] for v in range(NB // 8)]
        wh, wl = split(inverse_factor(tiles))
        wh_ref[pl.ds(c, NB)] = wh
        wl_ref[pl.ds(c, NB)] = wl
        for block in range(blocks - 1):
            pl.when(j == block)(functools.partial(column, block * NB))
        return 0

    lax.fori_loop(0, blocks, step, 0)


def factor_kernel(diag_ref, lh_ref, ll_ref, wh_ref, wl_ref, a_ref):
    a_ref[...] = diag_ref[...]
    factor_blocks(a_ref, lh_ref, ll_ref, wh_ref, wl_ref)


def fold_block(r, k):
    if k < 2:
        return r ^ (4 * k)
    m = k - 1
    low = r & 3
    second = (low >> (m.bit_length() - 1)) & 1
    return (r ^ m) ^ (4 * second)


def block_order(r):
    order = [fold_block(r, k) for k in range(5)]
    return order + [order[k] ^ 4 for k in (2, 3, 4)]


def unfold_kernel(place_ref, *refs):
    pieces_refs, (lh_ref, ll_ref, wh_ref, wl_ref, a_ref, g_ref) = refs[:8], refs[8:]
    row_pos = place_ref[0]
    panel_pos = place_ref[1]
    for i, ref in enumerate(pieces_refs):
        g_ref[4 * i : 4 * i + 4] = ref[...]

    def rows_of(r, _):
        away = r ^ row_pos
        slot = (away >> 1) | ((away & 1) << 2)
        low = r & 3
        ats = []
        for p in range(4):
            gone = p ^ panel_pos
            ats.append(slot | ((gone >> 1) << 3) | ((gone & 1) << 4))
        for k in range(5):
            block = jnp.concatenate([g_ref[at, :, NB * k : NB * k + NB] for at in ats], 0)
            if k < 2:
                s = r ^ (4 * k)
            else:
                m = k - 1
                second = (low >> (m.bit_length() - 1)) & 1
                s = (r ^ m) ^ (4 * second)
            rr = pl.multiple_of(r * NB, NB)
            ss = pl.multiple_of(s * NB, NB)

            @pl.when(r >= s)
            def _():
                a_ref[pl.ds(rr, NB), pl.ds(ss, NB)] = block

            if k >= 2:

                @pl.when(r < s)
                def _():
                    a_ref[pl.ds(ss, NB), pl.ds(rr, NB)] = block.T

        return 0

    lax.fori_loop(0, 8, rows_of, 0)
    factor_blocks(a_ref, lh_ref, ll_ref, wh_ref, wl_ref)


def factor(kernel, operands, n):
    in_specs = [pl.BlockSpec(memory_space=pltpu.VMEM)] * len(operands)
    scratch = [pltpu.VMEM((n, n), F32)]
    if kernel is unfold_kernel:
        in_specs[0] = pl.BlockSpec(memory_space=pltpu.SMEM)
        scratch.append(pltpu.VMEM((32, *operands[1].shape[1:]), F32))
    return pl.pallas_call(
        kernel,
        out_shape=[jax.ShapeDtypeStruct((n, n), BF)] * 2 + [jax.ShapeDtypeStruct((n, NB), BF)] * 2,
        in_specs=in_specs,
        out_specs=[pl.BlockSpec(memory_space=pltpu.VMEM)] * 4,
        scratch_shapes=scratch,
        compiler_params=pltpu.CompilerParams(vmem_limit_bytes=32 << 20),
        cost_estimate=pl.CostEstimate(flops=5 * 10**10, bytes_accessed=8 << 20, transcendentals=0),
        name="factor",
    )(*operands)


def solve_kernel(place_ref, *refs, covers, by_columns):
    cover_refs, parts_refs = refs[:covers], refs[covers:-7]
    lh_ref, ll_ref, wh_ref, wl_ref, o_ref, xh_ref, xl_ref = refs[-7:]
    n = o_ref.shape[1]

    def put(rows, cols, value):
        taken = parts_refs[0][rows, cols]
        for part in parts_refs[1:]:
            taken = taken + part[rows, cols]
        o_ref[rows, cols] = value - taken

    if by_columns:
        pieces_of = [ref[:, c : c + NB] for ref in cover_refs for c in range(0, ref.shape[1], NB)]
        for s, piece in zip(block_order(place_ref[0]), pieces_of):
            put(slice(None), pl.ds(pl.multiple_of(s * NB, NB), NB), piece)
    else:
        first = 0
        for ref in cover_refs:
            put(pl.ds(first, ref.shape[0]), slice(None), ref[...])
            first += ref.shape[0]
    for c in range(0, n, NB):
        here = o_ref[:, c : c + NB]
        if c:
            here = here - dot3(
                xh_ref[:, :c], xl_ref[:, :c], lh_ref[c : c + NB, :c], ll_ref[c : c + NB, :c]
            )
        bh, bl = split(here)
        x = dot3(bh, bl, wh_ref[c : c + NB], wl_ref[c : c + NB])
        o_ref[:, c : c + NB] = x
        xh, xl = split(x)
        xh_ref[:, c : c + NB] = xh
        xl_ref[:, c : c + NB] = xl


def solve(place, covers, parts, factors, by_columns):
    rows, n = parts[0].shape
    return vmem_call(
        functools.partial(solve_kernel, covers=len(covers), by_columns=by_columns),
        jax.ShapeDtypeStruct((rows, n), F32),
        place,
        [*covers, *parts, *factors],
        [pltpu.VMEM((rows, n), BF)] * 2,
        "solve",
    )


def vmem_call(kernel, out_shape, place, operands, scratch=(), name=None):
    return pl.pallas_call(
        kernel,
        out_shape=out_shape,
        in_specs=[pl.BlockSpec(memory_space=pltpu.SMEM)]
        + [pl.BlockSpec(memory_space=pltpu.VMEM)] * len(operands),
        out_specs=jax.tree.map(lambda _: pl.BlockSpec(memory_space=pltpu.VMEM), out_shape),
        scratch_shapes=list(scratch),
        compiler_params=pltpu.CompilerParams(vmem_limit_bytes=32 << 20),
        cost_estimate=pl.CostEstimate(flops=10**8, bytes_accessed=1 << 18, transcendentals=0),
        name=name,
    )(place, *operands)


def fold_products_kernel(place_ref, *refs):
    blocks, shares, total_ref = refs[:5], refs[5:-1], refs[-1]
    own_high, own_low = split(blocks[0][:NB])
    for k, ref in enumerate(blocks):
        high, low = split(ref[:NB])
        total_ref[:, NB * k : NB * k + NB] = dot3(own_high, own_low, high, low)
    rows = shares[0].shape[0]
    for m, ref in enumerate(shares):
        first = pl.multiple_of((place_ref[1] ^ m) * rows, rows)
        ref[...] = total_ref[pl.ds(first, rows)]


def gather_split_kernel(place_ref, *refs):
    blocks, (high_ref, low_ref) = refs[:-2], refs[-2:]
    for s, ref in zip(block_order(place_ref[0]), blocks):
        first = pl.multiple_of(s * NB, NB)
        high, low = split(ref[:NB])
        high_ref[pl.ds(first, NB)] = high
        low_ref[pl.ds(first, NB)] = low


def rest_products_kernel(place_ref, prior_ref, high_ref, low_ref, *refs, m):
    o_ref = refs[-1]
    rows = o_ref.shape[0]
    first = pl.multiple_of((place_ref[1] ^ m) * rows, rows)
    own_high, own_low = split(prior_ref[pl.ds(first, rows)])
    for c in range(0, o_ref.shape[1], 2 * NB):
        cols = slice(c, c + 2 * NB)
        total = dot3(own_high, own_low, high_ref[cols], low_ref[cols])
        for plus_ref in refs[:-1]:
            total = total + plus_ref[:, cols]
        o_ref[:, cols] = total


def swap(block, axis, bit):
    return lax.ppermute(block, axis, [(i, i ^ bit) for i in range(lax.axis_size(axis))])


def dot_rows(left, right):
    return lax.dot_general(
        left, right, NT, precision=lax.Precision.HIGH, preferred_element_type=F32
    )


def local(pixel_ids, quad_offsets, prior_factor):
    panel_count = lax.axis_size("panel")
    row_count = lax.axis_size("row")
    block_rows = pixel_ids.shape[0]
    quarter_rows = block_rows // panel_count
    per_device = B // (row_count * panel_count)
    span_cols = panel_count * per_device
    row_pos = lax.axis_index("row")
    panel_pos = lax.axis_index("panel")
    device_pos = row_pos * panel_count + panel_pos
    lead = 32

    points = jnp.stack(locate(pixel_ids, quad_offsets))
    count = points.shape[1]
    own_points = lax.dynamic_slice_in_dim(points, panel_pos * quarter_rows, quarter_rows, 2)
    local_points = points.reshape(2, count, panel_count, quarter_rows)[:, :, :, :per_device]
    local_points = local_points.reshape(2, count, span_cols)
    own_prior = prior_factor.reshape(panel_count, quarter_rows, -1)[:, :per_device]
    own_prior = own_prior.reshape(span_cols, -1)
    place = jnp.stack([row_pos, panel_pos]).astype(jnp.int32)
    lines = block_rows * row_count // 256 * 8
    folds = span_cols == NB and row_count == 8 and panel_count == 4 and lines == 256

    if not (folds and 2 * count * NB == 8 * own_prior.shape[1]):
        lead = 32
        row_ids = jnp.arange(lead, dtype=jnp.int32)[:, None]
        col_ids = jnp.arange(B, dtype=jnp.int32)[None, :]
        on_diagonal = (row_ids < per_device) & (col_ids == device_pos * per_device + row_ids)
        unit = jnp.where(on_diagonal, 1.0, 0.0).astype(F32)
        flat = local_points.reshape(1, 2 * count, span_cols)
        copies = jnp.broadcast_to(flat, (row_count, 2 * count, span_cols))
        spread = lax.all_to_all(copies, "row", split_axis=0, concat_axis=0, tiled=True)
        parted = features(own_points, spread.transpose(1, 0, 2).reshape(2, count, B))
        covers = [cover_rows(*parted, i, lead) for i in range(0, quarter_rows, lead)]
        covers[0] = covers[0] + unit
        panel_prior = lax.all_gather(own_prior, "row", axis=0, tiled=True)
        partial = dot_rows(prior_factor, panel_prior)
        parts = lax.all_to_all(
            partial.reshape(panel_count, quarter_rows, B), "panel", split_axis=0, concat_axis=0, tiled=True
        )
        parts = jnp.sum(parts, axis=0)
        mine = covers[0][:per_device] - parts[:per_device]
        diag_rows = lax.all_gather(mine, ("row", "panel"), axis=0, tiled=True)
        return solve(place, covers, [parts], factor(factor_kernel, (diag_rows,), B), False)

    own = pack(own_prior, local_points)
    far = swap(own, "row", 4)
    table = row_table(own_points, lines)
    far, table = lax.optimization_barrier((far, table))

    def beside(operands, transfer, work):
        operands, held = lax.optimization_barrier((operands, table))
        return lax.optimization_barrier((transfer(operands), work(operands, held)))

    def group_cover(held, blocks, unit=False):
        cols = NB * len(blocks)
        return vmem_call(
            functools.partial(group_cover_kernel, points=count, unit=unit),
            jax.ShapeDtypeStruct((quarter_rows, cols), F32),
            place,
            [*held, *blocks],
            [pltpu.VMEM((lines, 8 * cols), BF), pltpu.VMEM((15, 32, cols), F32)],
            "cover",
        )

    seconds = [((row_pos >> (m.bit_length() - 1)) & 1) == 1 for m in (1, 2, 3)]
    firsts, cover_1 = beside(
        [jnp.where(second, own, far) for second in seconds],
        lambda blocks: [swap(block, "row", m) for m, block in zip((1, 2, 3), blocks)],
        lambda _, held: group_cover(held, [own, far], True),
    )
    shares = vmem_call(
        fold_products_kernel,
        [jax.ShapeDtypeStruct((per_device, 5 * NB), F32)] * 4,
        place,
        [own, far, *firsts],
        [pltpu.VMEM((NB, 5 * NB), F32)],
        "fold_products",
    )
    others = [jnp.where(second, far, own) for second in seconds]
    shares, others = lax.optimization_barrier((shares, others))
    sums, cover_2 = beside(
        shares,
        lambda shares: [swap(share, "panel", m) for m, share in zip((1, 2, 3), shares[1:])],
        lambda _, held: group_cover(held, firsts),
    )
    rest = [swap(block, "row", m) for m, block in zip((1, 2, 3), others)]
    lead_cover = jnp.concatenate([cover_1[:per_device], cover_2[:per_device]], 1)
    shard = lead_cover - (shares[0] + sums[0] + sums[1] + sums[2])

    along, cover_3 = beside(
        shard[None],
        lambda x: [swap(x, "row", bit) for bit in (2, 4, 6)],
        lambda _, held: group_cover(held, rest),
    )
    held_rows = jnp.concatenate([shard[None]] + along, 0)

    def across(x):
        corner = [(i, i ^ 6) for i in range(32)]
        return swap(x, "row", 1), swap(x, "panel", 2), lax.ppermute(x, ("row", "panel"), corner)

    def rest_parts(x, _):
        x, blocks = lax.optimization_barrier((x, [own, far, *firsts, *rest]))
        panel_prior = vmem_call(
            gather_split_kernel,
            [jax.ShapeDtypeStruct((B, own_prior.shape[1]), BF)] * 2,
            place,
            blocks,
            name="gather_split",
        )

        def part(m, plus=()):
            return vmem_call(
                functools.partial(rest_products_kernel, m=m),
                jax.ShapeDtypeStruct((quarter_rows, B), F32),
                place,
                [prior_factor, *panel_prior, *plus],
                name="rest_products",
            )

        from_3 = swap(part(3), "panel", 1)
        from_1 = swap(part(1), "panel", 1)
        return part(0), part(2, [from_3]), from_1, swap(x, "panel", 1)

    received, (part_0, part_2, from_1, held_there) = beside(held_rows, across, rest_parts)
    there = [held_there] + [swap(x, "panel", 1) for x in received]
    parts = [part_0, from_1, swap(part_2, "panel", 2)]
    factors = factor(unfold_kernel, (place, held_rows, *received, *there), B)
    return solve(place, [cover_1, cover_2, cover_3], parts, factors, True)


def solution(mesh):
    return jax.shard_map(
        local,
        mesh=mesh,
        in_specs=(P("row"), P(None, None, "row"), P("row", "panel")),
        out_specs=P(("row", "panel"), None),
        check_vma=False,
    )
```

```python
import functools

import jax
import jax.numpy as jnp
from jax import lax
from jax.experimental import pallas as pl
from jax.experimental.pallas import tpu as pltpu
from jax.sharding import PartitionSpec as P

B = 1024
NB = 128
NEAR = 4
F32 = jnp.float32
BF = jnp.bfloat16
NT = (((1,), (1,)), ((), ()))
SCALE = -1.4426950408889634 / 64.0
CENTRE = 1024.0


def locate(pixel_ids, quad_offsets):
    column = (pixel_ids % 256) * 8
    lines = (pixel_ids // 256) * 8
    east = (column[None, :] + quad_offsets[0]).astype(F32) - CENTRE
    north = (lines[None, :] + quad_offsets[1]).astype(F32) - CENTRE
    return east, north


def pieces(value):
    high = jnp.floor(value * (1.0 / 65536.0)) * 65536.0
    rest = value - high
    mid = jnp.floor(rest * (1.0 / 256.0)) * 256.0
    return [high, mid, rest - mid]


def halves(value):
    high = jnp.floor(value * (1.0 / 128.0)) * 128.0
    return high, value - high


def row_features(x, y):
    xh, xl = halves(x)
    yh, yl = halves(y)
    one = jnp.ones_like(x)
    zero = jnp.zeros_like(x)
    cross = [-2 * xh, -2 * xh, -2 * xl, -2 * xl, -2 * yh, -2 * yh, -2 * yl, -2 * yl]
    return jnp.concatenate(cross + pieces(x * x + y * y) + [one] * 3 + [zero] * 2, 0)


def col_features(x, y):
    xh, xl = halves(x)
    yh, yl = halves(y)
    one = jnp.ones_like(x)
    zero = jnp.zeros_like(x)
    cross = [xh, xl, xh, xl, yh, yl, yh, yl]
    return jnp.concatenate(cross + [one] * 3 + pieces(x * x + y * y) + [zero] * 2, 0)


def feature_kernel(row_ref, col_ref, f_ref, g_ref):
    for a in range(row_ref.shape[1]):
        one = row_features(row_ref[0, a : a + 1, :], row_ref[1, a : a + 1, :])
        f_ref[a] = one.T.astype(BF)
        g_ref[a] = col_features(col_ref[0, a : a + 1, :], col_ref[1, a : a + 1, :]).astype(BF)


def features(row_points, col_points):
    count, rows = row_points.shape[1:]
    cols = col_points.shape[2]
    return pl.pallas_call(
        feature_kernel,
        out_shape=[
            jax.ShapeDtypeStruct((count, rows, 16), BF),
            jax.ShapeDtypeStruct((count, 16, cols), BF),
        ],
        in_specs=[pl.BlockSpec(memory_space=pltpu.VMEM)] * 2,
        out_specs=[pl.BlockSpec(memory_space=pltpu.VMEM)] * 2,
        compiler_params=pltpu.CompilerParams(vmem_limit_bytes=8 << 20),
        name="features",
    )(row_points, col_points)


def cover_kernel(f_ref, g_ref, o_ref):
    count, block = f_ref.shape[:2]
    rows_here = f_ref[...].reshape(count * block, 16)

    def column_point(b, total):
        apart = jnp.dot(rows_here, g_ref[b], preferred_element_type=F32)
        near = jnp.exp2(apart * SCALE)
        for a in range(count):
            total = total + near[a * block : (a + 1) * block]
        return total

    total = lax.fori_loop(0, count, column_point, jnp.zeros(o_ref.shape, F32), unroll=8)
    o_ref[...] = total * (1.0 / (count * count))


def cover_rows(row_part, col_part, first, block):
    count, rows, depth = row_part.shape
    cols = col_part.shape[2]
    index = first // block
    return pl.pallas_call(
        cover_kernel,
        grid=(1,),
        out_shape=jax.ShapeDtypeStruct((block, cols), F32),
        in_specs=[
            pl.BlockSpec((count, block, depth), lambda i: (0, index, 0)),
            pl.BlockSpec((count, depth, cols), lambda i: (0, 0, 0)),
        ],
        out_specs=pl.BlockSpec((block, cols), lambda i: (0, 0)),
        compiler_params=pltpu.CompilerParams(vmem_limit_bytes=16 << 20),
        cost_estimate=pl.CostEstimate(flops=10**8, bytes_accessed=1 << 18, transcendentals=0),
        name="cover",
    )(row_part, col_part)


def table_rows(offset, north, lines):
    line = lax.broadcasted_iota(jnp.int32, (16, lines), 1).astype(F32) - CENTRE
    total = [jnp.zeros((16, lines), F32) for _ in range(8)]
    for a in range(offset.shape[1]):
        apart = jnp.broadcast_to(north[:, a : a + 1], (16, lines)) - line
        near = jnp.exp2(apart * apart * SCALE)
        which = jnp.broadcast_to(offset[:, a : a + 1], (16, lines))
        for p in range(8):
            total[p] = total[p] + jnp.where(which == float(p), near, 0.0)
    return [split(x) for x in total]


def row_table_kernel(row_ref, t_ref, row_cell_ref, place_ref):
    rows = row_ref.shape[2]
    lines = t_ref.shape[2] // 2
    row_cell = jnp.floor(row_ref[0] * 0.125) * 8.0
    place_ref[0] = (row_ref[0] - row_cell).T
    place_ref[1] = row_ref[1].T
    row_cell_ref[...] = row_cell[0:1].T

    def row_tile(index, _):
        here = pl.ds(pl.multiple_of(index * 16, 16), 16)
        for p, (high, low) in enumerate(table_rows(place_ref[0, here], place_ref[1, here], lines)):
            t_ref[p, here, :lines] = high
            t_ref[p, here, lines:] = low
        return 0

    lax.fori_loop(0, rows // 16, row_tile, 0)


def row_table(row_points, lines):
    count, rows = row_points.shape[1:]
    return pl.pallas_call(
        row_table_kernel,
        out_shape=[
            jax.ShapeDtypeStruct((8, rows, 2 * lines), BF),
            jax.ShapeDtypeStruct((rows, 1), F32),
        ],
        in_specs=[pl.BlockSpec(memory_space=pltpu.VMEM)],
        out_specs=[pl.BlockSpec(memory_space=pltpu.VMEM)] * 2,
        scratch_shapes=[pltpu.VMEM((2, rows, count), F32)],
        compiler_params=pltpu.CompilerParams(vmem_limit_bytes=16 << 20),
        cost_estimate=pl.CostEstimate(flops=10**8, bytes_accessed=1 << 18, transcendentals=0),
        name="row_table",
    )(row_points)


def pack(prior, points):
    flat = points.reshape(-1, NB)
    tiles = prior.shape[1] // NB
    extra = flat.reshape(tiles, flat.shape[0] // tiles, NB).transpose(1, 0, 2)
    return jnp.concatenate([prior, extra.reshape(-1, prior.shape[1])], 0)


def unpack(block_ref):
    extra = block_ref.shape[0] - NB
    tiles = block_ref.shape[1] // NB
    flat = jnp.concatenate(
        [block_ref[NB : NB + extra, NB * t : NB * t + NB] for t in range(tiles)], 0
    )
    count = flat.shape[0] // 2
    return flat[:count], flat[count:]


def column_counts(block_ref, h_ref, at, stride):
    east, north = unpack(block_ref)
    lines = h_ref.shape[0]
    cell = jnp.floor(east[0:1] * 0.125) * 8.0
    line = jnp.floor(north[0:1] * 0.125) * 8.0
    east, north = east - cell, north - line
    sub = lax.broadcasted_iota(jnp.int32, (8, NB), 0).astype(F32)
    held = [jnp.zeros((8, NB), F32) for _ in range(8)]
    for b in range(east.shape[0]):
        one = jnp.where(sub == jnp.broadcast_to(north[b : b + 1], (8, NB)), 1.0, 0.0)
        which = jnp.broadcast_to(east[b : b + 1], (8, NB))
        for q in range(8):
            held[q] = held[q] + jnp.where(which == float(q), one, 0.0)
    line = jnp.broadcast_to(line, (8, NB))
    for r in range(0, lines, 16):
        low = line == float(r) - CENTRE
        high = line == float(r + 8) - CENTRE
        for q in range(8):
            pair = [jnp.where(low, held[q], 0.0), jnp.where(high, held[q], 0.0)]
            lanes = slice(q * stride + at, q * stride + at + NB)
            h_ref[r : r + 16, lanes] = jnp.concatenate(pair, 0).astype(BF)
    return cell


def cover_chunk(table, row_cell, col_cell, h_ref, east_ref, points):
    chunk, cols = east_ref.shape[1:]
    cell = jnp.broadcast_to(row_cell, (chunk, cols)) - col_cell
    for t in range(15):
        apart = cell + float(t - 7)
        east_ref[t] = jnp.exp2(apart * apart * SCALE)
    table = table.reshape(8 * chunk, table.shape[2])
    total = jnp.zeros((chunk, cols), F32)
    for q in range(8):
        counts = h_ref[:, q * cols : (q + 1) * cols]
        part = jnp.dot(table, jnp.concatenate([counts, counts], 0), preferred_element_type=F32)
        for p in range(8):
            total = total + part[p * chunk : (p + 1) * chunk] * east_ref[p - q + 7]
    return total * (1.0 / (points * points))


def lead_cover_kernel(
    place_ref, t_ref, row_cell_ref, *refs, points
):
    blocks, refs = refs[:4], refs[4:]
    folded_ref, own_ref, h_ref, col_cell_ref, east_ref, far_ref, far_cell_ref, far_table_ref = refs
    rows, cols = own_ref.shape
    lines = h_ref.shape[0]
    cells = [column_counts(ref, h_ref, NB * i, cols) for i, ref in enumerate(blocks)]
    col_cell = jnp.concatenate(cells, 1)
    col_cell_ref[...] = col_cell

    east, north = unpack(blocks[1])
    far_ref[0] = (east - cells[1]).T
    far_ref[1] = north.T
    far_cell_ref[...] = cells[1].T
    first = pl.multiple_of(place_ref[1] * rows, rows)
    for r in range(0, rows, 16):
        here = pl.ds(first + r, 16)
        for p, (high, low) in enumerate(table_rows(far_ref[0, here], far_ref[1, here], lines)):
            far_table_ref[p, r : r + 16, :lines] = high
            far_table_ref[p, r : r + 16, lines:] = low

    mine = cover_chunk(t_ref[:, :rows], row_cell_ref[:rows], col_cell, h_ref, east_ref, points)
    row = lax.broadcasted_iota(jnp.int32, (rows, cols), 0)
    col = lax.broadcasted_iota(jnp.int32, (rows, cols), 1)
    mine = mine + jnp.where(col == first + row, 1.0, 0.0)
    own_ref[...] = mine
    far = cover_chunk(
        far_table_ref[...], far_cell_ref[pl.ds(first, rows)], col_cell, h_ref, east_ref, points
    )
    folded_ref[:, : 3 * NB] = mine[:, : 3 * NB]
    folded_ref[:, 3 * NB : 4 * NB] = far[:, 2 * NB : 3 * NB]
    own_last = (place_ref[0] & 3) < 2
    folded_ref[:, 4 * NB :] = jnp.where(own_last, mine[:, 3 * NB :], far[:, 3 * NB :])


def later_cover_kernel(t_ref, row_cell_ref, h_ref, col_cell_ref, o_ref, east_ref, *, points):
    chunk = east_ref.shape[1]
    skipped = t_ref.shape[1] - o_ref.shape[0]

    def row_chunk(index, _):
        first = pl.multiple_of(index * chunk, chunk)
        here = pl.ds(pl.multiple_of(first + skipped, chunk), chunk)
        o_ref[pl.ds(first, chunk)] = cover_chunk(
            t_ref[:, here], row_cell_ref[here], col_cell_ref[...], h_ref, east_ref, points
        )
        return 0

    lax.fori_loop(0, o_ref.shape[0] // chunk, row_chunk, 0)


def block_cover_kernel(t_ref, row_cell_ref, *refs, points):
    blocks, (o_ref, h_ref, col_cell_ref, east_ref) = refs[:-4], refs[-4:]
    cells = [
        column_counts(ref, h_ref, NB * i, o_ref.shape[1]) for i, ref in enumerate(blocks)
    ]
    col_cell_ref[...] = jnp.concatenate(cells, 1)
    later_cover_kernel(t_ref, row_cell_ref, h_ref, col_cell_ref, o_ref, east_ref, points=points)


def inverse_factor(tiles):
    n = len(tiles)
    width = 8 * n
    lane = lax.broadcasted_iota(jnp.int32, (8, width), 1)
    sub = lax.broadcasted_iota(jnp.int32, (8, width), 0)
    tiles = list(tiles)
    out = []

    def spread(x):
        return jnp.broadcast_to(x, (8, width))

    def lanes(tile, v):
        return [spread(tile[:, 8 * v + q : 8 * v + q + 1]) for q in range(8)]

    following = lanes(tiles[0], 0)
    for v in range(n):
        near = min(n, v + NEAR)
        cols = {v: following}
        if v + 1 < n:
            cols[v] = cols[v] + lanes(tiles[v], v + 1)
            cols[v + 1] = lanes(tiles[v + 1], v) + lanes(tiles[v + 1], v + 1)
        for r in range(v + 2, near):
            cols[r] = lanes(tiles[r], v)
        here = (lane >= 8 * v) & (lane < 8 * v + 8)
        for r in range(v + 1, n):
            tiles[r] = jnp.where(here, 0.0, tiles[r])
        tiles[v] = jnp.where(here, jnp.where(lane == sub + 8 * v, 1.0, 0.0), tiles[v])
        pivots = jnp.ones((8, width), F32)
        for s in range(8):
            head = cols[v]
            pivot = spread(head[s][s : s + 1])
            inverse = 1.0 / pivot
            pivots = jnp.where(sub == s, pivot, pivots)
            row = spread(tiles[v][s : s + 1])
            heads = [spread(head[k][s : s + 1]) for k in range(s + 1, len(head))]
            for r in range(v, near):
                part = cols[r][s] * inverse
                if r == v:
                    part = jnp.where(sub > s, part, 0.0)
                tiles[r] = tiles[r] - part * row
                for k in range(s + 1, len(cols[r])):
                    cols[r][k] = cols[r][k] - part * heads[k - s - 1]
        if v + 1 < n:
            following = cols[v + 1][8:]
        rows = tiles[v] * lax.rsqrt(pivots)
        if near < n:
            high = rows.astype(BF).astype(F32)
            low = rows - high
            left = jnp.concatenate([high, high, low, low], 0).astype(BF)
            right = jnp.concatenate([high, low, high, low], 0).astype(BF)
            update = lax.dot_general(
                left, right, (((0,), (0,)), ((), ())), preferred_element_type=F32
            )
            for r in range(near, n):
                tiles[r] = tiles[r] - update[8 * r : 8 * r + 8]
        out.append(jnp.where(lane <= sub + 8 * v, rows, 0.0))
    return jnp.concatenate(out, 0)


def split(x):
    high = x.astype(BF)
    return high, (x - high.astype(F32)).astype(BF)


def dot3(ah, al, bh, bl):
    dot = functools.partial(lax.dot_general, dimension_numbers=NT, preferred_element_type=F32)
    return dot(ah, bh) + (dot(ah, bl) + dot(al, bh))


def factor_blocks(a_ref, lh_ref, ll_ref, wh_ref, wl_ref):
    n = a_ref.shape[0]
    blocks = n // NB

    def column(first):
        end = first + NB
        bh, bl = split(a_ref[end:, first:end])
        high, low = split(dot3(bh, bl, wh_ref[first:end], wl_ref[first:end]))
        lh_ref[end:, first:end] = high
        ll_ref[end:, first:end] = low
        a_ref[end:, end : end + NB] = a_ref[end:, end : end + NB] - dot3(
            lh_ref[end:, :end],
            ll_ref[end:, :end],
            lh_ref[end : end + NB, :end],
            ll_ref[end : end + NB, :end],
        )

    def step(j, _):
        c = pl.multiple_of(j * NB, NB)
        tiles = [a_ref[pl.ds(c + 8 * v, 8), pl.ds(c, NB)] for v in range(NB // 8)]
        wh, wl = split(inverse_factor(tiles))
        wh_ref[pl.ds(c, NB)] = wh
        wl_ref[pl.ds(c, NB)] = wl
        for block in range(blocks - 1):
            pl.when(j == block)(functools.partial(column, block * NB))
        return 0

    lax.fori_loop(0, blocks, step, 0)


def factor_kernel(diag_ref, lh_ref, ll_ref, wh_ref, wl_ref, a_ref):
    a_ref[...] = diag_ref[...]
    factor_blocks(a_ref, lh_ref, ll_ref, wh_ref, wl_ref)


def block_order(r):
    here, away, q = r & 4, (r & 4) ^ 4, r & 3
    turns = [(q + k) & 3 for k in (1, 2, 3)]
    return [r, r ^ 4, here | turns[0], here | turns[1], here | turns[2]] + [away | t for t in turns]


def folded_blocks(r):
    order = block_order(r)
    either = jnp.where((r & 3) < 2, r, r ^ 4)
    return [(r, r), (r, order[1]), (r, order[2]), (order[1], order[2]), (either, order[3])]


def unfold_kernel(place_ref, *refs):
    pieces_refs, (lh_ref, ll_ref, wh_ref, wl_ref, a_ref, g_ref) = refs[:8], refs[8:]
    row_pos = place_ref[0]
    panel_pos = place_ref[1]
    for i, ref in enumerate(pieces_refs):
        g_ref[4 * i : 4 * i + 4] = ref[...]

    def rows_of(r, _):
        away = r ^ row_pos
        slot = (away >> 1) | ((away & 1) << 2)
        ats = []
        for p in range(4):
            gone = p ^ panel_pos
            ats.append(slot | ((gone >> 1) << 3) | ((gone & 1) << 4))
        for k, (rows, cols) in enumerate(folded_blocks(r)):
            block = jnp.concatenate([g_ref[at, :, NB * k : NB * k + NB] for at in ats], 0)
            rr = pl.multiple_of(rows * NB, NB)
            cc = pl.multiple_of(cols * NB, NB)

            @pl.when(rows >= cols)
            def _():
                a_ref[pl.ds(rr, NB), pl.ds(cc, NB)] = block

            if k:

                @pl.when(rows < cols)
                def _():
                    a_ref[pl.ds(cc, NB), pl.ds(rr, NB)] = block.T

        return 0

    lax.fori_loop(0, 8, rows_of, 0)
    factor_blocks(a_ref, lh_ref, ll_ref, wh_ref, wl_ref)


def factor(kernel, operands, n):
    in_specs = [pl.BlockSpec(memory_space=pltpu.VMEM)] * len(operands)
    scratch = [pltpu.VMEM((n, n), F32)]
    if kernel is unfold_kernel:
        in_specs[0] = pl.BlockSpec(memory_space=pltpu.SMEM)
        scratch.append(pltpu.VMEM((32, *operands[1].shape[1:]), F32))
    return pl.pallas_call(
        kernel,
        out_shape=[jax.ShapeDtypeStruct((n, n), BF)] * 2 + [jax.ShapeDtypeStruct((n, NB), BF)] * 2,
        in_specs=in_specs,
        out_specs=[pl.BlockSpec(memory_space=pltpu.VMEM)] * 4,
        scratch_shapes=scratch,
        compiler_params=pltpu.CompilerParams(vmem_limit_bytes=32 << 20),
        cost_estimate=pl.CostEstimate(flops=5 * 10**10, bytes_accessed=8 << 20, transcendentals=0),
        name="factor",
    )(*operands)


def solve_kernel(place_ref, *refs, corners):
    cover_refs, parts_refs = refs[: len(corners)], refs[len(corners) : -7]
    lh_ref, ll_ref, wh_ref, wl_ref, o_ref, xh_ref, xl_ref = refs[-7:]
    n = o_ref.shape[1]

    def put(rows, cols, value):
        taken = parts_refs[0][rows, cols]
        for part in parts_refs[1:]:
            taken = taken + part[rows, cols]
        o_ref[rows, cols] = value - taken

    for (row, block), ref in zip(corners, cover_refs):
        rows = slice(row, row + ref.shape[0])
        if block is None:
            put(rows, slice(None), ref[...])
            continue
        for c, s in enumerate(block_order(place_ref[0])[block : block + ref.shape[1] // NB]):
            cols = pl.ds(pl.multiple_of(s * NB, NB), NB)
            put(rows, cols, ref[:, NB * c : NB * c + NB])
    for c in range(0, n, NB):
        here = o_ref[:, c : c + NB]
        if c:
            here = here - dot3(
                xh_ref[:, :c], xl_ref[:, :c], lh_ref[c : c + NB, :c], ll_ref[c : c + NB, :c]
            )
        bh, bl = split(here)
        x = dot3(bh, bl, wh_ref[c : c + NB], wl_ref[c : c + NB])
        o_ref[:, c : c + NB] = x
        xh, xl = split(x)
        xh_ref[:, c : c + NB] = xh
        xl_ref[:, c : c + NB] = xl


def solve(place, covers, corners, parts, factors):
    rows, n = parts[0].shape
    return vmem_call(
        functools.partial(solve_kernel, corners=corners),
        jax.ShapeDtypeStruct((rows, n), F32),
        place,
        [*covers, *parts, *factors],
        [pltpu.VMEM((rows, n), BF)] * 2,
        "solve",
    )


def vmem_call(kernel, out_shape, place, operands, scratch=(), name=None):
    return pl.pallas_call(
        kernel,
        out_shape=out_shape,
        in_specs=[pl.BlockSpec(memory_space=pltpu.SMEM)] * (place is not None)
        + [pl.BlockSpec(memory_space=pltpu.VMEM)] * len(operands),
        out_specs=jax.tree.map(lambda _: pl.BlockSpec(memory_space=pltpu.VMEM), out_shape),
        scratch_shapes=list(scratch),
        compiler_params=pltpu.CompilerParams(vmem_limit_bytes=32 << 20),
        cost_estimate=pl.CostEstimate(flops=10**8, bytes_accessed=1 << 18, transcendentals=0),
        name=name,
    )(*([] if place is None else [place]), *operands)


def fold_products_kernel(place_ref, *refs):
    blocks, shares, total_ref = refs[:4], refs[4:-1], refs[-1]
    own, far, one, two = [split(ref[:NB]) for ref in blocks]
    own_last = (place_ref[0] & 3) < 2
    either = split(jnp.where(own_last, blocks[0][:NB], blocks[1][:NB]))
    pairs = [(own, own), (own, far), (own, one), (far, one), (either, two)]
    for k, (left, right) in enumerate(pairs):
        total_ref[:, NB * k : NB * k + NB] = dot3(*left, *right)
    rows = shares[0].shape[0]
    for m, ref in enumerate(shares):
        first = pl.multiple_of((place_ref[1] ^ m) * rows, rows)
        ref[...] = total_ref[pl.ds(first, rows)]


def gather_split_kernel(place_ref, *refs):
    blocks, (high_ref, low_ref) = refs[:-2], refs[-2:]
    for s, ref in zip(block_order(place_ref[0]), blocks):
        first = pl.multiple_of(s * NB, NB)
        high, low = split(ref[:NB])
        high_ref[pl.ds(first, NB)] = high
        low_ref[pl.ds(first, NB)] = low


def rest_products_kernel(place_ref, prior_ref, high_ref, low_ref, *refs, m):
    o_ref = refs[-1]
    rows = o_ref.shape[0]
    first = pl.multiple_of((place_ref[1] ^ m) * rows, rows)
    own_high, own_low = split(prior_ref[pl.ds(first, rows)])
    for c in range(0, o_ref.shape[1], 2 * NB):
        cols = slice(c, c + 2 * NB)
        total = dot3(own_high, own_low, high_ref[cols], low_ref[cols])
        for plus_ref in refs[:-1]:
            total = total + plus_ref[:, cols]
        o_ref[:, cols] = total


def swap(block, axis, bit):
    return lax.ppermute(block, axis, [(i, i ^ bit) for i in range(lax.axis_size(axis))])


def dot_rows(left, right):
    return lax.dot_general(
        left, right, NT, precision=lax.Precision.HIGH, preferred_element_type=F32
    )


def local(pixel_ids, quad_offsets, prior_factor):
    panel_count = lax.axis_size("panel")
    row_count = lax.axis_size("row")
    block_rows = pixel_ids.shape[0]
    quarter_rows = block_rows // panel_count
    per_device = B // (row_count * panel_count)
    span_cols = panel_count * per_device
    row_pos = lax.axis_index("row")
    panel_pos = lax.axis_index("panel")
    device_pos = row_pos * panel_count + panel_pos
    lead = 32

    points = jnp.stack(locate(pixel_ids, quad_offsets))
    count = points.shape[1]
    own_points = lax.dynamic_slice_in_dim(points, panel_pos * quarter_rows, quarter_rows, 2)
    local_points = points.reshape(2, count, panel_count, quarter_rows)[:, :, :, :per_device]
    local_points = local_points.reshape(2, count, span_cols)
    own_prior = prior_factor.reshape(panel_count, quarter_rows, -1)[:, :per_device]
    own_prior = own_prior.reshape(span_cols, -1)
    place = jnp.stack([row_pos, panel_pos]).astype(jnp.int32)
    lines = block_rows * row_count // 256 * 8
    folds = span_cols == NB and row_count == 8 and panel_count == 4 and lines == 256

    if not (folds and 2 * count * NB == 8 * own_prior.shape[1]):
        lead = 32
        row_ids = jnp.arange(lead, dtype=jnp.int32)[:, None]
        col_ids = jnp.arange(B, dtype=jnp.int32)[None, :]
        on_diagonal = (row_ids < per_device) & (col_ids == device_pos * per_device + row_ids)
        unit = jnp.where(on_diagonal, 1.0, 0.0).astype(F32)
        flat = local_points.reshape(1, 2 * count, span_cols)
        copies = jnp.broadcast_to(flat, (row_count, 2 * count, span_cols))
        spread = lax.all_to_all(copies, "row", split_axis=0, concat_axis=0, tiled=True)
        parted = features(own_points, spread.transpose(1, 0, 2).reshape(2, count, B))
        covers = [cover_rows(*parted, i, lead) for i in range(0, quarter_rows, lead)]
        covers[0] = covers[0] + unit
        panel_prior = lax.all_gather(own_prior, "row", axis=0, tiled=True)
        partial = dot_rows(prior_factor, panel_prior)
        parts = lax.all_to_all(
            partial.reshape(panel_count, quarter_rows, B), "panel", split_axis=0, concat_axis=0, tiled=True
        )
        parts = jnp.sum(parts, axis=0)
        mine = covers[0][:per_device] - parts[:per_device]
        diag_rows = lax.all_gather(mine, ("row", "panel"), axis=0, tiled=True)
        corners = [(i * lead, None) for i in range(len(covers))]
        return solve(place, covers, corners, [parts], factor(factor_kernel, (diag_rows,), B))

    def turn(block, k):
        return lax.ppermute(block, "row", [((d & 4) | ((d + k) & 3), d) for d in range(8)])

    own = pack(own_prior, local_points)
    far, one, two = swap(own, "row", 4), turn(own, 1), turn(own, 2)
    table = row_table(own_points, lines)
    (far, one, two), table = lax.optimization_barrier(((far, one, two), table))
    shares = vmem_call(
        fold_products_kernel,
        [jax.ShapeDtypeStruct((per_device, 5 * NB), F32)] * 4,
        place,
        [own, far, one, two],
        [pltpu.VMEM((NB, 5 * NB), F32)],
        "fold_products",
    )
    shares, own, far = lax.optimization_barrier((shares, own, far))

    def beside(operands, transfer, work):
        operands, held = lax.optimization_barrier((operands, table))
        return lax.optimization_barrier((transfer(operands), work(operands, held)))

    half = 4 * NB
    east = pltpu.VMEM((15, per_device, half), F32)

    def lead_cover(_, held):
        return vmem_call(
            functools.partial(lead_cover_kernel, points=count),
            [
                jax.ShapeDtypeStruct((per_device, 5 * NB), F32),
                jax.ShapeDtypeStruct((per_device, half), F32),
                jax.ShapeDtypeStruct((lines, 8 * half), BF),
                jax.ShapeDtypeStruct((1, half), F32),
            ],
            place,
            [*held, own, far, one, two],
            [
                east,
                pltpu.VMEM((2, NB, count), F32),
                pltpu.VMEM((NB, 1), F32),
                pltpu.VMEM((8, per_device, 2 * lines), BF),
            ],
            "lead_cover",
        )

    sums, (folded, cover_lead, *counts) = beside(
        shares,
        lambda shares: [swap(share, "panel", m) for m, share in zip((1, 2, 3), shares[1:])],
        lead_cover,
    )
    rest = [turn(own, 3), turn(far, 1), turn(far, 2), turn(far, 3)]
    shard = folded - (shares[0] + sums[0] + sums[1] + sums[2])

    def rest_part(panel_prior, m, plus=()):
        return vmem_call(
            functools.partial(rest_products_kernel, m=m),
            jax.ShapeDtypeStruct((quarter_rows, B), F32),
            place,
            [prior_factor, *panel_prior, *plus],
            name="rest_products",
        )

    def beside_z(_, held):
        cover = vmem_call(
            functools.partial(later_cover_kernel, points=count),
            jax.ShapeDtypeStruct((quarter_rows - per_device, half), F32),
            None,
            [*held, *counts],
            [east],
            "cover",
        )
        cover, blocks = lax.optimization_barrier((cover, rest))
        panel_prior = vmem_call(
            gather_split_kernel,
            [jax.ShapeDtypeStruct((B, own_prior.shape[1]), BF)] * 2,
            place,
            [own, far, one, two, *blocks],
            name="gather_split",
        )
        return cover, panel_prior, rest_part(panel_prior, 3), rest_part(panel_prior, 1)

    along, (cover_first, panel_prior, part_3, part_1) = beside(
        shard[None], lambda x: [swap(x, "row", bit) for bit in (2, 4, 6)], beside_z
    )
    held_rows = jnp.concatenate([shard[None]] + along, 0)

    def across(x):
        corner = [(i, i ^ 6) for i in range(32)]
        return swap(x, "row", 1), swap(x, "panel", 2), lax.ppermute(x, ("row", "panel"), corner)

    def beside_xy(x, held):
        from_3 = swap(part_3, "panel", 1)
        cover = vmem_call(
            functools.partial(block_cover_kernel, points=count),
            jax.ShapeDtypeStruct((quarter_rows, half), F32),
            None,
            [*held, *rest],
            [pltpu.VMEM((lines, 8 * half), BF), pltpu.VMEM((1, half), F32), east],
            "cover",
        )
        part_0, part_2 = rest_part(panel_prior, 0), rest_part(panel_prior, 2, [from_3])
        return cover, part_0, part_2, swap(x, "panel", 1)

    received, (cover_last, part_0, part_2, held_there) = beside(
        held_rows, across, beside_xy
    )
    there = [held_there] + [swap(x, "panel", 1) for x in received]
    part_1, part_2 = lax.optimization_barrier((part_1, part_2))
    parts = [part_0, swap(part_1, "panel", 1), swap(part_2, "panel", 2)]
    factors = factor(unfold_kernel, (place, held_rows, *received, *there), B)
    corners = [(0, 0), (per_device, 0), (0, 4)]
    return solve(place, [cover_lead, cover_first, cover_last], corners, parts, factors)


def solution(mesh):
    return jax.shard_map(
        local,
        mesh=mesh,
        in_specs=(P("row"), P(None, None, "row"), P("row", "panel")),
        out_specs=P(("row", "panel"), None),
        check_vma=False,
    )
```

```python
import functools

import jax
import jax.numpy as jnp
from jax import lax
from jax.experimental import pallas as pl
from jax.experimental.pallas import tpu as pltpu
from jax.sharding import PartitionSpec as P

B = 1024
NB = 128
NEAR = 4
F32 = jnp.float32
BF = jnp.bfloat16
NT = (((1,), (1,)), ((), ()))
SCALE = -1.4426950408889634 / 64.0
CENTRE = 1024.0


def locate(pixel_ids, quad_offsets):
    column = (pixel_ids % 256) * 8
    lines = (pixel_ids // 256) * 8
    east = (column[None, :] + quad_offsets[0]).astype(F32) - CENTRE
    north = (lines[None, :] + quad_offsets[1]).astype(F32) - CENTRE
    return east, north


def pieces(value):
    high = jnp.floor(value * (1.0 / 65536.0)) * 65536.0
    rest = value - high
    mid = jnp.floor(rest * (1.0 / 256.0)) * 256.0
    return [high, mid, rest - mid]


def halves(value):
    high = jnp.floor(value * (1.0 / 128.0)) * 128.0
    return high, value - high


def row_features(x, y):
    xh, xl = halves(x)
    yh, yl = halves(y)
    one = jnp.ones_like(x)
    zero = jnp.zeros_like(x)
    cross = [-2 * xh, -2 * xh, -2 * xl, -2 * xl, -2 * yh, -2 * yh, -2 * yl, -2 * yl]
    return jnp.concatenate(cross + pieces(x * x + y * y) + [one] * 3 + [zero] * 2, 0)


def col_features(x, y):
    xh, xl = halves(x)
    yh, yl = halves(y)
    one = jnp.ones_like(x)
    zero = jnp.zeros_like(x)
    cross = [xh, xl, xh, xl, yh, yl, yh, yl]
    return jnp.concatenate(cross + [one] * 3 + pieces(x * x + y * y) + [zero] * 2, 0)


def feature_kernel(row_ref, col_ref, f_ref, g_ref):
    for a in range(row_ref.shape[1]):
        one = row_features(row_ref[0, a : a + 1, :], row_ref[1, a : a + 1, :])
        f_ref[a] = one.T.astype(BF)
        g_ref[a] = col_features(col_ref[0, a : a + 1, :], col_ref[1, a : a + 1, :]).astype(BF)


def features(row_points, col_points):
    count, rows = row_points.shape[1:]
    cols = col_points.shape[2]
    return pl.pallas_call(
        feature_kernel,
        out_shape=[
            jax.ShapeDtypeStruct((count, rows, 16), BF),
            jax.ShapeDtypeStruct((count, 16, cols), BF),
        ],
        in_specs=[pl.BlockSpec(memory_space=pltpu.VMEM)] * 2,
        out_specs=[pl.BlockSpec(memory_space=pltpu.VMEM)] * 2,
        compiler_params=pltpu.CompilerParams(vmem_limit_bytes=8 << 20),
        name="features",
    )(row_points, col_points)


def cover_kernel(f_ref, g_ref, o_ref):
    count, block = f_ref.shape[:2]
    rows_here = f_ref[...].reshape(count * block, 16)

    def column_point(b, total):
        apart = jnp.dot(rows_here, g_ref[b], preferred_element_type=F32)
        near = jnp.exp2(apart * SCALE)
        for a in range(count):
            total = total + near[a * block : (a + 1) * block]
        return total

    total = lax.fori_loop(0, count, column_point, jnp.zeros(o_ref.shape, F32), unroll=8)
    o_ref[...] = total * (1.0 / (count * count))


def cover_rows(row_part, col_part, first, block):
    count, rows, depth = row_part.shape
    cols = col_part.shape[2]
    index = first // block
    return pl.pallas_call(
        cover_kernel,
        grid=(1,),
        out_shape=jax.ShapeDtypeStruct((block, cols), F32),
        in_specs=[
            pl.BlockSpec((count, block, depth), lambda i: (0, index, 0)),
            pl.BlockSpec((count, depth, cols), lambda i: (0, 0, 0)),
        ],
        out_specs=pl.BlockSpec((block, cols), lambda i: (0, 0)),
        compiler_params=pltpu.CompilerParams(vmem_limit_bytes=16 << 20),
        cost_estimate=pl.CostEstimate(flops=10**8, bytes_accessed=1 << 18, transcendentals=0),
        name="cover",
    )(row_part, col_part)


def table_rows(offset, north, lines):
    line = lax.broadcasted_iota(jnp.int32, (16, lines), 1).astype(F32) - CENTRE
    total = [jnp.zeros((16, lines), F32) for _ in range(8)]
    for a in range(offset.shape[1]):
        apart = jnp.broadcast_to(north[:, a : a + 1], (16, lines)) - line
        near = jnp.exp2(apart * apart * SCALE)
        which = jnp.broadcast_to(offset[:, a : a + 1], (16, lines))
        for p in range(8):
            total[p] = total[p] + jnp.where(which == float(p), near, 0.0)
    return [split(x) for x in total]


def row_table_kernel(row_ref, t_ref, row_cell_ref, place_ref):
    rows = row_ref.shape[2]
    lines = t_ref.shape[2] // 2
    row_cell = jnp.floor(row_ref[0] * 0.125) * 8.0
    place_ref[0] = (row_ref[0] - row_cell).T
    place_ref[1] = row_ref[1].T
    row_cell_ref[...] = row_cell[0:1].T

    def row_tile(index, _):
        here = pl.ds(pl.multiple_of(index * 16, 16), 16)
        for p, (high, low) in enumerate(table_rows(place_ref[0, here], place_ref[1, here], lines)):
            t_ref[p, here, :lines] = high
            t_ref[p, here, lines:] = low
        return 0

    lax.fori_loop(0, rows // 16, row_tile, 0)


def row_table(row_points, lines):
    count, rows = row_points.shape[1:]
    return pl.pallas_call(
        row_table_kernel,
        out_shape=[
            jax.ShapeDtypeStruct((8, rows, 2 * lines), BF),
            jax.ShapeDtypeStruct((rows, 1), F32),
        ],
        in_specs=[pl.BlockSpec(memory_space=pltpu.VMEM)],
        out_specs=[pl.BlockSpec(memory_space=pltpu.VMEM)] * 2,
        scratch_shapes=[pltpu.VMEM((2, rows, count), F32)],
        compiler_params=pltpu.CompilerParams(vmem_limit_bytes=16 << 20),
        cost_estimate=pl.CostEstimate(flops=10**8, bytes_accessed=1 << 18, transcendentals=0),
        name="row_table",
    )(row_points)


def pack(prior, points):
    flat = points.reshape(-1, NB)
    tiles = prior.shape[1] // NB
    extra = flat.reshape(tiles, flat.shape[0] // tiles, NB).transpose(1, 0, 2)
    return jnp.concatenate([prior, extra.reshape(-1, prior.shape[1])], 0)


def unpack(block_ref):
    extra = block_ref.shape[0] - NB
    tiles = block_ref.shape[1] // NB
    flat = jnp.concatenate(
        [block_ref[NB : NB + extra, NB * t : NB * t + NB] for t in range(tiles)], 0
    )
    count = flat.shape[0] // 2
    return flat[:count], flat[count:]


def column_counts(block_ref, h_ref, at, stride):
    east, north = unpack(block_ref)
    lines = h_ref.shape[0]
    cell = jnp.floor(east[0:1] * 0.125) * 8.0
    line = jnp.floor(north[0:1] * 0.125) * 8.0
    east, north = east - cell, north - line
    sub = lax.broadcasted_iota(jnp.int32, (8, NB), 0).astype(F32)
    held = [jnp.zeros((8, NB), F32) for _ in range(8)]
    for b in range(east.shape[0]):
        one = jnp.where(sub == jnp.broadcast_to(north[b : b + 1], (8, NB)), 1.0, 0.0)
        which = jnp.broadcast_to(east[b : b + 1], (8, NB))
        for q in range(8):
            held[q] = held[q] + jnp.where(which == float(q), one, 0.0)
    line = jnp.broadcast_to(line, (8, NB))
    for r in range(0, lines, 16):
        low = line == float(r) - CENTRE
        high = line == float(r + 8) - CENTRE
        for q in range(8):
            pair = [jnp.where(low, held[q], 0.0), jnp.where(high, held[q], 0.0)]
            lanes = slice(q * stride + at, q * stride + at + NB)
            h_ref[r : r + 16, lanes] = jnp.concatenate(pair, 0).astype(BF)
    return cell


def cover_chunk(table, row_cell, col_cell, h_ref, east_ref, points):
    chunk, cols = east_ref.shape[1:]
    cell = jnp.broadcast_to(row_cell, (chunk, cols)) - col_cell
    for t in range(15):
        apart = cell + float(t - 7)
        east_ref[t] = jnp.exp2(apart * apart * SCALE)
    table = table.reshape(8 * chunk, table.shape[2])
    total = jnp.zeros((chunk, cols), F32)
    for q in range(8):
        counts = h_ref[:, q * cols : (q + 1) * cols]
        part = jnp.dot(table, jnp.concatenate([counts, counts], 0), preferred_element_type=F32)
        for p in range(8):
            total = total + part[p * chunk : (p + 1) * chunk] * east_ref[p - q + 7]
    return total * (1.0 / (points * points))


def lead_cover_kernel(
    place_ref, t_ref, row_cell_ref, *refs, points
):
    blocks, refs = refs[:4], refs[4:]
    folded_ref, own_ref, h_ref, col_cell_ref, east_ref, far_ref, far_cell_ref, far_table_ref = refs
    rows, cols = own_ref.shape
    lines = h_ref.shape[0]
    cells = [column_counts(ref, h_ref, NB * i, cols) for i, ref in enumerate(blocks)]
    col_cell = jnp.concatenate(cells, 1)
    col_cell_ref[...] = col_cell

    east, north = unpack(blocks[1])
    far_ref[0] = (east - cells[1]).T
    far_ref[1] = north.T
    far_cell_ref[...] = cells[1].T
    first = pl.multiple_of(place_ref[1] * rows, rows)
    for r in range(0, rows, 16):
        here = pl.ds(first + r, 16)
        for p, (high, low) in enumerate(table_rows(far_ref[0, here], far_ref[1, here], lines)):
            far_table_ref[p, r : r + 16, :lines] = high
            far_table_ref[p, r : r + 16, lines:] = low

    mine = cover_chunk(t_ref[:, :rows], row_cell_ref[:rows], col_cell, h_ref, east_ref, points)
    row = lax.broadcasted_iota(jnp.int32, (rows, cols), 0)
    col = lax.broadcasted_iota(jnp.int32, (rows, cols), 1)
    mine = mine + jnp.where(col == first + row, 1.0, 0.0)
    own_ref[...] = mine
    far = cover_chunk(
        far_table_ref[...], far_cell_ref[pl.ds(first, rows)], col_cell, h_ref, east_ref, points
    )
    folded_ref[:, : 3 * NB] = mine[:, : 3 * NB]
    folded_ref[:, 3 * NB : 4 * NB] = far[:, 2 * NB : 3 * NB]
    own_last = makes_own(place_ref[0])
    folded_ref[:, 4 * NB :] = jnp.where(own_last, mine[:, 3 * NB :], far[:, 3 * NB :])


def later_cover_kernel(t_ref, row_cell_ref, h_ref, col_cell_ref, o_ref, east_ref, *, points):
    chunk = east_ref.shape[1]
    skipped = t_ref.shape[1] - o_ref.shape[0]

    def row_chunk(index, _):
        first = pl.multiple_of(index * chunk, chunk)
        here = pl.ds(pl.multiple_of(first + skipped, chunk), chunk)
        o_ref[pl.ds(first, chunk)] = cover_chunk(
            t_ref[:, here], row_cell_ref[here], col_cell_ref[...], h_ref, east_ref, points
        )
        return 0

    lax.fori_loop(0, o_ref.shape[0] // chunk, row_chunk, 0)


def block_cover_kernel(t_ref, row_cell_ref, *refs, points):
    blocks, (o_ref, h_ref, col_cell_ref, east_ref) = blocks_in(refs[:-4]), refs[-4:]
    cells = [
        column_counts(ref, h_ref, NB * i, o_ref.shape[1]) for i, ref in enumerate(blocks)
    ]
    col_cell_ref[...] = jnp.concatenate(cells, 1)
    later_cover_kernel(t_ref, row_cell_ref, h_ref, col_cell_ref, o_ref, east_ref, points=points)


def inverse_factor(tiles):
    n = len(tiles)
    width = 8 * n
    lane = lax.broadcasted_iota(jnp.int32, (8, width), 1)
    sub = lax.broadcasted_iota(jnp.int32, (8, width), 0)
    tiles = list(tiles)
    out = []

    def spread(x):
        return jnp.broadcast_to(x, (8, width))

    def lanes(tile, v):
        return [spread(tile[:, 8 * v + q : 8 * v + q + 1]) for q in range(8)]

    following = lanes(tiles[0], 0)
    for v in range(n):
        near = min(n, v + NEAR)
        cols = {v: following}
        if v + 1 < n:
            cols[v] = cols[v] + lanes(tiles[v], v + 1)
            cols[v + 1] = lanes(tiles[v + 1], v) + lanes(tiles[v + 1], v + 1)
        for r in range(v + 2, near):
            cols[r] = lanes(tiles[r], v)
        here = (lane >= 8 * v) & (lane < 8 * v + 8)
        for r in range(v + 1, n):
            tiles[r] = jnp.where(here, 0.0, tiles[r])
        tiles[v] = jnp.where(here, jnp.where(lane == sub + 8 * v, 1.0, 0.0), tiles[v])
        pivots = jnp.ones((8, width), F32)
        for s in range(8):
            head = cols[v]
            pivot = spread(head[s][s : s + 1])
            inverse = 1.0 / pivot
            pivots = jnp.where(sub == s, pivot, pivots)
            row = spread(tiles[v][s : s + 1])
            heads = [spread(head[k][s : s + 1]) for k in range(s + 1, len(head))]
            for r in range(v, near):
                part = cols[r][s] * inverse
                if r == v:
                    part = jnp.where(sub > s, part, 0.0)
                tiles[r] = tiles[r] - part * row
                for k in range(s + 1, len(cols[r])):
                    cols[r][k] = cols[r][k] - part * heads[k - s - 1]
        if v + 1 < n:
            following = cols[v + 1][8:]
        rows = tiles[v] * lax.rsqrt(pivots)
        if near < n:
            high = rows.astype(BF).astype(F32)
            low = rows - high
            left = jnp.concatenate([high, high, low, low], 0).astype(BF)
            right = jnp.concatenate([high, low, high, low], 0).astype(BF)
            update = lax.dot_general(
                left, right, (((0,), (0,)), ((), ())), preferred_element_type=F32
            )
            for r in range(near, n):
                tiles[r] = tiles[r] - update[8 * r : 8 * r + 8]
        out.append(jnp.where(lane <= sub + 8 * v, rows, 0.0))
    return jnp.concatenate(out, 0)


def split(x):
    high = x.astype(BF)
    return high, (x - high.astype(F32)).astype(BF)


def dot3(ah, al, bh, bl):
    dot = functools.partial(lax.dot_general, dimension_numbers=NT, preferred_element_type=F32)
    return dot(ah, bh) + (dot(ah, bl) + dot(al, bh))


def factor_blocks(a_ref, lh_ref, ll_ref, wh_ref, wl_ref):
    n = a_ref.shape[0]
    blocks = n // NB

    def column(first):
        end = first + NB
        bh, bl = split(a_ref[end:, first:end])
        high, low = split(dot3(bh, bl, wh_ref[first:end], wl_ref[first:end]))
        lh_ref[end:, first:end] = high
        ll_ref[end:, first:end] = low
        a_ref[end:, end : end + NB] = a_ref[end:, end : end + NB] - dot3(
            lh_ref[end:, :end],
            ll_ref[end:, :end],
            lh_ref[end : end + NB, :end],
            ll_ref[end : end + NB, :end],
        )

    def step(j, _):
        c = pl.multiple_of(j * NB, NB)
        tiles = [a_ref[pl.ds(c + 8 * v, 8), pl.ds(c, NB)] for v in range(NB // 8)]
        wh, wl = split(inverse_factor(tiles))
        wh_ref[pl.ds(c, NB)] = wh
        wl_ref[pl.ds(c, NB)] = wl
        for block in range(blocks - 1):
            pl.when(j == block)(functools.partial(column, block * NB))
        return 0

    lax.fori_loop(0, blocks, step, 0)


def factor_kernel(diag_ref, lh_ref, ll_ref, wh_ref, wl_ref, a_ref):
    a_ref[...] = diag_ref[...]
    factor_blocks(a_ref, lh_ref, ll_ref, wh_ref, wl_ref)


def turned(r, k):
    at = ((r & 1) << 1 | (r >> 1) & 1) + k
    return (r & 4) | (at & 1) << 1 | (at >> 1) & 1


def block_order(r):
    own = [r, r ^ 4, turned(r, 1), turned(r, 2), turned(r, 3)]
    return own + [turned(r, 3) ^ 4, turned(r, 1) ^ 4, turned(r, 2) ^ 4]


def makes_own(r):
    return (r & 1) == 0


def folded_blocks(r):
    order = block_order(r)
    either = jnp.where(makes_own(r), r, r ^ 4)
    return [(r, r), (r, order[1]), (r, order[2]), (order[1], order[2]), (either, order[3])]


def blocks_in(refs):
    return [
        ref.at[first : first + ref.shape[0] // parts]
        for ref in refs
        for parts in [1 + (ref.shape[0] >= 2 * NB)]
        for first in range(0, ref.shape[0], ref.shape[0] // parts)
    ]


def unfold_kernel(place_ref, *refs):
    pieces_refs, (lh_ref, ll_ref, wh_ref, wl_ref, a_ref, g_ref) = refs[:8], refs[8:]
    row_pos = place_ref[0]
    panel_pos = place_ref[1]
    for i, ref in enumerate(pieces_refs):
        g_ref[4 * i : 4 * i + 4] = ref[...]

    def rows_of(r, _):
        away = r ^ row_pos
        slot = (away >> 1) | ((away & 1) << 2)
        ats = []
        for p in range(4):
            gone = p ^ panel_pos
            ats.append(slot | ((gone >> 1) << 3) | ((gone & 1) << 4))
        for k, (rows, cols) in enumerate(folded_blocks(r)):
            block = jnp.concatenate([g_ref[at, :, NB * k : NB * k + NB] for at in ats], 0)
            rr = pl.multiple_of(rows * NB, NB)
            cc = pl.multiple_of(cols * NB, NB)

            @pl.when(rows >= cols)
            def _():
                a_ref[pl.ds(rr, NB), pl.ds(cc, NB)] = block

            if k:

                @pl.when(rows < cols)
                def _():
                    a_ref[pl.ds(cc, NB), pl.ds(rr, NB)] = block.T

        return 0

    lax.fori_loop(0, 8, rows_of, 0)
    factor_blocks(a_ref, lh_ref, ll_ref, wh_ref, wl_ref)


def factor(kernel, operands, n):
    in_specs = [pl.BlockSpec(memory_space=pltpu.VMEM)] * len(operands)
    scratch = [pltpu.VMEM((n, n), F32)]
    if kernel is unfold_kernel:
        in_specs[0] = pl.BlockSpec(memory_space=pltpu.SMEM)
        scratch.append(pltpu.VMEM((32, *operands[1].shape[1:]), F32))
    return pl.pallas_call(
        kernel,
        out_shape=[jax.ShapeDtypeStruct((n, n), BF)] * 2 + [jax.ShapeDtypeStruct((n, NB), BF)] * 2,
        in_specs=in_specs,
        out_specs=[pl.BlockSpec(memory_space=pltpu.VMEM)] * 4,
        scratch_shapes=scratch,
        compiler_params=pltpu.CompilerParams(vmem_limit_bytes=32 << 20),
        cost_estimate=pl.CostEstimate(flops=5 * 10**10, bytes_accessed=8 << 20, transcendentals=0),
        name="factor",
    )(*operands)


def solve_kernel(place_ref, *refs, corners):
    cover_refs, parts_refs = refs[: len(corners)], refs[len(corners) : -7]
    lh_ref, ll_ref, wh_ref, wl_ref, o_ref, xh_ref, xl_ref = refs[-7:]
    n = o_ref.shape[1]

    def put(rows, cols, value):
        taken = parts_refs[0][parts_refs[0].shape[0] - 1, rows, cols]
        for part in parts_refs[1:]:
            taken = taken + part[part.shape[0] - 1, rows, cols]
        o_ref[rows, cols] = value - taken

    for (row, block), ref in zip(corners, cover_refs):
        rows = slice(row, row + ref.shape[0])
        if block is None:
            put(rows, slice(None), ref[...])
            continue
        for c, s in enumerate(block_order(place_ref[0])[block : block + ref.shape[1] // NB]):
            cols = pl.ds(pl.multiple_of(s * NB, NB), NB)
            put(rows, cols, ref[:, NB * c : NB * c + NB])
    for c in range(0, n, NB):
        here = o_ref[:, c : c + NB]
        if c:
            here = here - dot3(
                xh_ref[:, :c], xl_ref[:, :c], lh_ref[c : c + NB, :c], ll_ref[c : c + NB, :c]
            )
        bh, bl = split(here)
        x = dot3(bh, bl, wh_ref[c : c + NB], wl_ref[c : c + NB])
        o_ref[:, c : c + NB] = x
        xh, xl = split(x)
        xh_ref[:, c : c + NB] = xh
        xl_ref[:, c : c + NB] = xl


def solve(place, covers, corners, parts, factors):
    rows, n = parts[0].shape[1:]
    return vmem_call(
        functools.partial(solve_kernel, corners=corners),
        jax.ShapeDtypeStruct((rows, n), F32),
        place,
        [*covers, *parts, *factors],
        [pltpu.VMEM((rows, n), BF)] * 2,
        "solve",
    )


def vmem_call(kernel, out_shape, place, operands, scratch=(), name=None):
    return pl.pallas_call(
        kernel,
        out_shape=out_shape,
        in_specs=[pl.BlockSpec(memory_space=pltpu.SMEM)] * (place is not None)
        + [pl.BlockSpec(memory_space=pltpu.VMEM)] * len(operands),
        out_specs=jax.tree.map(lambda _: pl.BlockSpec(memory_space=pltpu.VMEM), out_shape),
        scratch_shapes=list(scratch),
        compiler_params=pltpu.CompilerParams(vmem_limit_bytes=32 << 20),
        cost_estimate=pl.CostEstimate(flops=10**8, bytes_accessed=1 << 18, transcendentals=0),
        name=name,
    )(*([] if place is None else [place]), *operands)


def fold_products_kernel(place_ref, *refs):
    blocks, shares, total_ref = refs[:4], refs[4:-1], refs[-1]
    own, far, one, two = [split(ref[:NB]) for ref in blocks]
    own_last = makes_own(place_ref[0])
    either = split(jnp.where(own_last, blocks[0][:NB], blocks[1][:NB]))
    pairs = [(own, own), (own, far), (own, one), (far, one), (either, two)]
    for k, (left, right) in enumerate(pairs):
        total_ref[:, NB * k : NB * k + NB] = dot3(*left, *right)
    rows = shares[0].shape[0]
    for m, ref in enumerate(shares):
        first = pl.multiple_of((place_ref[1] ^ m) * rows, rows)
        ref[...] = total_ref[pl.ds(first, rows)]


def gather_split_kernel(place_ref, *refs):
    blocks, (high_ref, low_ref) = blocks_in(refs[:-2]), refs[-2:]
    for s, ref in zip(block_order(place_ref[0]), blocks):
        first = pl.multiple_of(s * NB, NB)
        high, low = split(ref[:NB])
        high_ref[pl.ds(first, NB)] = high
        low_ref[pl.ds(first, NB)] = low


def rest_products_kernel(place_ref, prior_ref, high_ref, low_ref, *refs, turns):
    plus_refs, o_ref = refs[:-1], refs[-1]
    rows = o_ref.shape[1]
    for i, m in enumerate(turns):
        first = pl.multiple_of((place_ref[1] ^ m) * rows, rows)
        own_high, own_low = split(prior_ref[pl.ds(first, rows)])
        for c in range(0, o_ref.shape[2], 2 * NB):
            cols = slice(c, c + 2 * NB)
            total = dot3(own_high, own_low, high_ref[cols], low_ref[cols])
            for plus_ref in plus_refs:
                total = total + plus_ref[i, :, cols]
            o_ref[i, :, cols] = total


def swap(block, axis, bit):
    return lax.ppermute(block, axis, [(i, i ^ bit) for i in range(lax.axis_size(axis))])


def dot_rows(left, right):
    return lax.dot_general(
        left, right, NT, precision=lax.Precision.HIGH, preferred_element_type=F32
    )


def local(pixel_ids, quad_offsets, prior_factor):
    panel_count = lax.axis_size("panel")
    row_count = lax.axis_size("row")
    block_rows = pixel_ids.shape[0]
    quarter_rows = block_rows // panel_count
    per_device = B // (row_count * panel_count)
    span_cols = panel_count * per_device
    row_pos = lax.axis_index("row")
    panel_pos = lax.axis_index("panel")
    device_pos = row_pos * panel_count + panel_pos
    lead = 32

    points = jnp.stack(locate(pixel_ids, quad_offsets))
    count = points.shape[1]
    own_points = lax.dynamic_slice_in_dim(points, panel_pos * quarter_rows, quarter_rows, 2)
    local_points = points.reshape(2, count, panel_count, quarter_rows)[:, :, :, :per_device]
    local_points = local_points.reshape(2, count, span_cols)
    own_prior = prior_factor.reshape(panel_count, quarter_rows, -1)[:, :per_device]
    own_prior = own_prior.reshape(span_cols, -1)
    place = jnp.stack([row_pos, panel_pos]).astype(jnp.int32)
    lines = block_rows * row_count // 256 * 8
    folds = span_cols == NB and row_count == 8 and panel_count == 4 and lines == 256

    if not (folds and 2 * count * NB == 8 * own_prior.shape[1]):
        lead = 32
        row_ids = jnp.arange(lead, dtype=jnp.int32)[:, None]
        col_ids = jnp.arange(B, dtype=jnp.int32)[None, :]
        on_diagonal = (row_ids < per_device) & (col_ids == device_pos * per_device + row_ids)
        unit = jnp.where(on_diagonal, 1.0, 0.0).astype(F32)
        flat = local_points.reshape(1, 2 * count, span_cols)
        copies = jnp.broadcast_to(flat, (row_count, 2 * count, span_cols))
        spread = lax.all_to_all(copies, "row", split_axis=0, concat_axis=0, tiled=True)
        parted = features(own_points, spread.transpose(1, 0, 2).reshape(2, count, B))
        covers = [cover_rows(*parted, i, lead) for i in range(0, quarter_rows, lead)]
        covers[0] = covers[0] + unit
        panel_prior = lax.all_gather(own_prior, "row", axis=0, tiled=True)
        partial = dot_rows(prior_factor, panel_prior)
        parts = lax.all_to_all(
            partial.reshape(panel_count, quarter_rows, B), "panel", split_axis=0, concat_axis=0, tiled=True
        )
        parts = jnp.sum(parts, axis=0)
        mine = covers[0][:per_device] - parts[:per_device]
        diag_rows = lax.all_gather(mine, ("row", "panel"), axis=0, tiled=True)
        corners = [(i * lead, None) for i in range(len(covers))]
        return solve(place, covers, corners, [parts[None]], factor(factor_kernel, (diag_rows,), B))

    def turn(block, k):
        return lax.ppermute(block, "row", [(turned(d, k), d) for d in range(8)])

    own = pack(own_prior, local_points)
    two, one, far = turn(own, 2), turn(own, 1), swap(own, "row", 4)
    table = row_table(own_points, lines)
    (far, one, two), table = lax.optimization_barrier(((far, one, two), table))
    shares = vmem_call(
        fold_products_kernel,
        [jax.ShapeDtypeStruct((per_device, 5 * NB), F32)] * 4,
        place,
        [own, far, one, two],
        [pltpu.VMEM((NB, 5 * NB), F32)],
        "fold_products",
    )
    shares, own, far = lax.optimization_barrier((shares, own, far))

    def beside(operands, transfer, work):
        operands, held = lax.optimization_barrier((operands, table))
        return lax.optimization_barrier((transfer(operands), work(operands, held)))

    half = 4 * NB
    east = pltpu.VMEM((15, per_device, half), F32)

    def lead_cover(_, held):
        return vmem_call(
            functools.partial(lead_cover_kernel, points=count),
            [
                jax.ShapeDtypeStruct((per_device, 5 * NB), F32),
                jax.ShapeDtypeStruct((per_device, half), F32),
                jax.ShapeDtypeStruct((lines, 8 * half), BF),
                jax.ShapeDtypeStruct((1, half), F32),
            ],
            place,
            [*held, own, far, one, two],
            [
                east,
                pltpu.VMEM((2, NB, count), F32),
                pltpu.VMEM((NB, 1), F32),
                pltpu.VMEM((8, per_device, 2 * lines), BF),
            ],
            "lead_cover",
        )

    sums, (folded, cover_lead, *counts) = beside(
        shares,
        lambda shares: [swap(share, "panel", m) for m, share in zip((1, 2, 3), shares[1:])],
        lead_cover,
    )
    rest = [turn(jnp.concatenate([own, far], 0), 3), turn(far, 1), turn(far, 2)]
    shard = folded - (shares[0] + sums[0] + sums[1] + sums[2])

    def rest_part(panel_prior, turns, plus=()):
        return vmem_call(
            functools.partial(rest_products_kernel, turns=turns),
            jax.ShapeDtypeStruct((len(turns), quarter_rows, B), F32),
            place,
            [prior_factor, *panel_prior, *plus],
            name="rest_products",
        )

    def beside_z(_, held):
        cover = vmem_call(
            functools.partial(later_cover_kernel, points=count),
            jax.ShapeDtypeStruct((quarter_rows - per_device, half), F32),
            None,
            [*held, *counts],
            [east],
            "cover",
        )
        cover, blocks = lax.optimization_barrier((cover, rest))
        panel_prior = vmem_call(
            gather_split_kernel,
            [jax.ShapeDtypeStruct((B, own_prior.shape[1]), BF)] * 2,
            place,
            [own, far, one, two, *blocks],
            name="gather_split",
        )
        return cover, panel_prior, rest_part(panel_prior, (3, 1))

    along, (cover_first, panel_prior, for_core) = beside(
        shard[None], lambda x: [swap(x, "row", bit) for bit in (2, 4, 6)], beside_z
    )
    held_rows = jnp.concatenate([shard[None]] + along, 0)

    def across(x):
        corner = [(i, i ^ 6) for i in range(32)]
        return swap(x, "row", 1), swap(x, "panel", 2), lax.ppermute(x, ("row", "panel"), corner)

    def beside_xy(x, held):
        from_core = swap(for_core, "panel", 1)
        cover = vmem_call(
            functools.partial(block_cover_kernel, points=count),
            jax.ShapeDtypeStruct((quarter_rows, half), F32),
            None,
            [*held, *rest],
            [pltpu.VMEM((lines, 8 * half), BF), pltpu.VMEM((1, half), F32), east],
            "cover",
        )
        part_0, part_2 = rest_part(panel_prior, (0,)), rest_part(panel_prior, (2,), [from_core])
        return cover, part_0, part_2, from_core, swap(x, "panel", 1)

    received, (cover_last, part_0, part_2, from_core, held_there) = beside(
        held_rows, across, beside_xy
    )
    there = [held_there] + [swap(x, "panel", 1) for x in received]
    parts = [part_0, from_core, swap(part_2, "panel", 2)]
    factors = factor(unfold_kernel, (place, held_rows, *received, *there), B)
    corners = [(0, 0), (per_device, 0), (0, 4)]
    return solve(place, [cover_lead, cover_first, cover_last], corners, parts, factors)


def solution(mesh):
    return jax.shard_map(
        local,
        mesh=mesh,
        in_specs=(P("row"), P(None, None, "row"), P("row", "panel")),
        out_specs=P(("row", "panel"), None),
        check_vma=False,
    )
```

```python
import functools

import jax
import jax.numpy as jnp
from jax import lax
from jax.experimental import pallas as pl
from jax.experimental.pallas import tpu as pltpu
from jax.sharding import PartitionSpec as P

B = 1024
NB = 128
NEAR = 4
F32 = jnp.float32
BF = jnp.bfloat16
NT = (((1,), (1,)), ((), ()))
SCALE = -1.4426950408889634 / 64.0
CENTRE = 1024.0


def locate(pixel_ids, quad_offsets):
    column = (pixel_ids % 256) * 8
    lines = (pixel_ids // 256) * 8
    east = (column[None, :] + quad_offsets[0]).astype(F32) - CENTRE
    north = (lines[None, :] + quad_offsets[1]).astype(F32) - CENTRE
    return east, north


def pieces(value):
    high = jnp.floor(value * (1.0 / 65536.0)) * 65536.0
    rest = value - high
    mid = jnp.floor(rest * (1.0 / 256.0)) * 256.0
    return [high, mid, rest - mid]


def halves(value):
    high = jnp.floor(value * (1.0 / 128.0)) * 128.0
    return high, value - high


def row_features(x, y):
    xh, xl = halves(x)
    yh, yl = halves(y)
    one = jnp.ones_like(x)
    zero = jnp.zeros_like(x)
    cross = [-2 * xh, -2 * xh, -2 * xl, -2 * xl, -2 * yh, -2 * yh, -2 * yl, -2 * yl]
    return jnp.concatenate(cross + pieces(x * x + y * y) + [one] * 3 + [zero] * 2, 0)


def col_features(x, y):
    xh, xl = halves(x)
    yh, yl = halves(y)
    one = jnp.ones_like(x)
    zero = jnp.zeros_like(x)
    cross = [xh, xl, xh, xl, yh, yl, yh, yl]
    return jnp.concatenate(cross + [one] * 3 + pieces(x * x + y * y) + [zero] * 2, 0)


def feature_kernel(row_ref, col_ref, f_ref, g_ref):
    for a in range(row_ref.shape[1]):
        one = row_features(row_ref[0, a : a + 1, :], row_ref[1, a : a + 1, :])
        f_ref[a] = one.T.astype(BF)
        g_ref[a] = col_features(col_ref[0, a : a + 1, :], col_ref[1, a : a + 1, :]).astype(BF)


def features(row_points, col_points):
    count, rows = row_points.shape[1:]
    cols = col_points.shape[2]
    return pl.pallas_call(
        feature_kernel,
        out_shape=[
            jax.ShapeDtypeStruct((count, rows, 16), BF),
            jax.ShapeDtypeStruct((count, 16, cols), BF),
        ],
        in_specs=[pl.BlockSpec(memory_space=pltpu.VMEM)] * 2,
        out_specs=[pl.BlockSpec(memory_space=pltpu.VMEM)] * 2,
        compiler_params=pltpu.CompilerParams(vmem_limit_bytes=8 << 20),
        name="features",
    )(row_points, col_points)


def cover_kernel(f_ref, g_ref, o_ref):
    count, block = f_ref.shape[:2]
    rows_here = f_ref[...].reshape(count * block, 16)

    def column_point(b, total):
        apart = jnp.dot(rows_here, g_ref[b], preferred_element_type=F32)
        near = jnp.exp2(apart * SCALE)
        for a in range(count):
            total = total + near[a * block : (a + 1) * block]
        return total

    total = lax.fori_loop(0, count, column_point, jnp.zeros(o_ref.shape, F32), unroll=8)
    o_ref[...] = total * (1.0 / (count * count))


def cover_rows(row_part, col_part, first, block):
    count, rows, depth = row_part.shape
    cols = col_part.shape[2]
    index = first // block
    return pl.pallas_call(
        cover_kernel,
        grid=(1,),
        out_shape=jax.ShapeDtypeStruct((block, cols), F32),
        in_specs=[
            pl.BlockSpec((count, block, depth), lambda i: (0, index, 0)),
            pl.BlockSpec((count, depth, cols), lambda i: (0, 0, 0)),
        ],
        out_specs=pl.BlockSpec((block, cols), lambda i: (0, 0)),
        compiler_params=pltpu.CompilerParams(vmem_limit_bytes=16 << 20),
        cost_estimate=pl.CostEstimate(flops=10**8, bytes_accessed=1 << 18, transcendentals=0),
        name="cover",
    )(row_part, col_part)


def table_rows(offset, north, lines):
    line = lax.broadcasted_iota(jnp.int32, (16, lines), 1).astype(F32) - CENTRE
    total = [jnp.zeros((16, lines), F32) for _ in range(8)]
    for a in range(offset.shape[1]):
        apart = jnp.broadcast_to(north[:, a : a + 1], (16, lines)) - line
        near = jnp.exp2(apart * apart * SCALE)
        which = jnp.broadcast_to(offset[:, a : a + 1], (16, lines))
        for p in range(8):
            total[p] = total[p] + jnp.where(which == float(p), near, 0.0)
    return [split(x) for x in total]


def row_table_kernel(row_ref, t_ref, row_cell_ref, place_ref):
    rows = row_ref.shape[2]
    lines = t_ref.shape[2] // 2
    row_cell = jnp.floor(row_ref[0] * 0.125) * 8.0
    place_ref[0] = (row_ref[0] - row_cell).T
    place_ref[1] = row_ref[1].T
    row_cell_ref[...] = row_cell[0:1].T

    def row_tile(index, _):
        here = pl.ds(pl.multiple_of(index * 16, 16), 16)
        for p, (high, low) in enumerate(table_rows(place_ref[0, here], place_ref[1, here], lines)):
            t_ref[p, here, :lines] = high
            t_ref[p, here, lines:] = low
        return 0

    lax.fori_loop(0, rows // 16, row_tile, 0)


def row_table(row_points, lines):
    count, rows = row_points.shape[1:]
    return pl.pallas_call(
        row_table_kernel,
        out_shape=[
            jax.ShapeDtypeStruct((8, rows, 2 * lines), BF),
            jax.ShapeDtypeStruct((rows, 1), F32),
        ],
        in_specs=[pl.BlockSpec(memory_space=pltpu.VMEM)],
        out_specs=[pl.BlockSpec(memory_space=pltpu.VMEM)] * 2,
        scratch_shapes=[pltpu.VMEM((2, rows, count), F32)],
        compiler_params=pltpu.CompilerParams(vmem_limit_bytes=16 << 20),
        cost_estimate=pl.CostEstimate(flops=10**8, bytes_accessed=1 << 18, transcendentals=0),
        name="row_table",
    )(row_points)


def pack(prior, points):
    flat = points.reshape(-1, NB)
    tiles = prior.shape[1] // NB
    extra = flat.reshape(tiles, flat.shape[0] // tiles, NB).transpose(1, 0, 2)
    return jnp.concatenate([prior, extra.reshape(-1, prior.shape[1])], 0)


def unpack(block_ref):
    extra = block_ref.shape[0] - NB
    tiles = block_ref.shape[1] // NB
    flat = jnp.concatenate(
        [block_ref[NB : NB + extra, NB * t : NB * t + NB] for t in range(tiles)], 0
    )
    count = flat.shape[0] // 2
    return flat[:count], flat[count:]


def column_counts(block_ref, h_ref, at, stride):
    east, north = unpack(block_ref)
    lines = h_ref.shape[0]
    cell = jnp.floor(east[0:1] * 0.125) * 8.0
    line = jnp.floor(north[0:1] * 0.125) * 8.0
    east, north = east - cell, north - line
    sub = lax.broadcasted_iota(jnp.int32, (8, NB), 0).astype(F32)
    held = [jnp.zeros((8, NB), F32) for _ in range(8)]
    for b in range(east.shape[0]):
        one = jnp.where(sub == jnp.broadcast_to(north[b : b + 1], (8, NB)), 1.0, 0.0)
        which = jnp.broadcast_to(east[b : b + 1], (8, NB))
        for q in range(8):
            held[q] = held[q] + jnp.where(which == float(q), one, 0.0)
    line = jnp.broadcast_to(line, (8, NB))
    for r in range(0, lines, 16):
        low = line == float(r) - CENTRE
        high = line == float(r + 8) - CENTRE
        for q in range(8):
            pair = [jnp.where(low, held[q], 0.0), jnp.where(high, held[q], 0.0)]
            lanes = slice(q * stride + at, q * stride + at + NB)
            h_ref[r : r + 16, lanes] = jnp.concatenate(pair, 0).astype(BF)
    return cell


def cover_chunk(table, row_cell, col_cell, h_ref, east_ref, points):
    chunk, cols = east_ref.shape[1:]
    stride = h_ref.shape[1] // 8
    together = 1 + (cols % (2 * NB) > 0)
    cell = jnp.broadcast_to(row_cell, (chunk, cols)) - col_cell
    for t in range(15):
        apart = cell + float(t - 7)
        east_ref[t] = jnp.exp2(apart * apart * SCALE)
    table = table.reshape(8 * chunk, table.shape[2])
    total = jnp.zeros((chunk, cols), F32)
    for first in range(0, 8, together):
        offsets = range(first, first + together)
        counts = [h_ref[:, (q + 1) * stride - cols : (q + 1) * stride] for q in offsets]
        counts = jnp.concatenate(counts, 1)
        part = jnp.dot(table, jnp.concatenate([counts, counts], 0), preferred_element_type=F32)
        for p in range(8):
            for i, q in enumerate(offsets):
                piece = part[p * chunk : (p + 1) * chunk, i * cols : (i + 1) * cols]
                total = total + piece * east_ref[p - q + 7]
    return total * (1.0 / (points * points))


def lead_cover_kernel(
    place_ref, t_ref, row_cell_ref, *refs, points
):
    blocks, refs = refs[:4], refs[4:]
    folded_ref, own_ref, h_ref, col_cell_ref, east_ref, far_ref, far_cell_ref, far_table_ref = refs
    rows, cols = own_ref.shape
    lines = h_ref.shape[0]
    cells = [column_counts(ref, h_ref, NB * i, cols) for i, ref in enumerate(blocks)]
    col_cell = jnp.concatenate(cells, 1)
    col_cell_ref[...] = col_cell

    east, north = unpack(blocks[1])
    far_ref[0] = (east - cells[1]).T
    far_ref[1] = north.T
    far_cell_ref[...] = cells[1].T
    first = pl.multiple_of(place_ref[1] * rows, rows)
    for r in range(0, rows, 16):
        here = pl.ds(first + r, 16)
        for p, (high, low) in enumerate(table_rows(far_ref[0, here], far_ref[1, here], lines)):
            far_table_ref[p, r : r + 16, :lines] = high
            far_table_ref[p, r : r + 16, lines:] = low

    mine = cover_chunk(t_ref[:, :rows], row_cell_ref[:rows], col_cell, h_ref, east_ref, points)
    row = lax.broadcasted_iota(jnp.int32, (rows, cols), 0)
    col = lax.broadcasted_iota(jnp.int32, (rows, cols), 1)
    mine = mine + jnp.where(col == first + row, 1.0, 0.0)
    own_ref[...] = mine
    far = cover_chunk(
        far_table_ref[...], far_cell_ref[pl.ds(first, rows)], col_cell, h_ref, east_ref, points
    )
    folded_ref[:, : 3 * NB] = mine[:, : 3 * NB]
    folded_ref[:, 3 * NB : 4 * NB] = far[:, 2 * NB : 3 * NB]
    own_last = makes_own(place_ref[0])
    folded_ref[:, 4 * NB :] = jnp.where(own_last, mine[:, 3 * NB :], far[:, 3 * NB :])


def later_cover_kernel(t_ref, row_cell_ref, h_ref, col_cell_ref, o_ref, east_ref, *, points, start):
    chunk, cols = east_ref.shape[1:]
    col_cell = col_cell_ref[:, col_cell_ref.shape[1] - cols :]

    def row_chunk(index, _):
        first = pl.multiple_of(index * chunk, chunk)
        here = pl.ds(pl.multiple_of(first + start, chunk), chunk)
        o_ref[pl.ds(first, chunk)] = cover_chunk(
            t_ref[:, here], row_cell_ref[here], col_cell, h_ref, east_ref, points
        )
        return 0

    lax.fori_loop(0, o_ref.shape[0] // chunk, row_chunk, 0)


def block_cover_kernel(t_ref, row_cell_ref, *refs, points, start):
    blocks, (o_ref, h_ref, col_cell_ref, east_ref) = blocks_in(refs[:-4]), refs[-4:]
    cells = [
        column_counts(ref, h_ref, NB * i, o_ref.shape[1]) for i, ref in enumerate(blocks)
    ]
    col_cell_ref[...] = jnp.concatenate(cells, 1)
    later_cover_kernel(
        t_ref, row_cell_ref, h_ref, col_cell_ref, o_ref, east_ref, points=points, start=start
    )


def inverse_factor(tiles):
    n = len(tiles)
    width = 8 * n
    lane = lax.broadcasted_iota(jnp.int32, (8, width), 1)
    sub = lax.broadcasted_iota(jnp.int32, (8, width), 0)
    tiles = list(tiles)
    out = []

    def spread(x):
        return jnp.broadcast_to(x, (8, width))

    def lanes(tile, v):
        return [spread(tile[:, 8 * v + q : 8 * v + q + 1]) for q in range(8)]

    following = lanes(tiles[0], 0)
    for v in range(n):
        near = min(n, v + NEAR)
        cols = {v: following}
        if v + 1 < n:
            cols[v] = cols[v] + lanes(tiles[v], v + 1)
            cols[v + 1] = lanes(tiles[v + 1], v) + lanes(tiles[v + 1], v + 1)
        for r in range(v + 2, near):
            cols[r] = lanes(tiles[r], v)
        here = (lane >= 8 * v) & (lane < 8 * v + 8)
        for r in range(v + 1, n):
            tiles[r] = jnp.where(here, 0.0, tiles[r])
        tiles[v] = jnp.where(here, jnp.where(lane == sub + 8 * v, 1.0, 0.0), tiles[v])
        pivots = jnp.ones((8, width), F32)
        for s in range(8):
            head = cols[v]
            pivot = spread(head[s][s : s + 1])
            inverse = 1.0 / pivot
            pivots = jnp.where(sub == s, pivot, pivots)
            row = spread(tiles[v][s : s + 1])
            heads = [spread(head[k][s : s + 1]) for k in range(s + 1, len(head))]
            for r in range(v, near):
                part = cols[r][s] * inverse
                if r == v:
                    part = jnp.where(sub > s, part, 0.0)
                tiles[r] = tiles[r] - part * row
                for k in range(s + 1, len(cols[r])):
                    cols[r][k] = cols[r][k] - part * heads[k - s - 1]
        if v + 1 < n:
            following = cols[v + 1][8:]
        rows = tiles[v] * lax.rsqrt(pivots)
        if near < n:
            high = rows.astype(BF).astype(F32)
            low = rows - high
            left = jnp.concatenate([high, high, low, low], 0).astype(BF)
            right = jnp.concatenate([high, low, high, low], 0).astype(BF)
            update = lax.dot_general(
                left, right, (((0,), (0,)), ((), ())), preferred_element_type=F32
            )
            for r in range(near, n):
                tiles[r] = tiles[r] - update[8 * r : 8 * r + 8]
        out.append(jnp.where(lane <= sub + 8 * v, rows, 0.0))
    return jnp.concatenate(out, 0)


def split(x):
    high = x.astype(BF)
    return high, (x - high.astype(F32)).astype(BF)


def dot3(ah, al, bh, bl):
    dot = functools.partial(lax.dot_general, dimension_numbers=NT, preferred_element_type=F32)
    return dot(ah, bh) + (dot(ah, bl) + dot(al, bh))


def factor_blocks(a_ref, lh_ref, ll_ref, wh_ref, wl_ref):
    n = a_ref.shape[0]
    blocks = n // NB

    def column(first):
        end = first + NB
        bh, bl = split(a_ref[end:, first:end])
        high, low = split(dot3(bh, bl, wh_ref[first:end], wl_ref[first:end]))
        lh_ref[end:, first:end] = high
        ll_ref[end:, first:end] = low
        a_ref[end:, end : end + NB] = a_ref[end:, end : end + NB] - dot3(
            lh_ref[end:, :end],
            ll_ref[end:, :end],
            lh_ref[end : end + NB, :end],
            ll_ref[end : end + NB, :end],
        )

    def step(j, _):
        c = pl.multiple_of(j * NB, NB)
        tiles = [a_ref[pl.ds(c + 8 * v, 8), pl.ds(c, NB)] for v in range(NB // 8)]
        wh, wl = split(inverse_factor(tiles))
        wh_ref[pl.ds(c, NB)] = wh
        wl_ref[pl.ds(c, NB)] = wl
        for block in range(blocks - 1):
            pl.when(j == block)(functools.partial(column, block * NB))
        return 0

    lax.fori_loop(0, blocks, step, 0)


def factor_kernel(diag_ref, lh_ref, ll_ref, wh_ref, wl_ref, a_ref):
    a_ref[...] = diag_ref[...]
    factor_blocks(a_ref, lh_ref, ll_ref, wh_ref, wl_ref)


def turned(r, k):
    at = ((r & 1) << 1 | (r >> 1) & 1) + k
    return (r & 4) | (at & 1) << 1 | (at >> 1) & 1


def block_order(r):
    own = [r, r ^ 4, turned(r, 1), turned(r, 2), turned(r, 3)]
    return own + [turned(r, 3) ^ 4, turned(r, 1) ^ 4, turned(r, 2) ^ 4]


def makes_own(r):
    return (r & 1) == 0


def folded_blocks(r):
    order = block_order(r)
    either = jnp.where(makes_own(r), r, r ^ 4)
    return [(r, r), (r, order[1]), (r, order[2]), (order[1], order[2]), (either, order[3])]


def blocks_in(refs):
    return [
        ref.at[first : first + ref.shape[0] // parts]
        for ref in refs
        for parts in [1 + (ref.shape[0] >= 2 * NB)]
        for first in range(0, ref.shape[0], ref.shape[0] // parts)
    ]


def unfold_kernel(place_ref, *refs):
    pieces_refs, (lh_ref, ll_ref, wh_ref, wl_ref, a_ref, g_ref) = refs[:8], refs[8:]
    row_pos = place_ref[0]
    panel_pos = place_ref[1]
    for i, ref in enumerate(pieces_refs):
        g_ref[4 * i : 4 * i + 4] = ref[...]

    def rows_of(r, _):
        away = r ^ row_pos
        slot = (away >> 1) | ((away & 1) << 2)
        ats = []
        for p in range(4):
            gone = p ^ panel_pos
            ats.append(slot | ((gone >> 1) << 3) | ((gone & 1) << 4))
        for k, (rows, cols) in enumerate(folded_blocks(r)):
            block = jnp.concatenate([g_ref[at, :, NB * k : NB * k + NB] for at in ats], 0)
            rr = pl.multiple_of(rows * NB, NB)
            cc = pl.multiple_of(cols * NB, NB)

            @pl.when(rows >= cols)
            def _():
                a_ref[pl.ds(rr, NB), pl.ds(cc, NB)] = block

            if k:

                @pl.when(rows < cols)
                def _():
                    a_ref[pl.ds(cc, NB), pl.ds(rr, NB)] = block.T

        return 0

    lax.fori_loop(0, 8, rows_of, 0)
    factor_blocks(a_ref, lh_ref, ll_ref, wh_ref, wl_ref)


def factor(kernel, operands, n):
    in_specs = [pl.BlockSpec(memory_space=pltpu.VMEM)] * len(operands)
    scratch = [pltpu.VMEM((n, n), F32)]
    if kernel is unfold_kernel:
        in_specs[0] = pl.BlockSpec(memory_space=pltpu.SMEM)
        scratch.append(pltpu.VMEM((32, *operands[1].shape[1:]), F32))
    return pl.pallas_call(
        kernel,
        out_shape=[jax.ShapeDtypeStruct((n, n), BF)] * 2 + [jax.ShapeDtypeStruct((n, NB), BF)] * 2,
        in_specs=in_specs,
        out_specs=[pl.BlockSpec(memory_space=pltpu.VMEM)] * 4,
        scratch_shapes=scratch,
        compiler_params=pltpu.CompilerParams(vmem_limit_bytes=32 << 20),
        cost_estimate=pl.CostEstimate(flops=5 * 10**10, bytes_accessed=8 << 20, transcendentals=0),
        name="factor",
    )(*operands)


def solve_kernel(place_ref, *refs, corners):
    cover_refs, parts_refs = refs[: len(corners)], refs[len(corners) : -7]
    lh_ref, ll_ref, wh_ref, wl_ref, o_ref, xh_ref, xl_ref = refs[-7:]
    n = o_ref.shape[1]

    def put(rows, cols, value):
        taken = parts_refs[0][parts_refs[0].shape[0] - 1, rows, cols]
        for part in parts_refs[1:]:
            taken = taken + part[part.shape[0] - 1, rows, cols]
        o_ref[rows, cols] = value - taken

    for (row, block), ref in zip(corners, cover_refs):
        rows = slice(row, row + ref.shape[0])
        if block is None:
            put(rows, slice(None), ref[...])
            continue
        for c, s in enumerate(block_order(place_ref[0])[block : block + ref.shape[1] // NB]):
            cols = pl.ds(pl.multiple_of(s * NB, NB), NB)
            put(rows, cols, ref[:, NB * c : NB * c + NB])
    for c in range(0, n, NB):
        here = o_ref[:, c : c + NB]
        if c:
            here = here - dot3(
                xh_ref[:, :c], xl_ref[:, :c], lh_ref[c : c + NB, :c], ll_ref[c : c + NB, :c]
            )
        bh, bl = split(here)
        x = dot3(bh, bl, wh_ref[c : c + NB], wl_ref[c : c + NB])
        o_ref[:, c : c + NB] = x
        xh, xl = split(x)
        xh_ref[:, c : c + NB] = xh
        xl_ref[:, c : c + NB] = xl


def solve(place, covers, corners, parts, factors):
    rows, n = parts[0].shape[1:]
    return vmem_call(
        functools.partial(solve_kernel, corners=corners),
        jax.ShapeDtypeStruct((rows, n), F32),
        place,
        [*covers, *parts, *factors],
        [pltpu.VMEM((rows, n), BF)] * 2,
        "solve",
    )


def vmem_call(kernel, out_shape, place, operands, scratch=(), name=None):
    return pl.pallas_call(
        kernel,
        out_shape=out_shape,
        in_specs=[pl.BlockSpec(memory_space=pltpu.SMEM)] * (place is not None)
        + [pl.BlockSpec(memory_space=pltpu.VMEM)] * len(operands),
        out_specs=jax.tree.map(lambda _: pl.BlockSpec(memory_space=pltpu.VMEM), out_shape),
        scratch_shapes=list(scratch),
        compiler_params=pltpu.CompilerParams(vmem_limit_bytes=32 << 20),
        cost_estimate=pl.CostEstimate(flops=10**8, bytes_accessed=1 << 18, transcendentals=0),
        name=name,
    )(*([] if place is None else [place]), *operands)


def fold_products_kernel(place_ref, *refs):
    blocks, shares, total_ref = refs[:4], refs[4:-1], refs[-1]
    own, far, one, two = [split(ref[:NB]) for ref in blocks]
    own_last = makes_own(place_ref[0])
    either = split(jnp.where(own_last, blocks[0][:NB], blocks[1][:NB]))
    pairs = [(own, own), (own, far), (own, one), (far, one), (either, two)]
    for k, (left, right) in enumerate(pairs):
        total_ref[:, NB * k : NB * k + NB] = dot3(*left, *right)
    rows = shares[0].shape[0]
    for m, ref in enumerate(shares):
        first = pl.multiple_of((place_ref[1] ^ m) * rows, rows)
        ref[...] = total_ref[pl.ds(first, rows)]


def gather_split_kernel(place_ref, *refs):
    blocks, (high_ref, low_ref) = blocks_in(refs[:-2]), refs[-2:]
    for s, ref in zip(block_order(place_ref[0]), blocks):
        first = pl.multiple_of(s * NB, NB)
        high, low = split(ref[:NB])
        high_ref[pl.ds(first, NB)] = high
        low_ref[pl.ds(first, NB)] = low


def rest_products_kernel(place_ref, prior_ref, high_ref, low_ref, *refs, turns):
    plus_refs, o_ref = refs[:-1], refs[-1]
    rows = o_ref.shape[1]
    for i, m in enumerate(turns):
        first = pl.multiple_of((place_ref[1] ^ m) * rows, rows)
        own_high, own_low = split(prior_ref[pl.ds(first, rows)])
        for c in range(0, o_ref.shape[2], 2 * NB):
            cols = slice(c, c + 2 * NB)
            total = dot3(own_high, own_low, high_ref[cols], low_ref[cols])
            for plus_ref in plus_refs:
                total = total + plus_ref[i, :, cols]
            o_ref[i, :, cols] = total


def swap(block, axis, bit):
    return lax.ppermute(block, axis, [(i, i ^ bit) for i in range(lax.axis_size(axis))])


def dot_rows(left, right):
    return lax.dot_general(
        left, right, NT, precision=lax.Precision.HIGH, preferred_element_type=F32
    )


def local(pixel_ids, quad_offsets, prior_factor):
    panel_count = lax.axis_size("panel")
    row_count = lax.axis_size("row")
    block_rows = pixel_ids.shape[0]
    quarter_rows = block_rows // panel_count
    per_device = B // (row_count * panel_count)
    span_cols = panel_count * per_device
    row_pos = lax.axis_index("row")
    panel_pos = lax.axis_index("panel")
    device_pos = row_pos * panel_count + panel_pos
    lead = 32

    points = jnp.stack(locate(pixel_ids, quad_offsets))
    count = points.shape[1]
    own_points = lax.dynamic_slice_in_dim(points, panel_pos * quarter_rows, quarter_rows, 2)
    local_points = points.reshape(2, count, panel_count, quarter_rows)[:, :, :, :per_device]
    local_points = local_points.reshape(2, count, span_cols)
    own_prior = prior_factor.reshape(panel_count, quarter_rows, -1)[:, :per_device]
    own_prior = own_prior.reshape(span_cols, -1)
    place = jnp.stack([row_pos, panel_pos]).astype(jnp.int32)
    lines = block_rows * row_count // 256 * 8
    folds = span_cols == NB and row_count == 8 and panel_count == 4 and lines == 256

    if not (folds and 2 * count * NB == 8 * own_prior.shape[1]):
        lead = 32
        row_ids = jnp.arange(lead, dtype=jnp.int32)[:, None]
        col_ids = jnp.arange(B, dtype=jnp.int32)[None, :]
        on_diagonal = (row_ids < per_device) & (col_ids == device_pos * per_device + row_ids)
        unit = jnp.where(on_diagonal, 1.0, 0.0).astype(F32)
        flat = local_points.reshape(1, 2 * count, span_cols)
        copies = jnp.broadcast_to(flat, (row_count, 2 * count, span_cols))
        spread = lax.all_to_all(copies, "row", split_axis=0, concat_axis=0, tiled=True)
        parted = features(own_points, spread.transpose(1, 0, 2).reshape(2, count, B))
        covers = [cover_rows(*parted, i, lead) for i in range(0, quarter_rows, lead)]
        covers[0] = covers[0] + unit
        panel_prior = lax.all_gather(own_prior, "row", axis=0, tiled=True)
        partial = dot_rows(prior_factor, panel_prior)
        parts = lax.all_to_all(
            partial.reshape(panel_count, quarter_rows, B), "panel", split_axis=0, concat_axis=0, tiled=True
        )
        parts = jnp.sum(parts, axis=0)
        mine = covers[0][:per_device] - parts[:per_device]
        diag_rows = lax.all_gather(mine, ("row", "panel"), axis=0, tiled=True)
        corners = [(i * lead, None) for i in range(len(covers))]
        return solve(place, covers, corners, [parts[None]], factor(factor_kernel, (diag_rows,), B))

    def turn(block, k):
        return lax.ppermute(block, "row", [(turned(d, k), d) for d in range(8)])

    own = pack(own_prior, local_points)
    two, one, far = turn(own, 2), turn(own, 1), swap(own, "row", 4)
    table = row_table(own_points, lines)

    def block_cover(held, blocks, start, cols):
        return vmem_call(
            functools.partial(block_cover_kernel, points=count, start=start),
            jax.ShapeDtypeStruct((quarter_rows - start, cols), F32),
            None,
            [*held, *blocks],
            [
                pltpu.VMEM((lines, 8 * cols), BF),
                pltpu.VMEM((1, cols), F32),
                pltpu.VMEM((15, per_device, cols), F32),
            ],
            "cover",
        )

    cover_own = block_cover(table, [own], per_device, NB)
    (far, one, two), table, cover_own = lax.optimization_barrier(((far, one, two), table, cover_own))
    shares = vmem_call(
        fold_products_kernel,
        [jax.ShapeDtypeStruct((per_device, 5 * NB), F32)] * 4,
        place,
        [own, far, one, two],
        [pltpu.VMEM((NB, 5 * NB), F32)],
        "fold_products",
    )
    shares, own, far = lax.optimization_barrier((shares, own, far))

    def beside(operands, transfer, work):
        operands, held = lax.optimization_barrier((operands, table))
        return lax.optimization_barrier((transfer(operands), work(operands, held)))

    half = 4 * NB
    east = pltpu.VMEM((15, per_device, half), F32)

    def lead_cover(_, held):
        return vmem_call(
            functools.partial(lead_cover_kernel, points=count),
            [
                jax.ShapeDtypeStruct((per_device, 5 * NB), F32),
                jax.ShapeDtypeStruct((per_device, half), F32),
                jax.ShapeDtypeStruct((lines, 8 * half), BF),
                jax.ShapeDtypeStruct((1, half), F32),
            ],
            place,
            [*held, own, far, one, two],
            [
                east,
                pltpu.VMEM((2, NB, count), F32),
                pltpu.VMEM((NB, 1), F32),
                pltpu.VMEM((8, per_device, 2 * lines), BF),
            ],
            "lead_cover",
        )

    sums, (folded, cover_lead, *counts) = beside(
        shares,
        lambda shares: [swap(share, "panel", m) for m, share in zip((1, 2, 3), shares[1:])],
        lead_cover,
    )
    rest = [turn(jnp.concatenate([own, far], 0), 3), turn(far, 1), turn(far, 2)]
    shard = folded - (shares[0] + sums[0] + sums[1] + sums[2])

    def rest_part(panel_prior, turns, plus=()):
        return vmem_call(
            functools.partial(rest_products_kernel, turns=turns),
            jax.ShapeDtypeStruct((len(turns), quarter_rows, B), F32),
            place,
            [prior_factor, *panel_prior, *plus],
            name="rest_products",
        )

    def later_cover(held, start, rows):
        return vmem_call(
            functools.partial(later_cover_kernel, points=count, start=start),
            jax.ShapeDtypeStruct((rows, half - NB), F32),
            None,
            [*held, *counts],
            [pltpu.VMEM((15, per_device, half - NB), F32)],
            "cover",
        )

    middle = quarter_rows // 2

    def beside_far_z(_, held):
        cover = later_cover(held, middle, quarter_rows - middle)
        cover, blocks = lax.optimization_barrier((cover, rest))
        panel_prior = vmem_call(
            gather_split_kernel,
            [jax.ShapeDtypeStruct((B, own_prior.shape[1]), BF)] * 2,
            place,
            [own, far, one, two, *blocks],
            name="gather_split",
        )
        return cover, panel_prior, rest_part(panel_prior, (3, 1))

    shard = shard[None]
    near_rows, cover_first = beside(
        shard,
        lambda x: swap(x, "row", 2),
        lambda _, held: later_cover(held, per_device, middle - per_device),
    )
    near_rows = jnp.concatenate([shard, near_rows], 0)
    far_rows, (cover_second, panel_prior, for_core) = beside(
        near_rows, lambda x: swap(x, "row", 4), beside_far_z
    )
    held_rows = jnp.concatenate([near_rows, far_rows], 0)

    def across(x):
        corner = [(i, i ^ 6) for i in range(32)]
        return swap(x, "row", 1), swap(x, "panel", 2), lax.ppermute(x, ("row", "panel"), corner)

    def beside_xy(x, held):
        from_core = swap(for_core, "panel", 1)
        cover = block_cover(held, rest, 0, half)
        part_0, part_2 = rest_part(panel_prior, (0,)), rest_part(panel_prior, (2,), [from_core])
        return cover, part_0, part_2, from_core, swap(x, "panel", 1)

    received, (cover_last, part_0, part_2, from_core, held_there) = beside(
        held_rows, across, beside_xy
    )
    there = [held_there] + [swap(x, "panel", 1) for x in received]
    parts = [part_0, from_core, swap(part_2, "panel", 2)]
    factors = factor(unfold_kernel, (place, held_rows, *received, *there), B)
    covers = [cover_lead, cover_own, cover_first, cover_second, cover_last]
    corners = [(0, 0), (per_device, 0), (per_device, 1), (middle, 1), (0, 4)]
    return solve(place, covers, corners, parts, factors)


def solution(mesh):
    return jax.shard_map(
        local,
        mesh=mesh,
        in_specs=(P("row"), P(None, None, "row"), P("row", "panel")),
        out_specs=P(("row", "panel"), None),
        check_vma=False,
    )
```

```python
import functools

import jax
import jax.numpy as jnp
from jax import lax
from jax.experimental import pallas as pl
from jax.experimental.pallas import tpu as pltpu
from jax.sharding import PartitionSpec as P

B = 1024
NB = 128
NEAR = 4
F32 = jnp.float32
BF = jnp.bfloat16
NT = (((1,), (1,)), ((), ()))
SCALE = -1.4426950408889634 / 64.0
CENTRE = 1024.0


def locate(pixel_ids, quad_offsets):
    column = (pixel_ids % 256) * 8
    lines = (pixel_ids // 256) * 8
    east = (column[None, :] + quad_offsets[0]).astype(F32) - CENTRE
    north = (lines[None, :] + quad_offsets[1]).astype(F32) - CENTRE
    return east, north


def pieces(value):
    high = jnp.floor(value * (1.0 / 65536.0)) * 65536.0
    rest = value - high
    mid = jnp.floor(rest * (1.0 / 256.0)) * 256.0
    return [high, mid, rest - mid]


def halves(value):
    high = jnp.floor(value * (1.0 / 128.0)) * 128.0
    return high, value - high


def row_features(x, y):
    xh, xl = halves(x)
    yh, yl = halves(y)
    one = jnp.ones_like(x)
    zero = jnp.zeros_like(x)
    cross = [-2 * xh, -2 * xh, -2 * xl, -2 * xl, -2 * yh, -2 * yh, -2 * yl, -2 * yl]
    return jnp.concatenate(cross + pieces(x * x + y * y) + [one] * 3 + [zero] * 2, 0)


def col_features(x, y):
    xh, xl = halves(x)
    yh, yl = halves(y)
    one = jnp.ones_like(x)
    zero = jnp.zeros_like(x)
    cross = [xh, xl, xh, xl, yh, yl, yh, yl]
    return jnp.concatenate(cross + [one] * 3 + pieces(x * x + y * y) + [zero] * 2, 0)


def feature_kernel(row_ref, col_ref, f_ref, g_ref):
    for a in range(row_ref.shape[1]):
        one = row_features(row_ref[0, a : a + 1, :], row_ref[1, a : a + 1, :])
        f_ref[a] = one.T.astype(BF)
        g_ref[a] = col_features(col_ref[0, a : a + 1, :], col_ref[1, a : a + 1, :]).astype(BF)


def features(row_points, col_points):
    count, rows = row_points.shape[1:]
    cols = col_points.shape[2]
    return pl.pallas_call(
        feature_kernel,
        out_shape=[
            jax.ShapeDtypeStruct((count, rows, 16), BF),
            jax.ShapeDtypeStruct((count, 16, cols), BF),
        ],
        in_specs=[pl.BlockSpec(memory_space=pltpu.VMEM)] * 2,
        out_specs=[pl.BlockSpec(memory_space=pltpu.VMEM)] * 2,
        compiler_params=pltpu.CompilerParams(vmem_limit_bytes=8 << 20),
        name="features",
    )(row_points, col_points)


def cover_kernel(f_ref, g_ref, o_ref):
    count, block = f_ref.shape[:2]
    rows_here = f_ref[...].reshape(count * block, 16)

    def column_point(b, total):
        apart = jnp.dot(rows_here, g_ref[b], preferred_element_type=F32)
        near = jnp.exp2(apart * SCALE)
        for a in range(count):
            total = total + near[a * block : (a + 1) * block]
        return total

    total = lax.fori_loop(0, count, column_point, jnp.zeros(o_ref.shape, F32), unroll=8)
    o_ref[...] = total * (1.0 / (count * count))


def cover_rows(row_part, col_part, first, block):
    count, rows, depth = row_part.shape
    cols = col_part.shape[2]
    index = first // block
    return pl.pallas_call(
        cover_kernel,
        grid=(1,),
        out_shape=jax.ShapeDtypeStruct((block, cols), F32),
        in_specs=[
            pl.BlockSpec((count, block, depth), lambda i: (0, index, 0)),
            pl.BlockSpec((count, depth, cols), lambda i: (0, 0, 0)),
        ],
        out_specs=pl.BlockSpec((block, cols), lambda i: (0, 0)),
        compiler_params=pltpu.CompilerParams(vmem_limit_bytes=16 << 20),
        cost_estimate=pl.CostEstimate(flops=10**8, bytes_accessed=1 << 18, transcendentals=0),
        name="cover",
    )(row_part, col_part)


def table_rows(offset, north, lines):
    line = lax.broadcasted_iota(jnp.int32, (16, lines), 1).astype(F32) - CENTRE
    total = [jnp.zeros((16, lines), F32) for _ in range(8)]
    for a in range(offset.shape[1]):
        apart = jnp.broadcast_to(north[:, a : a + 1], (16, lines)) - line
        near = jnp.exp2(apart * apart * SCALE)
        which = jnp.broadcast_to(offset[:, a : a + 1], (16, lines))
        for p in range(8):
            total[p] = total[p] + jnp.where(which == float(p), near, 0.0)
    return [split(x) for x in total]


def row_table_kernel(row_ref, t_ref, row_cell_ref, place_ref):
    rows = row_ref.shape[2]
    lines = t_ref.shape[2] // 2
    row_cell = jnp.floor(row_ref[0] * 0.125) * 8.0
    place_ref[0] = (row_ref[0] - row_cell).T
    place_ref[1] = row_ref[1].T
    row_cell_ref[...] = row_cell[0:1].T

    def row_tile(index, _):
        here = pl.ds(pl.multiple_of(index * 16, 16), 16)
        for p, (high, low) in enumerate(table_rows(place_ref[0, here], place_ref[1, here], lines)):
            t_ref[p, here, :lines] = high
            t_ref[p, here, lines:] = low
        return 0

    lax.fori_loop(0, rows // 16, row_tile, 0)


def row_table(row_points, lines):
    count, rows = row_points.shape[1:]
    return pl.pallas_call(
        row_table_kernel,
        out_shape=[
            jax.ShapeDtypeStruct((8, rows, 2 * lines), BF),
            jax.ShapeDtypeStruct((rows, 1), F32),
        ],
        in_specs=[pl.BlockSpec(memory_space=pltpu.VMEM)],
        out_specs=[pl.BlockSpec(memory_space=pltpu.VMEM)] * 2,
        scratch_shapes=[pltpu.VMEM((2, rows, count), F32)],
        compiler_params=pltpu.CompilerParams(vmem_limit_bytes=16 << 20),
        cost_estimate=pl.CostEstimate(flops=10**8, bytes_accessed=1 << 18, transcendentals=0),
        name="row_table",
    )(row_points)


def pack(prior, points):
    flat = points.reshape(-1, NB)
    tiles = prior.shape[1] // NB
    extra = flat.reshape(tiles, flat.shape[0] // tiles, NB).transpose(1, 0, 2)
    return jnp.concatenate([prior, extra.reshape(-1, prior.shape[1])], 0)


def unpack(block_ref):
    extra = block_ref.shape[0] - NB
    tiles = block_ref.shape[1] // NB
    flat = jnp.concatenate(
        [block_ref[NB : NB + extra, NB * t : NB * t + NB] for t in range(tiles)], 0
    )
    count = flat.shape[0] // 2
    return flat[:count], flat[count:]


def column_counts(block_ref, h_ref, at, stride):
    east, north = unpack(block_ref)
    lines = h_ref.shape[0]
    cell = jnp.floor(east[0:1] * 0.125) * 8.0
    line = jnp.floor(north[0:1] * 0.125) * 8.0
    east, north = east - cell, north - line
    sub = lax.broadcasted_iota(jnp.int32, (8, NB), 0).astype(F32)
    held = [jnp.zeros((8, NB), F32) for _ in range(8)]
    for b in range(east.shape[0]):
        one = jnp.where(sub == jnp.broadcast_to(north[b : b + 1], (8, NB)), 1.0, 0.0)
        which = jnp.broadcast_to(east[b : b + 1], (8, NB))
        for q in range(8):
            held[q] = held[q] + jnp.where(which == float(q), one, 0.0)
    line = jnp.broadcast_to(line, (8, NB))
    for r in range(0, lines, 16):
        low = line == float(r) - CENTRE
        high = line == float(r + 8) - CENTRE
        for q in range(8):
            pair = [jnp.where(low, held[q], 0.0), jnp.where(high, held[q], 0.0)]
            lanes = slice(q * stride + at, q * stride + at + NB)
            h_ref[r : r + 16, lanes] = jnp.concatenate(pair, 0).astype(BF)
    return cell


def cover_chunk(table, row_cell, col_cell, h_ref, east_ref, points):
    chunk, cols = east_ref.shape[1:]
    stride = h_ref.shape[1] // 8
    together = 1 + (cols % (2 * NB) > 0)
    cell = jnp.broadcast_to(row_cell, (chunk, cols)) - col_cell
    for t in range(15):
        apart = cell + float(t - 7)
        east_ref[t] = jnp.exp2(apart * apart * SCALE)
    table = table.reshape(8 * chunk, table.shape[2])
    total = jnp.zeros((chunk, cols), F32)
    for first in range(0, 8, together):
        offsets = range(first, first + together)
        counts = [h_ref[:, (q + 1) * stride - cols : (q + 1) * stride] for q in offsets]
        counts = jnp.concatenate(counts, 1)
        part = jnp.dot(table, jnp.concatenate([counts, counts], 0), preferred_element_type=F32)
        for p in range(8):
            for i, q in enumerate(offsets):
                piece = part[p * chunk : (p + 1) * chunk, i * cols : (i + 1) * cols]
                total = total + piece * east_ref[p - q + 7]
    return total * (1.0 / (points * points))


def lead_cover_kernel(
    place_ref, t_ref, row_cell_ref, *refs, points
):
    blocks, refs = refs[:4], refs[4:]
    folded_ref, own_ref, h_ref, col_cell_ref, east_ref, far_ref, far_cell_ref, far_table_ref = refs
    rows, cols = own_ref.shape
    lines = h_ref.shape[0]
    cells = [column_counts(ref, h_ref, NB * i, cols) for i, ref in enumerate(blocks)]
    col_cell = jnp.concatenate(cells, 1)
    col_cell_ref[...] = col_cell

    east, north = unpack(blocks[1])
    far_ref[0] = (east - cells[1]).T
    far_ref[1] = north.T
    far_cell_ref[...] = cells[1].T
    first = pl.multiple_of(place_ref[1] * rows, rows)
    for r in range(0, rows, 16):
        here = pl.ds(first + r, 16)
        for p, (high, low) in enumerate(table_rows(far_ref[0, here], far_ref[1, here], lines)):
            far_table_ref[p, r : r + 16, :lines] = high
            far_table_ref[p, r : r + 16, lines:] = low

    mine = cover_chunk(t_ref[:, :rows], row_cell_ref[:rows], col_cell, h_ref, east_ref, points)
    row = lax.broadcasted_iota(jnp.int32, (rows, cols), 0)
    col = lax.broadcasted_iota(jnp.int32, (rows, cols), 1)
    mine = mine + jnp.where(col == first + row, 1.0, 0.0)
    own_ref[...] = mine
    far = cover_chunk(
        far_table_ref[...], far_cell_ref[pl.ds(first, rows)], col_cell, h_ref, east_ref, points
    )
    folded_ref[:, : 3 * NB] = mine[:, : 3 * NB]
    folded_ref[:, 3 * NB : 4 * NB] = far[:, 2 * NB : 3 * NB]
    own_last = makes_own(place_ref[0])
    folded_ref[:, 4 * NB :] = jnp.where(own_last, mine[:, 3 * NB :], far[:, 3 * NB :])


def later_cover_kernel(t_ref, row_cell_ref, h_ref, col_cell_ref, o_ref, east_ref, *, points, start):
    chunk, cols = east_ref.shape[1:]
    col_cell = col_cell_ref[:, col_cell_ref.shape[1] - cols :]

    def row_chunk(index, _):
        first = pl.multiple_of(index * chunk, chunk)
        here = pl.ds(pl.multiple_of(first + start, chunk), chunk)
        o_ref[pl.ds(first, chunk)] = cover_chunk(
            t_ref[:, here], row_cell_ref[here], col_cell, h_ref, east_ref, points
        )
        return 0

    lax.fori_loop(0, o_ref.shape[0] // chunk, row_chunk, 0)


def block_cover_kernel(t_ref, row_cell_ref, *refs, points, start):
    blocks, (o_ref, h_ref, col_cell_ref, east_ref) = blocks_in(refs[:-4]), refs[-4:]
    cells = [
        column_counts(ref, h_ref, NB * i, o_ref.shape[1]) for i, ref in enumerate(blocks)
    ]
    col_cell_ref[...] = jnp.concatenate(cells, 1)
    later_cover_kernel(
        t_ref, row_cell_ref, h_ref, col_cell_ref, o_ref, east_ref, points=points, start=start
    )


def inverse_factor(tiles):
    n = len(tiles)
    width = 8 * n
    lane = lax.broadcasted_iota(jnp.int32, (8, width), 1)
    sub = lax.broadcasted_iota(jnp.int32, (8, width), 0)
    tiles = list(tiles)
    out = []

    def spread(x):
        return jnp.broadcast_to(x, (8, width))

    def lanes(tile, v):
        return [spread(tile[:, 8 * v + q : 8 * v + q + 1]) for q in range(8)]

    following = lanes(tiles[0], 0)
    for v in range(n):
        near = min(n, v + NEAR)
        cols = {v: following}
        if v + 1 < n:
            cols[v] = cols[v] + lanes(tiles[v], v + 1)
            cols[v + 1] = lanes(tiles[v + 1], v) + lanes(tiles[v + 1], v + 1)
        for r in range(v + 2, near):
            cols[r] = lanes(tiles[r], v)
        here = (lane >= 8 * v) & (lane < 8 * v + 8)
        for r in range(v + 1, n):
            tiles[r] = jnp.where(here, 0.0, tiles[r])
        tiles[v] = jnp.where(here, jnp.where(lane == sub + 8 * v, 1.0, 0.0), tiles[v])
        pivots = jnp.ones((8, width), F32)
        for s in range(8):
            head = cols[v]
            pivot = spread(head[s][s : s + 1])
            inverse = 1.0 / pivot
            pivots = jnp.where(sub == s, pivot, pivots)
            row = spread(tiles[v][s : s + 1])
            heads = [spread(head[k][s : s + 1]) for k in range(s + 1, len(head))]
            for r in range(v, near):
                part = cols[r][s] * inverse
                if r == v:
                    part = jnp.where(sub > s, part, 0.0)
                tiles[r] = tiles[r] - part * row
                for k in range(s + 1, len(cols[r])):
                    cols[r][k] = cols[r][k] - part * heads[k - s - 1]
        if v + 1 < n:
            following = cols[v + 1][8:]
        rows = tiles[v] * lax.rsqrt(pivots)
        if near < n:
            high = rows.astype(BF).astype(F32)
            low = rows - high
            left = jnp.concatenate([high, high, low, low], 0).astype(BF)
            right = jnp.concatenate([high, low, high, low], 0).astype(BF)
            update = lax.dot_general(
                left, right, (((0,), (0,)), ((), ())), preferred_element_type=F32
            )
            for r in range(near, n):
                tiles[r] = tiles[r] - update[8 * r : 8 * r + 8]
        out.append(jnp.where(lane <= sub + 8 * v, rows, 0.0))
    return jnp.concatenate(out, 0)


def split(x):
    high = x.astype(BF)
    return high, (x - high.astype(F32)).astype(BF)


def dot3(ah, al, bh, bl):
    dot = functools.partial(lax.dot_general, dimension_numbers=NT, preferred_element_type=F32)
    return dot(ah, bh) + (dot(ah, bl) + dot(al, bh))


def factor_blocks(a_ref, lh_ref, ll_ref, wh_ref, wl_ref):
    n = a_ref.shape[0]
    blocks = n // NB

    def column(first):
        end = first + NB
        bh, bl = split(a_ref[end:, first:end])
        high, low = split(dot3(bh, bl, wh_ref[first:end], wl_ref[first:end]))
        lh_ref[end:, first:end] = high
        ll_ref[end:, first:end] = low
        a_ref[end:, end : end + NB] = a_ref[end:, end : end + NB] - dot3(
            lh_ref[end:, :end],
            ll_ref[end:, :end],
            lh_ref[end : end + NB, :end],
            ll_ref[end : end + NB, :end],
        )

    def step(j, _):
        c = pl.multiple_of(j * NB, NB)
        tiles = [a_ref[pl.ds(c + 8 * v, 8), pl.ds(c, NB)] for v in range(NB // 8)]
        wh, wl = split(inverse_factor(tiles))
        wh_ref[pl.ds(c, NB)] = wh
        wl_ref[pl.ds(c, NB)] = wl
        for block in range(blocks - 1):
            pl.when(j == block)(functools.partial(column, block * NB))
        return 0

    lax.fori_loop(0, blocks, step, 0)


def factor_kernel(diag_ref, lh_ref, ll_ref, wh_ref, wl_ref, a_ref):
    a_ref[...] = diag_ref[...]
    factor_blocks(a_ref, lh_ref, ll_ref, wh_ref, wl_ref)


def turned(r, k):
    at = ((r & 1) << 1 | (r >> 1) & 1) + k
    return (r & 4) | (at & 1) << 1 | (at >> 1) & 1


def block_order(r):
    return [r, r ^ 4, turned(r, 1), turned(r, 2), turned(r, 3), r ^ 5, r ^ 6, r ^ 7]


def makes_own(r):
    return (r & 1) == 0


def folded_blocks(r):
    order = block_order(r)
    either = jnp.where(makes_own(r), r, r ^ 4)
    return [(r, r), (r, order[1]), (r, order[2]), (order[1], order[2]), (either, order[3])]


def blocks_in(refs):
    return [
        ref.at[first : first + ref.shape[0] // parts]
        for ref in refs
        for parts in [1 + (ref.shape[0] >= 2 * NB)]
        for first in range(0, ref.shape[0], ref.shape[0] // parts)
    ]


def unfold_kernel(place_ref, *refs):
    pieces_refs, (lh_ref, ll_ref, wh_ref, wl_ref, a_ref, g_ref) = refs[:8], refs[8:]
    row_pos = place_ref[0]
    panel_pos = place_ref[1]
    for i, ref in enumerate(pieces_refs):
        g_ref[4 * i : 4 * i + 4] = ref[...]

    def rows_of(r, _):
        away = r ^ row_pos
        slot = (away >> 1) | ((away & 1) << 2)
        ats = []
        for p in range(4):
            gone = p ^ panel_pos
            ats.append(slot | ((gone >> 1) << 3) | ((gone & 1) << 4))
        for k, (rows, cols) in enumerate(folded_blocks(r)):
            block = jnp.concatenate([g_ref[at, :, NB * k : NB * k + NB] for at in ats], 0)
            rr = pl.multiple_of(rows * NB, NB)
            cc = pl.multiple_of(cols * NB, NB)

            @pl.when(rows >= cols)
            def _():
                a_ref[pl.ds(rr, NB), pl.ds(cc, NB)] = block

            if k:

                @pl.when(rows < cols)
                def _():
                    a_ref[pl.ds(cc, NB), pl.ds(rr, NB)] = block.T

        return 0

    lax.fori_loop(0, 8, rows_of, 0)
    factor_blocks(a_ref, lh_ref, ll_ref, wh_ref, wl_ref)


def factor(kernel, operands, n):
    in_specs = [pl.BlockSpec(memory_space=pltpu.VMEM)] * len(operands)
    scratch = [pltpu.VMEM((n, n), F32)]
    if kernel is unfold_kernel:
        in_specs[0] = pl.BlockSpec(memory_space=pltpu.SMEM)
        scratch.append(pltpu.VMEM((32, *operands[1].shape[1:]), F32))
    return pl.pallas_call(
        kernel,
        out_shape=[jax.ShapeDtypeStruct((n, n), BF)] * 2 + [jax.ShapeDtypeStruct((n, NB), BF)] * 2,
        in_specs=in_specs,
        out_specs=[pl.BlockSpec(memory_space=pltpu.VMEM)] * 4,
        scratch_shapes=scratch,
        compiler_params=pltpu.CompilerParams(vmem_limit_bytes=32 << 20),
        cost_estimate=pl.CostEstimate(flops=5 * 10**10, bytes_accessed=8 << 20, transcendentals=0),
        name="factor",
    )(*operands)


def solve_kernel(place_ref, *refs, corners):
    cover_refs, parts_refs = refs[: len(corners)], refs[len(corners) : -7]
    lh_ref, ll_ref, wh_ref, wl_ref, o_ref, xh_ref, xl_ref = refs[-7:]
    n = o_ref.shape[1]

    def put(rows, cols, value):
        taken = parts_refs[0][parts_refs[0].shape[0] - 1, rows, cols]
        for part in parts_refs[1:]:
            taken = taken + part[part.shape[0] - 1, rows, cols]
        o_ref[rows, cols] = value - taken

    for (row, block), ref in zip(corners, cover_refs):
        rows = slice(row, row + ref.shape[0])
        if block is None:
            put(rows, slice(None), ref[...])
            continue
        for c, s in enumerate(block_order(place_ref[0])[block : block + ref.shape[1] // NB]):
            cols = pl.ds(pl.multiple_of(s * NB, NB), NB)
            put(rows, cols, ref[:, NB * c : NB * c + NB])
    for c in range(0, n, NB):
        here = o_ref[:, c : c + NB]
        if c:
            here = here - dot3(
                xh_ref[:, :c], xl_ref[:, :c], lh_ref[c : c + NB, :c], ll_ref[c : c + NB, :c]
            )
        bh, bl = split(here)
        x = dot3(bh, bl, wh_ref[c : c + NB], wl_ref[c : c + NB])
        o_ref[:, c : c + NB] = x
        xh, xl = split(x)
        xh_ref[:, c : c + NB] = xh
        xl_ref[:, c : c + NB] = xl


def solve(place, covers, corners, parts, factors):
    rows, n = parts[0].shape[1:]
    return vmem_call(
        functools.partial(solve_kernel, corners=corners),
        jax.ShapeDtypeStruct((rows, n), F32),
        place,
        [*covers, *parts, *factors],
        [pltpu.VMEM((rows, n), BF)] * 2,
        "solve",
    )


def vmem_call(kernel, out_shape, place, operands, scratch=(), name=None):
    return pl.pallas_call(
        kernel,
        out_shape=out_shape,
        in_specs=[pl.BlockSpec(memory_space=pltpu.SMEM)] * (place is not None)
        + [pl.BlockSpec(memory_space=pltpu.VMEM)] * len(operands),
        out_specs=jax.tree.map(lambda _: pl.BlockSpec(memory_space=pltpu.VMEM), out_shape),
        scratch_shapes=list(scratch),
        compiler_params=pltpu.CompilerParams(vmem_limit_bytes=32 << 20),
        cost_estimate=pl.CostEstimate(flops=10**8, bytes_accessed=1 << 18, transcendentals=0),
        name=name,
    )(*([] if place is None else [place]), *operands)


def fold_products_kernel(place_ref, *refs):
    blocks, shares, total_ref = refs[:4], refs[4:-1], refs[-1]
    own, far, one, two = [split(ref[:NB]) for ref in blocks]
    own_last = makes_own(place_ref[0])
    either = split(jnp.where(own_last, blocks[0][:NB], blocks[1][:NB]))
    pairs = [(own, own), (own, far), (own, one), (far, one), (either, two)]
    for k, (left, right) in enumerate(pairs):
        total_ref[:, NB * k : NB * k + NB] = dot3(*left, *right)
    rows = shares[0].shape[0]
    for m, ref in enumerate(shares):
        first = pl.multiple_of((place_ref[1] ^ m) * rows, rows)
        ref[...] = total_ref[pl.ds(first, rows)]


def gather_split_kernel(place_ref, *refs):
    blocks, (high_ref, low_ref) = blocks_in(refs[:-2]), refs[-2:]
    for s, ref in zip(block_order(place_ref[0]), blocks):
        first = pl.multiple_of(s * NB, NB)
        high, low = split(ref[:NB])
        high_ref[pl.ds(first, NB)] = high
        low_ref[pl.ds(first, NB)] = low


def rest_products_kernel(place_ref, prior_ref, high_ref, low_ref, *refs, turns):
    plus_refs, o_ref = refs[:-1], refs[-1]
    rows = o_ref.shape[1]
    for i, m in enumerate(turns):
        first = pl.multiple_of((place_ref[1] ^ m) * rows, rows)
        own_high, own_low = split(prior_ref[pl.ds(first, rows)])
        for c in range(0, o_ref.shape[2], 2 * NB):
            cols = slice(c, c + 2 * NB)
            total = dot3(own_high, own_low, high_ref[cols], low_ref[cols])
            for plus_ref in plus_refs:
                total = total + plus_ref[i, :, cols]
            o_ref[i, :, cols] = total


def swap(block, axis, bit):
    return lax.ppermute(block, axis, [(i, i ^ bit) for i in range(lax.axis_size(axis))])


def dot_rows(left, right):
    return lax.dot_general(
        left, right, NT, precision=lax.Precision.HIGH, preferred_element_type=F32
    )


def local(pixel_ids, quad_offsets, prior_factor):
    panel_count = lax.axis_size("panel")
    row_count = lax.axis_size("row")
    block_rows = pixel_ids.shape[0]
    quarter_rows = block_rows // panel_count
    per_device = B // (row_count * panel_count)
    span_cols = panel_count * per_device
    row_pos = lax.axis_index("row")
    panel_pos = lax.axis_index("panel")
    device_pos = row_pos * panel_count + panel_pos
    lead = 32

    points = jnp.stack(locate(pixel_ids, quad_offsets))
    count = points.shape[1]
    own_points = lax.dynamic_slice_in_dim(points, panel_pos * quarter_rows, quarter_rows, 2)
    local_points = points.reshape(2, count, panel_count, quarter_rows)[:, :, :, :per_device]
    local_points = local_points.reshape(2, count, span_cols)
    own_prior = prior_factor.reshape(panel_count, quarter_rows, -1)[:, :per_device]
    own_prior = own_prior.reshape(span_cols, -1)
    place = jnp.stack([row_pos, panel_pos]).astype(jnp.int32)
    lines = block_rows * row_count // 256 * 8
    folds = span_cols == NB and row_count == 8 and panel_count == 4 and lines == 256

    if not (folds and 2 * count * NB == 8 * own_prior.shape[1]):
        lead = 32
        row_ids = jnp.arange(lead, dtype=jnp.int32)[:, None]
        col_ids = jnp.arange(B, dtype=jnp.int32)[None, :]
        on_diagonal = (row_ids < per_device) & (col_ids == device_pos * per_device + row_ids)
        unit = jnp.where(on_diagonal, 1.0, 0.0).astype(F32)
        flat = local_points.reshape(1, 2 * count, span_cols)
        copies = jnp.broadcast_to(flat, (row_count, 2 * count, span_cols))
        spread = lax.all_to_all(copies, "row", split_axis=0, concat_axis=0, tiled=True)
        parted = features(own_points, spread.transpose(1, 0, 2).reshape(2, count, B))
        covers = [cover_rows(*parted, i, lead) for i in range(0, quarter_rows, lead)]
        covers[0] = covers[0] + unit
        panel_prior = lax.all_gather(own_prior, "row", axis=0, tiled=True)
        partial = dot_rows(prior_factor, panel_prior)
        parts = lax.all_to_all(
            partial.reshape(panel_count, quarter_rows, B), "panel", split_axis=0, concat_axis=0, tiled=True
        )
        parts = jnp.sum(parts, axis=0)
        mine = covers[0][:per_device] - parts[:per_device]
        diag_rows = lax.all_gather(mine, ("row", "panel"), axis=0, tiled=True)
        corners = [(i * lead, None) for i in range(len(covers))]
        return solve(place, covers, corners, [parts[None]], factor(factor_kernel, (diag_rows,), B))

    def turn(block, k):
        return lax.ppermute(block, "row", [(turned(d, k), d) for d in range(8)])

    own = pack(own_prior, local_points)
    two, one, far = turn(own, 2), turn(own, 1), swap(own, "row", 4)
    table = row_table(own_points, lines)

    def block_cover(held, blocks, start, cols):
        return vmem_call(
            functools.partial(block_cover_kernel, points=count, start=start),
            jax.ShapeDtypeStruct((quarter_rows - start, cols), F32),
            None,
            [*held, *blocks],
            [
                pltpu.VMEM((lines, 8 * cols), BF),
                pltpu.VMEM((1, cols), F32),
                pltpu.VMEM((15, per_device, cols), F32),
            ],
            "cover",
        )

    cover_own = block_cover(table, [own], per_device, NB)
    (far, one, two), table, cover_own = lax.optimization_barrier(((far, one, two), table, cover_own))
    shares = vmem_call(
        fold_products_kernel,
        [jax.ShapeDtypeStruct((per_device, 5 * NB), F32)] * 4,
        place,
        [own, far, one, two],
        [pltpu.VMEM((NB, 5 * NB), F32)],
        "fold_products",
    )
    shares, own, far, one = lax.optimization_barrier((shares, own, far, one))

    def beside(operands, transfer, work):
        operands, held = lax.optimization_barrier((operands, table))
        return lax.optimization_barrier((transfer(operands), work(operands, held)))

    half = 4 * NB
    east = pltpu.VMEM((15, per_device, half), F32)

    def lead_cover(_, held):
        return vmem_call(
            functools.partial(lead_cover_kernel, points=count),
            [
                jax.ShapeDtypeStruct((per_device, 5 * NB), F32),
                jax.ShapeDtypeStruct((per_device, half), F32),
                jax.ShapeDtypeStruct((lines, 8 * half), BF),
                jax.ShapeDtypeStruct((1, half), F32),
            ],
            place,
            [*held, own, far, one, two],
            [
                east,
                pltpu.VMEM((2, NB, count), F32),
                pltpu.VMEM((NB, 1), F32),
                pltpu.VMEM((8, per_device, 2 * lines), BF),
            ],
            "lead_cover",
        )

    sums, (folded, cover_lead, *counts) = beside(
        shares,
        lambda shares: [swap(share, "panel", m) for m, share in zip((1, 2, 3), shares[1:])],
        lead_cover,
    )
    from_x = swap(jnp.concatenate([one, far], 0), "row", 1)
    from_z = swap(far, "row", 2)
    shard = folded - (shares[0] + sums[0] + sums[1] + sums[2])

    def rest_part(panel_prior, turns, plus=()):
        return vmem_call(
            functools.partial(rest_products_kernel, turns=turns),
            jax.ShapeDtypeStruct((len(turns), quarter_rows, B), F32),
            place,
            [prior_factor, *panel_prior, *plus],
            name="rest_products",
        )

    def later_cover(held, start, rows):
        return vmem_call(
            functools.partial(later_cover_kernel, points=count, start=start),
            jax.ShapeDtypeStruct((rows, half - NB), F32),
            None,
            [*held, *counts],
            [pltpu.VMEM((15, per_device, half - NB), F32)],
            "cover",
        )

    middle = quarter_rows // 2

    def beside_far_z(x, held):
        x, blocks = lax.optimization_barrier((x, [from_x, from_z]))
        rest = blocks + [swap(blocks[0][blocks[0].shape[0] // 2 :], "row", 2)]
        cover = later_cover(held, middle, quarter_rows - middle)
        cover, blocks = lax.optimization_barrier((cover, rest))
        panel_prior = vmem_call(
            gather_split_kernel,
            [jax.ShapeDtypeStruct((B, own_prior.shape[1]), BF)] * 2,
            place,
            [own, far, one, two, *blocks],
            name="gather_split",
        )
        return cover, panel_prior, rest_part(panel_prior, (3, 1)), rest

    shard = shard[None]
    near_rows, cover_first = beside(
        shard,
        lambda x: swap(x, "row", 2),
        lambda _, held: later_cover(held, per_device, middle - per_device),
    )
    near_rows = jnp.concatenate([shard, near_rows], 0)
    far_rows, (cover_second, panel_prior, for_core, rest) = beside(
        near_rows, lambda x: swap(x, "row", 4), beside_far_z
    )
    held_rows = jnp.concatenate([near_rows, far_rows], 0)

    def across(x):
        corner = [(i, i ^ 6) for i in range(32)]
        return swap(x, "row", 1), swap(x, "panel", 2), lax.ppermute(x, ("row", "panel"), corner)

    def beside_xy(x, held):
        from_core = swap(for_core, "panel", 1)
        cover = block_cover(held, rest, 0, half)
        part_0, part_2 = rest_part(panel_prior, (0,)), rest_part(panel_prior, (2,), [from_core])
        return cover, part_0, part_2, from_core, swap(x, "panel", 1)

    received, (cover_last, part_0, part_2, from_core, held_there) = beside(
        held_rows, across, beside_xy
    )
    there = [held_there] + [swap(x, "panel", 1) for x in received]
    parts = [part_0, from_core, swap(part_2, "panel", 2)]
    factors = factor(unfold_kernel, (place, held_rows, *received, *there), B)
    covers = [cover_lead, cover_own, cover_first, cover_second, cover_last]
    corners = [(0, 0), (per_device, 0), (per_device, 1), (middle, 1), (0, 4)]
    return solve(place, covers, corners, parts, factors)


def solution(mesh):
    return jax.shard_map(
        local,
        mesh=mesh,
        in_specs=(P("row"), P(None, None, "row"), P("row", "panel")),
        out_specs=P(("row", "panel"), None),
        check_vma=False,
    )
```

```python
import functools

import jax
import jax.numpy as jnp
from jax import lax
from jax.experimental import pallas as pl
from jax.experimental.pallas import tpu as pltpu
from jax.sharding import PartitionSpec as P

B = 1024
NB = 128
NEAR = 4
F32 = jnp.float32
BF = jnp.bfloat16
NT = (((1,), (1,)), ((), ()))
NN = (((1,), (0,)), ((), ()))
SCALE = -1.4426950408889634 / 64.0
CENTRE = 1024.0


def locate(pixel_ids, quad_offsets):
    column = (pixel_ids % 256) * 8
    lines = (pixel_ids // 256) * 8
    east = (column[None, :] + quad_offsets[0]).astype(F32) - CENTRE
    north = (lines[None, :] + quad_offsets[1]).astype(F32) - CENTRE
    return east, north


def pieces(value):
    high = jnp.floor(value * (1.0 / 65536.0)) * 65536.0
    rest = value - high
    mid = jnp.floor(rest * (1.0 / 256.0)) * 256.0
    return [high, mid, rest - mid]


def halves(value):
    high = jnp.floor(value * (1.0 / 128.0)) * 128.0
    return high, value - high


def row_features(x, y):
    xh, xl = halves(x)
    yh, yl = halves(y)
    one = jnp.ones_like(x)
    zero = jnp.zeros_like(x)
    cross = [-2 * xh, -2 * xh, -2 * xl, -2 * xl, -2 * yh, -2 * yh, -2 * yl, -2 * yl]
    return jnp.concatenate(cross + pieces(x * x + y * y) + [one] * 3 + [zero] * 2, 0)


def col_features(x, y):
    xh, xl = halves(x)
    yh, yl = halves(y)
    one = jnp.ones_like(x)
    zero = jnp.zeros_like(x)
    cross = [xh, xl, xh, xl, yh, yl, yh, yl]
    return jnp.concatenate(cross + [one] * 3 + pieces(x * x + y * y) + [zero] * 2, 0)


def feature_kernel(row_ref, col_ref, f_ref, g_ref):
    for a in range(row_ref.shape[1]):
        one = row_features(row_ref[0, a : a + 1, :], row_ref[1, a : a + 1, :])
        f_ref[a] = one.T.astype(BF)
        g_ref[a] = col_features(col_ref[0, a : a + 1, :], col_ref[1, a : a + 1, :]).astype(BF)


def features(row_points, col_points):
    count, rows = row_points.shape[1:]
    cols = col_points.shape[2]
    return pl.pallas_call(
        feature_kernel,
        out_shape=[
            jax.ShapeDtypeStruct((count, rows, 16), BF),
            jax.ShapeDtypeStruct((count, 16, cols), BF),
        ],
        in_specs=[pl.BlockSpec(memory_space=pltpu.VMEM)] * 2,
        out_specs=[pl.BlockSpec(memory_space=pltpu.VMEM)] * 2,
        compiler_params=pltpu.CompilerParams(vmem_limit_bytes=8 << 20),
        name="features",
    )(row_points, col_points)


def cover_kernel(f_ref, g_ref, o_ref):
    count, block = f_ref.shape[:2]
    rows_here = f_ref[...].reshape(count * block, 16)

    def column_point(b, total):
        apart = jnp.dot(rows_here, g_ref[b], preferred_element_type=F32)
        near = jnp.exp2(apart * SCALE)
        for a in range(count):
            total = total + near[a * block : (a + 1) * block]
        return total

    total = lax.fori_loop(0, count, column_point, jnp.zeros(o_ref.shape, F32), unroll=8)
    o_ref[...] = total * (1.0 / (count * count))


def cover_rows(row_part, col_part, first, block):
    count, rows, depth = row_part.shape
    cols = col_part.shape[2]
    index = first // block
    return pl.pallas_call(
        cover_kernel,
        grid=(1,),
        out_shape=jax.ShapeDtypeStruct((block, cols), F32),
        in_specs=[
            pl.BlockSpec((count, block, depth), lambda i: (0, index, 0)),
            pl.BlockSpec((count, depth, cols), lambda i: (0, 0, 0)),
        ],
        out_specs=pl.BlockSpec((block, cols), lambda i: (0, 0)),
        compiler_params=pltpu.CompilerParams(vmem_limit_bytes=16 << 20),
        cost_estimate=pl.CostEstimate(flops=10**8, bytes_accessed=1 << 18, transcendentals=0),
        name="cover",
    )(row_part, col_part)


def table_rows(offset, north, lines):
    line = lax.broadcasted_iota(jnp.int32, (16, lines), 1).astype(F32) - CENTRE
    total = [jnp.zeros((16, lines), F32) for _ in range(8)]
    for a in range(offset.shape[1]):
        apart = jnp.broadcast_to(north[:, a : a + 1], (16, lines)) - line
        near = jnp.exp2(apart * apart * SCALE)
        which = jnp.broadcast_to(offset[:, a : a + 1], (16, lines))
        for p in range(8):
            total[p] = total[p] + jnp.where(which == float(p), near, 0.0)
    return [split(x) for x in total]


def row_table_kernel(row_ref, t_ref, row_cell_ref, place_ref):
    rows = row_ref.shape[2]
    lines = t_ref.shape[2] // 2
    row_cell = jnp.floor(row_ref[0] * 0.125) * 8.0
    place_ref[0] = (row_ref[0] - row_cell).T
    place_ref[1] = row_ref[1].T
    row_cell_ref[...] = row_cell[0:1].T

    def row_tile(index, _):
        here = pl.ds(pl.multiple_of(index * 16, 16), 16)
        for p, (high, low) in enumerate(table_rows(place_ref[0, here], place_ref[1, here], lines)):
            t_ref[p, here, :lines] = high
            t_ref[p, here, lines:] = low
        return 0

    lax.fori_loop(0, rows // 16, row_tile, 0)


def row_table(row_points, lines):
    count, rows = row_points.shape[1:]
    return pl.pallas_call(
        row_table_kernel,
        out_shape=[
            jax.ShapeDtypeStruct((8, rows, 2 * lines), BF),
            jax.ShapeDtypeStruct((rows, 1), F32),
        ],
        in_specs=[pl.BlockSpec(memory_space=pltpu.VMEM)],
        out_specs=[pl.BlockSpec(memory_space=pltpu.VMEM)] * 2,
        scratch_shapes=[pltpu.VMEM((2, rows, count), F32)],
        compiler_params=pltpu.CompilerParams(vmem_limit_bytes=16 << 20),
        cost_estimate=pl.CostEstimate(flops=10**8, bytes_accessed=1 << 18, transcendentals=0),
        name="row_table",
    )(row_points)


def pack(prior, points):
    flat = points.reshape(-1, NB)
    tiles = prior.shape[1] // NB
    extra = flat.reshape(tiles, flat.shape[0] // tiles, NB).transpose(1, 0, 2)
    return jnp.concatenate([prior, extra.reshape(-1, prior.shape[1])], 0)


def unpack(block_ref):
    extra = block_ref.shape[0] - NB
    tiles = block_ref.shape[1] // NB
    flat = jnp.concatenate(
        [block_ref[NB : NB + extra, NB * t : NB * t + NB] for t in range(tiles)], 0
    )
    count = flat.shape[0] // 2
    return flat[:count], flat[count:]


def column_counts(block_ref, h_ref, at, stride):
    east, north = unpack(block_ref)
    lines = h_ref.shape[0]
    cell = jnp.floor(east[0:1] * 0.125) * 8.0
    line = jnp.floor(north[0:1] * 0.125) * 8.0
    east, north = east - cell, north - line
    sub = lax.broadcasted_iota(jnp.int32, (8, NB), 0).astype(F32)
    held = [jnp.zeros((8, NB), F32) for _ in range(8)]
    for b in range(east.shape[0]):
        one = jnp.where(sub == jnp.broadcast_to(north[b : b + 1], (8, NB)), 1.0, 0.0)
        which = jnp.broadcast_to(east[b : b + 1], (8, NB))
        for q in range(8):
            held[q] = held[q] + jnp.where(which == float(q), one, 0.0)
    line = jnp.broadcast_to(line, (8, NB))
    for r in range(0, lines, 16):
        low = line == float(r) - CENTRE
        high = line == float(r + 8) - CENTRE
        for q in range(8):
            pair = [jnp.where(low, held[q], 0.0), jnp.where(high, held[q], 0.0)]
            lanes = slice(q * stride + at, q * stride + at + NB)
            h_ref[r : r + 16, lanes] = jnp.concatenate(pair, 0).astype(BF)
    return cell


def cover_chunk(table, row_cell, col_cell, h_ref, east_ref, points):
    chunk, cols = east_ref.shape[1:]
    stride = h_ref.shape[1] // 8
    together = 1 + (cols % (2 * NB) > 0)
    cell = jnp.broadcast_to(row_cell, (chunk, cols)) - col_cell
    for t in range(15):
        apart = cell + float(t - 7)
        east_ref[t] = jnp.exp2(apart * apart * SCALE)
    table = table.reshape(8 * chunk, table.shape[2])
    total = jnp.zeros((chunk, cols), F32)
    for first in range(0, 8, together):
        offsets = range(first, first + together)
        counts = [h_ref[:, (q + 1) * stride - cols : (q + 1) * stride] for q in offsets]
        counts = jnp.concatenate(counts, 1)
        part = jnp.dot(table, jnp.concatenate([counts, counts], 0), preferred_element_type=F32)
        for p in range(8):
            for i, q in enumerate(offsets):
                piece = part[p * chunk : (p + 1) * chunk, i * cols : (i + 1) * cols]
                total = total + piece * east_ref[p - q + 7]
    return total * (1.0 / (points * points))


def lead_cover_kernel(
    place_ref, t_ref, row_cell_ref, *refs, points
):
    blocks, refs = refs[:4], refs[4:]
    folded_ref, own_ref, h_ref, col_cell_ref, east_ref, far_ref, far_cell_ref, far_table_ref = refs
    rows, cols = own_ref.shape
    lines = h_ref.shape[0]
    cells = [column_counts(ref, h_ref, NB * i, cols) for i, ref in enumerate(blocks)]
    col_cell = jnp.concatenate(cells, 1)
    col_cell_ref[...] = col_cell

    east, north = unpack(blocks[1])
    far_ref[0] = (east - cells[1]).T
    far_ref[1] = north.T
    far_cell_ref[...] = cells[1].T
    first = pl.multiple_of(place_ref[1] * rows, rows)
    for r in range(0, rows, 16):
        here = pl.ds(first + r, 16)
        for p, (high, low) in enumerate(table_rows(far_ref[0, here], far_ref[1, here], lines)):
            far_table_ref[p, r : r + 16, :lines] = high
            far_table_ref[p, r : r + 16, lines:] = low

    mine = cover_chunk(t_ref[:, :rows], row_cell_ref[:rows], col_cell, h_ref, east_ref, points)
    row = lax.broadcasted_iota(jnp.int32, (rows, cols), 0)
    col = lax.broadcasted_iota(jnp.int32, (rows, cols), 1)
    mine = mine + jnp.where(col == first + row, 1.0, 0.0)
    own_ref[...] = mine
    far = cover_chunk(
        far_table_ref[...], far_cell_ref[pl.ds(first, rows)], col_cell, h_ref, east_ref, points
    )
    folded_ref[:, : 3 * NB] = mine[:, : 3 * NB]
    folded_ref[:, 3 * NB : 4 * NB] = far[:, 2 * NB : 3 * NB]
    own_last = makes_own(place_ref[0])
    folded_ref[:, 4 * NB :] = jnp.where(own_last, mine[:, 3 * NB :], far[:, 3 * NB :])


def later_cover_kernel(t_ref, row_cell_ref, h_ref, col_cell_ref, o_ref, east_ref, *, points, start):
    chunk, cols = east_ref.shape[1:]
    col_cell = col_cell_ref[:, col_cell_ref.shape[1] - cols :]

    def row_chunk(index, _):
        first = pl.multiple_of(index * chunk, chunk)
        here = pl.ds(pl.multiple_of(first + start, chunk), chunk)
        o_ref[pl.ds(first, chunk)] = cover_chunk(
            t_ref[:, here], row_cell_ref[here], col_cell, h_ref, east_ref, points
        )
        return 0

    lax.fori_loop(0, o_ref.shape[0] // chunk, row_chunk, 0)


def block_cover_kernel(t_ref, row_cell_ref, *refs, points, start):
    blocks, (o_ref, h_ref, col_cell_ref, east_ref) = blocks_in(refs[:-4]), refs[-4:]
    cells = [
        column_counts(ref, h_ref, NB * i, o_ref.shape[1]) for i, ref in enumerate(blocks)
    ]
    col_cell_ref[...] = jnp.concatenate(cells, 1)
    later_cover_kernel(
        t_ref, row_cell_ref, h_ref, col_cell_ref, o_ref, east_ref, points=points, start=start
    )


def inverse_factor(tiles):
    n = len(tiles)
    width = 8 * n
    lane = lax.broadcasted_iota(jnp.int32, (8, width), 1)
    sub = lax.broadcasted_iota(jnp.int32, (8, width), 0)
    tiles = list(tiles)
    out = []

    def spread(x):
        return jnp.broadcast_to(x, (8, width))

    def lanes(tile, v):
        return [spread(tile[:, 8 * v + q : 8 * v + q + 1]) for q in range(8)]

    following = lanes(tiles[0], 0)
    for v in range(n):
        near = min(n, v + NEAR)
        cols = {v: following}
        if v + 1 < n:
            cols[v] = cols[v] + lanes(tiles[v], v + 1)
            cols[v + 1] = lanes(tiles[v + 1], v) + lanes(tiles[v + 1], v + 1)
        for r in range(v + 2, near):
            cols[r] = lanes(tiles[r], v)
        here = (lane >= 8 * v) & (lane < 8 * v + 8)
        for r in range(v + 1, n):
            tiles[r] = jnp.where(here, 0.0, tiles[r])
        tiles[v] = jnp.where(here, jnp.where(lane == sub + 8 * v, 1.0, 0.0), tiles[v])
        pivots = jnp.ones((8, width), F32)
        for s in range(8):
            head = cols[v]
            pivot = spread(head[s][s : s + 1])
            inverse = 1.0 / pivot
            pivots = jnp.where(sub == s, pivot, pivots)
            row = spread(tiles[v][s : s + 1])
            heads = [spread(head[k][s : s + 1]) for k in range(s + 1, len(head))]
            for r in range(v, near):
                part = cols[r][s] * inverse
                if r == v:
                    part = jnp.where(sub > s, part, 0.0)
                tiles[r] = tiles[r] - part * row
                for k in range(s + 1, len(cols[r])):
                    cols[r][k] = cols[r][k] - part * heads[k - s - 1]
        if v + 1 < n:
            following = cols[v + 1][8:]
        rows = tiles[v] * lax.rsqrt(pivots)
        if near < n:
            high = rows.astype(BF).astype(F32)
            low = rows - high
            left = jnp.concatenate([high, high, low, low], 0).astype(BF)
            right = jnp.concatenate([high, low, high, low], 0).astype(BF)
            update = lax.dot_general(
                left, right, (((0,), (0,)), ((), ())), preferred_element_type=F32
            )
            for r in range(near, n):
                tiles[r] = tiles[r] - update[8 * r : 8 * r + 8]
        out.append(jnp.where(lane <= sub + 8 * v, rows, 0.0))
    return jnp.concatenate(out, 0)


def split(x):
    high = x.astype(BF)
    return high, (x - high.astype(F32)).astype(BF)


def dot3(ah, al, bh, bl, numbers=NT):
    dot = functools.partial(lax.dot_general, dimension_numbers=numbers, preferred_element_type=F32)
    return dot(ah, bh) + (dot(ah, bl) + dot(al, bh))


def factor_blocks(a_ref, lh_ref, ll_ref, wh_ref, wl_ref):
    n = a_ref.shape[0]
    blocks = n // NB

    def column(first):
        end = first + NB
        bh, bl = split(a_ref[end:, first:end])
        high, low = split(dot3(bh, bl, wh_ref[first:end], wl_ref[first:end]))
        lh_ref[end:, first:end] = high
        ll_ref[end:, first:end] = low
        a_ref[end:, end : end + NB] = a_ref[end:, end : end + NB] - dot3(
            lh_ref[end:, :end],
            ll_ref[end:, :end],
            lh_ref[end : end + NB, :end],
            ll_ref[end : end + NB, :end],
        )

    def step(j, _):
        c = pl.multiple_of(j * NB, NB)
        tiles = [a_ref[pl.ds(c + 8 * v, 8), pl.ds(c, NB)] for v in range(NB // 8)]
        wh, wl = split(inverse_factor(tiles))
        wh_ref[pl.ds(c, NB)] = wh
        wl_ref[pl.ds(c, NB)] = wl
        for block in range(blocks - 1):
            pl.when(j == block)(functools.partial(column, block * NB))
        return 0

    lax.fori_loop(0, blocks, step, 0)


def factor_kernel(diag_ref, lh_ref, ll_ref, wh_ref, wl_ref, a_ref):
    a_ref[...] = diag_ref[...]
    factor_blocks(a_ref, lh_ref, ll_ref, wh_ref, wl_ref)


def turned(r, k):
    at = ((r & 1) << 1 | (r >> 1) & 1) + k
    return (r & 4) | (at & 1) << 1 | (at >> 1) & 1


def block_order(r):
    return [r, r ^ 4, turned(r, 1), turned(r, 2), turned(r, 3), r ^ 5, r ^ 6, r ^ 7]


def makes_own(r):
    return (r & 1) == 0


def folded_blocks(r):
    order = block_order(r)
    either = jnp.where(makes_own(r), r, r ^ 4)
    return [(r, r), (r, order[1]), (r, order[2]), (order[1], order[2]), (either, order[3])]


def blocks_in(refs):
    return [
        ref.at[first : first + ref.shape[0] // parts]
        for ref in refs
        for parts in [1 + (ref.shape[0] >= 2 * NB)]
        for first in range(0, ref.shape[0], ref.shape[0] // parts)
    ]


def unfold_kernel(place_ref, *refs):
    pieces_refs, (lh_ref, ll_ref, wh_ref, wl_ref, a_ref, g_ref) = refs[:8], refs[8:]
    row_pos = place_ref[0]
    panel_pos = place_ref[1]
    for i, ref in enumerate(pieces_refs):
        g_ref[4 * i : 4 * i + 4] = ref[...]

    def rows_of(r, _):
        away = r ^ row_pos
        slot = (away >> 1) | ((away & 1) << 2)
        ats = []
        for p in range(4):
            gone = p ^ panel_pos
            ats.append(slot | ((gone >> 1) << 3) | ((gone & 1) << 4))
        for k, (rows, cols) in enumerate(folded_blocks(r)):
            block = jnp.concatenate([g_ref[at, :, NB * k : NB * k + NB] for at in ats], 0)
            rr = pl.multiple_of(rows * NB, NB)
            cc = pl.multiple_of(cols * NB, NB)

            @pl.when(rows >= cols)
            def _():
                a_ref[pl.ds(rr, NB), pl.ds(cc, NB)] = block

            if k:

                @pl.when(rows < cols)
                def _():
                    a_ref[pl.ds(cc, NB), pl.ds(rr, NB)] = block.T

        return 0

    lax.fori_loop(0, 8, rows_of, 0)
    factor_blocks(a_ref, lh_ref, ll_ref, wh_ref, wl_ref)


def factor(kernel, operands, n):
    in_specs = [pl.BlockSpec(memory_space=pltpu.VMEM)] * len(operands)
    scratch = [pltpu.VMEM((n, n), F32)]
    if kernel is unfold_kernel:
        in_specs[0] = pl.BlockSpec(memory_space=pltpu.SMEM)
        scratch.append(pltpu.VMEM((32, *operands[1].shape[1:]), F32))
    return pl.pallas_call(
        kernel,
        out_shape=[jax.ShapeDtypeStruct((n, n), BF)] * 2 + [jax.ShapeDtypeStruct((n, NB), BF)] * 2,
        in_specs=in_specs,
        out_specs=[pl.BlockSpec(memory_space=pltpu.VMEM)] * 4,
        scratch_shapes=scratch,
        compiler_params=pltpu.CompilerParams(vmem_limit_bytes=32 << 20),
        cost_estimate=pl.CostEstimate(flops=5 * 10**10, bytes_accessed=8 << 20, transcendentals=0),
        name="factor",
    )(*operands)


def solve_kernel(place_ref, *refs, corners):
    cover_refs, parts_refs = refs[: len(corners)], refs[len(corners) : -7]
    lh_ref, ll_ref, wh_ref, wl_ref, o_ref, xh_ref, xl_ref = refs[-7:]
    n = o_ref.shape[1]

    def put(rows, cols, value):
        taken = parts_refs[0][parts_refs[0].shape[0] - 1, rows, cols]
        for part in parts_refs[1:]:
            taken = taken + part[part.shape[0] - 1, rows, cols]
        o_ref[rows, cols] = value - taken

    for (row, block), ref in zip(corners, cover_refs):
        rows = slice(row, row + ref.shape[0])
        if block is None:
            put(rows, slice(None), ref[...])
            continue
        for c, s in enumerate(block_order(place_ref[0])[block : block + ref.shape[1] // NB]):
            cols = pl.ds(pl.multiple_of(s * NB, NB), NB)
            put(rows, cols, ref[:, NB * c : NB * c + NB])
    wide = 2 * NB
    inverses = []
    for c in range(0, n, wide):
        upper, lower = slice(c, c + NB), slice(c + NB, c + wide)
        corner = dot3(lh_ref[lower, upper], ll_ref[lower, upper], wh_ref[upper], wl_ref[upper], NN)
        corner = split(-dot3(wh_ref[lower], wl_ref[lower], *split(corner), NN))
        zero = jnp.zeros((NB, NB), BF)
        inverses.append(
            [
                jnp.concatenate(
                    [
                        jnp.concatenate([ref[upper], zero], 1),
                        jnp.concatenate([part, ref[lower]], 1),
                    ],
                    0,
                )
                for ref, part in zip((wh_ref, wl_ref), corner)
            ]
        )
    for c, inverse in zip(range(0, n, wide), inverses):
        here = o_ref[:, c : c + wide]
        if c:
            here = here - dot3(
                xh_ref[:, :c], xl_ref[:, :c], lh_ref[c : c + wide, :c], ll_ref[c : c + wide, :c]
            )
        x = dot3(*split(here), *inverse)
        o_ref[:, c : c + wide] = x
        xh, xl = split(x)
        xh_ref[:, c : c + wide] = xh
        xl_ref[:, c : c + wide] = xl


def solve(place, covers, corners, parts, factors):
    rows, n = parts[0].shape[1:]
    return vmem_call(
        functools.partial(solve_kernel, corners=corners),
        jax.ShapeDtypeStruct((rows, n), F32),
        place,
        [*covers, *parts, *factors],
        [pltpu.VMEM((rows, n), BF)] * 2,
        "solve",
    )


def vmem_call(kernel, out_shape, place, operands, scratch=(), name=None):
    return pl.pallas_call(
        kernel,
        out_shape=out_shape,
        in_specs=[pl.BlockSpec(memory_space=pltpu.SMEM)] * (place is not None)
        + [pl.BlockSpec(memory_space=pltpu.VMEM)] * len(operands),
        out_specs=jax.tree.map(lambda _: pl.BlockSpec(memory_space=pltpu.VMEM), out_shape),
        scratch_shapes=list(scratch),
        compiler_params=pltpu.CompilerParams(vmem_limit_bytes=32 << 20),
        cost_estimate=pl.CostEstimate(flops=10**8, bytes_accessed=1 << 18, transcendentals=0),
        name=name,
    )(*([] if place is None else [place]), *operands)


def fold_products_kernel(place_ref, *refs):
    blocks, shares, total_ref = refs[:4], refs[4:-1], refs[-1]
    own, far, one, two = [split(ref[:NB]) for ref in blocks]
    own_last = makes_own(place_ref[0])
    either = split(jnp.where(own_last, blocks[0][:NB], blocks[1][:NB]))
    pairs = [(own, own), (own, far), (own, one), (far, one), (either, two)]
    for k, (left, right) in enumerate(pairs):
        total_ref[:, NB * k : NB * k + NB] = dot3(*left, *right)
    rows = shares[0].shape[0]
    for m, ref in enumerate(shares):
        first = pl.multiple_of((place_ref[1] ^ m) * rows, rows)
        ref[...] = total_ref[pl.ds(first, rows)]


def gather_split_kernel(place_ref, *refs):
    blocks, (high_ref, low_ref) = blocks_in(refs[:-2]), refs[-2:]
    for s, ref in zip(block_order(place_ref[0]), blocks):
        first = pl.multiple_of(s * NB, NB)
        high, low = split(ref[:NB])
        high_ref[pl.ds(first, NB)] = high
        low_ref[pl.ds(first, NB)] = low


def rest_products_kernel(place_ref, prior_ref, high_ref, low_ref, *refs, turns):
    plus_refs, o_ref = refs[:-1], refs[-1]
    rows = o_ref.shape[1]
    for i, m in enumerate(turns):
        first = pl.multiple_of((place_ref[1] ^ m) * rows, rows)
        own_high, own_low = split(prior_ref[pl.ds(first, rows)])
        for c in range(0, o_ref.shape[2], 2 * NB):
            cols = slice(c, c + 2 * NB)
            total = dot3(own_high, own_low, high_ref[cols], low_ref[cols])
            for plus_ref in plus_refs:
                total = total + plus_ref[i, :, cols]
            o_ref[i, :, cols] = total


def swap(block, axis, bit):
    return lax.ppermute(block, axis, [(i, i ^ bit) for i in range(lax.axis_size(axis))])


def dot_rows(left, right):
    return lax.dot_general(
        left, right, NT, precision=lax.Precision.HIGH, preferred_element_type=F32
    )


def local(pixel_ids, quad_offsets, prior_factor):
    panel_count = lax.axis_size("panel")
    row_count = lax.axis_size("row")
    block_rows = pixel_ids.shape[0]
    quarter_rows = block_rows // panel_count
    per_device = B // (row_count * panel_count)
    span_cols = panel_count * per_device
    row_pos = lax.axis_index("row")
    panel_pos = lax.axis_index("panel")
    device_pos = row_pos * panel_count + panel_pos
    lead = 32

    points = jnp.stack(locate(pixel_ids, quad_offsets))
    count = points.shape[1]
    own_points = lax.dynamic_slice_in_dim(points, panel_pos * quarter_rows, quarter_rows, 2)
    local_points = points.reshape(2, count, panel_count, quarter_rows)[:, :, :, :per_device]
    local_points = local_points.reshape(2, count, span_cols)
    own_prior = prior_factor.reshape(panel_count, quarter_rows, -1)[:, :per_device]
    own_prior = own_prior.reshape(span_cols, -1)
    place = jnp.stack([row_pos, panel_pos]).astype(jnp.int32)
    lines = block_rows * row_count // 256 * 8
    folds = span_cols == NB and row_count == 8 and panel_count == 4 and lines == 256

    if not (folds and 2 * count * NB == 8 * own_prior.shape[1]):
        lead = 32
        row_ids = jnp.arange(lead, dtype=jnp.int32)[:, None]
        col_ids = jnp.arange(B, dtype=jnp.int32)[None, :]
        on_diagonal = (row_ids < per_device) & (col_ids == device_pos * per_device + row_ids)
        unit = jnp.where(on_diagonal, 1.0, 0.0).astype(F32)
        flat = local_points.reshape(1, 2 * count, span_cols)
        copies = jnp.broadcast_to(flat, (row_count, 2 * count, span_cols))
        spread = lax.all_to_all(copies, "row", split_axis=0, concat_axis=0, tiled=True)
        parted = features(own_points, spread.transpose(1, 0, 2).reshape(2, count, B))
        covers = [cover_rows(*parted, i, lead) for i in range(0, quarter_rows, lead)]
        covers[0] = covers[0] + unit
        panel_prior = lax.all_gather(own_prior, "row", axis=0, tiled=True)
        partial = dot_rows(prior_factor, panel_prior)
        parts = lax.all_to_all(
            partial.reshape(panel_count, quarter_rows, B), "panel", split_axis=0, concat_axis=0, tiled=True
        )
        parts = jnp.sum(parts, axis=0)
        mine = covers[0][:per_device] - parts[:per_device]
        diag_rows = lax.all_gather(mine, ("row", "panel"), axis=0, tiled=True)
        corners = [(i * lead, None) for i in range(len(covers))]
        return solve(place, covers, corners, [parts[None]], factor(factor_kernel, (diag_rows,), B))

    def turn(block, k):
        return lax.ppermute(block, "row", [(turned(d, k), d) for d in range(8)])

    own = pack(own_prior, local_points)
    two, one, far = turn(own, 2), turn(own, 1), swap(own, "row", 4)
    table = row_table(own_points, lines)

    def block_cover(held, blocks, start, cols):
        return vmem_call(
            functools.partial(block_cover_kernel, points=count, start=start),
            jax.ShapeDtypeStruct((quarter_rows - start, cols), F32),
            None,
            [*held, *blocks],
            [
                pltpu.VMEM((lines, 8 * cols), BF),
                pltpu.VMEM((1, cols), F32),
                pltpu.VMEM((15, per_device, cols), F32),
            ],
            "cover",
        )

    cover_own = block_cover(table, [own], per_device, NB)
    one, cover_own = lax.optimization_barrier((one, cover_own))
    from_x = swap(one, "row", 1)
    (far, one, two), table, cover_own = lax.optimization_barrier(((far, one, two), table, cover_own))
    shares = vmem_call(
        fold_products_kernel,
        [jax.ShapeDtypeStruct((per_device, 5 * NB), F32)] * 4,
        place,
        [own, far, one, two],
        [pltpu.VMEM((NB, 5 * NB), F32)],
        "fold_products",
    )
    shares, own, far = lax.optimization_barrier((shares, own, far))

    def beside(operands, transfer, work):
        operands, held = lax.optimization_barrier((operands, table))
        return lax.optimization_barrier((transfer(operands), work(operands, held)))

    half = 4 * NB
    east = pltpu.VMEM((15, per_device, half), F32)

    def lead_cover(_, held):
        return vmem_call(
            functools.partial(lead_cover_kernel, points=count),
            [
                jax.ShapeDtypeStruct((per_device, 5 * NB), F32),
                jax.ShapeDtypeStruct((per_device, half), F32),
                jax.ShapeDtypeStruct((lines, 8 * half), BF),
                jax.ShapeDtypeStruct((1, half), F32),
            ],
            place,
            [*held, own, far, one, two],
            [
                east,
                pltpu.VMEM((2, NB, count), F32),
                pltpu.VMEM((NB, 1), F32),
                pltpu.VMEM((8, per_device, 2 * lines), BF),
            ],
            "lead_cover",
        )

    sums, (folded, cover_lead, *counts) = beside(
        shares,
        lambda shares: [swap(share, "panel", m) for m, share in zip((1, 2, 3), shares[1:])],
        lead_cover,
    )
    sums, from_x = lax.optimization_barrier((sums, from_x))
    far_x = swap(far, "row", 1)
    far_z = swap(far, "row", 2)
    shard = folded - (shares[0] + sums[0] + sums[1] + sums[2])

    def rest_part(panel_prior, turns, plus=()):
        return vmem_call(
            functools.partial(rest_products_kernel, turns=turns),
            jax.ShapeDtypeStruct((len(turns), quarter_rows, B), F32),
            place,
            [prior_factor, *panel_prior, *plus],
            name="rest_products",
        )

    def later_cover(held, start, rows):
        return vmem_call(
            functools.partial(later_cover_kernel, points=count, start=start),
            jax.ShapeDtypeStruct((rows, half - NB), F32),
            None,
            [*held, *counts],
            [pltpu.VMEM((15, per_device, half - NB), F32)],
            "cover",
        )

    middle = quarter_rows // 2

    def beside_far_z(_, held):
        rest = [from_x, far_x, far_z, last]
        cover = later_cover(held, middle, quarter_rows - middle)
        cover, blocks = lax.optimization_barrier((cover, rest))
        panel_prior = vmem_call(
            gather_split_kernel,
            [jax.ShapeDtypeStruct((B, own_prior.shape[1]), BF)] * 2,
            place,
            [own, far, one, two, *blocks],
            name="gather_split",
        )
        return cover, panel_prior, rest_part(panel_prior, (3, 1)), rest

    shard = shard[None]
    near_rows, cover_first = beside(
        shard,
        lambda x: swap(x, "row", 2),
        lambda _, held: later_cover(held, per_device, middle - per_device),
    )
    near_rows = jnp.concatenate([shard, near_rows], 0)
    cover_first, from_x, far_x, far_z = lax.optimization_barrier((cover_first, from_x, far_x, far_z))
    last = swap(far_x, "row", 2)
    far_rows, (cover_second, panel_prior, for_core, rest) = beside(
        near_rows, lambda x: swap(x, "row", 4), beside_far_z
    )
    held_rows = jnp.concatenate([near_rows, far_rows], 0)

    def across(x):
        corner = [(i, i ^ 6) for i in range(32)]
        return swap(x, "row", 1), swap(x, "panel", 2), lax.ppermute(x, ("row", "panel"), corner)

    def beside_xy(x, held):
        from_core = swap(for_core, "panel", 1)
        cover = block_cover(held, rest, 0, half)
        part_0, part_2 = rest_part(panel_prior, (0,)), rest_part(panel_prior, (2,), [from_core])
        return cover, part_0, part_2, from_core, swap(x, "panel", 1)

    received, (cover_last, part_0, part_2, from_core, held_there) = beside(
        held_rows, across, beside_xy
    )
    there = [held_there] + [swap(x, "panel", 1) for x in received]
    parts = [part_0, from_core, swap(part_2, "panel", 2)]
    factors = factor(unfold_kernel, (place, held_rows, *received, *there), B)
    covers = [cover_lead, cover_own, cover_first, cover_second, cover_last]
    corners = [(0, 0), (per_device, 0), (per_device, 1), (middle, 1), (0, 4)]
    return solve(place, covers, corners, parts, factors)


def solution(mesh):
    return jax.shard_map(
        local,
        mesh=mesh,
        in_specs=(P("row"), P(None, None, "row"), P("row", "panel")),
        out_specs=P(("row", "panel"), None),
        check_vma=False,
    )
```

```python
import functools

import jax
import jax.numpy as jnp
from jax import lax
from jax.experimental import pallas as pl
from jax.experimental.pallas import tpu as pltpu
from jax.sharding import PartitionSpec as P

B = 1024
NB = 128
NEAR = 4
F32 = jnp.float32
BF = jnp.bfloat16
NT = (((1,), (1,)), ((), ()))
NN = (((1,), (0,)), ((), ()))
SCALE = -1.4426950408889634 / 64.0
CENTRE = 1024.0


def locate(pixel_ids, quad_offsets):
    column = (pixel_ids % 256) * 8
    lines = (pixel_ids // 256) * 8
    east = (column[None, :] + quad_offsets[0]).astype(F32) - CENTRE
    north = (lines[None, :] + quad_offsets[1]).astype(F32) - CENTRE
    return east, north


def pieces(value):
    high = jnp.floor(value * (1.0 / 65536.0)) * 65536.0
    rest = value - high
    mid = jnp.floor(rest * (1.0 / 256.0)) * 256.0
    return [high, mid, rest - mid]


def halves(value):
    high = jnp.floor(value * (1.0 / 128.0)) * 128.0
    return high, value - high


def row_features(x, y):
    xh, xl = halves(x)
    yh, yl = halves(y)
    one = jnp.ones_like(x)
    zero = jnp.zeros_like(x)
    cross = [-2 * xh, -2 * xh, -2 * xl, -2 * xl, -2 * yh, -2 * yh, -2 * yl, -2 * yl]
    return jnp.concatenate(cross + pieces(x * x + y * y) + [one] * 3 + [zero] * 2, 0)


def col_features(x, y):
    xh, xl = halves(x)
    yh, yl = halves(y)
    one = jnp.ones_like(x)
    zero = jnp.zeros_like(x)
    cross = [xh, xl, xh, xl, yh, yl, yh, yl]
    return jnp.concatenate(cross + [one] * 3 + pieces(x * x + y * y) + [zero] * 2, 0)


def feature_kernel(row_ref, col_ref, f_ref, g_ref):
    for a in range(row_ref.shape[1]):
        one = row_features(row_ref[0, a : a + 1, :], row_ref[1, a : a + 1, :])
        f_ref[a] = one.T.astype(BF)
        g_ref[a] = col_features(col_ref[0, a : a + 1, :], col_ref[1, a : a + 1, :]).astype(BF)


def features(row_points, col_points):
    count, rows = row_points.shape[1:]
    cols = col_points.shape[2]
    return pl.pallas_call(
        feature_kernel,
        out_shape=[
            jax.ShapeDtypeStruct((count, rows, 16), BF),
            jax.ShapeDtypeStruct((count, 16, cols), BF),
        ],
        in_specs=[pl.BlockSpec(memory_space=pltpu.VMEM)] * 2,
        out_specs=[pl.BlockSpec(memory_space=pltpu.VMEM)] * 2,
        compiler_params=pltpu.CompilerParams(vmem_limit_bytes=8 << 20),
        name="features",
    )(row_points, col_points)


def cover_kernel(f_ref, g_ref, o_ref):
    count, block = f_ref.shape[:2]
    rows_here = f_ref[...].reshape(count * block, 16)

    def column_point(b, total):
        apart = jnp.dot(rows_here, g_ref[b], preferred_element_type=F32)
        near = jnp.exp2(apart * SCALE)
        for a in range(count):
            total = total + near[a * block : (a + 1) * block]
        return total

    total = lax.fori_loop(0, count, column_point, jnp.zeros(o_ref.shape, F32), unroll=8)
    o_ref[...] = total * (1.0 / (count * count))


def cover_rows(row_part, col_part, first, block):
    count, rows, depth = row_part.shape
    cols = col_part.shape[2]
    index = first // block
    return pl.pallas_call(
        cover_kernel,
        grid=(1,),
        out_shape=jax.ShapeDtypeStruct((block, cols), F32),
        in_specs=[
            pl.BlockSpec((count, block, depth), lambda i: (0, index, 0)),
            pl.BlockSpec((count, depth, cols), lambda i: (0, 0, 0)),
        ],
        out_specs=pl.BlockSpec((block, cols), lambda i: (0, 0)),
        compiler_params=pltpu.CompilerParams(vmem_limit_bytes=16 << 20),
        cost_estimate=pl.CostEstimate(flops=10**8, bytes_accessed=1 << 18, transcendentals=0),
        name="cover",
    )(row_part, col_part)


def table_rows(offset, north, lines):
    line = lax.broadcasted_iota(jnp.int32, (16, lines), 1).astype(F32) - CENTRE
    total = [jnp.zeros((16, lines), F32) for _ in range(8)]
    for a in range(offset.shape[1]):
        apart = jnp.broadcast_to(north[:, a : a + 1], (16, lines)) - line
        near = jnp.exp2(apart * apart * SCALE)
        which = jnp.broadcast_to(offset[:, a : a + 1], (16, lines))
        for p in range(8):
            total[p] = total[p] + jnp.where(which == float(p), near, 0.0)
    return [split(x) for x in total]


def row_table_kernel(row_ref, t_ref, row_cell_ref, place_ref):
    rows = row_ref.shape[2]
    lines = t_ref.shape[2] // 2
    row_cell = jnp.floor(row_ref[0] * 0.125) * 8.0
    place_ref[0] = (row_ref[0] - row_cell).T
    place_ref[1] = row_ref[1].T
    row_cell_ref[...] = row_cell[0:1].T

    def row_tile(index, _):
        here = pl.ds(pl.multiple_of(index * 16, 16), 16)
        for p, (high, low) in enumerate(table_rows(place_ref[0, here], place_ref[1, here], lines)):
            t_ref[p, here, :lines] = high
            t_ref[p, here, lines:] = low
        return 0

    lax.fori_loop(0, rows // 16, row_tile, 0)


def row_table(row_points, lines):
    count, rows = row_points.shape[1:]
    return pl.pallas_call(
        row_table_kernel,
        out_shape=[
            jax.ShapeDtypeStruct((8, rows, 2 * lines), BF),
            jax.ShapeDtypeStruct((rows, 1), F32),
        ],
        in_specs=[pl.BlockSpec(memory_space=pltpu.VMEM)],
        out_specs=[pl.BlockSpec(memory_space=pltpu.VMEM)] * 2,
        scratch_shapes=[pltpu.VMEM((2, rows, count), F32)],
        compiler_params=pltpu.CompilerParams(vmem_limit_bytes=16 << 20),
        cost_estimate=pl.CostEstimate(flops=10**8, bytes_accessed=1 << 18, transcendentals=0),
        name="row_table",
    )(row_points)


def pack(prior, points):
    flat = points.reshape(-1, NB)
    tiles = prior.shape[1] // NB
    extra = flat.reshape(tiles, flat.shape[0] // tiles, NB).transpose(1, 0, 2)
    return jnp.concatenate([prior, extra.reshape(-1, prior.shape[1])], 0)


def unpack(block_ref):
    extra = block_ref.shape[0] - NB
    tiles = block_ref.shape[1] // NB
    flat = jnp.concatenate(
        [block_ref[NB : NB + extra, NB * t : NB * t + NB] for t in range(tiles)], 0
    )
    count = flat.shape[0] // 2
    return flat[:count], flat[count:]


def column_counts(block_ref, h_ref, at, stride):
    east, north = unpack(block_ref)
    lines = h_ref.shape[0]
    cell = jnp.floor(east[0:1] * 0.125) * 8.0
    line = jnp.floor(north[0:1] * 0.125) * 8.0
    east, north = east - cell, north - line
    sub = lax.broadcasted_iota(jnp.int32, (8, NB), 0).astype(F32)
    held = [jnp.zeros((8, NB), F32) for _ in range(8)]
    for b in range(east.shape[0]):
        one = jnp.where(sub == jnp.broadcast_to(north[b : b + 1], (8, NB)), 1.0, 0.0)
        which = jnp.broadcast_to(east[b : b + 1], (8, NB))
        for q in range(8):
            held[q] = held[q] + jnp.where(which == float(q), one, 0.0)
    line = jnp.broadcast_to(line, (8, NB))
    for r in range(0, lines, 16):
        low = line == float(r) - CENTRE
        high = line == float(r + 8) - CENTRE
        for q in range(8):
            pair = [jnp.where(low, held[q], 0.0), jnp.where(high, held[q], 0.0)]
            lanes = slice(q * stride + at, q * stride + at + NB)
            h_ref[r : r + 16, lanes] = jnp.concatenate(pair, 0).astype(BF)
    return cell


def cover_chunk(table, row_cell, col_cell, h_ref, east_ref, points):
    chunk, cols = east_ref.shape[1:]
    stride = h_ref.shape[1] // 8
    together = 1 + (cols % (2 * NB) > 0)
    cell = jnp.broadcast_to(row_cell, (chunk, cols)) - col_cell
    for t in range(15):
        apart = cell + float(t - 7)
        east_ref[t] = jnp.exp2(apart * apart * SCALE)
    table = table.reshape(8 * chunk, table.shape[2])
    total = jnp.zeros((chunk, cols), F32)
    for first in range(0, 8, together):
        offsets = range(first, first + together)
        counts = [h_ref[:, (q + 1) * stride - cols : (q + 1) * stride] for q in offsets]
        counts = jnp.concatenate(counts, 1)
        part = jnp.dot(table, jnp.concatenate([counts, counts], 0), preferred_element_type=F32)
        for p in range(8):
            for i, q in enumerate(offsets):
                piece = part[p * chunk : (p + 1) * chunk, i * cols : (i + 1) * cols]
                total = total + piece * east_ref[p - q + 7]
    return total * (1.0 / (points * points))


def lead_cover_kernel(
    place_ref, t_ref, row_cell_ref, *refs, points
):
    blocks, refs = refs[:4], refs[4:]
    folded_ref, own_ref, h_ref, col_cell_ref, east_ref, far_ref, far_cell_ref, far_table_ref = refs
    rows, cols = own_ref.shape
    lines = h_ref.shape[0]
    cells = [column_counts(ref, h_ref, NB * i, cols) for i, ref in enumerate(blocks)]
    col_cell = jnp.concatenate(cells, 1)
    col_cell_ref[...] = col_cell

    east, north = unpack(blocks[1])
    far_ref[0] = (east - cells[1]).T
    far_ref[1] = north.T
    far_cell_ref[...] = cells[1].T
    first = pl.multiple_of(place_ref[1] * rows, rows)
    for r in range(0, rows, 16):
        here = pl.ds(first + r, 16)
        for p, (high, low) in enumerate(table_rows(far_ref[0, here], far_ref[1, here], lines)):
            far_table_ref[p, r : r + 16, :lines] = high
            far_table_ref[p, r : r + 16, lines:] = low

    mine = cover_chunk(t_ref[:, :rows], row_cell_ref[:rows], col_cell, h_ref, east_ref, points)
    row = lax.broadcasted_iota(jnp.int32, (rows, cols), 0)
    col = lax.broadcasted_iota(jnp.int32, (rows, cols), 1)
    mine = mine + jnp.where(col == first + row, 1.0, 0.0)
    own_ref[...] = mine
    far = cover_chunk(
        far_table_ref[...], far_cell_ref[pl.ds(first, rows)], col_cell, h_ref, east_ref, points
    )
    folded_ref[:, : 3 * NB] = mine[:, : 3 * NB]
    folded_ref[:, 3 * NB : 4 * NB] = far[:, 2 * NB : 3 * NB]
    own_last = makes_own(place_ref[0])
    folded_ref[:, 4 * NB :] = jnp.where(own_last, mine[:, 3 * NB :], far[:, 3 * NB :])


def later_cover_kernel(t_ref, row_cell_ref, h_ref, col_cell_ref, o_ref, east_ref, *, points, start):
    chunk, cols = east_ref.shape[1:]
    col_cell = col_cell_ref[:, col_cell_ref.shape[1] - cols :]

    def row_chunk(index, _):
        first = pl.multiple_of(index * chunk, chunk)
        here = pl.ds(pl.multiple_of(first + start, chunk), chunk)
        o_ref[pl.ds(first, chunk)] = cover_chunk(
            t_ref[:, here], row_cell_ref[here], col_cell, h_ref, east_ref, points
        )
        return 0

    lax.fori_loop(0, o_ref.shape[0] // chunk, row_chunk, 0)


def block_cover_kernel(t_ref, row_cell_ref, *refs, points, start):
    blocks, (o_ref, h_ref, col_cell_ref, east_ref) = blocks_in(refs[:-4]), refs[-4:]
    cells = [
        column_counts(ref, h_ref, NB * i, o_ref.shape[1]) for i, ref in enumerate(blocks)
    ]
    col_cell_ref[...] = jnp.concatenate(cells, 1)
    later_cover_kernel(
        t_ref, row_cell_ref, h_ref, col_cell_ref, o_ref, east_ref, points=points, start=start
    )


def inverse_factor(tiles):
    n = len(tiles)
    width = 8 * n
    lane = lax.broadcasted_iota(jnp.int32, (8, width), 1)
    sub = lax.broadcasted_iota(jnp.int32, (8, width), 0)
    tiles = list(tiles)
    out = []

    def spread(x):
        return jnp.broadcast_to(x, (8, width))

    def lanes(tile, v):
        return [spread(tile[:, 8 * v + q : 8 * v + q + 1]) for q in range(8)]

    following = lanes(tiles[0], 0)
    for v in range(n):
        near = min(n, v + NEAR)
        cols = {v: following}
        if v + 1 < n:
            cols[v] = cols[v] + lanes(tiles[v], v + 1)
            cols[v + 1] = lanes(tiles[v + 1], v) + lanes(tiles[v + 1], v + 1)
        for r in range(v + 2, near):
            cols[r] = lanes(tiles[r], v)
        here = (lane >= 8 * v) & (lane < 8 * v + 8)
        for r in range(v + 1, n):
            tiles[r] = jnp.where(here, 0.0, tiles[r])
        tiles[v] = jnp.where(here, jnp.where(lane == sub + 8 * v, 1.0, 0.0), tiles[v])
        pivots = jnp.ones((8, width), F32)
        for s in range(8):
            head = cols[v]
            pivot = spread(head[s][s : s + 1])
            inverse = 1.0 / pivot
            pivots = jnp.where(sub == s, pivot, pivots)
            row = spread(tiles[v][s : s + 1])
            heads = [spread(head[k][s : s + 1]) for k in range(s + 1, len(head))]
            for r in range(v, near):
                part = cols[r][s] * inverse
                if r == v:
                    part = jnp.where(sub > s, part, 0.0)
                tiles[r] = tiles[r] - part * row
                for k in range(s + 1, len(cols[r])):
                    cols[r][k] = cols[r][k] - part * heads[k - s - 1]
        if v + 1 < n:
            following = cols[v + 1][8:]
        rows = tiles[v] * lax.rsqrt(pivots)
        if near < n:
            high = rows.astype(BF).astype(F32)
            low = rows - high
            left = jnp.concatenate([high, high, low, low], 0).astype(BF)
            right = jnp.concatenate([high, low, high, low], 0).astype(BF)
            update = lax.dot_general(
                left, right, (((0,), (0,)), ((), ())), preferred_element_type=F32
            )
            for r in range(near, n):
                tiles[r] = tiles[r] - update[8 * r : 8 * r + 8]
        out.append(jnp.where(lane <= sub + 8 * v, rows, 0.0))
    return jnp.concatenate(out, 0)


def split(x):
    high = x.astype(BF)
    return high, (x - high.astype(F32)).astype(BF)


def dot3(ah, al, bh, bl, numbers=NT):
    dot = functools.partial(lax.dot_general, dimension_numbers=numbers, preferred_element_type=F32)
    return dot(ah, bh) + (dot(ah, bl) + dot(al, bh))


def factor_blocks(a_ref, lh_ref, ll_ref, wh_ref, wl_ref):
    n = a_ref.shape[0]
    blocks = n // NB

    def column(first):
        end = first + NB
        bh, bl = split(a_ref[end:, first:end])
        high, low = split(dot3(bh, bl, wh_ref[first:end], wl_ref[first:end]))
        lh_ref[end:, first:end] = high
        ll_ref[end:, first:end] = low
        a_ref[end:, end : end + NB] = a_ref[end:, end : end + NB] - dot3(
            lh_ref[end:, :end],
            ll_ref[end:, :end],
            lh_ref[end : end + NB, :end],
            ll_ref[end : end + NB, :end],
        )

    def step(j, _):
        c = pl.multiple_of(j * NB, NB)
        tiles = [a_ref[pl.ds(c + 8 * v, 8), pl.ds(c, NB)] for v in range(NB // 8)]
        wh, wl = split(inverse_factor(tiles))
        wh_ref[pl.ds(c, NB)] = wh
        wl_ref[pl.ds(c, NB)] = wl
        for block in range(blocks - 1):
            pl.when(j == block)(functools.partial(column, block * NB))
        return 0

    lax.fori_loop(0, blocks, step, 0)


def factor_kernel(diag_ref, lh_ref, ll_ref, wh_ref, wl_ref, a_ref):
    a_ref[...] = diag_ref[...]
    factor_blocks(a_ref, lh_ref, ll_ref, wh_ref, wl_ref)


def turned(r, k):
    at = ((r & 1) << 1 | (r >> 1) & 1) + k
    return (r & 4) | (at & 1) << 1 | (at >> 1) & 1


def block_order(r):
    return [r, r ^ 4, turned(r, 1), turned(r, 2), turned(r, 3), r ^ 5, r ^ 6, r ^ 7]


def makes_own(r):
    return (r & 1) == 0


def folded_blocks(r):
    order = block_order(r)
    either = jnp.where(makes_own(r), r, r ^ 4)
    return [(r, r), (r, order[1]), (r, order[2]), (order[1], order[2]), (either, order[3])]


def blocks_in(refs):
    return [
        ref.at[first : first + ref.shape[0] // parts]
        for ref in refs
        for parts in [1 + (ref.shape[0] >= 2 * NB)]
        for first in range(0, ref.shape[0], ref.shape[0] // parts)
    ]


def unfold_kernel(place_ref, *refs):
    pieces_refs, (lh_ref, ll_ref, wh_ref, wl_ref, a_ref, g_ref) = refs[:8], refs[8:]
    row_pos = place_ref[0]
    panel_pos = place_ref[1]
    for i, ref in enumerate(pieces_refs):
        g_ref[4 * i : 4 * i + 4] = ref[...]

    def rows_of(r, _):
        away = r ^ row_pos
        slot = (away >> 1) | ((away & 1) << 2)
        ats = []
        for p in range(4):
            gone = p ^ panel_pos
            ats.append(slot | ((gone >> 1) << 3) | ((gone & 1) << 4))
        for k, (rows, cols) in enumerate(folded_blocks(r)):
            block = jnp.concatenate([g_ref[at, :, NB * k : NB * k + NB] for at in ats], 0)
            rr = pl.multiple_of(rows * NB, NB)
            cc = pl.multiple_of(cols * NB, NB)

            @pl.when(rows >= cols)
            def _():
                a_ref[pl.ds(rr, NB), pl.ds(cc, NB)] = block

            if k:

                @pl.when(rows < cols)
                def _():
                    a_ref[pl.ds(cc, NB), pl.ds(rr, NB)] = block.T

        return 0

    lax.fori_loop(0, 8, rows_of, 0)
    factor_blocks(a_ref, lh_ref, ll_ref, wh_ref, wl_ref)


def factor(kernel, operands, n):
    in_specs = [pl.BlockSpec(memory_space=pltpu.VMEM)] * len(operands)
    scratch = [pltpu.VMEM((n, n), F32)]
    if kernel is unfold_kernel:
        in_specs[0] = pl.BlockSpec(memory_space=pltpu.SMEM)
        scratch.append(pltpu.VMEM((32, *operands[1].shape[1:]), F32))
    return pl.pallas_call(
        kernel,
        out_shape=[jax.ShapeDtypeStruct((n, n), BF)] * 2 + [jax.ShapeDtypeStruct((n, NB), BF)] * 2,
        in_specs=in_specs,
        out_specs=[pl.BlockSpec(memory_space=pltpu.VMEM)] * 4,
        scratch_shapes=scratch,
        compiler_params=pltpu.CompilerParams(vmem_limit_bytes=32 << 20),
        cost_estimate=pl.CostEstimate(flops=5 * 10**10, bytes_accessed=8 << 20, transcendentals=0),
        name="factor",
    )(*operands)


def solve_kernel(place_ref, *refs, corners):
    cover_refs, parts_refs = refs[: len(corners)], refs[len(corners) : -7]
    lh_ref, ll_ref, wh_ref, wl_ref, o_ref, xh_ref, xl_ref = refs[-7:]
    n = o_ref.shape[1]

    def put(rows, cols, value):
        taken = parts_refs[0][parts_refs[0].shape[0] - 1, rows, cols]
        for part in parts_refs[1:]:
            taken = taken + part[part.shape[0] - 1, rows, cols]
        o_ref[rows, cols] = value - taken

    for (row, block), ref in zip(corners, cover_refs):
        rows = slice(row, row + ref.shape[0])
        if block is None:
            put(rows, slice(None), ref[...])
            continue
        for c, s in enumerate(block_order(place_ref[0])[block : block + ref.shape[1] // NB]):
            cols = pl.ds(pl.multiple_of(s * NB, NB), NB)
            put(rows, cols, ref[:, NB * c : NB * c + NB])
    wide = 2 * NB
    inverses = []
    for c in range(0, n, wide):
        upper, lower = slice(c, c + NB), slice(c + NB, c + wide)
        corner = dot3(lh_ref[lower, upper], ll_ref[lower, upper], wh_ref[upper], wl_ref[upper], NN)
        corner = split(-dot3(wh_ref[lower], wl_ref[lower], *split(corner), NN))
        zero = jnp.zeros((NB, NB), BF)
        inverses.append(
            [
                jnp.concatenate(
                    [
                        jnp.concatenate([ref[upper], zero], 1),
                        jnp.concatenate([part, ref[lower]], 1),
                    ],
                    0,
                )
                for ref, part in zip((wh_ref, wl_ref), corner)
            ]
        )
    for c, inverse in zip(range(0, n, wide), inverses):
        here = o_ref[:, c : c + wide]
        if c:
            here = here - dot3(
                xh_ref[:, :c], xl_ref[:, :c], lh_ref[c : c + wide, :c], ll_ref[c : c + wide, :c]
            )
        x = dot3(*split(here), *inverse)
        o_ref[:, c : c + wide] = x
        xh, xl = split(x)
        xh_ref[:, c : c + wide] = xh
        xl_ref[:, c : c + wide] = xl


def solve(place, covers, corners, parts, factors):
    rows, n = parts[0].shape[1:]
    return vmem_call(
        functools.partial(solve_kernel, corners=corners),
        jax.ShapeDtypeStruct((rows, n), F32),
        place,
        [*covers, *parts, *factors],
        [pltpu.VMEM((rows, n), BF)] * 2,
        "solve",
    )


def vmem_call(kernel, out_shape, place, operands, scratch=(), name=None):
    return pl.pallas_call(
        kernel,
        out_shape=out_shape,
        in_specs=[pl.BlockSpec(memory_space=pltpu.SMEM)] * (place is not None)
        + [pl.BlockSpec(memory_space=pltpu.VMEM)] * len(operands),
        out_specs=jax.tree.map(lambda _: pl.BlockSpec(memory_space=pltpu.VMEM), out_shape),
        scratch_shapes=list(scratch),
        compiler_params=pltpu.CompilerParams(vmem_limit_bytes=32 << 20),
        cost_estimate=pl.CostEstimate(flops=10**8, bytes_accessed=1 << 18, transcendentals=0),
        name=name,
    )(*([] if place is None else [place]), *operands)


def fold_products_kernel(place_ref, *refs):
    blocks, shares, total_ref = refs[:4], refs[4:-1], refs[-1]
    own, far, one, two = [split(ref[:NB]) for ref in blocks]
    own_last = makes_own(place_ref[0])
    either = split(jnp.where(own_last, blocks[0][:NB], blocks[1][:NB]))
    pairs = [(own, own), (own, far), (own, one), (far, one), (either, two)]
    for k, (left, right) in enumerate(pairs):
        total_ref[:, NB * k : NB * k + NB] = dot3(*left, *right)
    rows = shares[0].shape[0]
    for m, ref in enumerate(shares):
        first = pl.multiple_of((place_ref[1] ^ m) * rows, rows)
        ref[...] = total_ref[pl.ds(first, rows)]


def gather_split_kernel(place_ref, *refs):
    blocks, (high_ref, low_ref) = blocks_in(refs[:-2]), refs[-2:]
    for s, ref in zip(block_order(place_ref[0]), blocks):
        first = pl.multiple_of(s * NB, NB)
        high, low = split(ref[:NB])
        high_ref[pl.ds(first, NB)] = high
        low_ref[pl.ds(first, NB)] = low


def rest_products_kernel(place_ref, prior_ref, high_ref, low_ref, *refs, turns):
    plus_refs, o_ref = refs[:-1], refs[-1]
    rows = o_ref.shape[1]
    for i, m in enumerate(turns):
        first = pl.multiple_of((place_ref[1] ^ m) * rows, rows)
        own_high, own_low = split(prior_ref[pl.ds(first, rows)])
        for c in range(0, o_ref.shape[2], 2 * NB):
            cols = slice(c, c + 2 * NB)
            total = dot3(own_high, own_low, high_ref[cols], low_ref[cols])
            for plus_ref in plus_refs:
                total = total + plus_ref[i, :, cols]
            o_ref[i, :, cols] = total


def swap(block, axis, bit):
    return lax.ppermute(block, axis, [(i, i ^ bit) for i in range(lax.axis_size(axis))])


def dot_rows(left, right):
    return lax.dot_general(
        left, right, NT, precision=lax.Precision.HIGH, preferred_element_type=F32
    )


def local(pixel_ids, quad_offsets, prior_factor):
    panel_count = lax.axis_size("panel")
    row_count = lax.axis_size("row")
    block_rows = pixel_ids.shape[0]
    quarter_rows = block_rows // panel_count
    per_device = B // (row_count * panel_count)
    span_cols = panel_count * per_device
    row_pos = lax.axis_index("row")
    panel_pos = lax.axis_index("panel")
    device_pos = row_pos * panel_count + panel_pos
    lead = 32

    points = jnp.stack(locate(pixel_ids, quad_offsets))
    count = points.shape[1]
    own_points = lax.dynamic_slice_in_dim(points, panel_pos * quarter_rows, quarter_rows, 2)
    local_points = points.reshape(2, count, panel_count, quarter_rows)[:, :, :, :per_device]
    local_points = local_points.reshape(2, count, span_cols)
    own_prior = prior_factor.reshape(panel_count, quarter_rows, -1)[:, :per_device]
    own_prior = own_prior.reshape(span_cols, -1)
    place = jnp.stack([row_pos, panel_pos]).astype(jnp.int32)
    lines = block_rows * row_count // 256 * 8
    folds = span_cols == NB and row_count == 8 and panel_count == 4 and lines == 256

    if not (folds and 2 * count * NB == 8 * own_prior.shape[1]):
        lead = 32
        row_ids = jnp.arange(lead, dtype=jnp.int32)[:, None]
        col_ids = jnp.arange(B, dtype=jnp.int32)[None, :]
        on_diagonal = (row_ids < per_device) & (col_ids == device_pos * per_device + row_ids)
        unit = jnp.where(on_diagonal, 1.0, 0.0).astype(F32)
        flat = local_points.reshape(1, 2 * count, span_cols)
        copies = jnp.broadcast_to(flat, (row_count, 2 * count, span_cols))
        spread = lax.all_to_all(copies, "row", split_axis=0, concat_axis=0, tiled=True)
        parted = features(own_points, spread.transpose(1, 0, 2).reshape(2, count, B))
        covers = [cover_rows(*parted, i, lead) for i in range(0, quarter_rows, lead)]
        covers[0] = covers[0] + unit
        panel_prior = lax.all_gather(own_prior, "row", axis=0, tiled=True)
        partial = dot_rows(prior_factor, panel_prior)
        parts = lax.all_to_all(
            partial.reshape(panel_count, quarter_rows, B), "panel", split_axis=0, concat_axis=0, tiled=True
        )
        parts = jnp.sum(parts, axis=0)
        mine = covers[0][:per_device] - parts[:per_device]
        diag_rows = lax.all_gather(mine, ("row", "panel"), axis=0, tiled=True)
        corners = [(i * lead, None) for i in range(len(covers))]
        return solve(place, covers, corners, [parts[None]], factor(factor_kernel, (diag_rows,), B))

    def turn(block, k):
        return lax.ppermute(block, "row", [(turned(d, k), d) for d in range(8)])

    own = pack(own_prior, local_points)
    two, one, far = turn(own, 2), turn(own, 1), swap(own, "row", 4)
    table = row_table(own_points, lines)

    def block_cover(held, blocks, start, cols):
        return vmem_call(
            functools.partial(block_cover_kernel, points=count, start=start),
            jax.ShapeDtypeStruct((quarter_rows - start, cols), F32),
            None,
            [*held, *blocks],
            [
                pltpu.VMEM((lines, 8 * cols), BF),
                pltpu.VMEM((1, cols), F32),
                pltpu.VMEM((15, per_device, cols), F32),
            ],
            "cover",
        )

    cover_own = block_cover(table, [own], per_device, NB)
    one, cover_own = lax.optimization_barrier((one, cover_own))
    from_x = swap(one, "row", 1)
    (far, one, two), table, cover_own = lax.optimization_barrier(((far, one, two), table, cover_own))
    shares = vmem_call(
        fold_products_kernel,
        [jax.ShapeDtypeStruct((per_device, 5 * NB), F32)] * 4,
        place,
        [own, far, one, two],
        [pltpu.VMEM((NB, 5 * NB), F32)],
        "fold_products",
    )
    shares, own, far = lax.optimization_barrier((shares, own, far))

    def beside(operands, transfer, work):
        operands, held = lax.optimization_barrier((operands, table))
        return lax.optimization_barrier((transfer(operands), work(operands, held)))

    half = 4 * NB
    east = pltpu.VMEM((15, per_device, half), F32)

    def lead_cover(_, held):
        return vmem_call(
            functools.partial(lead_cover_kernel, points=count),
            [
                jax.ShapeDtypeStruct((per_device, 5 * NB), F32),
                jax.ShapeDtypeStruct((per_device, half), F32),
                jax.ShapeDtypeStruct((lines, 8 * half), BF),
                jax.ShapeDtypeStruct((1, half), F32),
            ],
            place,
            [*held, own, far, one, two],
            [
                east,
                pltpu.VMEM((2, NB, count), F32),
                pltpu.VMEM((NB, 1), F32),
                pltpu.VMEM((8, per_device, 2 * lines), BF),
            ],
            "lead_cover",
        )

    sums, (folded, cover_lead, *counts) = beside(
        shares,
        lambda shares: [swap(share, "panel", m) for m, share in zip((1, 2, 3), shares[1:])],
        lead_cover,
    )
    sums, from_x = lax.optimization_barrier((sums, from_x))
    far_x = swap(far, "row", 1)
    far_z = swap(far, "row", 2)
    shard = folded - (shares[0] + sums[0] + sums[1] + sums[2])

    def rest_part(panel_prior, turns, plus=()):
        return vmem_call(
            functools.partial(rest_products_kernel, turns=turns),
            jax.ShapeDtypeStruct((len(turns), quarter_rows, B), F32),
            place,
            [prior_factor, *panel_prior, *plus],
            name="rest_products",
        )

    def later_cover(held, start, rows):
        return vmem_call(
            functools.partial(later_cover_kernel, points=count, start=start),
            jax.ShapeDtypeStruct((rows, half - NB), F32),
            None,
            [*held, *counts],
            [pltpu.VMEM((15, per_device, half - NB), F32)],
            "cover",
        )

    middle = quarter_rows // 2

    def beside_far_z(_, held):
        rest = [from_x, far_x, far_z, last]
        cover = later_cover(held, middle, quarter_rows - middle)
        cover, blocks = lax.optimization_barrier((cover, rest))
        panel_prior = vmem_call(
            gather_split_kernel,
            [jax.ShapeDtypeStruct((B, own_prior.shape[1]), BF)] * 2,
            place,
            [own, far, one, two, *blocks],
            name="gather_split",
        )
        return cover, panel_prior, rest_part(panel_prior, (3, 1)), rest

    shard = shard[None]
    near_rows, cover_first = beside(
        shard,
        lambda x: swap(x, "row", 2),
        lambda _, held: later_cover(held, per_device, middle - per_device),
    )
    near_rows = jnp.concatenate([shard, near_rows], 0)
    cover_first, from_x, far_x, far_z = lax.optimization_barrier((cover_first, from_x, far_x, far_z))
    last = swap(far_z, "row", 1)
    far_rows, (cover_second, panel_prior, for_core, rest) = beside(
        near_rows, lambda x: swap(x, "row", 4), beside_far_z
    )
    held_rows = jnp.concatenate([near_rows, far_rows], 0)

    def across(x):
        corner = [(i, i ^ 6) for i in range(32)]
        return swap(x, "row", 1), swap(x, "panel", 2), lax.ppermute(x, ("row", "panel"), corner)

    def beside_xy(x, held):
        from_core = swap(for_core, "panel", 1)
        cover = block_cover(held, rest, 0, half)
        part_0, part_2 = rest_part(panel_prior, (0,)), rest_part(panel_prior, (2,), [from_core])
        return cover, part_0, part_2, from_core, swap(x, "panel", 1)

    received, (cover_last, part_0, part_2, from_core, held_there) = beside(
        held_rows, across, beside_xy
    )
    there = [held_there] + [swap(x, "panel", 1) for x in received]
    parts = [part_0, from_core, swap(part_2, "panel", 2)]
    factors = factor(unfold_kernel, (place, held_rows, *received, *there), B)
    covers = [cover_lead, cover_own, cover_first, cover_second, cover_last]
    corners = [(0, 0), (per_device, 0), (per_device, 1), (middle, 1), (0, 4)]
    return solve(place, covers, corners, parts, factors)


def solution(mesh):
    return jax.shard_map(
        local,
        mesh=mesh,
        in_specs=(P("row"), P(None, None, "row"), P("row", "panel")),
        out_specs=P(("row", "panel"), None),
        check_vma=False,
    )
```

```python
import functools

import jax
import jax.numpy as jnp
from jax import lax
from jax.experimental import pallas as pl
from jax.experimental.pallas import tpu as pltpu
from jax.sharding import PartitionSpec as P

B = 1024
NB = 128
NEAR = 4
F32 = jnp.float32
BF = jnp.bfloat16
NT = (((1,), (1,)), ((), ()))
NN = (((1,), (0,)), ((), ()))
SCALE = -1.4426950408889634 / 64.0
CENTRE = 1024.0


def locate(pixel_ids, quad_offsets):
    column = (pixel_ids % 256) * 8
    lines = (pixel_ids // 256) * 8
    east = (column[None, :] + quad_offsets[0]).astype(F32) - CENTRE
    north = (lines[None, :] + quad_offsets[1]).astype(F32) - CENTRE
    return east, north


def pieces(value):
    high = jnp.floor(value * (1.0 / 65536.0)) * 65536.0
    rest = value - high
    mid = jnp.floor(rest * (1.0 / 256.0)) * 256.0
    return [high, mid, rest - mid]


def halves(value):
    high = jnp.floor(value * (1.0 / 128.0)) * 128.0
    return high, value - high


def row_features(x, y):
    xh, xl = halves(x)
    yh, yl = halves(y)
    one = jnp.ones_like(x)
    zero = jnp.zeros_like(x)
    cross = [-2 * xh, -2 * xh, -2 * xl, -2 * xl, -2 * yh, -2 * yh, -2 * yl, -2 * yl]
    return jnp.concatenate(cross + pieces(x * x + y * y) + [one] * 3 + [zero] * 2, 0)


def col_features(x, y):
    xh, xl = halves(x)
    yh, yl = halves(y)
    one = jnp.ones_like(x)
    zero = jnp.zeros_like(x)
    cross = [xh, xl, xh, xl, yh, yl, yh, yl]
    return jnp.concatenate(cross + [one] * 3 + pieces(x * x + y * y) + [zero] * 2, 0)


def feature_kernel(row_ref, col_ref, f_ref, g_ref):
    for a in range(row_ref.shape[1]):
        one = row_features(row_ref[0, a : a + 1, :], row_ref[1, a : a + 1, :])
        f_ref[a] = one.T.astype(BF)
        g_ref[a] = col_features(col_ref[0, a : a + 1, :], col_ref[1, a : a + 1, :]).astype(BF)


def features(row_points, col_points):
    count, rows = row_points.shape[1:]
    cols = col_points.shape[2]
    return pl.pallas_call(
        feature_kernel,
        out_shape=[
            jax.ShapeDtypeStruct((count, rows, 16), BF),
            jax.ShapeDtypeStruct((count, 16, cols), BF),
        ],
        in_specs=[pl.BlockSpec(memory_space=pltpu.VMEM)] * 2,
        out_specs=[pl.BlockSpec(memory_space=pltpu.VMEM)] * 2,
        compiler_params=pltpu.CompilerParams(vmem_limit_bytes=8 << 20),
        name="features",
    )(row_points, col_points)


def cover_kernel(f_ref, g_ref, o_ref):
    count, block = f_ref.shape[:2]
    rows_here = f_ref[...].reshape(count * block, 16)

    def column_point(b, total):
        apart = jnp.dot(rows_here, g_ref[b], preferred_element_type=F32)
        near = jnp.exp2(apart * SCALE)
        for a in range(count):
            total = total + near[a * block : (a + 1) * block]
        return total

    total = lax.fori_loop(0, count, column_point, jnp.zeros(o_ref.shape, F32), unroll=8)
    o_ref[...] = total * (1.0 / (count * count))


def cover_rows(row_part, col_part, first, block):
    count, rows, depth = row_part.shape
    cols = col_part.shape[2]
    index = first // block
    return pl.pallas_call(
        cover_kernel,
        grid=(1,),
        out_shape=jax.ShapeDtypeStruct((block, cols), F32),
        in_specs=[
            pl.BlockSpec((count, block, depth), lambda i: (0, index, 0)),
            pl.BlockSpec((count, depth, cols), lambda i: (0, 0, 0)),
        ],
        out_specs=pl.BlockSpec((block, cols), lambda i: (0, 0)),
        compiler_params=pltpu.CompilerParams(vmem_limit_bytes=16 << 20),
        cost_estimate=pl.CostEstimate(flops=10**8, bytes_accessed=1 << 18, transcendentals=0),
        name="cover",
    )(row_part, col_part)


def table_rows(offset, north, lines):
    line = lax.broadcasted_iota(jnp.int32, (16, lines), 1).astype(F32) - CENTRE
    total = [jnp.zeros((16, lines), F32) for _ in range(8)]
    for a in range(offset.shape[1]):
        apart = jnp.broadcast_to(north[:, a : a + 1], (16, lines)) - line
        near = jnp.exp2(apart * apart * SCALE)
        which = jnp.broadcast_to(offset[:, a : a + 1], (16, lines))
        for p in range(8):
            total[p] = total[p] + jnp.where(which == float(p), near, 0.0)
    return [split(x) for x in total]


def row_table_kernel(row_ref, t_ref, row_cell_ref, place_ref):
    rows = row_ref.shape[2]
    lines = t_ref.shape[2] // 2
    row_cell = jnp.floor(row_ref[0] * 0.125) * 8.0
    place_ref[0] = (row_ref[0] - row_cell).T
    place_ref[1] = row_ref[1].T
    row_cell_ref[...] = row_cell[0:1].T

    def row_tile(index, _):
        here = pl.ds(pl.multiple_of(index * 16, 16), 16)
        for p, (high, low) in enumerate(table_rows(place_ref[0, here], place_ref[1, here], lines)):
            t_ref[p, here, :lines] = high
            t_ref[p, here, lines:] = low
        return 0

    lax.fori_loop(0, rows // 16, row_tile, 0)


def row_table(row_points, lines):
    count, rows = row_points.shape[1:]
    return pl.pallas_call(
        row_table_kernel,
        out_shape=[
            jax.ShapeDtypeStruct((8, rows, 2 * lines), BF),
            jax.ShapeDtypeStruct((rows, 1), F32),
        ],
        in_specs=[pl.BlockSpec(memory_space=pltpu.VMEM)],
        out_specs=[pl.BlockSpec(memory_space=pltpu.VMEM)] * 2,
        scratch_shapes=[pltpu.VMEM((2, rows, count), F32)],
        compiler_params=pltpu.CompilerParams(vmem_limit_bytes=16 << 20),
        cost_estimate=pl.CostEstimate(flops=10**8, bytes_accessed=1 << 18, transcendentals=0),
        name="row_table",
    )(row_points)


def pack(prior, points):
    flat = points.reshape(-1, NB)
    tiles = prior.shape[1] // NB
    extra = flat.reshape(tiles, flat.shape[0] // tiles, NB).transpose(1, 0, 2)
    return jnp.concatenate([prior, extra.reshape(-1, prior.shape[1])], 0)


def unpack(block_ref):
    extra = block_ref.shape[0] - NB
    tiles = block_ref.shape[1] // NB
    flat = jnp.concatenate(
        [block_ref[NB : NB + extra, NB * t : NB * t + NB] for t in range(tiles)], 0
    )
    count = flat.shape[0] // 2
    return flat[:count], flat[count:]


def column_counts(block_ref, h_ref, at, stride):
    east, north = unpack(block_ref)
    lines = h_ref.shape[0]
    cell = jnp.floor(east[0:1] * 0.125) * 8.0
    line = jnp.floor(north[0:1] * 0.125) * 8.0
    east, north = east - cell, north - line
    sub = lax.broadcasted_iota(jnp.int32, (8, NB), 0).astype(F32)
    held = [jnp.zeros((8, NB), F32) for _ in range(8)]
    for b in range(east.shape[0]):
        one = jnp.where(sub == jnp.broadcast_to(north[b : b + 1], (8, NB)), 1.0, 0.0)
        which = jnp.broadcast_to(east[b : b + 1], (8, NB))
        for q in range(8):
            held[q] = held[q] + jnp.where(which == float(q), one, 0.0)
    line = jnp.broadcast_to(line, (8, NB))
    for r in range(0, lines, 16):
        low = line == float(r) - CENTRE
        high = line == float(r + 8) - CENTRE
        for q in range(8):
            pair = [jnp.where(low, held[q], 0.0), jnp.where(high, held[q], 0.0)]
            lanes = slice(q * stride + at, q * stride + at + NB)
            h_ref[r : r + 16, lanes] = jnp.concatenate(pair, 0).astype(BF)
    return cell


def cover_chunk(table, row_cell, col_cell, h_ref, east_ref, points):
    chunk, cols = east_ref.shape[1:]
    stride = h_ref.shape[1] // 8
    together = 1 + (cols % (2 * NB) > 0)
    cell = jnp.broadcast_to(row_cell, (chunk, cols)) - col_cell
    for t in range(15):
        apart = cell + float(t - 7)
        east_ref[t] = jnp.exp2(apart * apart * SCALE)
    table = table.reshape(8 * chunk, table.shape[2])
    total = jnp.zeros((chunk, cols), F32)
    for first in range(0, 8, together):
        offsets = range(first, first + together)
        counts = [h_ref[:, (q + 1) * stride - cols : (q + 1) * stride] for q in offsets]
        counts = jnp.concatenate(counts, 1)
        part = jnp.dot(table, jnp.concatenate([counts, counts], 0), preferred_element_type=F32)
        for p in range(8):
            for i, q in enumerate(offsets):
                piece = part[p * chunk : (p + 1) * chunk, i * cols : (i + 1) * cols]
                total = total + piece * east_ref[p - q + 7]
    return total * (1.0 / (points * points))


def lead_cover_kernel(
    place_ref, t_ref, row_cell_ref, *refs, points
):
    blocks, refs = refs[:4], refs[4:]
    folded_ref, own_ref, h_ref, col_cell_ref, east_ref, far_east_ref = refs[:6]
    far_ref, far_cell_ref, far_table_ref = refs[6:]
    rows, cols = own_ref.shape
    lines = h_ref.shape[0]
    cells = [column_counts(ref, h_ref, NB * i, cols) for i, ref in enumerate(blocks)]
    col_cell = jnp.concatenate(cells, 1)
    col_cell_ref[...] = col_cell

    east, north = unpack(blocks[1])
    far_ref[0] = (east - cells[1]).T
    far_ref[1] = north.T
    far_cell_ref[...] = cells[1].T
    first = pl.multiple_of(place_ref[1] * rows, rows)
    for r in range(0, rows, 16):
        here = pl.ds(first + r, 16)
        for p, (high, low) in enumerate(table_rows(far_ref[0, here], far_ref[1, here], lines)):
            far_table_ref[p, r : r + 16, :lines] = high
            far_table_ref[p, r : r + 16, lines:] = low

    mine = cover_chunk(t_ref[:, :rows], row_cell_ref[:rows], col_cell, h_ref, east_ref, points)
    row = lax.broadcasted_iota(jnp.int32, (rows, cols), 0)
    col = lax.broadcasted_iota(jnp.int32, (rows, cols), 1)
    mine = mine + jnp.where(col == first + row, 1.0, 0.0)
    own_ref[...] = mine
    far = cover_chunk(
        far_table_ref[...],
        far_cell_ref[pl.ds(first, rows)],
        col_cell[:, 2 * NB :],
        h_ref,
        far_east_ref,
        points,
    )
    folded_ref[:, : 3 * NB] = mine[:, : 3 * NB]
    folded_ref[:, 3 * NB : 4 * NB] = far[:, :NB]
    own_last = makes_own(place_ref[0])
    folded_ref[:, 4 * NB :] = jnp.where(own_last, mine[:, 3 * NB :], far[:, NB:])


def later_cover_kernel(t_ref, row_cell_ref, h_ref, col_cell_ref, o_ref, east_ref, *, points, start):
    chunk, cols = east_ref.shape[1:]
    col_cell = col_cell_ref[:, col_cell_ref.shape[1] - cols :]

    def row_chunk(index, _):
        first = pl.multiple_of(index * chunk, chunk)
        here = pl.ds(pl.multiple_of(first + start, chunk), chunk)
        o_ref[pl.ds(first, chunk)] = cover_chunk(
            t_ref[:, here], row_cell_ref[here], col_cell, h_ref, east_ref, points
        )
        return 0

    lax.fori_loop(0, o_ref.shape[0] // chunk, row_chunk, 0)


def block_cover_kernel(t_ref, row_cell_ref, *refs, points, start):
    blocks, (o_ref, h_ref, col_cell_ref, east_ref) = blocks_in(refs[:-4]), refs[-4:]
    cells = [
        column_counts(ref, h_ref, NB * i, o_ref.shape[1]) for i, ref in enumerate(blocks)
    ]
    col_cell_ref[...] = jnp.concatenate(cells, 1)
    later_cover_kernel(
        t_ref, row_cell_ref, h_ref, col_cell_ref, o_ref, east_ref, points=points, start=start
    )


def inverse_factor(tiles):
    n = len(tiles)
    width = 8 * n
    lane = lax.broadcasted_iota(jnp.int32, (8, width), 1)
    sub = lax.broadcasted_iota(jnp.int32, (8, width), 0)
    tiles = list(tiles)
    out = []

    def spread(x):
        return jnp.broadcast_to(x, (8, width))

    def lanes(tile, v):
        return [spread(tile[:, 8 * v + q : 8 * v + q + 1]) for q in range(8)]

    following = lanes(tiles[0], 0)
    for v in range(n):
        near = min(n, v + NEAR)
        cols = {v: following}
        if v + 1 < n:
            cols[v] = cols[v] + lanes(tiles[v], v + 1)
            cols[v + 1] = lanes(tiles[v + 1], v) + lanes(tiles[v + 1], v + 1)
        for r in range(v + 2, near):
            cols[r] = lanes(tiles[r], v)
        here = (lane >= 8 * v) & (lane < 8 * v + 8)
        for r in range(v + 1, n):
            tiles[r] = jnp.where(here, 0.0, tiles[r])
        tiles[v] = jnp.where(here, jnp.where(lane == sub + 8 * v, 1.0, 0.0), tiles[v])
        pivots = jnp.ones((8, width), F32)
        for s in range(8):
            head = cols[v]
            pivot = spread(head[s][s : s + 1])
            inverse = 1.0 / pivot
            pivots = jnp.where(sub == s, pivot, pivots)
            row = spread(tiles[v][s : s + 1])
            heads = [spread(head[k][s : s + 1]) for k in range(s + 1, len(head))]
            for r in range(v, near):
                part = cols[r][s] * inverse
                if r == v:
                    part = jnp.where(sub > s, part, 0.0)
                tiles[r] = tiles[r] - part * row
                for k in range(s + 1, len(cols[r])):
                    cols[r][k] = cols[r][k] - part * heads[k - s - 1]
        if v + 1 < n:
            following = cols[v + 1][8:]
        rows = tiles[v] * lax.rsqrt(pivots)
        if near < n:
            high = rows.astype(BF).astype(F32)
            low = rows - high
            left = jnp.concatenate([high, high, low, low], 0).astype(BF)
            right = jnp.concatenate([high, low, high, low], 0).astype(BF)
            update = lax.dot_general(
                left, right, (((0,), (0,)), ((), ())), preferred_element_type=F32
            )
            for r in range(near, n):
                tiles[r] = tiles[r] - update[8 * r : 8 * r + 8]
        out.append(jnp.where(lane <= sub + 8 * v, rows, 0.0))
    return jnp.concatenate(out, 0)


def split(x):
    high = x.astype(BF)
    return high, (x - high.astype(F32)).astype(BF)


def dot3(ah, al, bh, bl, numbers=NT):
    dot = functools.partial(lax.dot_general, dimension_numbers=numbers, preferred_element_type=F32)
    return dot(ah, bh) + (dot(ah, bl) + dot(al, bh))


def factor_blocks(a_ref, lh_ref, ll_ref, wh_ref, wl_ref):
    n = a_ref.shape[0]
    blocks = n // NB

    def column(first):
        end = first + NB
        bh, bl = split(a_ref[end:, first:end])
        high, low = split(dot3(bh, bl, wh_ref[first:end], wl_ref[first:end]))
        lh_ref[end:, first:end] = high
        ll_ref[end:, first:end] = low
        a_ref[end:, end : end + NB] = a_ref[end:, end : end + NB] - dot3(
            lh_ref[end:, :end],
            ll_ref[end:, :end],
            lh_ref[end : end + NB, :end],
            ll_ref[end : end + NB, :end],
        )

    def step(j, _):
        c = pl.multiple_of(j * NB, NB)
        tiles = [a_ref[pl.ds(c + 8 * v, 8), pl.ds(c, NB)] for v in range(NB // 8)]
        wh, wl = split(inverse_factor(tiles))
        wh_ref[pl.ds(c, NB)] = wh
        wl_ref[pl.ds(c, NB)] = wl
        for block in range(blocks - 1):
            pl.when(j == block)(functools.partial(column, block * NB))
        return 0

    lax.fori_loop(0, blocks, step, 0)


def factor_kernel(diag_ref, lh_ref, ll_ref, wh_ref, wl_ref, a_ref):
    a_ref[...] = diag_ref[...]
    factor_blocks(a_ref, lh_ref, ll_ref, wh_ref, wl_ref)


def turned(r, k):
    at = ((r & 1) << 1 | (r >> 1) & 1) + k
    return (r & 4) | (at & 1) << 1 | (at >> 1) & 1


def block_order(r):
    return [r, r ^ 4, turned(r, 1), turned(r, 2), turned(r, 3), r ^ 5, r ^ 6, r ^ 7]


def makes_own(r):
    return (r & 1) == 0


def folded_blocks(r):
    order = block_order(r)
    either = jnp.where(makes_own(r), r, r ^ 4)
    return [(r, r), (r, order[1]), (r, order[2]), (order[1], order[2]), (either, order[3])]


def blocks_in(refs):
    return [
        ref.at[first : first + ref.shape[0] // parts]
        for ref in refs
        for parts in [1 + (ref.shape[0] >= 2 * NB)]
        for first in range(0, ref.shape[0], ref.shape[0] // parts)
    ]


def unfold_kernel(place_ref, *refs):
    pieces_refs, (lh_ref, ll_ref, wh_ref, wl_ref, a_ref, g_ref) = refs[:8], refs[8:]
    row_pos = place_ref[0]
    panel_pos = place_ref[1]
    for i, ref in enumerate(pieces_refs):
        g_ref[4 * i : 4 * i + 4] = ref[...]

    def rows_of(r, _):
        away = r ^ row_pos
        slot = (away >> 1) | ((away & 1) << 2)
        ats = []
        for p in range(4):
            gone = p ^ panel_pos
            ats.append(slot | ((gone >> 1) << 3) | ((gone & 1) << 4))
        for k, (rows, cols) in enumerate(folded_blocks(r)):
            block = jnp.concatenate([g_ref[at, :, NB * k : NB * k + NB] for at in ats], 0)
            rr = pl.multiple_of(rows * NB, NB)
            cc = pl.multiple_of(cols * NB, NB)

            @pl.when(rows >= cols)
            def _():
                a_ref[pl.ds(rr, NB), pl.ds(cc, NB)] = block

            if k:

                @pl.when(rows < cols)
                def _():
                    a_ref[pl.ds(cc, NB), pl.ds(rr, NB)] = block.T

        return 0

    lax.fori_loop(0, 8, rows_of, 0)
    factor_blocks(a_ref, lh_ref, ll_ref, wh_ref, wl_ref)


def factor(kernel, operands, n):
    in_specs = [pl.BlockSpec(memory_space=pltpu.VMEM)] * len(operands)
    scratch = [pltpu.VMEM((n, n), F32)]
    if kernel is unfold_kernel:
        in_specs[0] = pl.BlockSpec(memory_space=pltpu.SMEM)
        scratch.append(pltpu.VMEM((32, *operands[1].shape[1:]), F32))
    return pl.pallas_call(
        kernel,
        out_shape=[jax.ShapeDtypeStruct((n, n), BF)] * 2 + [jax.ShapeDtypeStruct((n, NB), BF)] * 2,
        in_specs=in_specs,
        out_specs=[pl.BlockSpec(memory_space=pltpu.VMEM)] * 4,
        scratch_shapes=scratch,
        compiler_params=pltpu.CompilerParams(vmem_limit_bytes=32 << 20),
        cost_estimate=pl.CostEstimate(flops=5 * 10**10, bytes_accessed=8 << 20, transcendentals=0),
        name="factor",
    )(*operands)


def solve_kernel(place_ref, *refs, corners):
    cover_refs, parts_refs = refs[: len(corners)], refs[len(corners) : -7]
    lh_ref, ll_ref, wh_ref, wl_ref, o_ref, xh_ref, xl_ref = refs[-7:]
    n = o_ref.shape[1]

    def put(rows, cols, value):
        taken = parts_refs[0][parts_refs[0].shape[0] - 1, rows, cols]
        for part in parts_refs[1:]:
            taken = taken + part[part.shape[0] - 1, rows, cols]
        o_ref[rows, cols] = value - taken

    for (row, block), ref in zip(corners, cover_refs):
        rows = slice(row, row + ref.shape[0])
        if block is None:
            put(rows, slice(None), ref[...])
            continue
        for c, s in enumerate(block_order(place_ref[0])[block : block + ref.shape[1] // NB]):
            cols = pl.ds(pl.multiple_of(s * NB, NB), NB)
            put(rows, cols, ref[:, NB * c : NB * c + NB])
    wide = 2 * NB
    inverses = []
    for c in range(0, n, wide):
        upper, lower = slice(c, c + NB), slice(c + NB, c + wide)
        corner = dot3(lh_ref[lower, upper], ll_ref[lower, upper], wh_ref[upper], wl_ref[upper], NN)
        corner = split(-dot3(wh_ref[lower], wl_ref[lower], *split(corner), NN))
        zero = jnp.zeros((NB, NB), BF)
        inverses.append(
            [
                jnp.concatenate(
                    [
                        jnp.concatenate([ref[upper], zero], 1),
                        jnp.concatenate([part, ref[lower]], 1),
                    ],
                    0,
                )
                for ref, part in zip((wh_ref, wl_ref), corner)
            ]
        )
    for c, inverse in zip(range(0, n, wide), inverses):
        here = o_ref[:, c : c + wide]
        if c:
            here = here - dot3(
                xh_ref[:, :c], xl_ref[:, :c], lh_ref[c : c + wide, :c], ll_ref[c : c + wide, :c]
            )
        x = dot3(*split(here), *inverse)
        o_ref[:, c : c + wide] = x
        xh, xl = split(x)
        xh_ref[:, c : c + wide] = xh
        xl_ref[:, c : c + wide] = xl


def solve(place, covers, corners, parts, factors):
    rows, n = parts[0].shape[1:]
    return vmem_call(
        functools.partial(solve_kernel, corners=corners),
        jax.ShapeDtypeStruct((rows, n), F32),
        place,
        [*covers, *parts, *factors],
        [pltpu.VMEM((rows, n), BF)] * 2,
        "solve",
    )


def vmem_call(kernel, out_shape, place, operands, scratch=(), name=None):
    return pl.pallas_call(
        kernel,
        out_shape=out_shape,
        in_specs=[pl.BlockSpec(memory_space=pltpu.SMEM)] * (place is not None)
        + [pl.BlockSpec(memory_space=pltpu.VMEM)] * len(operands),
        out_specs=jax.tree.map(lambda _: pl.BlockSpec(memory_space=pltpu.VMEM), out_shape),
        scratch_shapes=list(scratch),
        compiler_params=pltpu.CompilerParams(vmem_limit_bytes=32 << 20),
        cost_estimate=pl.CostEstimate(flops=10**8, bytes_accessed=1 << 18, transcendentals=0),
        name=name,
    )(*([] if place is None else [place]), *operands)


def fold_products_kernel(place_ref, *refs):
    blocks, shares, total_ref = refs[:4], refs[4:-1], refs[-1]
    own, far, one, two = [split(ref[:NB]) for ref in blocks]
    own_last = makes_own(place_ref[0])
    either = split(jnp.where(own_last, blocks[0][:NB], blocks[1][:NB]))
    pairs = [(own, own), (own, far), (own, one), (far, one), (either, two)]
    for k, (left, right) in enumerate(pairs):
        total_ref[:, NB * k : NB * k + NB] = dot3(*left, *right)
    rows = shares[0].shape[0]
    for m, ref in enumerate(shares):
        first = pl.multiple_of((place_ref[1] ^ m) * rows, rows)
        ref[...] = total_ref[pl.ds(first, rows)]


def gather_split_kernel(place_ref, *refs):
    blocks, (high_ref, low_ref) = blocks_in(refs[:-2]), refs[-2:]
    for s, ref in zip(block_order(place_ref[0]), blocks):
        first = pl.multiple_of(s * NB, NB)
        high, low = split(ref[:NB])
        high_ref[pl.ds(first, NB)] = high
        low_ref[pl.ds(first, NB)] = low


def rest_products_kernel(place_ref, prior_ref, high_ref, low_ref, *refs, turns, outs):
    plus_refs, members = refs[:-outs], [ref.at[i] for ref in refs[-outs:] for i in range(ref.shape[0])]
    for m, o_ref in zip(turns, members):
        rows = o_ref.shape[0]
        first = pl.multiple_of((place_ref[1] ^ m) * rows, rows)
        own_high, own_low = split(prior_ref[pl.ds(first, rows)])
        for c in range(0, o_ref.shape[1], 2 * NB):
            cols = slice(c, c + 2 * NB)
            total = dot3(own_high, own_low, high_ref[cols], low_ref[cols])
            if m == turns[-1]:
                for plus_ref in plus_refs:
                    total = total + plus_ref[0, :, cols]
            o_ref[:, cols] = total


def swap(block, axis, bit):
    return lax.ppermute(block, axis, [(i, i ^ bit) for i in range(lax.axis_size(axis))])


def dot_rows(left, right):
    return lax.dot_general(
        left, right, NT, precision=lax.Precision.HIGH, preferred_element_type=F32
    )


def local(pixel_ids, quad_offsets, prior_factor):
    panel_count = lax.axis_size("panel")
    row_count = lax.axis_size("row")
    block_rows = pixel_ids.shape[0]
    quarter_rows = block_rows // panel_count
    per_device = B // (row_count * panel_count)
    span_cols = panel_count * per_device
    row_pos = lax.axis_index("row")
    panel_pos = lax.axis_index("panel")
    device_pos = row_pos * panel_count + panel_pos
    lead = 32

    points = jnp.stack(locate(pixel_ids, quad_offsets))
    count = points.shape[1]
    own_points = lax.dynamic_slice_in_dim(points, panel_pos * quarter_rows, quarter_rows, 2)
    local_points = points.reshape(2, count, panel_count, quarter_rows)[:, :, :, :per_device]
    local_points = local_points.reshape(2, count, span_cols)
    own_prior = prior_factor.reshape(panel_count, quarter_rows, -1)[:, :per_device]
    own_prior = own_prior.reshape(span_cols, -1)
    place = jnp.stack([row_pos, panel_pos]).astype(jnp.int32)
    lines = block_rows * row_count // 256 * 8
    folds = span_cols == NB and row_count == 8 and panel_count == 4 and lines == 256

    if not (folds and 2 * count * NB == 8 * own_prior.shape[1]):
        lead = 32
        row_ids = jnp.arange(lead, dtype=jnp.int32)[:, None]
        col_ids = jnp.arange(B, dtype=jnp.int32)[None, :]
        on_diagonal = (row_ids < per_device) & (col_ids == device_pos * per_device + row_ids)
        unit = jnp.where(on_diagonal, 1.0, 0.0).astype(F32)
        flat = local_points.reshape(1, 2 * count, span_cols)
        copies = jnp.broadcast_to(flat, (row_count, 2 * count, span_cols))
        spread = lax.all_to_all(copies, "row", split_axis=0, concat_axis=0, tiled=True)
        parted = features(own_points, spread.transpose(1, 0, 2).reshape(2, count, B))
        covers = [cover_rows(*parted, i, lead) for i in range(0, quarter_rows, lead)]
        covers[0] = covers[0] + unit
        panel_prior = lax.all_gather(own_prior, "row", axis=0, tiled=True)
        partial = dot_rows(prior_factor, panel_prior)
        parts = lax.all_to_all(
            partial.reshape(panel_count, quarter_rows, B), "panel", split_axis=0, concat_axis=0, tiled=True
        )
        parts = jnp.sum(parts, axis=0)
        mine = covers[0][:per_device] - parts[:per_device]
        diag_rows = lax.all_gather(mine, ("row", "panel"), axis=0, tiled=True)
        corners = [(i * lead, None) for i in range(len(covers))]
        return solve(place, covers, corners, [parts[None]], factor(factor_kernel, (diag_rows,), B))

    def turn(block, k):
        return lax.ppermute(block, "row", [(turned(d, k), d) for d in range(8)])

    own = pack(own_prior, local_points)
    two, one, far = turn(own, 2), turn(own, 1), swap(own, "row", 4)
    table = row_table(own_points, lines)

    def block_cover(held, blocks, start, cols):
        return vmem_call(
            functools.partial(block_cover_kernel, points=count, start=start),
            jax.ShapeDtypeStruct((quarter_rows - start, cols), F32),
            None,
            [*held, *blocks],
            [
                pltpu.VMEM((lines, 8 * cols), BF),
                pltpu.VMEM((1, cols), F32),
                pltpu.VMEM((15, per_device, cols), F32),
            ],
            "cover",
        )

    cover_own = block_cover(table, [own], per_device, NB)
    one, cover_own = lax.optimization_barrier((one, cover_own))
    from_x = swap(one, "row", 1)
    (far, one, two), table, cover_own = lax.optimization_barrier(((far, one, two), table, cover_own))
    shares = vmem_call(
        fold_products_kernel,
        [jax.ShapeDtypeStruct((per_device, 5 * NB), F32)] * 4,
        place,
        [own, far, one, two],
        [pltpu.VMEM((NB, 5 * NB), F32)],
        "fold_products",
    )
    shares, own, far = lax.optimization_barrier((shares, own, far))

    def beside(operands, transfer, work):
        operands, held = lax.optimization_barrier((operands, table))
        return lax.optimization_barrier((transfer(operands), work(operands, held)))

    half = 4 * NB

    def lead_cover(_, held):
        return vmem_call(
            functools.partial(lead_cover_kernel, points=count),
            [
                jax.ShapeDtypeStruct((per_device, 5 * NB), F32),
                jax.ShapeDtypeStruct((per_device, half), F32),
                jax.ShapeDtypeStruct((lines, 8 * half), BF),
                jax.ShapeDtypeStruct((1, half), F32),
            ],
            place,
            [*held, own, far, one, two],
            [
                pltpu.VMEM((15, per_device, half), F32),
                pltpu.VMEM((15, per_device, 2 * NB), F32),
                pltpu.VMEM((2, NB, count), F32),
                pltpu.VMEM((NB, 1), F32),
                pltpu.VMEM((8, per_device, 2 * lines), BF),
            ],
            "lead_cover",
        )

    sums, (folded, cover_lead, *counts) = beside(
        shares,
        lambda shares: [swap(share, "panel", m) for m, share in zip((1, 2, 3), shares[1:])],
        lead_cover,
    )
    sums, from_x = lax.optimization_barrier((sums, from_x))
    far_x = swap(far, "row", 1)
    far_z = swap(far, "row", 2)
    shard = folded - (shares[0] + sums[0] + sums[1] + sums[2])

    def rest_part(panel_prior, turns, members, plus=()):
        return vmem_call(
            functools.partial(rest_products_kernel, turns=turns, outs=len(members)),
            [jax.ShapeDtypeStruct((n, quarter_rows, B), F32) for n in members],
            place,
            [prior_factor, *panel_prior, *plus],
            name="rest_products",
        )

    def later_cover(held, start, rows):
        return vmem_call(
            functools.partial(later_cover_kernel, points=count, start=start),
            jax.ShapeDtypeStruct((rows, half - NB), F32),
            None,
            [*held, *counts],
            [pltpu.VMEM((15, per_device, half - NB), F32)],
            "cover",
        )

    middle = quarter_rows // 2

    def beside_far_z(_, held):
        held, arrived = lax.optimization_barrier((held, far_x))
        rest = [from_x, arrived, far_z, last]
        cover = later_cover(held, middle, quarter_rows - middle)
        cover, blocks = lax.optimization_barrier((cover, rest))
        panel_prior = vmem_call(
            gather_split_kernel,
            [jax.ShapeDtypeStruct((B, own_prior.shape[1]), BF)] * 2,
            place,
            [own, far, one, two, *blocks],
            name="gather_split",
        )
        return cover, panel_prior, rest_part(panel_prior, (3, 1), (2,))[0], rest

    shard = shard[None]
    near_rows, cover_first = beside(
        shard,
        lambda x: swap(x, "row", 2),
        lambda _, held: later_cover(held, per_device, middle - per_device),
    )
    near_rows = jnp.concatenate([shard, near_rows], 0)
    cover_first, from_x, far_z = lax.optimization_barrier((cover_first, from_x, far_z))
    last = swap(far_z, "row", 1)
    far_rows, (cover_second, panel_prior, for_core, rest) = beside(
        near_rows, lambda x: swap(x, "row", 4), beside_far_z
    )
    held_rows = jnp.concatenate([near_rows, far_rows], 0)

    def across(x):
        corner = [(i, i ^ 6) for i in range(32)]
        return swap(x, "row", 1), swap(x, "panel", 2), lax.ppermute(x, ("row", "panel"), corner)

    def beside_xy(x, held):
        from_core = swap(for_core, "panel", 1)
        cover = block_cover(held, rest, 0, half)
        part_0, part_2 = rest_part(panel_prior, (0, 2), (1, 1), [from_core])
        return cover, part_0, part_2, from_core, swap(x, "panel", 1)

    received, (cover_last, part_0, part_2, from_core, held_there) = beside(
        held_rows, across, beside_xy
    )
    there = [held_there] + [swap(x, "panel", 1) for x in received]
    parts = [part_0, from_core, swap(part_2, "panel", 2)]
    factors = factor(unfold_kernel, (place, held_rows, *received, *there), B)
    covers = [cover_lead, cover_own, cover_first, cover_second, cover_last]
    corners = [(0, 0), (per_device, 0), (per_device, 1), (middle, 1), (0, 4)]
    return solve(place, covers, corners, parts, factors)


def solution(mesh):
    return jax.shard_map(
        local,
        mesh=mesh,
        in_specs=(P("row"), P(None, None, "row"), P("row", "panel")),
        out_specs=P(("row", "panel"), None),
        check_vma=False,
    )
```

```python
import functools

import jax
import jax.numpy as jnp
from jax import lax
from jax.experimental import pallas as pl
from jax.experimental.pallas import tpu as pltpu
from jax.sharding import PartitionSpec as P

B = 1024
NB = 128
NEAR = 4
F32 = jnp.float32
BF = jnp.bfloat16
NT = (((1,), (1,)), ((), ()))
NN = (((1,), (0,)), ((), ()))
SCALE = -1.4426950408889634 / 64.0
CENTRE = 1024.0


def locate(pixel_ids, quad_offsets):
    column = (pixel_ids % 256) * 8
    lines = (pixel_ids // 256) * 8
    east = (column[None, :] + quad_offsets[0]).astype(F32) - CENTRE
    north = (lines[None, :] + quad_offsets[1]).astype(F32) - CENTRE
    return east, north


def pieces(value):
    high = jnp.floor(value * (1.0 / 65536.0)) * 65536.0
    rest = value - high
    mid = jnp.floor(rest * (1.0 / 256.0)) * 256.0
    return [high, mid, rest - mid]


def halves(value):
    high = jnp.floor(value * (1.0 / 128.0)) * 128.0
    return high, value - high


def row_features(x, y):
    xh, xl = halves(x)
    yh, yl = halves(y)
    one = jnp.ones_like(x)
    zero = jnp.zeros_like(x)
    cross = [-2 * xh, -2 * xh, -2 * xl, -2 * xl, -2 * yh, -2 * yh, -2 * yl, -2 * yl]
    return jnp.concatenate(cross + pieces(x * x + y * y) + [one] * 3 + [zero] * 2, 0)


def col_features(x, y):
    xh, xl = halves(x)
    yh, yl = halves(y)
    one = jnp.ones_like(x)
    zero = jnp.zeros_like(x)
    cross = [xh, xl, xh, xl, yh, yl, yh, yl]
    return jnp.concatenate(cross + [one] * 3 + pieces(x * x + y * y) + [zero] * 2, 0)


def feature_kernel(row_ref, col_ref, f_ref, g_ref):
    for a in range(row_ref.shape[1]):
        one = row_features(row_ref[0, a : a + 1, :], row_ref[1, a : a + 1, :])
        f_ref[a] = one.T.astype(BF)
        g_ref[a] = col_features(col_ref[0, a : a + 1, :], col_ref[1, a : a + 1, :]).astype(BF)


def features(row_points, col_points):
    count, rows = row_points.shape[1:]
    cols = col_points.shape[2]
    return pl.pallas_call(
        feature_kernel,
        out_shape=[
            jax.ShapeDtypeStruct((count, rows, 16), BF),
            jax.ShapeDtypeStruct((count, 16, cols), BF),
        ],
        in_specs=[pl.BlockSpec(memory_space=pltpu.VMEM)] * 2,
        out_specs=[pl.BlockSpec(memory_space=pltpu.VMEM)] * 2,
        compiler_params=pltpu.CompilerParams(vmem_limit_bytes=8 << 20),
        name="features",
    )(row_points, col_points)


def cover_kernel(f_ref, g_ref, o_ref):
    count, block = f_ref.shape[:2]
    rows_here = f_ref[...].reshape(count * block, 16)

    def column_point(b, total):
        apart = jnp.dot(rows_here, g_ref[b], preferred_element_type=F32)
        near = jnp.exp2(apart * SCALE)
        for a in range(count):
            total = total + near[a * block : (a + 1) * block]
        return total

    total = lax.fori_loop(0, count, column_point, jnp.zeros(o_ref.shape, F32), unroll=8)
    o_ref[...] = total * (1.0 / (count * count))


def cover_rows(row_part, col_part, first, block):
    count, rows, depth = row_part.shape
    cols = col_part.shape[2]
    index = first // block
    return pl.pallas_call(
        cover_kernel,
        grid=(1,),
        out_shape=jax.ShapeDtypeStruct((block, cols), F32),
        in_specs=[
            pl.BlockSpec((count, block, depth), lambda i: (0, index, 0)),
            pl.BlockSpec((count, depth, cols), lambda i: (0, 0, 0)),
        ],
        out_specs=pl.BlockSpec((block, cols), lambda i: (0, 0)),
        compiler_params=pltpu.CompilerParams(vmem_limit_bytes=16 << 20),
        cost_estimate=pl.CostEstimate(flops=10**8, bytes_accessed=1 << 18, transcendentals=0),
        name="cover",
    )(row_part, col_part)


def table_rows(offset, north, lines):
    line = lax.broadcasted_iota(jnp.int32, (16, lines), 1).astype(F32) - CENTRE
    total = [jnp.zeros((16, lines), F32) for _ in range(8)]
    for a in range(offset.shape[1]):
        apart = jnp.broadcast_to(north[:, a : a + 1], (16, lines)) - line
        near = jnp.exp2(apart * apart * SCALE)
        which = jnp.broadcast_to(offset[:, a : a + 1], (16, lines))
        for p in range(8):
            total[p] = total[p] + jnp.where(which == float(p), near, 0.0)
    return [split(x) for x in total]


def row_table_kernel(row_ref, t_ref, row_cell_ref, place_ref):
    rows = row_ref.shape[2]
    lines = t_ref.shape[2] // 2
    row_cell = jnp.floor(row_ref[0] * 0.125) * 8.0
    place_ref[0] = (row_ref[0] - row_cell).T
    place_ref[1] = row_ref[1].T
    row_cell_ref[...] = row_cell[0:1].T

    def row_tile(index, _):
        here = pl.ds(pl.multiple_of(index * 16, 16), 16)
        for p, (high, low) in enumerate(table_rows(place_ref[0, here], place_ref[1, here], lines)):
            t_ref[p, here, :lines] = high
            t_ref[p, here, lines:] = low
        return 0

    lax.fori_loop(0, rows // 16, row_tile, 0)


def row_table(row_points, lines):
    count, rows = row_points.shape[1:]
    return pl.pallas_call(
        row_table_kernel,
        out_shape=[
            jax.ShapeDtypeStruct((8, rows, 2 * lines), BF),
            jax.ShapeDtypeStruct((rows, 1), F32),
        ],
        in_specs=[pl.BlockSpec(memory_space=pltpu.VMEM)],
        out_specs=[pl.BlockSpec(memory_space=pltpu.VMEM)] * 2,
        scratch_shapes=[pltpu.VMEM((2, rows, count), F32)],
        compiler_params=pltpu.CompilerParams(vmem_limit_bytes=16 << 20),
        cost_estimate=pl.CostEstimate(flops=10**8, bytes_accessed=1 << 18, transcendentals=0),
        name="row_table",
    )(row_points)


def pack(prior, points):
    flat = points.reshape(-1, NB)
    tiles = prior.shape[1] // NB
    extra = flat.reshape(tiles, flat.shape[0] // tiles, NB).transpose(1, 0, 2)
    return jnp.concatenate([prior, extra.reshape(-1, prior.shape[1])], 0)


def unpack(block_ref):
    extra = block_ref.shape[0] - NB
    tiles = block_ref.shape[1] // NB
    flat = jnp.concatenate(
        [block_ref[NB : NB + extra, NB * t : NB * t + NB] for t in range(tiles)], 0
    )
    count = flat.shape[0] // 2
    return flat[:count], flat[count:]


def column_counts(block_ref, h_ref, at, stride):
    east, north = unpack(block_ref)
    lines = h_ref.shape[0]
    cell = jnp.floor(east[0:1] * 0.125) * 8.0
    line = jnp.floor(north[0:1] * 0.125) * 8.0
    east, north = east - cell, north - line
    sub = lax.broadcasted_iota(jnp.int32, (8, NB), 0).astype(F32)
    held = [jnp.zeros((8, NB), F32) for _ in range(8)]
    for b in range(east.shape[0]):
        one = jnp.where(sub == jnp.broadcast_to(north[b : b + 1], (8, NB)), 1.0, 0.0)
        which = jnp.broadcast_to(east[b : b + 1], (8, NB))
        for q in range(8):
            held[q] = held[q] + jnp.where(which == float(q), one, 0.0)
    line = jnp.broadcast_to(line, (8, NB))
    for r in range(0, lines, 16):
        low = line == float(r) - CENTRE
        high = line == float(r + 8) - CENTRE
        for q in range(8):
            pair = [jnp.where(low, held[q], 0.0), jnp.where(high, held[q], 0.0)]
            lanes = slice(q * stride + at, q * stride + at + NB)
            h_ref[r : r + 16, lanes] = jnp.concatenate(pair, 0).astype(BF)
    return cell


def cover_chunk(table, row_cell, col_cell, h_ref, east_ref, points):
    chunk, cols = east_ref.shape[1:]
    stride = h_ref.shape[1] // 8
    together = 1 + (cols % (2 * NB) > 0)
    cell = jnp.broadcast_to(row_cell, (chunk, cols)) - col_cell
    for t in range(15):
        apart = cell + float(t - 7)
        east_ref[t] = jnp.exp2(apart * apart * SCALE)
    table = table.reshape(8 * chunk, table.shape[2])
    total = jnp.zeros((chunk, cols), F32)
    for first in range(0, 8, together):
        offsets = range(first, first + together)
        counts = [h_ref[:, (q + 1) * stride - cols : (q + 1) * stride] for q in offsets]
        counts = jnp.concatenate(counts, 1)
        part = jnp.dot(table, jnp.concatenate([counts, counts], 0), preferred_element_type=F32)
        for p in range(8):
            for i, q in enumerate(offsets):
                piece = part[p * chunk : (p + 1) * chunk, i * cols : (i + 1) * cols]
                total = total + piece * east_ref[p - q + 7]
    return total * (1.0 / (points * points))


def lead_cover_kernel(
    place_ref, t_ref, row_cell_ref, *refs, points
):
    blocks, refs = refs[:4], refs[4:]
    folded_ref, own_ref, h_ref, col_cell_ref, east_ref, far_east_ref = refs[:6]
    far_ref, far_cell_ref, far_table_ref = refs[6:]
    rows, cols = own_ref.shape
    lines = h_ref.shape[0]
    cells = [column_counts(ref, h_ref, NB * i, cols) for i, ref in enumerate(blocks)]
    col_cell = jnp.concatenate(cells, 1)
    col_cell_ref[...] = col_cell

    east, north = unpack(blocks[1])
    far_ref[0] = (east - cells[1]).T
    far_ref[1] = north.T
    far_cell_ref[...] = cells[1].T
    first = pl.multiple_of(place_ref[1] * rows, rows)
    for r in range(0, rows, 16):
        here = pl.ds(first + r, 16)
        for p, (high, low) in enumerate(table_rows(far_ref[0, here], far_ref[1, here], lines)):
            far_table_ref[p, r : r + 16, :lines] = high
            far_table_ref[p, r : r + 16, lines:] = low

    mine = cover_chunk(t_ref[:, :rows], row_cell_ref[:rows], col_cell, h_ref, east_ref, points)
    row = lax.broadcasted_iota(jnp.int32, (rows, cols), 0)
    col = lax.broadcasted_iota(jnp.int32, (rows, cols), 1)
    mine = mine + jnp.where(col == first + row, 1.0, 0.0)
    own_ref[...] = mine
    far = cover_chunk(
        far_table_ref[...],
        far_cell_ref[pl.ds(first, rows)],
        col_cell[:, 2 * NB :],
        h_ref,
        far_east_ref,
        points,
    )
    folded_ref[:, : 3 * NB] = mine[:, : 3 * NB]
    folded_ref[:, 3 * NB : 4 * NB] = far[:, :NB]
    own_last = makes_own(place_ref[0])
    folded_ref[:, 4 * NB :] = jnp.where(own_last, mine[:, 3 * NB :], far[:, NB:])


def later_cover_kernel(t_ref, row_cell_ref, h_ref, col_cell_ref, o_ref, east_ref, *, points, start):
    chunk, cols = east_ref.shape[1:]
    col_cell = col_cell_ref[:, col_cell_ref.shape[1] - cols :]

    def row_chunk(index, _):
        first = pl.multiple_of(index * chunk, chunk)
        here = pl.ds(pl.multiple_of(first + start, chunk), chunk)
        o_ref[pl.ds(first, chunk)] = cover_chunk(
            t_ref[:, here], row_cell_ref[here], col_cell, h_ref, east_ref, points
        )
        return 0

    lax.fori_loop(0, o_ref.shape[0] // chunk, row_chunk, 0)


def block_cover_kernel(t_ref, row_cell_ref, *refs, points, start):
    blocks, (o_ref, h_ref, col_cell_ref, east_ref) = blocks_in(refs[:-4]), refs[-4:]
    cells = [
        column_counts(ref, h_ref, NB * i, o_ref.shape[1]) for i, ref in enumerate(blocks)
    ]
    col_cell_ref[...] = jnp.concatenate(cells, 1)
    later_cover_kernel(
        t_ref, row_cell_ref, h_ref, col_cell_ref, o_ref, east_ref, points=points, start=start
    )


def inverse_factor(tiles):
    n = len(tiles)
    width = 8 * n
    lane = lax.broadcasted_iota(jnp.int32, (8, width), 1)
    sub = lax.broadcasted_iota(jnp.int32, (8, width), 0)
    tiles = list(tiles)
    out = []

    def spread(x):
        return jnp.broadcast_to(x, (8, width))

    def lanes(tile, v):
        return [spread(tile[:, 8 * v + q : 8 * v + q + 1]) for q in range(8)]

    following = lanes(tiles[0], 0)
    for v in range(n):
        near = min(n, v + NEAR)
        cols = {v: following}
        if v + 1 < n:
            cols[v] = cols[v] + lanes(tiles[v], v + 1)
            cols[v + 1] = lanes(tiles[v + 1], v) + lanes(tiles[v + 1], v + 1)
        for r in range(v + 2, near):
            cols[r] = lanes(tiles[r], v)
        here = (lane >= 8 * v) & (lane < 8 * v + 8)
        for r in range(v + 1, n):
            tiles[r] = jnp.where(here, 0.0, tiles[r])
        tiles[v] = jnp.where(here, jnp.where(lane == sub + 8 * v, 1.0, 0.0), tiles[v])
        pivots = jnp.ones((8, width), F32)
        for s in range(8):
            head = cols[v]
            pivot = spread(head[s][s : s + 1])
            inverse = 1.0 / pivot
            pivots = jnp.where(sub == s, pivot, pivots)
            row = spread(tiles[v][s : s + 1])
            heads = [spread(head[k][s : s + 1]) for k in range(s + 1, len(head))]
            for r in range(v, near):
                part = cols[r][s] * inverse
                if r == v:
                    part = jnp.where(sub > s, part, 0.0)
                tiles[r] = tiles[r] - part * row
                for k in range(s + 1, len(cols[r])):
                    cols[r][k] = cols[r][k] - part * heads[k - s - 1]
        if v + 1 < n:
            following = cols[v + 1][8:]
        rows = tiles[v] * lax.rsqrt(pivots)
        if near < n:
            high = rows.astype(BF).astype(F32)
            low = rows - high
            left = jnp.concatenate([high, high, low, low], 0).astype(BF)
            right = jnp.concatenate([high, low, high, low], 0).astype(BF)
            update = lax.dot_general(
                left, right, (((0,), (0,)), ((), ())), preferred_element_type=F32
            )
            for r in range(near, n):
                tiles[r] = tiles[r] - update[8 * r : 8 * r + 8]
        out.append(jnp.where(lane <= sub + 8 * v, rows, 0.0))
    return jnp.concatenate(out, 0)


def split(x):
    high = x.astype(BF)
    return high, (x - high.astype(F32)).astype(BF)


def dot3(ah, al, bh, bl, numbers=NT):
    dot = functools.partial(lax.dot_general, dimension_numbers=numbers, preferred_element_type=F32)
    return dot(ah, bh) + (dot(ah, bl) + dot(al, bh))


def factor_blocks(a_ref, lh_ref, ll_ref, wh_ref, wl_ref):
    n = a_ref.shape[0]
    blocks = n // NB

    def column(first):
        end = first + NB
        bh, bl = split(a_ref[end:, first:end])
        high, low = split(dot3(bh, bl, wh_ref[first:end], wl_ref[first:end]))
        lh_ref[end:, first:end] = high
        ll_ref[end:, first:end] = low
        a_ref[end:, end : end + NB] = a_ref[end:, end : end + NB] - dot3(
            lh_ref[end:, :end],
            ll_ref[end:, :end],
            lh_ref[end : end + NB, :end],
            ll_ref[end : end + NB, :end],
        )

    def step(j, _):
        c = pl.multiple_of(j * NB, NB)
        tiles = [a_ref[pl.ds(c + 8 * v, 8), pl.ds(c, NB)] for v in range(NB // 8)]
        wh, wl = split(inverse_factor(tiles))
        wh_ref[pl.ds(c, NB)] = wh
        wl_ref[pl.ds(c, NB)] = wl
        for block in range(blocks - 1):
            pl.when(j == block)(functools.partial(column, block * NB))
        return 0

    lax.fori_loop(0, blocks, step, 0)


def factor_kernel(diag_ref, lh_ref, ll_ref, wh_ref, wl_ref, a_ref):
    a_ref[...] = diag_ref[...]
    factor_blocks(a_ref, lh_ref, ll_ref, wh_ref, wl_ref)


def turned(r, k):
    at = ((r & 1) << 1 | (r >> 1) & 1) + k
    return (r & 4) | (at & 1) << 1 | (at >> 1) & 1


def block_order(r):
    return [r, r ^ 4, turned(r, 1), turned(r, 2), turned(r, 3), r ^ 5, r ^ 6, r ^ 7]


def makes_own(r):
    return (r & 1) == 0


def folded_blocks(r):
    order = block_order(r)
    either = jnp.where(makes_own(r), r, r ^ 4)
    return [(r, r), (r, order[1]), (r, order[2]), (order[1], order[2]), (either, order[3])]


def blocks_in(refs):
    return [
        ref.at[first : first + ref.shape[0] // parts]
        for ref in refs
        for parts in [1 + (ref.shape[0] >= 2 * NB)]
        for first in range(0, ref.shape[0], ref.shape[0] // parts)
    ]


def unfold_kernel(place_ref, *refs):
    pieces_refs, (lh_ref, ll_ref, wh_ref, wl_ref, a_ref, g_ref) = refs[:8], refs[8:]
    row_pos = place_ref[0]
    panel_pos = place_ref[1]
    for i, ref in enumerate(pieces_refs):
        g_ref[4 * i : 4 * i + 4] = ref[...]

    def rows_of(r, _):
        away = r ^ row_pos
        slot = (away >> 1) | ((away & 1) << 2)
        ats = []
        for p in range(4):
            gone = p ^ panel_pos
            ats.append(slot | ((gone >> 1) << 3) | ((gone & 1) << 4))
        for k, (rows, cols) in enumerate(folded_blocks(r)):
            block = jnp.concatenate([g_ref[at, :, NB * k : NB * k + NB] for at in ats], 0)
            rr = pl.multiple_of(rows * NB, NB)
            cc = pl.multiple_of(cols * NB, NB)

            @pl.when(rows >= cols)
            def _():
                a_ref[pl.ds(rr, NB), pl.ds(cc, NB)] = block

            if k:

                @pl.when(rows < cols)
                def _():
                    a_ref[pl.ds(cc, NB), pl.ds(rr, NB)] = block.T

        return 0

    lax.fori_loop(0, 8, rows_of, 0)
    factor_blocks(a_ref, lh_ref, ll_ref, wh_ref, wl_ref)


def factor(kernel, operands, n):
    in_specs = [pl.BlockSpec(memory_space=pltpu.VMEM)] * len(operands)
    scratch = [pltpu.VMEM((n, n), F32)]
    if kernel is unfold_kernel:
        in_specs[0] = pl.BlockSpec(memory_space=pltpu.SMEM)
        scratch.append(pltpu.VMEM((32, *operands[1].shape[1:]), F32))
    return pl.pallas_call(
        kernel,
        out_shape=[jax.ShapeDtypeStruct((n, n), BF)] * 2 + [jax.ShapeDtypeStruct((n, NB), BF)] * 2,
        in_specs=in_specs,
        out_specs=[pl.BlockSpec(memory_space=pltpu.VMEM)] * 4,
        scratch_shapes=scratch,
        compiler_params=pltpu.CompilerParams(vmem_limit_bytes=32 << 20),
        cost_estimate=pl.CostEstimate(flops=5 * 10**10, bytes_accessed=8 << 20, transcendentals=0),
        name="factor",
    )(*operands)


def solve_kernel(place_ref, *refs, corners):
    cover_refs, parts_refs = refs[: len(corners)], refs[len(corners) : -7]
    lh_ref, ll_ref, wh_ref, wl_ref, o_ref, xh_ref, xl_ref = refs[-7:]
    n = o_ref.shape[1]

    def put(rows, cols, value):
        taken = parts_refs[0][parts_refs[0].shape[0] - 1, rows, cols]
        for part in parts_refs[1:]:
            taken = taken + part[part.shape[0] - 1, rows, cols]
        o_ref[rows, cols] = value - taken

    for (row, block), ref in zip(corners, cover_refs):
        rows = slice(row, row + ref.shape[0])
        if block is None:
            put(rows, slice(None), ref[...])
            continue
        for c, s in enumerate(block_order(place_ref[0])[block : block + ref.shape[1] // NB]):
            cols = pl.ds(pl.multiple_of(s * NB, NB), NB)
            put(rows, cols, ref[:, NB * c : NB * c + NB])
    wide = 2 * NB
    inverses = []
    for c in range(0, n, wide):
        upper, lower = slice(c, c + NB), slice(c + NB, c + wide)
        corner = dot3(lh_ref[lower, upper], ll_ref[lower, upper], wh_ref[upper], wl_ref[upper], NN)
        corner = split(-dot3(wh_ref[lower], wl_ref[lower], *split(corner), NN))
        zero = jnp.zeros((NB, NB), BF)
        inverses.append(
            [
                jnp.concatenate(
                    [
                        jnp.concatenate([ref[upper], zero], 1),
                        jnp.concatenate([part, ref[lower]], 1),
                    ],
                    0,
                )
                for ref, part in zip((wh_ref, wl_ref), corner)
            ]
        )
    for c, inverse in zip(range(0, n, wide), inverses):
        here = o_ref[:, c : c + wide]
        if c:
            here = here - dot3(
                xh_ref[:, :c], xl_ref[:, :c], lh_ref[c : c + wide, :c], ll_ref[c : c + wide, :c]
            )
        x = dot3(*split(here), *inverse)
        o_ref[:, c : c + wide] = x
        xh, xl = split(x)
        xh_ref[:, c : c + wide] = xh
        xl_ref[:, c : c + wide] = xl


def solve(place, covers, corners, parts, factors):
    rows, n = parts[0].shape[1:]
    return vmem_call(
        functools.partial(solve_kernel, corners=corners),
        jax.ShapeDtypeStruct((rows, n), F32),
        place,
        [*covers, *parts, *factors],
        [pltpu.VMEM((rows, n), BF)] * 2,
        "solve",
    )


def vmem_call(kernel, out_shape, place, operands, scratch=(), name=None):
    return pl.pallas_call(
        kernel,
        out_shape=out_shape,
        in_specs=[pl.BlockSpec(memory_space=pltpu.SMEM)] * (place is not None)
        + [pl.BlockSpec(memory_space=pltpu.VMEM)] * len(operands),
        out_specs=jax.tree.map(lambda _: pl.BlockSpec(memory_space=pltpu.VMEM), out_shape),
        scratch_shapes=list(scratch),
        compiler_params=pltpu.CompilerParams(vmem_limit_bytes=32 << 20),
        cost_estimate=pl.CostEstimate(flops=10**8, bytes_accessed=1 << 18, transcendentals=0),
        name=name,
    )(*([] if place is None else [place]), *operands)


def fold_products_kernel(place_ref, *refs):
    blocks, shares, total_ref = refs[:4], refs[4:-1], refs[-1]
    own, far, one, two = [split(ref[:NB]) for ref in blocks]
    own_last = makes_own(place_ref[0])
    either = split(jnp.where(own_last, blocks[0][:NB], blocks[1][:NB]))
    pairs = [(own, own), (own, far), (own, one), (far, one), (either, two)]
    for k, (left, right) in enumerate(pairs):
        total_ref[:, NB * k : NB * k + NB] = dot3(*left, *right)
    rows = shares[0].shape[0]
    for m, ref in enumerate(shares):
        first = pl.multiple_of((place_ref[1] ^ m) * rows, rows)
        ref[...] = total_ref[pl.ds(first, rows)]


def gather_split_kernel(place_ref, *refs):
    blocks, (high_ref, low_ref) = blocks_in(refs[:-2]), refs[-2:]
    for s, ref in zip(block_order(place_ref[0]), blocks):
        first = pl.multiple_of(s * NB, NB)
        high, low = split(ref[:NB])
        high_ref[pl.ds(first, NB)] = high
        low_ref[pl.ds(first, NB)] = low


def rest_products_kernel(place_ref, prior_ref, high_ref, low_ref, *refs, turns, outs):
    plus_refs, members = refs[:-outs], [ref.at[i] for ref in refs[-outs:] for i in range(ref.shape[0])]
    for m, o_ref in zip(turns, members):
        rows = o_ref.shape[0]
        first = pl.multiple_of((place_ref[1] ^ m) * rows, rows)
        own_high, own_low = split(prior_ref[pl.ds(first, rows)])
        for c in range(0, o_ref.shape[1], 2 * NB):
            cols = slice(c, c + 2 * NB)
            total = dot3(own_high, own_low, high_ref[cols], low_ref[cols])
            if m == turns[-1]:
                for plus_ref in plus_refs:
                    total = total + plus_ref[0, :, cols]
            o_ref[:, cols] = total


def swap(block, axis, bit):
    return lax.ppermute(block, axis, [(i, i ^ bit) for i in range(lax.axis_size(axis))])


def dot_rows(left, right):
    return lax.dot_general(
        left, right, NT, precision=lax.Precision.HIGH, preferred_element_type=F32
    )


def local(pixel_ids, quad_offsets, prior_factor):
    panel_count = lax.axis_size("panel")
    row_count = lax.axis_size("row")
    block_rows = pixel_ids.shape[0]
    quarter_rows = block_rows // panel_count
    per_device = B // (row_count * panel_count)
    span_cols = panel_count * per_device
    row_pos = lax.axis_index("row")
    panel_pos = lax.axis_index("panel")
    device_pos = row_pos * panel_count + panel_pos
    lead = 32

    points = jnp.stack(locate(pixel_ids, quad_offsets))
    count = points.shape[1]
    own_points = lax.dynamic_slice_in_dim(points, panel_pos * quarter_rows, quarter_rows, 2)
    local_points = points.reshape(2, count, panel_count, quarter_rows)[:, :, :, :per_device]
    local_points = local_points.reshape(2, count, span_cols)
    own_prior = prior_factor.reshape(panel_count, quarter_rows, -1)[:, :per_device]
    own_prior = own_prior.reshape(span_cols, -1)
    place = jnp.stack([row_pos, panel_pos]).astype(jnp.int32)
    lines = block_rows * row_count // 256 * 8
    folds = span_cols == NB and row_count == 8 and panel_count == 4 and lines == 256

    if not (folds and 2 * count * NB == 8 * own_prior.shape[1]):
        lead = 32
        row_ids = jnp.arange(lead, dtype=jnp.int32)[:, None]
        col_ids = jnp.arange(B, dtype=jnp.int32)[None, :]
        on_diagonal = (row_ids < per_device) & (col_ids == device_pos * per_device + row_ids)
        unit = jnp.where(on_diagonal, 1.0, 0.0).astype(F32)
        flat = local_points.reshape(1, 2 * count, span_cols)
        copies = jnp.broadcast_to(flat, (row_count, 2 * count, span_cols))
        spread = lax.all_to_all(copies, "row", split_axis=0, concat_axis=0, tiled=True)
        parted = features(own_points, spread.transpose(1, 0, 2).reshape(2, count, B))
        covers = [cover_rows(*parted, i, lead) for i in range(0, quarter_rows, lead)]
        covers[0] = covers[0] + unit
        panel_prior = lax.all_gather(own_prior, "row", axis=0, tiled=True)
        partial = dot_rows(prior_factor, panel_prior)
        parts = lax.all_to_all(
            partial.reshape(panel_count, quarter_rows, B), "panel", split_axis=0, concat_axis=0, tiled=True
        )
        parts = jnp.sum(parts, axis=0)
        mine = covers[0][:per_device] - parts[:per_device]
        diag_rows = lax.all_gather(mine, ("row", "panel"), axis=0, tiled=True)
        corners = [(i * lead, None) for i in range(len(covers))]
        return solve(place, covers, corners, [parts[None]], factor(factor_kernel, (diag_rows,), B))

    def turn(block, k):
        return lax.ppermute(block, "row", [(turned(d, k), d) for d in range(8)])

    own = pack(own_prior, local_points)
    two, one, far = turn(own, 2), turn(own, 1), swap(own, "row", 4)
    table = row_table(own_points, lines)

    def block_cover(held, blocks, start, cols):
        return vmem_call(
            functools.partial(block_cover_kernel, points=count, start=start),
            jax.ShapeDtypeStruct((quarter_rows - start, cols), F32),
            None,
            [*held, *blocks],
            [
                pltpu.VMEM((lines, 8 * cols), BF),
                pltpu.VMEM((1, cols), F32),
                pltpu.VMEM((15, per_device, cols), F32),
            ],
            "cover",
        )

    cover_own = block_cover(table, [own], per_device, NB)
    one, cover_own = lax.optimization_barrier((one, cover_own))
    from_x = swap(one, "row", 1)
    (far, one, two), table, cover_own = lax.optimization_barrier(((far, one, two), table, cover_own))
    shares = vmem_call(
        fold_products_kernel,
        [jax.ShapeDtypeStruct((per_device, 5 * NB), F32)] * 4,
        place,
        [own, far, one, two],
        [pltpu.VMEM((NB, 5 * NB), F32)],
        "fold_products",
    )
    shares, own, far = lax.optimization_barrier((shares, own, far))

    def beside(operands, transfer, work):
        operands, held = lax.optimization_barrier((operands, table))
        return lax.optimization_barrier((transfer(operands), work(operands, held)))

    half = 4 * NB

    def lead_cover(_, held):
        return vmem_call(
            functools.partial(lead_cover_kernel, points=count),
            [
                jax.ShapeDtypeStruct((per_device, 5 * NB), F32),
                jax.ShapeDtypeStruct((per_device, half), F32),
                jax.ShapeDtypeStruct((lines, 8 * half), BF),
                jax.ShapeDtypeStruct((1, half), F32),
            ],
            place,
            [*held, own, far, one, two],
            [
                pltpu.VMEM((15, per_device, half), F32),
                pltpu.VMEM((15, per_device, 2 * NB), F32),
                pltpu.VMEM((2, NB, count), F32),
                pltpu.VMEM((NB, 1), F32),
                pltpu.VMEM((8, per_device, 2 * lines), BF),
            ],
            "lead_cover",
        )

    sums, (folded, cover_lead, *counts) = beside(
        shares,
        lambda shares: [swap(share, "panel", m) for m, share in zip((1, 2, 3), shares[1:])],
        lead_cover,
    )
    sums, from_x = lax.optimization_barrier((sums, from_x))
    far_x = swap(far, "row", 1)
    far_z = swap(far, "row", 2)
    shard = folded - (shares[0] + sums[0] + sums[1] + sums[2])

    def rest_part(panel_prior, turns, members, plus=()):
        return vmem_call(
            functools.partial(rest_products_kernel, turns=turns, outs=len(members)),
            [jax.ShapeDtypeStruct((n, quarter_rows, B), F32) for n in members],
            place,
            [prior_factor, *panel_prior, *plus],
            name="rest_products",
        )

    def later_cover(held, start, rows):
        return vmem_call(
            functools.partial(later_cover_kernel, points=count, start=start),
            jax.ShapeDtypeStruct((rows, half - NB), F32),
            None,
            [*held, *counts],
            [pltpu.VMEM((15, per_device, half - NB), F32)],
            "cover",
        )

    middle = quarter_rows // 2

    def beside_far_z(_, held):
        rest = [from_x, far_x, far_z, last]
        cover = later_cover(held, middle, quarter_rows - middle)
        cover, blocks = lax.optimization_barrier((cover, rest))
        panel_prior = vmem_call(
            gather_split_kernel,
            [jax.ShapeDtypeStruct((B, own_prior.shape[1]), BF)] * 2,
            place,
            [own, far, one, two, *blocks],
            name="gather_split",
        )
        return cover, panel_prior, rest_part(panel_prior, (3, 1), (2,))[0], rest

    shard = shard[None]
    near_rows, cover_first = beside(
        shard,
        lambda x: swap(x, "row", 2),
        lambda _, held: later_cover(held, per_device, middle - per_device),
    )
    near_rows = jnp.concatenate([shard, near_rows], 0)
    cover_first, from_x, far_z = lax.optimization_barrier((cover_first, from_x, far_z))
    last = swap(far_z, "row", 1)
    far_rows, (cover_second, panel_prior, for_core, rest) = beside(
        near_rows, lambda x: swap(x, "row", 4), beside_far_z
    )
    held_rows = jnp.concatenate([near_rows, far_rows], 0)

    def across(x):
        corner = [(i, i ^ 6) for i in range(32)]
        return swap(x, "row", 1), swap(x, "panel", 2), lax.ppermute(x, ("row", "panel"), corner)

    def beside_xy(x, held):
        from_core = swap(for_core, "panel", 1)
        cover = block_cover(held, rest, 0, half)
        part_0, part_2 = rest_part(panel_prior, (0, 2), (1, 1), [from_core])
        return cover, part_0, part_2, from_core, swap(x, "panel", 1)

    received, (cover_last, part_0, part_2, from_core, held_there) = beside(
        held_rows, across, beside_xy
    )
    there = [held_there] + [swap(x, "panel", 1) for x in received]
    parts = [part_0, from_core, swap(part_2, "panel", 2)]
    factors = factor(unfold_kernel, (place, held_rows, *received, *there), B)
    covers = [cover_lead, cover_own, cover_first, cover_second, cover_last]
    corners = [(0, 0), (per_device, 0), (per_device, 1), (middle, 1), (0, 4)]
    return solve(place, covers, corners, parts, factors)


def solution(mesh):
    return jax.shard_map(
        local,
        mesh=mesh,
        in_specs=(P("row"), P(None, None, "row"), P("row", "panel")),
        out_specs=P(("row", "panel"), None),
        check_vma=False,
    )
```

```python
import functools

import jax
import jax.numpy as jnp
from jax import lax
from jax.experimental import pallas as pl
from jax.experimental.pallas import tpu as pltpu
from jax.sharding import PartitionSpec as P

B = 1024
NB = 128
NEAR = 4
F32 = jnp.float32
BF = jnp.bfloat16
NT = (((1,), (1,)), ((), ()))
NN = (((1,), (0,)), ((), ()))
SCALE = -1.4426950408889634 / 64.0
CENTRE = 1024.0


def locate(pixel_ids, quad_offsets):
    column = (pixel_ids % 256) * 8
    lines = (pixel_ids // 256) * 8
    east = (column[None, :] + quad_offsets[0]).astype(F32) - CENTRE
    north = (lines[None, :] + quad_offsets[1]).astype(F32) - CENTRE
    return east, north


def pieces(value):
    high = jnp.floor(value * (1.0 / 65536.0)) * 65536.0
    rest = value - high
    mid = jnp.floor(rest * (1.0 / 256.0)) * 256.0
    return [high, mid, rest - mid]


def halves(value):
    high = jnp.floor(value * (1.0 / 128.0)) * 128.0
    return high, value - high


def row_features(x, y):
    xh, xl = halves(x)
    yh, yl = halves(y)
    one = jnp.ones_like(x)
    zero = jnp.zeros_like(x)
    cross = [-2 * xh, -2 * xh, -2 * xl, -2 * xl, -2 * yh, -2 * yh, -2 * yl, -2 * yl]
    return jnp.concatenate(cross + pieces(x * x + y * y) + [one] * 3 + [zero] * 2, 0)


def col_features(x, y):
    xh, xl = halves(x)
    yh, yl = halves(y)
    one = jnp.ones_like(x)
    zero = jnp.zeros_like(x)
    cross = [xh, xl, xh, xl, yh, yl, yh, yl]
    return jnp.concatenate(cross + [one] * 3 + pieces(x * x + y * y) + [zero] * 2, 0)


def feature_kernel(row_ref, col_ref, f_ref, g_ref):
    for a in range(row_ref.shape[1]):
        one = row_features(row_ref[0, a : a + 1, :], row_ref[1, a : a + 1, :])
        f_ref[a] = one.T.astype(BF)
        g_ref[a] = col_features(col_ref[0, a : a + 1, :], col_ref[1, a : a + 1, :]).astype(BF)


def features(row_points, col_points):
    count, rows = row_points.shape[1:]
    cols = col_points.shape[2]
    return pl.pallas_call(
        feature_kernel,
        out_shape=[
            jax.ShapeDtypeStruct((count, rows, 16), BF),
            jax.ShapeDtypeStruct((count, 16, cols), BF),
        ],
        in_specs=[pl.BlockSpec(memory_space=pltpu.VMEM)] * 2,
        out_specs=[pl.BlockSpec(memory_space=pltpu.VMEM)] * 2,
        compiler_params=pltpu.CompilerParams(vmem_limit_bytes=8 << 20),
        name="features",
    )(row_points, col_points)


def cover_kernel(f_ref, g_ref, o_ref):
    count, block = f_ref.shape[:2]
    rows_here = f_ref[...].reshape(count * block, 16)

    def column_point(b, total):
        apart = jnp.dot(rows_here, g_ref[b], preferred_element_type=F32)
        near = jnp.exp2(apart * SCALE)
        for a in range(count):
            total = total + near[a * block : (a + 1) * block]
        return total

    total = lax.fori_loop(0, count, column_point, jnp.zeros(o_ref.shape, F32), unroll=8)
    o_ref[...] = total * (1.0 / (count * count))


def cover_rows(row_part, col_part, first, block):
    count, rows, depth = row_part.shape
    cols = col_part.shape[2]
    index = first // block
    return pl.pallas_call(
        cover_kernel,
        grid=(1,),
        out_shape=jax.ShapeDtypeStruct((block, cols), F32),
        in_specs=[
            pl.BlockSpec((count, block, depth), lambda i: (0, index, 0)),
            pl.BlockSpec((count, depth, cols), lambda i: (0, 0, 0)),
        ],
        out_specs=pl.BlockSpec((block, cols), lambda i: (0, 0)),
        compiler_params=pltpu.CompilerParams(vmem_limit_bytes=16 << 20),
        cost_estimate=pl.CostEstimate(flops=10**8, bytes_accessed=1 << 18, transcendentals=0),
        name="cover",
    )(row_part, col_part)


def table_rows(offset, north, lines):
    line = lax.broadcasted_iota(jnp.int32, (16, lines), 1).astype(F32) - CENTRE
    total = [jnp.zeros((16, lines), F32) for _ in range(8)]
    for a in range(offset.shape[1]):
        apart = jnp.broadcast_to(north[:, a : a + 1], (16, lines)) - line
        near = jnp.exp2(apart * apart * SCALE)
        which = jnp.broadcast_to(offset[:, a : a + 1], (16, lines))
        for p in range(8):
            total[p] = total[p] + jnp.where(which == float(p), near, 0.0)
    return [split(x) for x in total]


def row_table_kernel(row_ref, t_ref, row_cell_ref, place_ref):
    rows = row_ref.shape[2]
    lines = t_ref.shape[2] // 2
    row_cell = jnp.floor(row_ref[0] * 0.125) * 8.0
    place_ref[0] = (row_ref[0] - row_cell).T
    place_ref[1] = row_ref[1].T
    row_cell_ref[...] = row_cell[0:1].T

    def row_tile(index, _):
        here = pl.ds(pl.multiple_of(index * 16, 16), 16)
        for p, (high, low) in enumerate(table_rows(place_ref[0, here], place_ref[1, here], lines)):
            t_ref[p, here, :lines] = high
            t_ref[p, here, lines:] = low
        return 0

    lax.fori_loop(0, rows // 16, row_tile, 0)


def row_table(row_points, lines):
    count, rows = row_points.shape[1:]
    return pl.pallas_call(
        row_table_kernel,
        out_shape=[
            jax.ShapeDtypeStruct((8, rows, 2 * lines), BF),
            jax.ShapeDtypeStruct((rows, 1), F32),
        ],
        in_specs=[pl.BlockSpec(memory_space=pltpu.VMEM)],
        out_specs=[pl.BlockSpec(memory_space=pltpu.VMEM)] * 2,
        scratch_shapes=[pltpu.VMEM((2, rows, count), F32)],
        compiler_params=pltpu.CompilerParams(vmem_limit_bytes=16 << 20),
        cost_estimate=pl.CostEstimate(flops=10**8, bytes_accessed=1 << 18, transcendentals=0),
        name="row_table",
    )(row_points)


def pack(prior, points):
    flat = points.reshape(-1, NB)
    tiles = prior.shape[1] // NB
    extra = flat.reshape(tiles, flat.shape[0] // tiles, NB).transpose(1, 0, 2)
    return jnp.concatenate([prior, extra.reshape(-1, prior.shape[1])], 0)


def unpack(block_ref):
    extra = block_ref.shape[0] - NB
    tiles = block_ref.shape[1] // NB
    flat = jnp.concatenate(
        [block_ref[NB : NB + extra, NB * t : NB * t + NB] for t in range(tiles)], 0
    )
    count = flat.shape[0] // 2
    return flat[:count], flat[count:]


def column_counts(block_ref, h_ref, at, stride):
    east, north = unpack(block_ref)
    lines = h_ref.shape[0]
    cell = jnp.floor(east[0:1] * 0.125) * 8.0
    line = jnp.floor(north[0:1] * 0.125) * 8.0
    east, north = east - cell, north - line
    sub = lax.broadcasted_iota(jnp.int32, (8, NB), 0).astype(F32)
    held = [jnp.zeros((8, NB), F32) for _ in range(8)]
    for b in range(east.shape[0]):
        one = jnp.where(sub == jnp.broadcast_to(north[b : b + 1], (8, NB)), 1.0, 0.0)
        which = jnp.broadcast_to(east[b : b + 1], (8, NB))
        for q in range(8):
            held[q] = held[q] + jnp.where(which == float(q), one, 0.0)
    line = jnp.broadcast_to(line, (8, NB))
    for r in range(0, lines, 16):
        low = line == float(r) - CENTRE
        high = line == float(r + 8) - CENTRE
        for q in range(8):
            pair = [jnp.where(low, held[q], 0.0), jnp.where(high, held[q], 0.0)]
            lanes = slice(q * stride + at, q * stride + at + NB)
            h_ref[r : r + 16, lanes] = jnp.concatenate(pair, 0).astype(BF)
    return cell


def cover_chunk(table, row_cell, col_cell, h_ref, east_ref, points):
    chunk, cols = east_ref.shape[1:]
    stride = h_ref.shape[1] // 8
    together = 1 + (cols % (2 * NB) > 0)
    cell = jnp.broadcast_to(row_cell, (chunk, cols)) - col_cell
    for t in range(15):
        apart = cell + float(t - 7)
        east_ref[t] = jnp.exp2(apart * apart * SCALE)
    table = table.reshape(8 * chunk, table.shape[2])
    total = jnp.zeros((chunk, cols), F32)
    for first in range(0, 8, together):
        offsets = range(first, first + together)
        counts = [h_ref[:, (q + 1) * stride - cols : (q + 1) * stride] for q in offsets]
        counts = jnp.concatenate(counts, 1)
        part = jnp.dot(table, jnp.concatenate([counts, counts], 0), preferred_element_type=F32)
        for p in range(8):
            for i, q in enumerate(offsets):
                piece = part[p * chunk : (p + 1) * chunk, i * cols : (i + 1) * cols]
                total = total + piece * east_ref[p - q + 7]
    return total * (1.0 / (points * points))


def lead_cover_kernel(
    place_ref, t_ref, row_cell_ref, *refs, points
):
    blocks, refs = refs[:4], refs[4:]
    folded_ref, own_ref, h_ref, col_cell_ref, east_ref, far_east_ref = refs[:6]
    far_ref, far_cell_ref, far_table_ref = refs[6:]
    rows, cols = own_ref.shape
    lines = h_ref.shape[0]
    cells = [column_counts(ref, h_ref, NB * i, cols) for i, ref in enumerate(blocks)]
    col_cell = jnp.concatenate(cells, 1)
    col_cell_ref[...] = col_cell

    east, north = unpack(blocks[1])
    far_ref[0] = (east - cells[1]).T
    far_ref[1] = north.T
    far_cell_ref[...] = cells[1].T
    first = pl.multiple_of(place_ref[1] * rows, rows)
    for r in range(0, rows, 16):
        here = pl.ds(first + r, 16)
        for p, (high, low) in enumerate(table_rows(far_ref[0, here], far_ref[1, here], lines)):
            far_table_ref[p, r : r + 16, :lines] = high
            far_table_ref[p, r : r + 16, lines:] = low

    mine = cover_chunk(t_ref[:, :rows], row_cell_ref[:rows], col_cell, h_ref, east_ref, points)
    row = lax.broadcasted_iota(jnp.int32, (rows, cols), 0)
    col = lax.broadcasted_iota(jnp.int32, (rows, cols), 1)
    mine = mine + jnp.where(col == first + row, 1.0, 0.0)
    own_ref[...] = mine
    far = cover_chunk(
        far_table_ref[...],
        far_cell_ref[pl.ds(first, rows)],
        col_cell[:, 2 * NB :],
        h_ref,
        far_east_ref,
        points,
    )
    folded_ref[:, : 3 * NB] = mine[:, : 3 * NB]
    folded_ref[:, 3 * NB : 4 * NB] = far[:, :NB]
    own_last = makes_own(place_ref[0])
    folded_ref[:, 4 * NB :] = jnp.where(own_last, mine[:, 3 * NB :], far[:, NB:])


def later_cover_kernel(t_ref, row_cell_ref, h_ref, col_cell_ref, o_ref, east_ref, *, points, start):
    chunk, cols = east_ref.shape[1:]
    col_cell = col_cell_ref[:, col_cell_ref.shape[1] - cols :]

    def row_chunk(index, _):
        first = pl.multiple_of(index * chunk, chunk)
        here = pl.ds(pl.multiple_of(first + start, chunk), chunk)
        o_ref[pl.ds(first, chunk)] = cover_chunk(
            t_ref[:, here], row_cell_ref[here], col_cell, h_ref, east_ref, points
        )
        return 0

    lax.fori_loop(0, o_ref.shape[0] // chunk, row_chunk, 0)


def block_cover_kernel(t_ref, row_cell_ref, *refs, points, start):
    blocks, (o_ref, h_ref, col_cell_ref, east_ref) = blocks_in(refs[:-4]), refs[-4:]
    cells = [
        column_counts(ref, h_ref, NB * i, o_ref.shape[1]) for i, ref in enumerate(blocks)
    ]
    col_cell_ref[...] = jnp.concatenate(cells, 1)
    later_cover_kernel(
        t_ref, row_cell_ref, h_ref, col_cell_ref, o_ref, east_ref, points=points, start=start
    )


def inverse_factor(tiles):
    n = len(tiles)
    width = 8 * n
    lane = lax.broadcasted_iota(jnp.int32, (8, width), 1)
    sub = lax.broadcasted_iota(jnp.int32, (8, width), 0)
    tiles = list(tiles)
    out = []

    def spread(x):
        return jnp.broadcast_to(x, (8, width))

    def lanes(tile, v):
        return [spread(tile[:, 8 * v + q : 8 * v + q + 1]) for q in range(8)]

    following = lanes(tiles[0], 0)
    for v in range(n):
        near = min(n, v + NEAR)
        cols = {v: following}
        if v + 1 < n:
            cols[v] = cols[v] + lanes(tiles[v], v + 1)
            cols[v + 1] = lanes(tiles[v + 1], v) + lanes(tiles[v + 1], v + 1)
        for r in range(v + 2, near):
            cols[r] = lanes(tiles[r], v)
        here = (lane >= 8 * v) & (lane < 8 * v + 8)
        for r in range(v + 1, n):
            tiles[r] = jnp.where(here, 0.0, tiles[r])
        tiles[v] = jnp.where(here, jnp.where(lane == sub + 8 * v, 1.0, 0.0), tiles[v])
        pivots = jnp.ones((8, width), F32)
        for s in range(8):
            head = cols[v]
            pivot = spread(head[s][s : s + 1])
            inverse = 1.0 / pivot
            pivots = jnp.where(sub == s, pivot, pivots)
            row = spread(tiles[v][s : s + 1])
            heads = [spread(head[k][s : s + 1]) for k in range(s + 1, len(head))]
            for r in range(v, near):
                part = cols[r][s] * inverse
                if r == v:
                    part = jnp.where(sub > s, part, 0.0)
                tiles[r] = tiles[r] - part * row
                for k in range(s + 1, len(cols[r])):
                    cols[r][k] = cols[r][k] - part * heads[k - s - 1]
        if v + 1 < n:
            following = cols[v + 1][8:]
        rows = tiles[v] * lax.rsqrt(pivots)
        if near < n:
            high = rows.astype(BF).astype(F32)
            low = rows - high
            left = jnp.concatenate([high, high, low, low], 0).astype(BF)
            right = jnp.concatenate([high, low, high, low], 0).astype(BF)
            update = lax.dot_general(
                left, right, (((0,), (0,)), ((), ())), preferred_element_type=F32
            )
            for r in range(near, n):
                tiles[r] = tiles[r] - update[8 * r : 8 * r + 8]
        out.append(jnp.where(lane <= sub + 8 * v, rows, 0.0))
    return jnp.concatenate(out, 0)


def split(x):
    high = x.astype(BF)
    return high, (x - high.astype(F32)).astype(BF)


def dot3(ah, al, bh, bl, numbers=NT):
    dot = functools.partial(lax.dot_general, dimension_numbers=numbers, preferred_element_type=F32)
    return dot(ah, bh) + (dot(ah, bl) + dot(al, bh))


def factor_blocks(a_ref, lh_ref, ll_ref, wh_ref, wl_ref):
    n = a_ref.shape[0]
    blocks = n // NB

    def column(first):
        end = first + NB
        bh, bl = split(a_ref[end:, first:end])
        high, low = split(dot3(bh, bl, wh_ref[first:end], wl_ref[first:end]))
        lh_ref[end:, first:end] = high
        ll_ref[end:, first:end] = low
        a_ref[end:, end : end + NB] = a_ref[end:, end : end + NB] - dot3(
            lh_ref[end:, :end],
            ll_ref[end:, :end],
            lh_ref[end : end + NB, :end],
            ll_ref[end : end + NB, :end],
        )

    def step(j, _):
        c = pl.multiple_of(j * NB, NB)
        tiles = [a_ref[pl.ds(c + 8 * v, 8), pl.ds(c, NB)] for v in range(NB // 8)]
        wh, wl = split(inverse_factor(tiles))
        wh_ref[pl.ds(c, NB)] = wh
        wl_ref[pl.ds(c, NB)] = wl
        for block in range(blocks - 1):
            pl.when(j == block)(functools.partial(column, block * NB))
        return 0

    lax.fori_loop(0, blocks, step, 0)


def factor_kernel(diag_ref, lh_ref, ll_ref, wh_ref, wl_ref, a_ref):
    a_ref[...] = diag_ref[...]
    factor_blocks(a_ref, lh_ref, ll_ref, wh_ref, wl_ref)


def turned(r, k):
    at = ((r & 1) << 1 | (r >> 1) & 1) + k
    return (r & 4) | (at & 1) << 1 | (at >> 1) & 1


def block_order(r):
    return [r, r ^ 4, turned(r, 1), turned(r, 2), turned(r, 3), r ^ 5, r ^ 6, r ^ 7]


def makes_own(r):
    return (r & 1) == 0


def folded_blocks(r):
    order = block_order(r)
    either = jnp.where(makes_own(r), r, r ^ 4)
    return [(r, r), (r, order[1]), (r, order[2]), (order[1], order[2]), (either, order[3])]


def blocks_in(refs):
    return [
        ref.at[first : first + ref.shape[0] // parts]
        for ref in refs
        for parts in [1 + (ref.shape[0] >= 2 * NB)]
        for first in range(0, ref.shape[0], ref.shape[0] // parts)
    ]


def unfold_kernel(place_ref, *refs):
    pieces_refs, (lh_ref, ll_ref, wh_ref, wl_ref, a_ref, g_ref) = refs[:8], refs[8:]
    row_pos = place_ref[0]
    panel_pos = place_ref[1]
    for i, ref in enumerate(pieces_refs):
        g_ref[4 * i : 4 * i + 4] = ref[...]

    def rows_of(r, _):
        away = r ^ row_pos
        slot = (away >> 1) | ((away & 1) << 2)
        ats = []
        for p in range(4):
            gone = p ^ panel_pos
            ats.append(slot | ((gone >> 1) << 3) | ((gone & 1) << 4))
        for k, (rows, cols) in enumerate(folded_blocks(r)):
            block = jnp.concatenate([g_ref[at, :, NB * k : NB * k + NB] for at in ats], 0)
            rr = pl.multiple_of(rows * NB, NB)
            cc = pl.multiple_of(cols * NB, NB)

            @pl.when(rows >= cols)
            def _():
                a_ref[pl.ds(rr, NB), pl.ds(cc, NB)] = block

            if k:

                @pl.when(rows < cols)
                def _():
                    a_ref[pl.ds(cc, NB), pl.ds(rr, NB)] = block.T

        return 0

    lax.fori_loop(0, 8, rows_of, 0)
    factor_blocks(a_ref, lh_ref, ll_ref, wh_ref, wl_ref)


def factor(kernel, operands, n):
    in_specs = [pl.BlockSpec(memory_space=pltpu.VMEM)] * len(operands)
    scratch = [pltpu.VMEM((n, n), F32)]
    if kernel is unfold_kernel:
        in_specs[0] = pl.BlockSpec(memory_space=pltpu.SMEM)
        scratch.append(pltpu.VMEM((32, *operands[1].shape[1:]), F32))
    return pl.pallas_call(
        kernel,
        out_shape=[jax.ShapeDtypeStruct((n, n), BF)] * 2 + [jax.ShapeDtypeStruct((n, NB), BF)] * 2,
        in_specs=in_specs,
        out_specs=[pl.BlockSpec(memory_space=pltpu.VMEM)] * 4,
        scratch_shapes=scratch,
        compiler_params=pltpu.CompilerParams(vmem_limit_bytes=32 << 20),
        cost_estimate=pl.CostEstimate(flops=5 * 10**10, bytes_accessed=8 << 20, transcendentals=0),
        name="factor",
    )(*operands)


def solve_kernel(place_ref, *refs, corners):
    cover_refs, parts_refs = refs[: len(corners)], refs[len(corners) : -7]
    lh_ref, ll_ref, wh_ref, wl_ref, o_ref, xh_ref, xl_ref = refs[-7:]
    n = o_ref.shape[1]

    def put(rows, cols, value):
        taken = parts_refs[0][parts_refs[0].shape[0] - 1, rows, cols]
        for part in parts_refs[1:]:
            taken = taken + part[part.shape[0] - 1, rows, cols]
        o_ref[rows, cols] = value - taken

    for (row, block), ref in zip(corners, cover_refs):
        rows = slice(row, row + ref.shape[0])
        if block is None:
            put(rows, slice(None), ref[...])
            continue
        for c, s in enumerate(block_order(place_ref[0])[block : block + ref.shape[1] // NB]):
            cols = pl.ds(pl.multiple_of(s * NB, NB), NB)
            put(rows, cols, ref[:, NB * c : NB * c + NB])
    wide = 2 * NB
    inverses = []
    for c in range(0, n, wide):
        upper, lower = slice(c, c + NB), slice(c + NB, c + wide)
        corner = dot3(lh_ref[lower, upper], ll_ref[lower, upper], wh_ref[upper], wl_ref[upper], NN)
        corner = split(-dot3(wh_ref[lower], wl_ref[lower], *split(corner), NN))
        zero = jnp.zeros((NB, NB), BF)
        inverses.append(
            [
                jnp.concatenate(
                    [
                        jnp.concatenate([ref[upper], zero], 1),
                        jnp.concatenate([part, ref[lower]], 1),
                    ],
                    0,
                )
                for ref, part in zip((wh_ref, wl_ref), corner)
            ]
        )
    for c, inverse in zip(range(0, n, wide), inverses):
        here = o_ref[:, c : c + wide]
        if c:
            here = here - dot3(
                xh_ref[:, :c], xl_ref[:, :c], lh_ref[c : c + wide, :c], ll_ref[c : c + wide, :c]
            )
        x = dot3(*split(here), *inverse)
        o_ref[:, c : c + wide] = x
        xh, xl = split(x)
        xh_ref[:, c : c + wide] = xh
        xl_ref[:, c : c + wide] = xl


def solve(place, covers, corners, parts, factors):
    rows, n = parts[0].shape[1:]
    return vmem_call(
        functools.partial(solve_kernel, corners=corners),
        jax.ShapeDtypeStruct((rows, n), F32),
        place,
        [*covers, *parts, *factors],
        [pltpu.VMEM((rows, n), BF)] * 2,
        "solve",
    )


def vmem_call(kernel, out_shape, place, operands, scratch=(), name=None):
    return pl.pallas_call(
        kernel,
        out_shape=out_shape,
        in_specs=[pl.BlockSpec(memory_space=pltpu.SMEM)] * (place is not None)
        + [pl.BlockSpec(memory_space=pltpu.VMEM)] * len(operands),
        out_specs=jax.tree.map(lambda _: pl.BlockSpec(memory_space=pltpu.VMEM), out_shape),
        scratch_shapes=list(scratch),
        compiler_params=pltpu.CompilerParams(vmem_limit_bytes=32 << 20),
        cost_estimate=pl.CostEstimate(flops=10**8, bytes_accessed=1 << 18, transcendentals=0),
        name=name,
    )(*([] if place is None else [place]), *operands)


def fold_products_kernel(place_ref, *refs):
    blocks, shares, total_ref = refs[:4], refs[4:-1], refs[-1]
    own, far, one, two = [split(ref[:NB]) for ref in blocks]
    own_last = makes_own(place_ref[0])
    either = split(jnp.where(own_last, blocks[0][:NB], blocks[1][:NB]))
    pairs = [(own, own), (own, far), (own, one), (far, one), (either, two)]
    for k, (left, right) in enumerate(pairs):
        total_ref[:, NB * k : NB * k + NB] = dot3(*left, *right)
    rows = shares[0].shape[0]
    for m, ref in enumerate(shares):
        first = pl.multiple_of((place_ref[1] ^ m) * rows, rows)
        ref[...] = total_ref[pl.ds(first, rows)]


def gather_split_kernel(place_ref, *refs):
    blocks, (high_ref, low_ref) = blocks_in(refs[:-2]), refs[-2:]
    for s, ref in zip(block_order(place_ref[0]), blocks):
        first = pl.multiple_of(s * NB, NB)
        high, low = split(ref[:NB])
        high_ref[pl.ds(first, NB)] = high
        low_ref[pl.ds(first, NB)] = low


def rest_products_kernel(place_ref, prior_ref, high_ref, low_ref, *refs, turns, outs):
    plus_refs, members = refs[:-outs], [ref.at[i] for ref in refs[-outs:] for i in range(ref.shape[0])]
    rows, width = members[0].shape
    own = [prior_ref[pl.ds(pl.multiple_of((place_ref[1] ^ m) * rows, rows), rows)] for m in turns]
    own_high, own_low = split(jnp.concatenate(own, 0))
    for c in range(0, width, 2 * NB):
        cols = slice(c, c + 2 * NB)
        total = dot3(own_high, own_low, high_ref[cols], low_ref[cols])
        for i, o_ref in enumerate(members):
            part = total[i * rows : (i + 1) * rows]
            if i == len(members) - 1:
                for plus_ref in plus_refs:
                    part = part + plus_ref[0, :, cols]
            o_ref[:, cols] = part


def swap(block, axis, bit):
    return lax.ppermute(block, axis, [(i, i ^ bit) for i in range(lax.axis_size(axis))])


def dot_rows(left, right):
    return lax.dot_general(
        left, right, NT, precision=lax.Precision.HIGH, preferred_element_type=F32
    )


def local(pixel_ids, quad_offsets, prior_factor):
    panel_count = lax.axis_size("panel")
    row_count = lax.axis_size("row")
    block_rows = pixel_ids.shape[0]
    quarter_rows = block_rows // panel_count
    per_device = B // (row_count * panel_count)
    span_cols = panel_count * per_device
    row_pos = lax.axis_index("row")
    panel_pos = lax.axis_index("panel")
    device_pos = row_pos * panel_count + panel_pos
    lead = 32

    points = jnp.stack(locate(pixel_ids, quad_offsets))
    count = points.shape[1]
    own_points = lax.dynamic_slice_in_dim(points, panel_pos * quarter_rows, quarter_rows, 2)
    local_points = points.reshape(2, count, panel_count, quarter_rows)[:, :, :, :per_device]
    local_points = local_points.reshape(2, count, span_cols)
    own_prior = prior_factor.reshape(panel_count, quarter_rows, -1)[:, :per_device]
    own_prior = own_prior.reshape(span_cols, -1)
    place = jnp.stack([row_pos, panel_pos]).astype(jnp.int32)
    lines = block_rows * row_count // 256 * 8
    folds = span_cols == NB and row_count == 8 and panel_count == 4 and lines == 256

    if not (folds and 2 * count * NB == 8 * own_prior.shape[1]):
        lead = 32
        row_ids = jnp.arange(lead, dtype=jnp.int32)[:, None]
        col_ids = jnp.arange(B, dtype=jnp.int32)[None, :]
        on_diagonal = (row_ids < per_device) & (col_ids == device_pos * per_device + row_ids)
        unit = jnp.where(on_diagonal, 1.0, 0.0).astype(F32)
        flat = local_points.reshape(1, 2 * count, span_cols)
        copies = jnp.broadcast_to(flat, (row_count, 2 * count, span_cols))
        spread = lax.all_to_all(copies, "row", split_axis=0, concat_axis=0, tiled=True)
        parted = features(own_points, spread.transpose(1, 0, 2).reshape(2, count, B))
        covers = [cover_rows(*parted, i, lead) for i in range(0, quarter_rows, lead)]
        covers[0] = covers[0] + unit
        panel_prior = lax.all_gather(own_prior, "row", axis=0, tiled=True)
        partial = dot_rows(prior_factor, panel_prior)
        parts = lax.all_to_all(
            partial.reshape(panel_count, quarter_rows, B), "panel", split_axis=0, concat_axis=0, tiled=True
        )
        parts = jnp.sum(parts, axis=0)
        mine = covers[0][:per_device] - parts[:per_device]
        diag_rows = lax.all_gather(mine, ("row", "panel"), axis=0, tiled=True)
        corners = [(i * lead, None) for i in range(len(covers))]
        return solve(place, covers, corners, [parts[None]], factor(factor_kernel, (diag_rows,), B))

    def turn(block, k):
        return lax.ppermute(block, "row", [(turned(d, k), d) for d in range(8)])

    own = pack(own_prior, local_points)
    two, one, far = turn(own, 2), turn(own, 1), swap(own, "row", 4)
    table = row_table(own_points, lines)

    def block_cover(held, blocks, start, cols):
        return vmem_call(
            functools.partial(block_cover_kernel, points=count, start=start),
            jax.ShapeDtypeStruct((quarter_rows - start, cols), F32),
            None,
            [*held, *blocks],
            [
                pltpu.VMEM((lines, 8 * cols), BF),
                pltpu.VMEM((1, cols), F32),
                pltpu.VMEM((15, per_device, cols), F32),
            ],
            "cover",
        )

    cover_own = block_cover(table, [own], per_device, NB)
    one, cover_own = lax.optimization_barrier((one, cover_own))
    from_x = swap(one, "row", 1)
    (far, one, two), table, cover_own = lax.optimization_barrier(((far, one, two), table, cover_own))
    shares = vmem_call(
        fold_products_kernel,
        [jax.ShapeDtypeStruct((per_device, 5 * NB), F32)] * 4,
        place,
        [own, far, one, two],
        [pltpu.VMEM((NB, 5 * NB), F32)],
        "fold_products",
    )
    shares, own, far = lax.optimization_barrier((shares, own, far))

    def beside(operands, transfer, work):
        operands, held = lax.optimization_barrier((operands, table))
        return lax.optimization_barrier((transfer(operands), work(operands, held)))

    half = 4 * NB

    def lead_cover(_, held):
        return vmem_call(
            functools.partial(lead_cover_kernel, points=count),
            [
                jax.ShapeDtypeStruct((per_device, 5 * NB), F32),
                jax.ShapeDtypeStruct((per_device, half), F32),
                jax.ShapeDtypeStruct((lines, 8 * half), BF),
                jax.ShapeDtypeStruct((1, half), F32),
            ],
            place,
            [*held, own, far, one, two],
            [
                pltpu.VMEM((15, per_device, half), F32),
                pltpu.VMEM((15, per_device, 2 * NB), F32),
                pltpu.VMEM((2, NB, count), F32),
                pltpu.VMEM((NB, 1), F32),
                pltpu.VMEM((8, per_device, 2 * lines), BF),
            ],
            "lead_cover",
        )

    sums, (folded, cover_lead, *counts) = beside(
        shares,
        lambda shares: [swap(share, "panel", m) for m, share in zip((1, 2, 3), shares[1:])],
        lead_cover,
    )
    sums, from_x = lax.optimization_barrier((sums, from_x))
    far_x = swap(far, "row", 1)
    far_z = swap(far, "row", 2)
    shard = folded - (shares[0] + sums[0] + sums[1] + sums[2])

    def rest_part(panel_prior, turns, members, plus=()):
        return vmem_call(
            functools.partial(rest_products_kernel, turns=turns, outs=len(members)),
            [jax.ShapeDtypeStruct((n, quarter_rows, B), F32) for n in members],
            place,
            [prior_factor, *panel_prior, *plus],
            name="rest_products",
        )

    def later_cover(held, start, rows):
        return vmem_call(
            functools.partial(later_cover_kernel, points=count, start=start),
            jax.ShapeDtypeStruct((rows, half - NB), F32),
            None,
            [*held, *counts],
            [pltpu.VMEM((15, per_device, half - NB), F32)],
            "cover",
        )

    middle = quarter_rows // 2

    def beside_far_z(_, held):
        rest = [from_x, far_x, far_z, last]
        cover = later_cover(held, middle, quarter_rows - middle)
        cover, blocks = lax.optimization_barrier((cover, rest))
        panel_prior = vmem_call(
            gather_split_kernel,
            [jax.ShapeDtypeStruct((B, own_prior.shape[1]), BF)] * 2,
            place,
            [own, far, one, two, *blocks],
            name="gather_split",
        )
        return cover, panel_prior, rest_part(panel_prior, (3, 1), (2,))[0], rest

    shard = shard[None]
    near_rows, cover_first = beside(
        shard,
        lambda x: swap(x, "row", 2),
        lambda _, held: later_cover(held, per_device, middle - per_device),
    )
    near_rows = jnp.concatenate([shard, near_rows], 0)
    cover_first, from_x, far_z = lax.optimization_barrier((cover_first, from_x, far_z))
    last = swap(far_z, "row", 1)
    far_rows, (cover_second, panel_prior, for_core, rest) = beside(
        near_rows, lambda x: swap(x, "row", 4), beside_far_z
    )
    held_rows = jnp.concatenate([near_rows, far_rows], 0)

    def across(x):
        corner = [(i, i ^ 6) for i in range(32)]
        return swap(x, "row", 1), swap(x, "panel", 2), lax.ppermute(x, ("row", "panel"), corner)

    def beside_xy(x, held):
        from_core = swap(for_core, "panel", 1)
        cover = block_cover(held, rest, 0, half)
        part_0, part_2 = rest_part(panel_prior, (0, 2), (1, 1), [from_core])
        return cover, part_0, part_2, from_core, swap(x, "panel", 1)

    received, (cover_last, part_0, part_2, from_core, held_there) = beside(
        held_rows, across, beside_xy
    )
    there = [held_there] + [swap(x, "panel", 1) for x in received]
    parts = [part_0, from_core, swap(part_2, "panel", 2)]
    factors = factor(unfold_kernel, (place, held_rows, *received, *there), B)
    covers = [cover_lead, cover_own, cover_first, cover_second, cover_last]
    corners = [(0, 0), (per_device, 0), (per_device, 1), (middle, 1), (0, 4)]
    return solve(place, covers, corners, parts, factors)


def solution(mesh):
    return jax.shard_map(
        local,
        mesh=mesh,
        in_specs=(P("row"), P(None, None, "row"), P("row", "panel")),
        out_specs=P(("row", "panel"), None),
        check_vma=False,
    )
```
